32 devices in a mesh: seq: 8 (over z, y), chan: 2 (over x), dp: 2 (over core).
Axes of the slice: x: 2, y: 2, z: 4, core: 2. Of those that a mesh axis runs over, the one named last changes fastest.
Arguments:
- hidden: bfloat16 [2048, 2048], P(('dp', 'seq')), parts along dimension 0, may hold values from -6 to 6
- complement: bfloat16 [2048, 2048], P(('dp', 'seq')), parts along dimension 0, may hold values from -6 to 6
- inner_weight: bfloat16 [2048, 4096], P(None, 'chan'), may hold values from -0.125 to 0.125
- select_weight: bfloat16 [2048, 256], replicated, may hold values from -0.015625 to 0.015625
- step_weight: bfloat16 [2048, 64], P(None, 'chan'), may hold values from -0.125 to 0.125
- step_bias: float32 [64], P('chan'), may hold values from -4 to -2
- decay_rate: float32 [64], P('chan'), as said below
- skip_gain: float32 [64], P('chan'), may hold values from 0.5 to 2
- cotangent: bfloat16 [2048, 4096], P(('dp', 'seq'), 'chan'), parts along dimension 0, may hold values from -6 to 6
- complement_cotangent: bfloat16 [2048, 4096], P(('dp', 'seq'), 'chan'), parts along dimension 0, may hold values from -6 to 6
Outputs:
- mixed: bfloat16 [2048, 4096], P(('dp', 'seq'), 'chan'), parts along dimension 0
- mixed_complement: bfloat16 [2048, 4096], P(('dp', 'seq'), 'chan'), parts along dimension 0
- grad_hidden: bfloat16 [2048, 2048], P(('dp', 'seq'), 'chan'), parts along dimension 0
- grad_complement: bfloat16 [2048, 2048], P(('dp', 'seq'), 'chan'), parts along dimension 0
The draws below stay inside these ranges and needn't reach their ends.
There are 2 independent parts, one for each index of `dp`. The reference program is written for one: setup_inputs(seed, part) draws one part's arguments, and reference() takes and returns one part's arrays. A program takes and returns all parts, laid end to end along the dimension named above; an argument that names none is the same for every part. Nothing has to cross between parts.
Inputs may be any that keep to these rules, and one draw needn't show every extreme that they name: `decay_rate`: each head's decay rate lies between 7 / 1024 and 0.5.
All inputs are finite; a program needn't handle non-finite values.
Results may differ from the reference program's by a relative error of at most 0.006.
Values sent between devices are 32-bit elements; how exact they have to be, the bound alone decides.
No kernel may reach another device: no remote copies, remote signals or barrier semaphores. Data moves between devices by JAX's collectives and lax.ppermute only.
A program may use at most 192 MiB of HBM per device.

```python
import math
import jax
import jax.numpy as jnp
from jax import lax

D = 2048
HEAD_DIM = 64
STATE = 128
RD = 128
INNER = 4096
HEADS = 64
SEQ_LEN = 1024


def draw_decay_rate(key, part):
    pick_key, fast_key, slow_key = jax.random.split(key, 3)
    fast_share = 0.5
    chosen = jax.random.uniform(pick_key, (HEADS,)) < fast_share
    fast_rate = jnp.exp(jax.random.uniform(fast_key, (HEADS,), minval=math.log(0.3), maxval=math.log(0.5)))
    slow_rate = jnp.exp(jax.random.uniform(slow_key, (HEADS,), minval=math.log(7.0), maxval=math.log(28.0))) / SEQ_LEN
    return jnp.where(chosen, fast_rate, slow_rate).astype(jnp.float32)


def shard_levels(rng, dims, shards, low, largest):
    factor_of = 1.0
    for axis_at, parts in shards:
        heights = jax.random.uniform(jax.random.fold_in(jax.random.fold_in(rng, 6), axis_at), (parts,), jnp.float32, low / len(shards), largest / len(shards))
        factor_of = factor_of * jnp.repeat(jnp.exp(heights), dims[axis_at] // parts).reshape((-1,) + (1,) * (len(dims) - 1 - axis_at))
    return factor_of


def gaussian(stream_key, dims, deviation, most, pieces=(), held_as=jnp.bfloat16):
    level = shard_levels(stream_key, dims, pieces, -0.22, 0.18) if pieces else 1.0
    drawn = jax.random.normal(stream_key, dims, jnp.float32) * deviation * level
    return jnp.minimum(jnp.maximum(drawn, -most), most).astype(held_as)


def setup_inputs(seed: int = 0, part: int = 0) -> dict:
    arg_keys = jax.random.split(jax.random.key(seed), 11)
    part_splits = jax.random.split(jax.random.fold_in(arg_keys[10], part), 11)
    hidden = gaussian(part_splits[0], (SEQ_LEN, D), 1.0, 6.0, ((0, 8),))
    complement = gaussian(part_splits[1], (SEQ_LEN, D), 1.0, 6.0, ((0, 8),))
    inner_weight = gaussian(arg_keys[2], (D, INNER), D ** -0.5, 0.125, ((1, 2),))
    select_weight = gaussian(arg_keys[3], (D, 2 * STATE), (64 * D) ** -0.5, 0.015625)
    step_weight = gaussian(arg_keys[4], (D, HEADS), D ** -0.5, 0.125, ((1, 2),))
    step_bias = jnp.clip(-4.0 + 2.0 * jax.random.uniform(arg_keys[5], (HEADS,), jnp.float32) ** shard_levels(arg_keys[5], (HEADS,), ((0, 2),), -0.2, 0.2), -4.0, -2.0)
    decay_rate = draw_decay_rate(jax.random.fold_in(arg_keys[10], 71), part)
    skip_gain = jnp.clip(jnp.exp(math.log(2.0) - 1.3862944 * jax.random.uniform(arg_keys[7], (HEADS,), jnp.float32) ** shard_levels(arg_keys[7], (HEADS,), ((0, 2),), -0.2, 0.2)), 0.5, 2.0)
    cotangent = gaussian(part_splits[8], (SEQ_LEN, INNER), 1.0, 6.0, ((0, 8), (1, 2)))
    complement_cotangent = gaussian(part_splits[9], (SEQ_LEN, INNER), 1.0, 6.0, ((0, 8), (1, 2)))
    return {"hidden": hidden, "complement": complement, "inner_weight": inner_weight, "select_weight": select_weight, "step_weight": step_weight, "step_bias": step_bias, "decay_rate": decay_rate, "skip_gain": skip_gain, "cotangent": cotangent, "complement_cotangent": complement_cotangent}


highest = lax.Precision.HIGHEST

def summary(values, write_keys, step_sizes, decay_rate):
    cumulative = jnp.cumsum(-step_sizes * decay_rate[None, :], axis=0)
    tail_weights = jnp.exp(cumulative[-1][None, :] - cumulative) * step_sizes
    state_out = jnp.einsum('sh,shp,sn->hpn', tail_weights, values, write_keys, precision=highest)
    return (state_out, cumulative[-1])

def response(values, write_keys, read_keys, step_sizes, decay_rate, state_in):
    cumulative = jnp.cumsum(-step_sizes * decay_rate[None, :], axis=0)
    length = values.shape[0]
    causal = lax.broadcasted_iota(jnp.int32, (length, length), 0) >= lax.broadcasted_iota(jnp.int32, (length, length), 1)
    cum_heads = cumulative.T
    log_gaps = cum_heads[:, :, None] - cum_heads[:, None, :]
    decays = jnp.exp(jnp.where(causal[None, :, :], log_gaps, -1e+30))
    scores = jnp.dot(read_keys, write_keys.T, precision=highest)
    weights = decays * scores[None, :, :] * step_sizes.T[:, None, :]
    within = jnp.einsum('hts,shp->thp', weights, values, precision=highest)
    carried = jnp.exp(cumulative)[:, :, None] * jnp.einsum('tn,hpn->thp', read_keys, state_in, precision=highest)
    return within + carried

def one_direction(values, write_keys, read_keys, step_sizes, decay_rate):
    blocks = values.shape[0] // RD
    block_data = (values.reshape(blocks, RD, HEADS, HEAD_DIM), write_keys.reshape(blocks, RD, STATE), read_keys.reshape(blocks, RD, STATE), step_sizes.reshape(blocks, RD, HEADS))

    def advance(state_now, piece):
        output = response(piece[0], piece[1], piece[2], piece[3], decay_rate, state_now)
        state_part, total = summary(piece[0], piece[1], piece[3], decay_rate)
        return (jnp.exp(total)[:, None, None] * state_now + state_part, output)
    initial = jnp.zeros((HEADS, HEAD_DIM, STATE), jnp.float32)
    _, outputs = lax.scan(advance, initial, block_data)
    return outputs.reshape(values.shape)

def mixer_core(values, write_keys, read_keys, raw_steps, decay_rate, step_bias, skip_gain):
    step_sizes = jax.nn.softplus(raw_steps + step_bias[None, :])
    forward_out = one_direction(values, write_keys, read_keys, step_sizes, decay_rate)
    backward_out = jnp.flip(one_direction(jnp.flip(values, 0), jnp.flip(write_keys, 0), jnp.flip(read_keys, 0), jnp.flip(step_sizes, 0), decay_rate), 0)
    return forward_out + backward_out + skip_gain[None, :, None] * values

def strand(source, grad_out, inner_weight, select_weight, step_weight, step_bias, decay_rate, skip_gain):
    values = jnp.dot(source, inner_weight, preferred_element_type=jnp.float32).astype(jnp.bfloat16)
    keys = jnp.dot(source, select_weight, preferred_element_type=jnp.float32).astype(jnp.bfloat16)
    raw_steps = jnp.dot(source, step_weight, preferred_element_type=jnp.float32)
    length = source.shape[0]

    def run(value_in, write_in, read_in, raw_in):
        result = mixer_core(value_in.reshape(length, HEADS, HEAD_DIM), write_in, read_in, raw_in, decay_rate, step_bias, skip_gain)
        return result.reshape(length, HEADS * HEAD_DIM)
    output, pullback = jax.vjp(run, values.astype(jnp.float32), keys[:, :STATE].astype(jnp.float32), keys[:, STATE:].astype(jnp.float32), raw_steps)
    d_values, d_write, d_read, d_raw = pullback(grad_out.astype(jnp.float32))
    grad_term = jnp.dot(d_values.astype(jnp.bfloat16), inner_weight.T, preferred_element_type=jnp.float32)
    grad_term = grad_term + jnp.dot(jnp.concatenate([d_write, d_read], axis=1), select_weight.astype(jnp.float32).T, precision=highest)
    grad_term = grad_term + jnp.dot(d_raw, step_weight.astype(jnp.float32).T, precision=highest)
    return (output.astype(jnp.bfloat16), grad_term)

def reference(hidden, complement, inner_weight, select_weight, step_weight, step_bias, decay_rate, skip_gain, cotangent, complement_cotangent):
    mixed, grad_term = strand(hidden, cotangent, inner_weight, select_weight, step_weight, step_bias, decay_rate, skip_gain)
    source = jnp.flip(jnp.flip(complement, 1), 0)
    other_out, other_term = strand(source, jnp.flip(complement_cotangent, 0), inner_weight, select_weight, step_weight, step_bias, decay_rate, skip_gain)
    mixed_complement = jnp.flip(other_out, 0)
    grad_hidden = grad_term.astype(jnp.bfloat16)
    grad_complement = jnp.flip(jnp.flip(other_term, 0), 1).astype(jnp.bfloat16)
    return (mixed, mixed_complement, grad_hidden, grad_complement)
```

```python
import jax
import jax.numpy as jnp
from jax import lax
from jax.experimental import pallas as pl
from jax.experimental.pallas import tpu as pltpu
from jax.sharding import PartitionSpec as P

BF = jnp.bfloat16
F32 = jnp.float32
LANES = 128
VMEM_LIMIT = 56 * 1024 * 1024


def mm(a, b, ca=1, cb=0):
    return lax.dot_general(a, b, (((ca,), (cb,)), ((), ())), preferred_element_type=F32)


def halves(x):
    high = x.astype(BF)
    return high, (x - high.astype(F32)).astype(BF)


def mm_exact(a, b, ca=1, cb=0):
    first, rest = b.astype(BF), None
    rest = b - first.astype(F32)
    second = rest.astype(BF)
    third = (rest - second.astype(F32)).astype(BF)
    return mm(a, first, ca, cb) + mm(a, second, ca, cb) + mm(a, third, ca, cb)


def iotas(rows, columns):
    return (
        lax.broadcasted_iota(jnp.int32, (rows, columns), 0),
        lax.broadcasted_iota(jnp.int32, (rows, columns), 1),
    )


def spread(weights, base, width, head_width):
    heads = weights.shape[1]
    head, channel = iotas(heads, width)
    start = (head - base) * head_width
    pick = ((channel >= start) & (channel < start + head_width)).astype(BF)
    high, low = halves(weights)
    return mm(high, pick) + mm(low, pick)


def gather_heads(x, base, head_width):
    width = x.shape[1]
    channel, head = iotas(width, LANES)
    start = (head - base) * head_width
    pick = ((channel >= start) & (channel < start + head_width)).astype(BF)
    high, low = halves(x)
    return mm(high, pick) + mm(low, pick)


def reversal(size):
    i, j = iotas(size, size)
    return (i + j == size - 1).astype(BF)


def flip_block(size):
    return 256 if size % 256 == 0 else 128


def run(body, ins, outs, flops=0, scratch=(), bytes_moved=None):
    specs, arrays = [], []
    for item in ins:
        if isinstance(item, tuple):
            array, block, index = item
            specs.append(pl.BlockSpec(block, lambda i, index=index: index))
            arrays.append(array)
        elif item.dtype == jnp.int32:
            specs.append(pl.BlockSpec(memory_space=pltpu.SMEM))
            arrays.append(item)
        else:
            specs.append(pl.BlockSpec(item.shape, lambda i, n=item.ndim: (0,) * n))
            arrays.append(item)
    out_specs = [pl.BlockSpec(o.shape, lambda i, n=len(o.shape): (0,) * n) for o in outs]
    if bytes_moved is None:
        bytes_moved = sum(
            a.size * a.dtype.itemsize if not isinstance(t, tuple) else 2 * 128 * 1024
            for a, t in zip(arrays, ins)
        ) + sum(o.size * o.dtype.itemsize for o in outs)
    return pl.pallas_call(
        body,
        grid=(1,),
        in_specs=specs,
        out_specs=out_specs,
        out_shape=outs,
        scratch_shapes=list(scratch),
        compiler_params=pltpu.CompilerParams(vmem_limit_bytes=VMEM_LIMIT),
        cost_estimate=pl.CostEstimate(
            flops=flops, bytes_accessed=bytes_moved, transcendentals=0
        ),
    )(*arrays)


def sds(shape, dtype=F32):
    return jax.ShapeDtypeStruct(shape, dtype)


def project_body(hidden, other, weight, select, step, bias, rate, *rest):
    v_out, pack = rest[0], rest[1]
    wide = rest[2:-1]
    source = rest[-1]
    length, width = hidden.shape
    inner = weight.shape[1]
    heads = bias.shape[1]
    groups = len(wide) // 2
    chunk = inner // groups
    source[0:length, :] = hidden[...]
    block = flip_block(width)
    turn = reversal(block)
    for j in range(width // block):
        source[length : 2 * length, j * block : (j + 1) * block] = mm(
            other[:, width - (j + 1) * block : width - j * block], turn
        ).astype(BF)
    keys = mm(source[...], select[...]).astype(BF).astype(F32)
    state = keys.shape[1] // 2
    raw = mm(source[...], step[...]) + bias[...]
    dt = jnp.maximum(raw, 0.0) + jnp.log1p(jnp.exp(-jnp.abs(raw)))
    rise = jax.nn.sigmoid(raw)
    i, j = iotas(length, length)
    lower = (i >= j).astype(BF)
    pack[...] = jnp.zeros(pack.shape, F32)
    for s in range(2):
        rows = slice(s * length, (s + 1) * length)
        drop = dt[rows] * rate[...]
        total = mm_exact(lower, drop)
        pack[s, :, 0 : 2 * state] = keys[rows]
        at = 2 * state
        for part in (dt[rows], total, total - drop, rise[rows]):
            pack[s, :, at : at + heads] = part
            at += heads
    step_width = min(256, chunk)
    for k in range(inner // step_width):
        columns = slice(k * step_width, (k + 1) * step_width)
        piece = mm(source[...], weight[:, columns]).astype(BF)
        group, start = divmod(k * step_width, chunk)
        for s in range(2):
            rows = slice(s * length, (s + 1) * length)
            v_out[s, :, columns] = piece[rows]
            wide[s * groups + group][:, start : start + step_width] = piece[rows].astype(F32)


class Pack:
    def __init__(self, ref, heads):
        state = LANES
        self.write = ref[0, :, 0:state]
        self.read = ref[0, :, state : 2 * state]
        at = 2 * state
        self.dt = ref[0, :, at : at + heads]
        self.total = ref[0, :, at + heads : at + 2 * heads]
        self.before = ref[0, :, at + 2 * heads : at + 3 * heads]
        self.rise = ref[0, :, at + 3 * heads : at + 4 * heads]
        last = self.total.shape[0]
        self.whole = self.total[last - 1 : last, :]
        self.from_start = jnp.exp(-self.total)
        self.from_end = jnp.exp(self.before - self.whole)
        self.to_end = jnp.exp(self.total - self.whole)
        self.to_start = jnp.exp(-self.before)
        self.through = jnp.exp(-self.whole)


def pair_states(kind, base, heads, head_width):
    def body(place, x_own, x_far, own_ref, far_ref, up, down, near, keep):
        first = place[0] == 0
        own, far = Pack(own_ref, heads), Pack(far_ref, heads)
        width = x_far.shape[1]

        def local(pack, x):
            if kind == "value":
                key, w_up, w_down = pack.write, pack.dt * pack.to_end, pack.dt * pack.to_start
            else:
                key, w_up, w_down = pack.read, pack.from_end, pack.from_start
            key = key.astype(BF)
            x = x.astype(F32)
            return (
                mm(key, (spread(w_up, base, width, head_width) * x).astype(BF), 0, 0),
                mm(key, (spread(w_down, base, width, head_width) * x).astype(BF), 0, 0),
            )

        own_up, own_down = local(own, x_own[0])
        far_up, far_down = local(far, x_far[...])
        wide = lambda row: spread(jnp.broadcast_to(row, (8, heads)), base, width, head_width)[0:1]
        own_row, far_row = wide(own.through), wide(far.through)
        up[...] = jnp.where(first, own_up * far_row + far_up, far_up * own_row + own_up)
        down[...] = jnp.where(first, far_down * own_row + own_down, own_down * far_row + far_down)
        near[...] = jnp.where(first, far_down, far_up)
        keep[...] = jnp.broadcast_to(own_row * far_row, keep.shape)

    return body


def within_body(heads, head_width):
    def body(own_ref, v_ref, g_ref, skip, rate, y_out, x_out, keys_out, steps_out, rows_s, cols_s):
        own = Pack(own_ref, heads)
        length = own.dt.shape[0]
        write, read = own.write.astype(BF), own.read.astype(BF)
        scores = mm(read, write, 1, 1)
        i, j = iotas(length, length)
        low = i > j
        high = i < j
        doubled = jnp.where(i == j, 2.0, 1.0).astype(F32)
        scores2 = scores * doubled
        turned = own_ref[0, :, 2 * LANES : 3 * LANES].T
        lane = lax.broadcasted_iota(jnp.int32, (length, LANES), 1)
        d_scores = jnp.zeros((length, length), F32)
        out_low = jnp.zeros((length, LANES), F32)
        out_high = jnp.zeros((length, LANES), F32)
        cols_s[...] = jnp.zeros(cols_s.shape, F32)
        ys, xs = [], []
        for h in range(heads):
            c_col = own.total[:, h : h + 1]
            e_col = own.before[:, h : h + 1]
            dt_row = turned[h : h + 1, :]
            c_row = turned[heads + h : heads + h + 1, :]
            e_row = turned[2 * heads + h : 2 * heads + h + 1, :]
            decay = jnp.exp(jnp.where(low, c_row - c_col, e_col - e_row))
            v = v_ref[0, :, h * head_width : (h + 1) * head_width]
            g = g_ref[:, h * head_width : (h + 1) * head_width]
            plain = decay * scores2
            stepped = decay * dt_row
            ys.append(mm((plain * dt_row).astype(BF), v))
            xs.append(mm(plain.astype(BF), g, 0, 0))
            inner = stepped * mm(g, v, 1, 1)
            d_scores = d_scores + inner
            flow = inner * scores
            flow_low = jnp.where(low, flow, 0.0)
            flow_high = jnp.where(high, flow, 0.0)
            out_low = jnp.where(lane == h, jnp.sum(flow_low, 1, keepdims=True), out_low)
            out_high = jnp.where(lane == h, jnp.sum(flow_high, 1, keepdims=True), out_high)
            cols_s[0, h : h + 1, :] = jnp.sum(flow_low, 0, keepdims=True)
            cols_s[1, h : h + 1, :] = jnp.sum(flow_high, 0, keepdims=True)
            if (h + 1) * head_width % LANES == 0:
                per = LANES // head_width
                at = slice((h + 1) * head_width - LANES, (h + 1) * head_width)
                y_out[:, at] = jnp.concatenate(ys[-per:], axis=1)
                x_out[:, at] = jnp.concatenate(xs[-per:], axis=1)
        d_scores = (d_scores * doubled).astype(BF)
        keys_out[:, 0:LANES] = mm(d_scores, read, 0, 0)
        keys_out[:, LANES : 2 * LANES] = mm(d_scores, write)
        net_low = out_low - cols_s[0].T
        net_high = out_high - cols_s[1].T
        at_or_after = (j >= i).astype(BF)
        after = (j > i).astype(BF)
        steps_out[...] = -rate[...] * (mm_exact(at_or_after, net_low) - mm_exact(after, net_high))

    return body


def post_body(base, heads, head_width):
    def body(
        place, own_ref, far_ref, v_ref, g_ref, yw, xw, p_in, q_in, af_in, ab_in, near_v, near_g,
        skip, rate, mixed, dv_out, keys_out, steps_out,
    ):
        first = place[0] == 0
        own, far = Pack(own_ref, heads), Pack(far_ref, heads)
        width = p_in.shape[1]
        wide = lambda w: spread(w, base, width, head_width)
        far_row = wide(jnp.broadcast_to(far.through, (8, heads)))[0:1]
        up_row = jnp.where(first, 1.0, far_row)
        down_row = jnp.where(first, far_row, 1.0)
        own_v, own_g = near_v[...], near_g[...]
        p = up_row * p_in[...] + jnp.where(first, 0.0, own_v)
        ab = up_row * ab_in[...] + jnp.where(first, 0.0, own_g)
        q = down_row * q_in[...] + jnp.where(first, own_v, 0.0)
        af = down_row * af_in[...] + jnp.where(first, own_g, 0.0)
        crossing = jnp.sum(p * af + q * ab, axis=0, keepdims=True)
        p, q, af, ab = p.astype(BF), q.astype(BF), af.astype(BF), ab.astype(BF)
        write, read = own.write.astype(BF), own.read.astype(BF)
        v = v_ref[0].astype(F32)
        g = g_ref[...].astype(F32)
        dt = wide(own.dt)
        from_start, from_end = wide(own.from_start), wide(own.from_end)
        to_end, to_start = wide(own.to_end), wide(own.to_start)
        gain = wide(jnp.broadcast_to(skip[...], (8, heads)))[0:1]
        y_p = from_start * mm(read, p)
        y_q = from_end * mm(read, q)
        x_f = to_end * mm(write, af)
        x_b = to_start * mm(write, ab)
        mixed[...] = (yw[...] + y_p + y_q + gain * v).astype(BF)
        x = xw[...] + x_f + x_b
        dv_out[...] = (dt * x + gain * g).astype(BF)
        keys_out[:, 0:LANES] = mm((dt * to_end * v).astype(BF), af, 1, 1) + mm(
            (dt * to_start * v).astype(BF), ab, 1, 1
        )
        keys_out[:, LANES : 2 * LANES] = mm((from_start * g).astype(BF), p, 1, 1) + mm(
            (from_end * g).astype(BF), q, 1, 1
        )
        length = v.shape[0]
        lane = lax.broadcasted_iota(jnp.int32, (length, LANES), 1)
        steps = jnp.where(lane < heads, own_ref[0, :, 2 * LANES : 3 * LANES], 0.0)
        direct = gather_heads(v * x, base, head_width)
        a_p = gather_heads(g * y_p, base, head_width)
        a_q = gather_heads(g * y_q, base, head_width)
        b_f = gather_heads(v * x_f, base, head_width) * steps
        b_b = gather_heads(v * x_b, base, head_width) * steps
        through = gather_heads(
            jnp.broadcast_to(crossing * wide(jnp.broadcast_to(own.through, (8, heads)))[0:1], (8, width)),
            base, head_width,
        )[0:1]
        i, j = iotas(length, length)
        flow = (
            mm_exact((j >= i).astype(BF), a_p)
            + mm_exact((j < i).astype(BF), b_f)
            + mm_exact((j <= i).astype(BF), a_q)
            + mm_exact((j > i).astype(BF), b_b)
            + through
        )
        steps_out[...] = direct - rate[...] * flow

    return body


def term_body(groups, heads, parts, swap):
    def body(place, own_ref, weight, select, step, keys_w, steps_w, *rest):
        dvs = rest[0:groups]
        keys = rest[groups : 2 * groups]
        steps = rest[2 * groups : 3 * groups]
        outs = rest[3 * groups :]
        chunk = dvs[0].shape[1]
        d_keys = keys_w[...]
        d_steps = steps_w[...]
        for a, b in zip(keys, steps):
            d_keys = d_keys + a[...]
            d_steps = d_steps + b[...]
        d_raw = d_steps[:, 0:heads] * own_ref[0, :, 2 * LANES + 3 * heads : 2 * LANES + 4 * heads]
        keys_high, keys_low = halves(d_keys)
        raw_high, raw_low = halves(d_raw)
        width = weight.shape[0]
        block = width // parts
        tiles = []
        for b in range(parts):
            rows = slice(b * block, (b + 1) * block)
            total = mm(keys_high, select[rows, :], 1, 1) + mm(keys_low, select[rows, :], 1, 1)
            total = total + mm(raw_high, step[rows, :], 1, 1) + mm(raw_low, step[rows, :], 1, 1)
            for k in range(groups):
                total = total + mm(
                    dvs[k][...], weight[rows, k * chunk : (k + 1) * chunk], 1, 1
                )
            tiles.append(total)
        if swap:
            tiles = tiles[::-1]
        if parts == 2:
            first = place[1] == 0
            outs[0][...] = jnp.where(first, tiles[0], tiles[1])
            outs[1][...] = jnp.where(first, tiles[1], tiles[0])
        else:
            for b in range(parts):
                outs[0][:, b * block : (b + 1) * block] = tiles[b]

    return body


def finish_body(flip):
    def body(a, b, out):
        total = (a[...] + b[...]).astype(BF)
        if not flip:
            out[...] = total
            return
        width = total.shape[1]
        block = flip_block(width)
        turn = reversal(block)
        for j in range(width // block):
            out[:, j * block : (j + 1) * block] = mm(
                total[:, width - (j + 1) * block : width - j * block], turn
            ).astype(BF)

    return body


def widen_body(x, *outs):
    chunk = outs[0].shape[1]
    for k, out in enumerate(outs):
        out[...] = x[:, k * chunk : (k + 1) * chunk].astype(F32)


def choose(options, index):
    like = next(o for o in options if o is not None)
    result = None
    for k, option in enumerate(options):
        option = jnp.zeros_like(like) if option is None else option
        result = option if result is None else jnp.where(index == k, option, result)
    return result


def local(shards, parts):
    pairs = shards // 2

    def body(
        hidden, complement, inner_weight, select_weight, step_weight, step_bias, decay_rate,
        skip_gain, cotangent, complement_cotangent,
    ):
        length, width = hidden.shape
        inner = inner_weight.shape[1]
        heads = step_bias.shape[0]
        head_width = inner // heads
        groups = 2
        chunk = inner // groups
        group_heads = heads // groups
        seq = lax.axis_index("seq")
        pair = seq // 2
        place = jnp.stack([seq % 2, lax.axis_index("chan")]).astype(jnp.int32)
        bias = step_bias.reshape(1, heads)
        rate = decay_rate.reshape(1, heads)
        rate_row = jnp.pad(rate, ((0, 0), (0, LANES - heads)))
        gain = skip_gain.reshape(1, heads)
        cots = (cotangent, complement_cotangent)

        swap_pairs = [(a, a ^ 1) for a in range(shards)]
        up_pairs = [(a, a + 2) for a in range(shards - 2)]
        down_pairs = [(a + 2, a) for a in range(shards - 2)]
        swap = lambda x: lax.ppermute(x, "seq", swap_pairs)

        wide_g = [
            run(widen_body, [cots[s]], [sds((length, chunk))] * groups) for s in range(2)
        ]
        far_g = [[None] * groups for _ in range(2)]
        far_v = [[None] * groups for _ in range(2)]
        projected = run(
            project_body,
            [hidden, complement, inner_weight, select_weight, step_weight, bias, rate],
            [sds((2, length, inner), BF), sds((2, length, 3 * LANES))]
            + [sds((length, chunk))] * (2 * groups),
            flops=4 * length * width * inner,
            scratch=[pltpu.VMEM((2 * length, width), BF)],
        )
        values, pack = projected[0], projected[1]
        wide_v = [projected[2 + s * groups : 2 + (s + 1) * groups] for s in range(2)]
        far_pack = swap(pack)
        for s in range(2):
            for k in range(groups):
                far_g[s][k] = swap(wide_g[s][k])
                far_v[s][k] = swap(wide_v[s][k])

        def pack_of(array, s):
            return (array, (1, length, 3 * LANES), (s, 0, 0))

        within = [
            run(
                within_body(heads, head_width),
                [pack_of(pack, s), (values, (1, length, inner), (s, 0, 0)), cots[s], gain, rate_row],
                [sds((length, inner)), sds((length, inner)), sds((length, 2 * LANES)), sds((length, LANES))],
                flops=heads * 6 * length * length * head_width,
                scratch=[pltpu.VMEM((8, LANES), F32), pltpu.VMEM((2, LANES, length), F32)],
                bytes_moved=24 * 1024 * 1024,
            )
            for s in range(2)
        ]

        order = [(s, kind, k) for s in range(2) for k in range(groups) for kind in ("grad", "value")]
        totals = {}
        for s, kind, k in order:
            own = (
                (values, (1, length, chunk), (s, 0, k))
                if kind == "value"
                else (cots[s][None], (1, length, chunk), (0, 0, k))
            )
            far = far_v[s][k] if kind == "value" else far_g[s][k]
            totals[s, kind, k] = run(
                pair_states(kind, k * group_heads, heads, head_width),
                [place, own, far, pack_of(pack, s), pack_of(far_pack, s)],
                [sds((LANES, chunk))] * 3 + [sds((8, chunk))],
                flops=8 * length * LANES * chunk,
            )

        chunks = len(order)
        up_got, down_got = [], []
        for step in range(chunks + pairs - 2):
            def at(item):
                return [
                    totals[order[step - z]][item] if 0 <= step - z < chunks else None
                    for z in range(pairs)
                ]

            back = pairs - 1 - pair
            up_now, down_now = choose(at(0), pair), choose(at(1), back)
            if step > 0:
                keeps = at(3)
                up_now = up_now + choose(keeps, pair)[0:1] * up_got[-1]
                down_now = down_now + choose(keeps, back)[0:1] * down_got[-1]
            up_got.append(lax.ppermute(up_now, "seq", up_pairs))
            down_got.append(lax.ppermute(down_now, "seq", down_pairs))

        def incoming(got, number, position):
            return choose([got[number]] + [got[number + z - 1] for z in range(1, pairs)], position)

        outs = []
        grads = []
        for s in range(2):
            mixed, dvs, d_keys, d_steps = [], [], [], []
            for k in range(groups):
                at_v, at_g = order.index((s, "value", k)), order.index((s, "grad", k))
                back = pairs - 1 - pair
                part = run(
                    post_body(k * group_heads, heads, head_width),
                    [
                        place, pack_of(pack, s), pack_of(far_pack, s),
                        (values, (1, length, chunk), (s, 0, k)),
                        (cots[s], (length, chunk), (0, k)),
                        (within[s][0], (length, chunk), (0, k)),
                        (within[s][1], (length, chunk), (0, k)),
                        incoming(up_got, at_v, pair), incoming(down_got, at_v, back),
                        incoming(down_got, at_g, back), incoming(up_got, at_g, pair),
                        totals[s, "value", k][2], totals[s, "grad", k][2],
                        gain, rate_row,
                    ],
                    [sds((length, chunk), BF), sds((length, chunk), BF), sds((length, 2 * LANES)), sds((length, LANES))],
                    flops=16 * length * LANES * chunk,
                )
                mixed.append(part[0])
                dvs.append(part[1])
                d_keys.append(part[2])
                d_steps.append(part[3])
            outs.append(jnp.concatenate(mixed, axis=1))
            shares = (
                [sds((length, width // 2))] * 2 if parts == 2 else [sds((length, width))]
            )
            term = run(
                term_body(groups, heads, parts, s == 1),
                [place, pack_of(pack, s), inner_weight, select_weight, step_weight,
                 within[s][2], within[s][3], *dvs, *d_keys, *d_steps],
                shares,
                flops=2 * length * width * inner,
            )
            if parts == 2:
                mine, other = term[0], lax.ppermute(term[1], "chan", [(0, 1), (1, 0)])
            else:
                mine = lax.psum_scatter(term[0], "chan", scatter_dimension=1, tiled=True)
                other = jnp.zeros_like(mine)
            grads.append(
                run(finish_body(s == 1), [mine, other], [sds((length, width // parts), BF)])[0]
            )
        return (outs[0], outs[1], grads[0], grads[1])

    return body


def solution(mesh):
    rows = P(("dp", "seq"), None)
    both = P(("dp", "seq"), "chan")
    in_specs = (
        rows, rows, P(None, "chan"), P(), P(None, "chan"),
        P("chan"), P("chan"), P("chan"), both, both,
    )
    return jax.shard_map(
        local(mesh.shape["seq"], mesh.shape["chan"]),
        mesh=mesh,
        in_specs=in_specs,
        out_specs=(both,) * 4,
        check_vma=False,
    )
```

```python
import jax
import jax.numpy as jnp
from jax import lax
from jax.experimental import pallas as pl
from jax.experimental.pallas import tpu as pltpu
from jax.sharding import PartitionSpec as P

BF = jnp.bfloat16
F32 = jnp.float32
LANES = 128


def mm(a, b, ca=1, cb=0):
    return lax.dot_general(a, b, (((ca,), (cb,)), ((), ())), preferred_element_type=F32)


def halves(x):
    high = x.astype(BF)
    return high, (x - high.astype(F32)).astype(BF)


def mm_exact(a, b, ca=1, cb=0):
    first, rest = b.astype(BF), None
    rest = b - first.astype(F32)
    second = rest.astype(BF)
    third = (rest - second.astype(F32)).astype(BF)
    return mm(a, first, ca, cb) + mm(a, second, ca, cb) + mm(a, third, ca, cb)


def iotas(rows, columns):
    return (
        lax.broadcasted_iota(jnp.int32, (rows, columns), 0),
        lax.broadcasted_iota(jnp.int32, (rows, columns), 1),
    )


def spread(weights, base, width, head_width):
    heads = weights.shape[1]
    head, channel = iotas(heads, width)
    start = (head - base) * head_width
    pick = ((channel >= start) & (channel < start + head_width)).astype(BF)
    high, low = halves(weights)
    return mm(high, pick) + mm(low, pick)


def gather_heads(x, base, head_width):
    width = x.shape[1]
    channel, head = iotas(width, LANES)
    start = (head - base) * head_width
    pick = ((channel >= start) & (channel < start + head_width)).astype(BF)
    high, low = halves(x)
    return mm(high, pick) + mm(low, pick)


def reversal(size):
    i, j = iotas(size, size)
    return (i + j == size - 1).astype(BF)


def flip_block(size):
    return 256 if size % 256 == 0 else 128


def sds(shape, dtype=F32):
    return jax.ShapeDtypeStruct(shape, dtype)


class Block:
    def __init__(self, array, shape, index):
        self.array, self.shape, self.index = array, shape, index


class Far:
    def __init__(self, array):
        self.array = array


def run(body, ins, outs, scratch=(), limit=24):
    specs, arrays = [], []
    for item in ins:
        if isinstance(item, Block):
            specs.append(pl.BlockSpec(item.shape, lambda i, index=item.index: index))
            arrays.append(item.array)
        elif isinstance(item, Far):
            specs.append(pl.BlockSpec(memory_space=pl.ANY))
            arrays.append(item.array)
        elif item.dtype == jnp.int32:
            specs.append(pl.BlockSpec(memory_space=pltpu.SMEM))
            arrays.append(item)
        else:
            specs.append(pl.BlockSpec(item.shape, lambda i, n=item.ndim: (0,) * n))
            arrays.append(item)
    out_specs = [pl.BlockSpec(o.shape, lambda i, n=len(o.shape): (0,) * n) for o in outs]
    return pl.pallas_call(
        body,
        grid=(1,),
        in_specs=specs,
        out_specs=out_specs,
        out_shape=outs,
        scratch_shapes=list(scratch),
        compiler_params=pltpu.CompilerParams(vmem_limit_bytes=limit * 1024 * 1024),
        cost_estimate=pl.CostEstimate(flops=0, bytes_accessed=1024, transcendentals=0),
    )(*arrays)


def start_body(hidden, other, weight, select, step, bias, rate, cot, v_out, source, pack0, pack1, wide):
    length, width = hidden.shape
    heads = bias.shape[1]
    source[0:length, :] = hidden[...]
    block = flip_block(width)
    turn = reversal(block)
    for j in range(width // block):
        source[length : 2 * length, j * block : (j + 1) * block] = mm(
            other[:, width - (j + 1) * block : width - j * block], turn
        ).astype(BF)
    keys = mm(source[...], select[...]).astype(BF).astype(F32)
    state = keys.shape[1] // 2
    raw = mm(source[...], step[...]) + bias[...]
    dt = jnp.maximum(raw, 0.0) + jnp.log1p(jnp.exp(-jnp.abs(raw)))
    rise = jax.nn.sigmoid(raw)
    i, j = iotas(length, length)
    lower = (i >= j).astype(BF)
    for s, pack in enumerate((pack0, pack1)):
        rows = slice(s * length, (s + 1) * length)
        drop = dt[rows] * rate[...]
        total = mm_exact(lower, drop)
        pack[...] = jnp.zeros(pack.shape, F32)
        pack[:, 0 : 2 * state] = keys[rows]
        at = 2 * state
        for part in (dt[rows], total, total - drop, rise[rows]):
            pack[:, at : at + heads] = part
            at += heads
    piece = mm(source[...], weight[...]).astype(BF)
    for s in range(2):
        v_out[s] = piece[s * length : (s + 1) * length]
    wide[0:length, :] = piece[0:length].astype(F32)
    wide[length : 2 * length, :] = cot[...].astype(F32)


def more_body(source, weight, v_out):
    length = v_out.shape[2]
    piece = mm(source[...], weight[...]).astype(BF)
    for s in range(2):
        v_out[0, s] = piece[s * length : (s + 1) * length]


class Pack:
    def __init__(self, ref, heads):
        state = LANES
        self.write = ref[:, 0:state]
        self.read = ref[:, state : 2 * state]
        at = 2 * state
        self.dt = ref[:, at : at + heads]
        self.total = ref[:, at + heads : at + 2 * heads]
        self.before = ref[:, at + 2 * heads : at + 3 * heads]
        self.rise = ref[:, at + 3 * heads : at + 4 * heads]
        last = self.total.shape[0]
        self.whole = self.total[last - 1 : last, :]
        self.from_start = jnp.exp(-self.total)
        self.from_end = jnp.exp(self.before - self.whole)
        self.to_end = jnp.exp(self.total - self.whole)
        self.to_start = jnp.exp(-self.before)
        self.through = jnp.exp(-self.whole)


def pair_body(base, heads, head_width):
    def body(place, v_own, g_own, x_far, own_ref, far_ref, token, up, down, near, keep):
        first = place[0] == 0
        own, far = Pack(own_ref, heads), Pack(far_ref, heads)
        length, width = g_own.shape
        wide = lambda row: spread(jnp.broadcast_to(row, (8, heads)), base, width, head_width)[0:1]
        own_row, far_row = wide(own.through), wide(far.through)
        keep[...] = jnp.broadcast_to(own_row * far_row, keep.shape)

        def local(key, w_up, w_down, x):
            key = key.astype(BF)
            return (
                mm(key, (spread(w_up, base, width, head_width) * x).astype(BF), 0, 0),
                mm(key, (spread(w_down, base, width, head_width) * x).astype(BF), 0, 0),
            )

        def value(pack, x):
            return local(pack.write, pack.dt * pack.to_end, pack.dt * pack.to_start, x)

        def grad(pack, x):
            return local(pack.read, pack.from_end, pack.from_start, x)

        for kind, x_own, at in ((value, v_own, 0), (grad, g_own, length)):
            rows = slice(at, at + LANES)
            x = x_own[...].reshape(length, width).astype(F32)
            own_up, own_down = kind(own, x)
            far_up, far_down = kind(far, x_far[at : at + length, :])
            up[rows, :] = jnp.where(first, own_up * far_row + far_up, far_up * own_row + own_up)
            down[rows, :] = jnp.where(
                first, far_down * own_row + own_down, own_down * far_row + far_down
            )
            near[rows, :] = jnp.where(first, far_down, far_up)

    return body


def fetch_start(options, index, target, sem):
    for z, option in enumerate(options):
        if option is not None:

            @pl.when(index == z)
            def _():
                pltpu.make_async_copy(option, target, sem).start()


def fetch_wait(options, index, target, sem):
    for z, option in enumerate(options):
        if option is not None:

            @pl.when(index == z)
            def _():
                pltpu.make_async_copy(option, target, sem).wait()


def step_body(up_has, down_has, first_step, widen, tokens):
    pairs = len(up_has)

    def body(place, *rest):
        rest = list(rest)
        take = lambda n: [rest.pop(0) for _ in range(n)]
        sides = []
        for has in (up_has, down_has):
            totals = [take(1)[0] if h else None for h in has]
            keeps = [take(1)[0] if h else None for h in has]
            got = None if first_step else take(1)[0]
            sides.append((totals, keeps, got, has))
        if widen:
            v_ref, g_ref = take(2)
        take(tokens)
        sends = take(2)
        token = take(1)[0]
        wide = take(1)[0] if widen else None
        bufs, sems = take(2)
        spots = (place[1], pairs - 1 - place[1])
        for d, (totals, keeps, got, has) in enumerate(sides):
            fetch_start(totals, spots[d], bufs.at[d], sems.at[d])
        if widen:
            length, width = g_ref.shape
            wide[0:length, :] = v_ref[...].reshape(length, width).astype(F32)
            wide[length : 2 * length, :] = g_ref[...].astype(F32)
        token[...] = jnp.zeros(token.shape, F32)
        for d, (totals, keeps, got, has) in enumerate(sides):
            fetch_wait(totals, spots[d], bufs.at[d], sems.at[d])
            for z in range(pairs):

                @pl.when(spots[d] == z)
                def _():
                    if not has[z]:
                        sends[d][...] = jnp.zeros(sends[d].shape, F32)
                    elif got is None or z == 0:
                        sends[d][...] = bufs[d]
                    else:
                        sends[d][...] = bufs[d] + keeps[z][0:1, :] * got[...]

    return body


def within_body(base, heads, head_width):
    def body(own_ref, v_ref, g_ref, rate, token, y_out, x_out, keys_out, steps_out, cols_s):
        own = Pack(own_ref, heads)
        length, width = g_ref.shape
        write, read = own.write.astype(BF), own.read.astype(BF)
        scores = mm(read, write, 1, 1)
        i, j = iotas(length, length)
        low = i > j
        high = i < j
        doubled = jnp.where(i == j, 2.0, 1.0).astype(F32)
        scores2 = scores * doubled
        turned = own_ref[:, 2 * LANES : 3 * LANES].T
        lane = lax.broadcasted_iota(jnp.int32, (length, LANES), 1)
        d_scores = jnp.zeros((length, length), F32)
        out_low = jnp.zeros((length, LANES), F32)
        out_high = jnp.zeros((length, LANES), F32)
        cols_s[...] = jnp.zeros(cols_s.shape, F32)
        v_all = v_ref[...].reshape(length, width)
        ys, xs = [], []
        for n in range(width // head_width):
            h = base + n
            c_col = own.total[:, h : h + 1]
            e_col = own.before[:, h : h + 1]
            dt_row = turned[h : h + 1, :]
            c_row = turned[heads + h : heads + h + 1, :]
            e_row = turned[2 * heads + h : 2 * heads + h + 1, :]
            decay = jnp.exp(jnp.where(low, c_row - c_col, e_col - e_row))
            v = v_all[:, n * head_width : (n + 1) * head_width]
            g = g_ref[:, n * head_width : (n + 1) * head_width]
            plain = decay * scores2
            ys.append(mm((plain * dt_row).astype(BF), v))
            xs.append(mm(plain.astype(BF), g, 0, 0))
            inner = decay * dt_row * mm(g, v, 1, 1)
            d_scores = d_scores + inner
            flow = inner * scores
            flow_low = jnp.where(low, flow, 0.0)
            flow_high = jnp.where(high, flow, 0.0)
            out_low = jnp.where(lane == h, jnp.sum(flow_low, 1, keepdims=True), out_low)
            out_high = jnp.where(lane == h, jnp.sum(flow_high, 1, keepdims=True), out_high)
            cols_s[0, h : h + 1, :] = jnp.sum(flow_low, 0, keepdims=True)
            cols_s[1, h : h + 1, :] = jnp.sum(flow_high, 0, keepdims=True)
            if (n + 1) * head_width % LANES == 0:
                per = LANES // head_width
                at = slice((n + 1) * head_width - LANES, (n + 1) * head_width)
                y_out[:, at] = jnp.concatenate(ys[-per:], axis=1)
                x_out[:, at] = jnp.concatenate(xs[-per:], axis=1)
        d_scores = (d_scores * doubled).astype(BF)
        keys_out[:, 0:LANES] = mm(d_scores, read, 0, 0)
        keys_out[:, LANES : 2 * LANES] = mm(d_scores, write)
        net_low = out_low - cols_s[0].T
        net_high = out_high - cols_s[1].T
        at_or_after = (j >= i).astype(BF)
        after = (j > i).astype(BF)
        steps_out[...] = -rate[...] * (mm_exact(at_or_after, net_low) - mm_exact(after, net_high))

    return body


def post_body(base, heads, head_width, ups, downs):
    def body(
        place, own_ref, far_ref, v_ref, g_ref, yw, xw, keys_w, steps_w, near, skip, rate, token, *rest
    ):
        up_in, down_in = rest[0:ups], rest[ups : ups + downs]
        mixed, dv_out, keys_out, steps_out, bufs, sems = rest[ups + downs :]
        last = len(up_in)
        up_spot = jnp.maximum(place[1] - 1, 0)
        down_spot = jnp.maximum(last - 1 - place[1], 0)
        fetch_start(up_in, up_spot, bufs.at[0], sems.at[0])
        fetch_start(down_in, down_spot, bufs.at[1], sems.at[1])
        first = place[0] == 0
        own, far = Pack(own_ref, heads), Pack(far_ref, heads)
        length, width = g_ref.shape
        wide = lambda w: spread(w, base, width, head_width)
        far_row = wide(jnp.broadcast_to(far.through, (8, heads)))[0:1]
        own_row = wide(jnp.broadcast_to(own.through, (8, heads)))[0:1]
        gain = wide(jnp.broadcast_to(skip[...], (8, heads)))[0:1]
        up_row = jnp.where(first, 1.0, far_row)
        down_row = jnp.where(first, far_row, 1.0)
        dt = wide(own.dt)
        from_start, from_end = wide(own.from_start), wide(own.from_end)
        to_end, to_start = wide(own.to_end), wide(own.to_start)
        write, read = own.write.astype(BF), own.read.astype(BF)
        v = v_ref[...].reshape(length, width).astype(F32)
        g = g_ref[...].astype(F32)
        fetch_wait(up_in, up_spot, bufs.at[0], sems.at[0])
        fetch_wait(down_in, down_spot, bufs.at[1], sems.at[1])
        up = up_row * bufs[0] + jnp.where(first, 0.0, near[...])
        down = down_row * bufs[1] + jnp.where(first, near[...], 0.0)
        p, ab = up[0:LANES], up[LANES : 2 * LANES]
        q, af = down[0:LANES], down[LANES : 2 * LANES]
        crossing = jnp.sum(p * af + q * ab, axis=0, keepdims=True)
        p, q, af, ab = p.astype(BF), q.astype(BF), af.astype(BF), ab.astype(BF)
        y_p = from_start * mm(read, p)
        y_q = from_end * mm(read, q)
        x_f = to_end * mm(write, af)
        x_b = to_start * mm(write, ab)
        mixed[...] = (yw[...] + y_p + y_q + gain * v).astype(BF)
        x = xw[...] + x_f + x_b
        dv_out[...] = (dt * x + gain * g).astype(BF)
        dtv = dt * v
        keys_out[:, 0:LANES] = (
            keys_w[:, 0:LANES]
            + mm((to_end * dtv).astype(BF), af, 1, 1)
            + mm((to_start * dtv).astype(BF), ab, 1, 1)
        )
        keys_out[:, LANES : 2 * LANES] = (
            keys_w[:, LANES : 2 * LANES]
            + mm((from_start * g).astype(BF), p, 1, 1)
            + mm((from_end * g).astype(BF), q, 1, 1)
        )
        lane = lax.broadcasted_iota(jnp.int32, (length, LANES), 1)
        steps = jnp.where(lane < heads, own_ref[:, 2 * LANES : 3 * LANES], 0.0)
        direct = gather_heads(v * x, base, head_width)
        a_p = gather_heads(g * y_p, base, head_width)
        a_q = gather_heads(g * y_q, base, head_width)
        b_f = gather_heads(v * x_f, base, head_width) * steps
        b_b = gather_heads(v * x_b, base, head_width) * steps
        through = gather_heads(
            jnp.broadcast_to(crossing * own_row, (8, width)), base, head_width
        )[0:1]
        i, j = iotas(length, length)
        flow = (
            mm_exact((j >= i).astype(BF), a_p)
            + mm_exact((j < i).astype(BF), b_f)
            + mm_exact((j <= i).astype(BF), a_q)
            + mm_exact((j > i).astype(BF), b_b)
            + through
        )
        steps_out[...] = steps_w[...] + direct - rate[...] * flow

    return body


def partial_body(groups):
    def body(token, *rest):
        dvs, weights, out = rest[0:groups], rest[groups : 2 * groups], rest[2 * groups]
        total = mm(dvs[0][...], weights[0][...], 1, 1)
        for k in range(1, groups):
            total = total + mm(dvs[k][...], weights[k][...], 1, 1)
        out[...] = total

    return body


def term_body(groups, tails, heads, parts, swap):
    def body(place, own_ref, select, step, before, *rest):
        dvs, weights = rest[0:tails], rest[tails : 2 * tails]
        rest = rest[2 * tails :]
        keys, steps = rest[0:groups], rest[groups : 2 * groups]
        outs = rest[2 * groups :]
        d_keys, d_steps = keys[0][...], steps[0][...]
        for a, b in zip(keys[1:], steps[1:]):
            d_keys = d_keys + a[...]
            d_steps = d_steps + b[...]
        d_raw = d_steps[:, 0:heads] * own_ref[:, 2 * LANES + 3 * heads : 2 * LANES + 4 * heads]
        keys_high, keys_low = halves(d_keys)
        raw_high, raw_low = halves(d_raw)
        width = select.shape[0]
        block = width // parts
        tiles = []
        for b in range(parts):
            rows = slice(b * block, (b + 1) * block)
            total = before[:, rows]
            total = total + mm(keys_high, select[rows, :], 1, 1) + mm(keys_low, select[rows, :], 1, 1)
            total = total + mm(raw_high, step[rows, :], 1, 1) + mm(raw_low, step[rows, :], 1, 1)
            for k in range(tails):
                total = total + mm(dvs[k][...], weights[k][rows, :], 1, 1)
            tiles.append(total)
        if swap:
            tiles = tiles[::-1]
        if parts == 2:
            first = place[2] == 0
            outs[0][...] = jnp.where(first, tiles[0], tiles[1])
            outs[1][...] = jnp.where(first, tiles[1], tiles[0])
        else:
            for b in range(parts):
                outs[0][:, b * block : (b + 1) * block] = tiles[b]

    return body


def finish_body(flip):
    def body(a, b, out):
        total = (a[...] + b[...]).astype(BF)
        if not flip:
            out[...] = total
            return
        width = total.shape[1]
        block = flip_block(width)
        turn = reversal(block)
        for j in range(width // block):
            out[:, j * block : (j + 1) * block] = mm(
                total[:, width - (j + 1) * block : width - j * block], turn
            ).astype(BF)

    return body


def widen_body(v_ref, g_ref, token, wide):
    length, width = g_ref.shape
    wide[0:length, :] = v_ref[...].reshape(length, width).astype(F32)
    wide[length : 2 * length, :] = g_ref[...].astype(F32)

def local(shards, parts):
    pairs = shards // 2

    def body(
        hidden, complement, inner_weight, select_weight, step_weight, step_bias, decay_rate,
        skip_gain, cotangent, complement_cotangent,
    ):
        length, width = hidden.shape
        inner = inner_weight.shape[1]
        heads = step_bias.shape[0]
        head_width = inner // heads
        groups = 4
        chunk = inner // groups
        group_heads = heads // groups
        seq = lax.axis_index("seq")
        place = jnp.stack([seq % 2, seq // 2, lax.axis_index("chan")]).astype(jnp.int32)
        bias = step_bias.reshape(1, heads)
        rate = decay_rate.reshape(1, heads)
        rate_row = jnp.pad(rate, ((0, 0), (0, LANES - heads)))
        gain = skip_gain.reshape(1, heads)
        cots = (cotangent, complement_cotangent)
        swap_pairs = [(a, a ^ 1) for a in range(shards)]
        up_pairs = [(a, a + 2) for a in range(shards - 2)]
        down_pairs = [(a + 2, a) for a in range(shards - 2)]
        swap = lambda x: lax.ppermute(x, "seq", swap_pairs)
        pack_shape = (length, 3 * LANES)
        pair_shape = (2 * LANES, chunk)
        wide_shape = (2 * length, chunk)
        token_shape = sds((8, LANES))
        work = lambda: [pltpu.VMEM((2,) + pair_shape, F32), pltpu.SemaphoreType.DMA((2,))]
        order = [(s, k) for s in range(2) for k in range(groups)]
        chunks = len(order)

        v_first, source, pack0, pack1, wide = run(
            start_body,
            [hidden, complement, Block(inner_weight, (width, chunk), (0, 0)), select_weight,
             step_weight, bias, rate, Block(cots[0], (length, chunk), (0, 0))],
            [sds((2, length, chunk), BF), sds((2 * length, width), BF), sds(pack_shape),
             sds(pack_shape), sds(wide_shape)],
            limit=32,
        )
        packs = (pack0, pack1)
        v_more = pl.pallas_call(
            more_body,
            grid=(groups - 1,),
            in_specs=[
                pl.BlockSpec((2 * length, width), lambda i: (0, 0)),
                pl.BlockSpec((width, chunk), lambda i: (0, i + 1)),
            ],
            out_specs=pl.BlockSpec((1, 2, length, chunk), lambda i: (i, 0, 0, 0)),
            out_shape=sds((groups - 1, 2, length, chunk), BF),
            compiler_params=pltpu.CompilerParams(vmem_limit_bytes=24 * 1024 * 1024),
            cost_estimate=pl.CostEstimate(flops=0, bytes_accessed=1024, transcendentals=0),
        )(source, inner_weight)

        def value_block(c):
            s, k = order[c]
            if k == 0:
                return Block(v_first, (1, length, chunk), (s, 0, 0))
            return Block(v_more, (1, 1, length, chunk), (k - 1, s, 0, 0))

        def cot_block(c):
            s, k = order[c]
            return Block(cots[s], (length, chunk), (0, k))

        def weight_block(c):
            return Block(inner_weight, (width, chunk), (0, order[c][1]))

        far_packs = [None, None]
        far = {}
        totals, within, post = {}, {}, {}
        got = ([], [])
        grads = [None, None]

        def do_pair(c, token):
            s, k = order[c]
            totals[c] = run(
                pair_body(k * group_heads, heads, head_width),
                [place, value_block(c), cot_block(c), far[c], packs[s], far_packs[s], token],
                [sds(pair_shape), sds(pair_shape), sds(pair_shape), sds((8, chunk))],
            )
            return totals[c][3]

        def do_within(c, token):
            s, k = order[c]
            within[c] = run(
                within_body(k * group_heads, heads, head_width),
                [packs[s], value_block(c), cot_block(c), rate_row, token],
                [sds((length, chunk)), sds((length, chunk)), sds((length, 2 * LANES)), sds((length, LANES))],
                scratch=[pltpu.VMEM((2, LANES, length), F32)],
            )
            return within[c][3]

        def do_post(c, token):
            s, k = order[c]
            ups = [got[0][c + z - 1] for z in range(1, pairs)]
            downs = [got[1][c + z - 1] for z in range(1, pairs)]
            post[c] = run(
                post_body(k * group_heads, heads, head_width, len(ups), len(downs)),
                [place, packs[s], far_packs[s], value_block(c), cot_block(c), *within[c],
                 totals[c][2], gain, rate_row, token, *map(Far, ups), *map(Far, downs)],
                [sds((length, chunk), BF), sds((length, chunk), BF), sds((length, 2 * LANES)), sds((length, LANES))],
                scratch=work(),
            )
            return post[c][3]

        def do_partial(cs, token):
            return run(
                partial_body(len(cs)),
                [token, *[post[c][1] for c in cs], *[weight_block(c) for c in cs]],
                [sds((length, width))],
            )[0]

        def do_term(s, cs, before, token):
            mine = [c for c in range(chunks) if order[c][0] == s]
            shares = [sds((length, width // parts))] * 2 if parts == 2 else [sds((length, width))]
            term = run(
                term_body(len(mine), len(cs), heads, parts, s == 1),
                [place, packs[s], select_weight, step_weight, before,
                 *[post[c][1] for c in cs], *[weight_block(c) for c in cs],
                 *[post[c][2] for c in mine], *[post[c][3] for c in mine]],
                shares,
            )
            if parts == 2:
                return term[0], lax.ppermute(term[1], "chan", [(0, 1), (1, 0)])
            share = lax.psum_scatter(term[0], "chan", scatter_dimension=1, tiled=True)
            return share, jnp.zeros_like(share)

        def do_finish(s, share):
            return run(finish_body(s == 1), list(share), [sds((length, width // parts), BF)])[0]

        def do_step(k, widen, ends):
            steps = chunks + pairs - 2
            sending = 0 <= k < steps
            has = [sending and 0 <= k - z < chunks and z < pairs - 1 for z in range(pairs)]
            ins = [place]
            for d in range(2):
                ins += [Far(totals[k - z][d]) for z in range(pairs) if has[z]]
                ins += [totals[k - z][3] for z in range(pairs) if has[z]]
                if k > 0:
                    ins.append(got[d][-1])
            if widen is not None:
                ins += [value_block(widen), cot_block(widen)]
            ins += [Far(e) for e in ends]
            outs = [sds(pair_shape), sds(pair_shape), token_shape]
            if widen is not None:
                outs.append(sds(wide_shape))
            return run(
                step_body(has, has, k <= 0, widen is not None, len(ends)), ins, outs, scratch=work()
            )

        far[0] = swap(wide)
        far_packs[0] = swap(pack0)
        wide1 = run(
            widen_body, [value_block(1), cot_block(1), Far(far[0])], [sds(wide_shape)]
        )[0]
        far[1] = swap(wide1)
        far_packs[1] = swap(pack1)
        ends = [do_pair(0, Far(wide1)), do_within(0, Far(wide1)), far[1], far_packs[1]]
        steps = chunks + pairs - 2
        halfway = None
        share = [None, None]
        for k in range(steps):
            made = do_step(k, k + 2 if k + 2 < chunks else None, ends)
            token = Far(made[2])
            got[0].append(lax.ppermute(made[0], "seq", up_pairs))
            got[1].append(lax.ppermute(made[1], "seq", down_pairs))
            ends = []
            if k + 2 < chunks:
                far[k + 2] = swap(made[3])
                ends.append(far[k + 2])
            if k + 1 < chunks:
                ends.append(do_pair(k + 1, token))
                ends.append(do_within(k + 1, token))
            c = k - pairs + 1
            if c >= 0:
                ends.append(do_post(c, token))
                if c == groups:
                    halfway = do_partial(list(range(groups)), token)
                    share[0] = do_term(0, [], halfway, token)
                    ends.append(share[0][0])
                if c == groups + 2:
                    grads[0] = do_finish(0, share[0])
                    halfway = do_partial(list(range(groups, groups + 2)), token)
                    ends += [grads[0], halfway]
        for c in range(chunks):
            if c not in post:
                do_post(c, Far(post[c - 1][3]))
        grads[1] = do_finish(1, do_term(1, list(range(groups + 2, chunks)), halfway, None))
        outs = [
            jnp.concatenate([post[c][0] for c in range(s * groups, (s + 1) * groups)], axis=1)
            for s in range(2)
        ]
        return (outs[0], outs[1], grads[0], grads[1])

    return body


def solution(mesh):
    rows = P(("dp", "seq"), None)
    both = P(("dp", "seq"), "chan")
    in_specs = (
        rows, rows, P(None, "chan"), P(), P(None, "chan"),
        P("chan"), P("chan"), P("chan"), both, both,
    )
    return jax.shard_map(
        local(mesh.shape["seq"], mesh.shape["chan"]),
        mesh=mesh,
        in_specs=in_specs,
        out_specs=(both,) * 4,
        check_vma=False,
    )
```

```python
import jax
import jax.numpy as jnp
from jax import lax
from jax.experimental import pallas as pl
from jax.experimental.pallas import tpu as pltpu
from jax.sharding import PartitionSpec as P

BF = jnp.bfloat16
F32 = jnp.float32
LANES = 128


def mm(a, b, ca=1, cb=0):
    return lax.dot_general(a, b, (((ca,), (cb,)), ((), ())), preferred_element_type=F32)


def halves(x):
    high = x.astype(BF)
    return high, (x - high.astype(F32)).astype(BF)


def mm_exact(a, b, ca=1, cb=0):
    first, rest = b.astype(BF), None
    rest = b - first.astype(F32)
    second = rest.astype(BF)
    third = (rest - second.astype(F32)).astype(BF)
    return mm(a, first, ca, cb) + mm(a, second, ca, cb) + mm(a, third, ca, cb)


def iotas(rows, columns):
    return (
        lax.broadcasted_iota(jnp.int32, (rows, columns), 0),
        lax.broadcasted_iota(jnp.int32, (rows, columns), 1),
    )


def spread(weights, base, width, head_width):
    heads = weights.shape[1]
    head, channel = iotas(heads, width)
    start = (head - base) * head_width
    pick = ((channel >= start) & (channel < start + head_width)).astype(BF)
    high, low = halves(weights)
    return mm(high, pick) + mm(low, pick)


def gather_heads(x, base, head_width):
    width = x.shape[1]
    channel, head = iotas(width, LANES)
    start = (head - base) * head_width
    pick = ((channel >= start) & (channel < start + head_width)).astype(BF)
    high, low = halves(x)
    return mm(high, pick) + mm(low, pick)


def reversal(size):
    i, j = iotas(size, size)
    return (i + j == size - 1).astype(BF)


def flip_block(size):
    return 256 if size % 256 == 0 else 128


def sds(shape, dtype=F32):
    return jax.ShapeDtypeStruct(shape, dtype)


class Block:
    def __init__(self, array, shape, index):
        self.array, self.shape, self.index = array, shape, index


class Near:
    def __init__(self, array):
        self.array = array


class Far:
    def __init__(self, array):
        self.array = array


def run(body, ins, outs, scratch=(), limit=24, near_outs=()):
    specs, arrays = [], []
    for item in ins:
        if isinstance(item, Block):
            specs.append(pl.BlockSpec(item.shape, lambda i, index=item.index: index))
            arrays.append(item.array)
        elif isinstance(item, Near):
            specs.append(pl.BlockSpec(memory_space=pltpu.VMEM))
            arrays.append(item.array)
        elif isinstance(item, Far):
            specs.append(pl.BlockSpec(memory_space=pl.ANY))
            arrays.append(item.array)
        elif item.dtype == jnp.int32:
            specs.append(pl.BlockSpec(memory_space=pltpu.SMEM))
            arrays.append(item)
        else:
            specs.append(pl.BlockSpec(item.shape, lambda i, n=item.ndim: (0,) * n))
            arrays.append(item)
    out_specs = [
        pl.BlockSpec(memory_space=pltpu.VMEM)
        if n in near_outs
        else pl.BlockSpec(o.shape, lambda i, n=len(o.shape): (0,) * n)
        for n, o in enumerate(outs)
    ]
    return pl.pallas_call(
        body,
        grid=(1,),
        in_specs=specs,
        out_specs=out_specs,
        out_shape=outs,
        scratch_shapes=list(scratch),
        compiler_params=pltpu.CompilerParams(vmem_limit_bytes=limit * 1024 * 1024),
        cost_estimate=pl.CostEstimate(flops=0, bytes_accessed=1024, transcendentals=0),
    )(*arrays)


def start_body(hidden, other, weight, select, step, bias, rate, cot, v_out, source, pack0, pack1, wide):
    length, width = hidden.shape
    heads = bias.shape[1]
    source[0:length, :] = hidden[...]
    block = flip_block(width)
    turn = reversal(block)
    for j in range(width // block):
        source[length : 2 * length, j * block : (j + 1) * block] = mm(
            other[:, width - (j + 1) * block : width - j * block], turn
        ).astype(BF)
    keys = mm(source[...], select[...]).astype(BF).astype(F32)
    state = keys.shape[1] // 2
    raw = mm(source[...], step[...], 1, 1) + bias[...]
    dt = jnp.maximum(raw, 0.0) + jnp.log1p(jnp.exp(-jnp.abs(raw)))
    rise = jax.nn.sigmoid(raw)
    i, j = iotas(length, length)
    lower = (i >= j).astype(BF)
    for s, pack in enumerate((pack0, pack1)):
        rows = slice(s * length, (s + 1) * length)
        drop = dt[rows] * rate[...]
        total = mm_exact(lower, drop)
        pack[...] = jnp.zeros(pack.shape, F32)
        pack[:, 0 : 2 * state] = keys[rows]
        at = 2 * state
        for part in (dt[rows], total, total - drop, rise[rows]):
            pack[:, at : at + heads] = part
            at += heads
    piece = mm(source[...], weight[...]).astype(BF)
    for s in range(2):
        v_out[s] = piece[s * length : (s + 1) * length]
    wide[0:length, :] = piece[0:length].astype(F32)
    wide[length : 2 * length, :] = cot[...].astype(F32)


def more_body(source, weight, v_out):
    length = v_out.shape[2]
    piece = mm(source[...], weight[...]).astype(BF)
    for s in range(2):
        v_out[0, s] = piece[s * length : (s + 1) * length]


class Pack:
    def __init__(self, ref, heads):
        state = LANES
        self.write = ref[:, 0:state]
        self.read = ref[:, state : 2 * state]
        at = 2 * state
        self.dt = ref[:, at : at + heads]
        self.total = ref[:, at + heads : at + 2 * heads]
        self.before = ref[:, at + 2 * heads : at + 3 * heads]
        self.rise = ref[:, at + 3 * heads : at + 4 * heads]
        last = self.total.shape[0]
        self.whole = self.total[last - 1 : last, :]
        self.from_start = jnp.exp(-self.total)
        self.from_end = jnp.exp(self.before - self.whole)
        self.to_end = jnp.exp(self.total - self.whole)
        self.to_start = jnp.exp(-self.before)
        self.through = jnp.exp(-self.whole)


def pair_body(base, heads, head_width):
    def body(place, v_own, g_own, x_far, own_ref, far_ref, token, up, down, near, keep):
        first = place[0] == 0
        own, far = Pack(own_ref, heads), Pack(far_ref, heads)
        length, width = g_own.shape
        wide = lambda row: spread(jnp.broadcast_to(row, (8, heads)), base, width, head_width)[0:1]
        own_row, far_row = wide(own.through), wide(far.through)
        keep[...] = jnp.broadcast_to(own_row * far_row, keep.shape)

        def local(key, w_up, w_down, x):
            key = key.astype(BF)
            return (
                mm(key, (spread(w_up, base, width, head_width) * x).astype(BF), 0, 0),
                mm(key, (spread(w_down, base, width, head_width) * x).astype(BF), 0, 0),
            )

        def value(pack, x):
            return local(pack.write, pack.dt * pack.to_end, pack.dt * pack.to_start, x)

        def grad(pack, x):
            return local(pack.read, pack.from_end, pack.from_start, x)

        for kind, x_own, at in ((value, v_own, 0), (grad, g_own, length)):
            rows = slice(at, at + LANES)
            x = x_own[...].reshape(length, width).astype(F32)
            own_up, own_down = kind(own, x)
            far_up, far_down = kind(far, x_far[at : at + length, :])
            up[rows, :] = jnp.where(first, own_up * far_row + far_up, far_up * own_row + own_up)
            down[rows, :] = jnp.where(
                first, far_down * own_row + own_down, own_down * far_row + far_down
            )
            near[rows, :] = jnp.where(first, far_down, far_up)

    return body


def fetch_start(options, index, target, sem):
    for z, option in enumerate(options):
        if option is not None:

            @pl.when(index == z)
            def _():
                pltpu.make_async_copy(option, target, sem).start()


def fetch_wait(options, index, target, sem):
    for z, option in enumerate(options):
        if option is not None:

            @pl.when(index == z)
            def _():
                pltpu.make_async_copy(option, target, sem).wait()


def step_body(has, first_step, widen, tokens):
    pairs = len(has)

    def body(place, *rest):
        rest = list(rest)
        take = lambda n: [rest.pop(0) for _ in range(n)]
        sides = []
        for d in range(2):
            totals = [take(1)[0] if h else None for h in has]
            keeps = [take(1)[0] if h else None for h in has]
            sides.append((totals, keeps))
        got = None if first_step else take(2)
        if widen:
            v_ref, g_ref = take(2)
        take(tokens)
        sends = take(2)
        token = take(1)[0]
        wide = take(1)[0] if widen else None
        bufs, sems = take(2)
        spots = (place[1], pairs - 1 - place[1])
        for d, (totals, keeps) in enumerate(sides):
            fetch_start(totals, spots[d], bufs.at[d], sems.at[d])
        if widen:
            length, width = g_ref.shape
            wide[0:length, :] = v_ref[...].reshape(length, width).astype(F32)
            wide[length : 2 * length, :] = g_ref[...].astype(F32)
        token[...] = jnp.zeros(token.shape, F32)
        for d, (totals, keeps) in enumerate(sides):
            fetch_wait(totals, spots[d], bufs.at[d], sems.at[d])
            for n in range(pairs):
                z = n if d == 0 else pairs - 1 - n
                send = sends[(z + d) % 2]

                @pl.when(spots[d] == n)
                def _():
                    if not has[n]:
                        send[...] = jnp.zeros(send.shape, F32)
                    elif got is None or n == 0:
                        send[...] = bufs[d]
                    else:
                        send[...] = bufs[d] + keeps[n][0:1, :] * got[(z + 1 + d) % 2][...]

    return body


def within_body(base, heads, head_width):
    def body(own_ref, v_ref, g_ref, rate, token, y_out, x_out, keys_out, steps_out, cols_s):
        own = Pack(own_ref, heads)
        length, width = g_ref.shape
        write, read = own.write.astype(BF), own.read.astype(BF)
        scores = mm(read, write, 1, 1)
        i, j = iotas(length, length)
        low = i > j
        high = i < j
        doubled = jnp.where(i == j, 2.0, 1.0).astype(F32)
        scores2 = scores * doubled
        turned = own_ref[:, 2 * LANES : 3 * LANES].T
        lane = lax.broadcasted_iota(jnp.int32, (length, LANES), 1)
        d_scores = jnp.zeros((length, length), F32)
        out_low = jnp.zeros((length, LANES), F32)
        out_high = jnp.zeros((length, LANES), F32)
        cols_s[...] = jnp.zeros(cols_s.shape, F32)
        v_all = v_ref[...].reshape(length, width)
        ys, xs = [], []
        for n in range(width // head_width):
            h = base + n
            c_col = own.total[:, h : h + 1]
            e_col = own.before[:, h : h + 1]
            dt_row = turned[h : h + 1, :]
            c_row = turned[heads + h : heads + h + 1, :]
            e_row = turned[2 * heads + h : 2 * heads + h + 1, :]
            decay = jnp.exp(jnp.where(low, c_row - c_col, e_col - e_row))
            v = v_all[:, n * head_width : (n + 1) * head_width]
            g = g_ref[:, n * head_width : (n + 1) * head_width]
            plain = decay * scores2
            ys.append(mm((plain * dt_row).astype(BF), v))
            xs.append(mm(plain.astype(BF), g, 0, 0))
            inner = decay * dt_row * mm(g, v, 1, 1)
            d_scores = d_scores + inner
            flow = inner * scores
            flow_low = jnp.where(low, flow, 0.0)
            flow_high = jnp.where(high, flow, 0.0)
            out_low = jnp.where(lane == h, jnp.sum(flow_low, 1, keepdims=True), out_low)
            out_high = jnp.where(lane == h, jnp.sum(flow_high, 1, keepdims=True), out_high)
            cols_s[0, h : h + 1, :] = jnp.sum(flow_low, 0, keepdims=True)
            cols_s[1, h : h + 1, :] = jnp.sum(flow_high, 0, keepdims=True)
            if (n + 1) * head_width % LANES == 0:
                per = LANES // head_width
                at = slice((n + 1) * head_width - LANES, (n + 1) * head_width)
                y_out[:, at] = jnp.concatenate(ys[-per:], axis=1)
                x_out[:, at] = jnp.concatenate(xs[-per:], axis=1)
        d_scores = (d_scores * doubled).astype(BF)
        keys_out[:, 0:LANES] = mm(d_scores, read, 0, 0)
        keys_out[:, LANES : 2 * LANES] = mm(d_scores, write)
        net_low = out_low - cols_s[0].T
        net_high = out_high - cols_s[1].T
        at_or_after = (j >= i).astype(BF)
        after = (j > i).astype(BF)
        steps_out[...] = -rate[...] * (mm_exact(at_or_after, net_low) - mm_exact(after, net_high))

    return body


def post_body(base, heads, head_width, ups, downs):
    def body(
        place, own_ref, far_ref, v_ref, g_ref, yw, xw, keys_w, steps_w, near, skip, rate, token, *rest
    ):
        up_in, down_in = rest[0:ups], rest[ups : ups + downs]
        mixed, dv_out, keys_out, steps_out, bufs, sems = rest[ups + downs :]
        up_spot, down_spot = place[1], len(up_in) - 1 - place[1]
        fetch_start(up_in, up_spot, bufs.at[0], sems.at[0])
        fetch_start(down_in, down_spot, bufs.at[1], sems.at[1])
        first = place[0] == 0
        own, far = Pack(own_ref, heads), Pack(far_ref, heads)
        length, width = g_ref.shape
        wide = lambda w: spread(w, base, width, head_width)
        far_row = wide(jnp.broadcast_to(far.through, (8, heads)))[0:1]
        own_row = wide(jnp.broadcast_to(own.through, (8, heads)))[0:1]
        gain = wide(jnp.broadcast_to(skip[...], (8, heads)))[0:1]
        up_row = jnp.where(first, 1.0, far_row)
        down_row = jnp.where(first, far_row, 1.0)
        dt = wide(own.dt)
        from_start, from_end = wide(own.from_start), wide(own.from_end)
        to_end, to_start = wide(own.to_end), wide(own.to_start)
        write, read = own.write.astype(BF), own.read.astype(BF)
        v = v_ref[...].reshape(length, width).astype(F32)
        g = g_ref[...].astype(F32)
        fetch_wait(up_in, up_spot, bufs.at[0], sems.at[0])
        fetch_wait(down_in, down_spot, bufs.at[1], sems.at[1])
        up = up_row * bufs[0] + jnp.where(first, 0.0, near[...])
        down = down_row * bufs[1] + jnp.where(first, near[...], 0.0)
        p, ab = up[0:LANES], up[LANES : 2 * LANES]
        q, af = down[0:LANES], down[LANES : 2 * LANES]
        crossing = jnp.sum(p * af + q * ab, axis=0, keepdims=True)
        p, q, af, ab = p.astype(BF), q.astype(BF), af.astype(BF), ab.astype(BF)
        y_p = from_start * mm(read, p)
        y_q = from_end * mm(read, q)
        x_f = to_end * mm(write, af)
        x_b = to_start * mm(write, ab)
        mixed[...] = (yw[...] + y_p + y_q + gain * v).astype(BF)
        x = xw[...] + x_f + x_b
        dv_out[...] = (dt * x + gain * g).astype(BF)
        dtv = dt * v
        keys_out[:, 0:LANES] = (
            keys_w[:, 0:LANES]
            + mm((to_end * dtv).astype(BF), af, 1, 1)
            + mm((to_start * dtv).astype(BF), ab, 1, 1)
        )
        keys_out[:, LANES : 2 * LANES] = (
            keys_w[:, LANES : 2 * LANES]
            + mm((from_start * g).astype(BF), p, 1, 1)
            + mm((from_end * g).astype(BF), q, 1, 1)
        )
        lane = lax.broadcasted_iota(jnp.int32, (length, LANES), 1)
        steps = jnp.where(lane < heads, own_ref[:, 2 * LANES : 3 * LANES], 0.0)
        direct = gather_heads(v * x, base, head_width)
        a_p = gather_heads(g * y_p, base, head_width)
        a_q = gather_heads(g * y_q, base, head_width)
        b_f = gather_heads(v * x_f, base, head_width) * steps
        b_b = gather_heads(v * x_b, base, head_width) * steps
        through = gather_heads(
            jnp.broadcast_to(crossing * own_row, (8, width)), base, head_width
        )[0:1]
        i, j = iotas(length, length)
        flow = (
            mm_exact((j >= i).astype(BF), a_p)
            + mm_exact((j < i).astype(BF), b_f)
            + mm_exact((j <= i).astype(BF), a_q)
            + mm_exact((j > i).astype(BF), b_b)
            + through
        )
        steps_out[...] = steps_w[...] + direct - rate[...] * flow

    return body


def partial_body(groups):
    def body(token, *rest):
        dvs, weights, out = rest[0:groups], rest[groups : 2 * groups], rest[2 * groups]
        total = mm(dvs[0][...], weights[0][...], 1, 1)
        for k in range(1, groups):
            total = total + mm(dvs[k][...], weights[k][...], 1, 1)
        out[...] = total

    return body


def term_body(groups, tails, heads, parts, swap):
    def body(place, own_ref, select, step, before, *rest):
        dvs, weights = rest[0:tails], rest[tails : 2 * tails]
        rest = rest[2 * tails :]
        keys, steps = rest[0:groups], rest[groups : 2 * groups]
        outs = rest[2 * groups :]
        d_keys, d_steps = keys[0][...], steps[0][...]
        for a, b in zip(keys[1:], steps[1:]):
            d_keys = d_keys + a[...]
            d_steps = d_steps + b[...]
        d_raw = d_steps[:, 0:heads] * own_ref[:, 2 * LANES + 3 * heads : 2 * LANES + 4 * heads]
        keys_high, keys_low = halves(d_keys)
        raw_high, raw_low = halves(d_raw)
        width = select.shape[0]
        block = width // parts
        tiles = []
        for b in range(parts):
            rows = slice(b * block, (b + 1) * block)
            total = before[:, rows]
            total = total + mm(keys_high, select[rows, :], 1, 1) + mm(keys_low, select[rows, :], 1, 1)
            total = total + mm(raw_high, step[:, rows]) + mm(raw_low, step[:, rows])
            for k in range(tails):
                total = total + mm(dvs[k][...], weights[k][rows, :], 1, 1)
            tiles.append(total)
        if swap:
            tiles = tiles[::-1]
        if parts == 2:
            first = place[2] == 0
            outs[0][...] = jnp.where(first, tiles[0], tiles[1])
            outs[1][...] = jnp.where(first, tiles[1], tiles[0])
        else:
            for b in range(parts):
                outs[0][:, b * block : (b + 1) * block] = tiles[b]

    return body


def finish_body(flip):
    def body(a, b, out):
        total = (a[...] + b[...]).astype(BF)
        if not flip:
            out[...] = total
            return
        width = total.shape[1]
        block = flip_block(width)
        turn = reversal(block)
        for j in range(width // block):
            out[:, j * block : (j + 1) * block] = mm(
                total[:, width - (j + 1) * block : width - j * block], turn
            ).astype(BF)

    return body


def widen_body(v_ref, g_ref, pack_in, token0, token1, wide, pack_out):
    pack_out[...] = pack_in[...]
    length, width = g_ref.shape
    wide[0:length, :] = v_ref[...].reshape(length, width).astype(F32)
    wide[length : 2 * length, :] = g_ref[...].astype(F32)

def local(shards, parts):
    pairs = shards // 2

    def body(
        hidden, complement, inner_weight, select_weight, step_weight, step_bias, decay_rate,
        skip_gain, cotangent, complement_cotangent,
    ):
        length, width = hidden.shape
        inner = inner_weight.shape[1]
        heads = step_bias.shape[0]
        head_width = inner // heads
        groups = 4
        chunk = inner // groups
        group_heads = heads // groups
        seq = lax.axis_index("seq")
        place = jnp.stack([seq % 2, seq // 2, lax.axis_index("chan")]).astype(jnp.int32)
        bias = step_bias.reshape(1, heads)
        rate = decay_rate.reshape(1, heads)
        rate_row = jnp.pad(rate, ((0, 0), (0, LANES - heads)))
        gain = skip_gain.reshape(1, heads)
        step_rows = step_weight.T
        cots = (cotangent, complement_cotangent)
        swap_pairs = [(a, a ^ 1) for a in range(shards)]
        edges = [
            [
                (2 * a + y, 2 * b + y)
                for z in range(start, pairs - 1, 2)
                for a, b in ((z, z + 1), (z + 1, z))
                for y in range(2)
            ]
            for start in range(2)
        ]
        swap = lambda x: lax.ppermute(x, "seq", swap_pairs)
        pack_shape = (length, 3 * LANES)
        pair_shape = (2 * LANES, chunk)
        wide_shape = (2 * length, chunk)
        token_shape = sds((8, LANES))
        work = lambda: [pltpu.VMEM((2,) + pair_shape, F32), pltpu.SemaphoreType.DMA((2,))]
        order = [(s, k) for s in range(2) for k in range(groups)]
        chunks = len(order)

        v_first, source, pack0, pack1, wide = run(
            start_body,
            [hidden, complement, Block(inner_weight, (width, chunk), (0, 0)), select_weight,
             step_rows, bias, rate, Block(cots[0], (length, chunk), (0, 0))],
            [sds((2, length, chunk), BF), sds((2 * length, width), BF), sds(pack_shape),
             sds(pack_shape), sds(wide_shape)],
            limit=60,
        )
        packs = (pack0, pack1)
        v_more = pl.pallas_call(
            more_body,
            grid=(groups - 1,),
            in_specs=[
                pl.BlockSpec((2 * length, width), lambda i: (0, 0)),
                pl.BlockSpec((width, chunk), lambda i: (0, i + 1)),
            ],
            out_specs=pl.BlockSpec((1, 2, length, chunk), lambda i: (i, 0, 0, 0)),
            out_shape=sds((groups - 1, 2, length, chunk), BF),
            compiler_params=pltpu.CompilerParams(vmem_limit_bytes=60 * 1024 * 1024),
            cost_estimate=pl.CostEstimate(flops=0, bytes_accessed=1024, transcendentals=0),
        )(source, inner_weight)

        def value_block(c):
            s, k = order[c]
            if k == 0:
                return Block(v_first, (1, length, chunk), (s, 0, 0))
            return Block(v_more, (1, 1, length, chunk), (k - 1, s, 0, 0))

        def cot_block(c):
            s, k = order[c]
            return Block(cots[s], (length, chunk), (0, k))

        def weight_block(c):
            return Block(inner_weight, (width, chunk), (0, order[c][1]))

        far_packs = [None, None]
        far = {}
        totals, within, post = {}, {}, {}
        got = ([], [])
        grads = [None, None]

        def do_pair(c, token):
            s, k = order[c]
            totals[c] = run(
                pair_body(k * group_heads, heads, head_width),
                [place, value_block(c), cot_block(c), far[c], packs[s], far_packs[s], token],
                [sds(pair_shape), sds(pair_shape), sds(pair_shape), sds((8, chunk))],
            )
            return totals[c][3]

        def do_within(c, token):
            s, k = order[c]
            within[c] = run(
                within_body(k * group_heads, heads, head_width),
                [packs[s], value_block(c), cot_block(c), rate_row, token],
                [sds((length, chunk)), sds((length, chunk)), sds((length, 2 * LANES)), sds((length, LANES))],
                scratch=[pltpu.VMEM((2, LANES, length), F32)],
            )
            return within[c][3]

        def do_post(c, token):
            s, k = order[c]
            last = pairs - 1
            ups = [got[(z + 1) % 2][max(c + z - 1, c)] for z in range(pairs)]
            downs = [got[(last - z) % 2][max(c + z - 1, c)] for z in range(pairs)]
            post[c] = run(
                post_body(k * group_heads, heads, head_width, len(ups), len(downs)),
                [place, packs[s], far_packs[s], value_block(c), cot_block(c), *within[c],
                 totals[c][2], gain, rate_row, token, *map(Far, ups), *map(Far, downs)],
                [sds((length, chunk), BF), sds((length, chunk), BF), sds((length, 2 * LANES)), sds((length, LANES))],
                scratch=work(),
            )
            return post[c][3]

        def do_partial(cs, token):
            return run(
                partial_body(len(cs)),
                [token, *[post[c][1] for c in cs], *[weight_block(c) for c in cs]],
                [sds((length, width))],
            )[0]

        def do_term(s, cs, before, token):
            mine = [c for c in range(chunks) if order[c][0] == s]
            shares = [sds((length, width // parts))] * 2 if parts == 2 else [sds((length, width))]
            term = run(
                term_body(len(mine), len(cs), heads, parts, s == 1),
                [place, packs[s], select_weight, step_rows, before,
                 *[post[c][1] for c in cs], *[weight_block(c) for c in cs],
                 *[post[c][2] for c in mine], *[post[c][3] for c in mine]],
                shares,
            )
            if parts == 2:
                return term[0], lax.ppermute(term[1], "chan", [(0, 1), (1, 0)])
            share = lax.psum_scatter(term[0], "chan", scatter_dimension=1, tiled=True)
            return share, jnp.zeros_like(share)

        def do_finish(s, share):
            return run(finish_body(s == 1), list(share), [sds((length, width // parts), BF)])[0]

        def do_step(k, widen, ends):
            steps = chunks + pairs - 2
            sending = 0 <= k < steps
            has = [sending and 0 <= k - z < chunks and z < pairs - 1 for z in range(pairs)]
            ins = [place]
            for d in range(2):
                ins += [Far(totals[k - z][d]) for z in range(pairs) if has[z]]
                ins += [totals[k - z][3] for z in range(pairs) if has[z]]
            if k > 0:
                ins += [Near(got[0][-1]), Near(got[1][-1])]
            if widen is not None:
                ins += [value_block(widen), cot_block(widen)]
            ins += [Far(e) for e in ends]
            outs = [sds(pair_shape), sds(pair_shape), token_shape]
            if widen is not None:
                outs.append(sds(wide_shape))
            return run(
                step_body(has, k <= 0, widen is not None, len(ends)), ins, outs, scratch=work(),
                near_outs=(0, 1, 3),
            )

        far[0] = swap(wide)
        far_packs[0] = swap(pack0)
        wide1, pack_late = run(
            widen_body,
            [value_block(1), cot_block(1), pack1, Far(far[0]), Far(far_packs[0])],
            [sds(wide_shape), sds(pack_shape)],
        )
        far[1] = swap(wide1)
        ends = [do_pair(0, Far(wide1)), do_within(0, Far(wide1)), far[1]]
        steps = chunks + pairs - 2
        halfway = None
        share = [None, None]
        for k in range(steps):
            made = do_step(k, k + 2 if k + 2 < chunks else None, ends)
            token = Far(made[2])
            for d in range(2):
                got[d].append(lax.ppermute(made[d], "seq", edges[d]))
            ends = []
            if k + 2 < chunks:
                far[k + 2] = swap(made[3])
                ends.append(far[k + 2])
            if k == 0:
                far_packs[1] = swap(pack_late)
                ends.append(far_packs[1])
            if k + 1 < chunks:
                ends.append(do_pair(k + 1, token))
                ends.append(do_within(k + 1, token))
            c = k - pairs + 1
            if c >= 0:
                ends.append(do_post(c, token))
                if c == groups:
                    halfway = do_partial(list(range(groups)), token)
                    share[0] = do_term(0, [], halfway, token)
                    ends.append(share[0][0])
                if c == groups + 2:
                    grads[0] = do_finish(0, share[0])
                    halfway = do_partial(list(range(groups, groups + 2)), token)
                    ends += [grads[0], halfway]
        for c in range(chunks):
            if c not in post:
                do_post(c, Far(post[c - 1][3]))
        grads[1] = do_finish(1, do_term(1, list(range(groups + 2, chunks)), halfway, None))
        outs = [
            jnp.concatenate([post[c][0] for c in range(s * groups, (s + 1) * groups)], axis=1)
            for s in range(2)
        ]
        return (outs[0], outs[1], grads[0], grads[1])

    return body


def solution(mesh):
    rows = P(("dp", "seq"), None)
    both = P(("dp", "seq"), "chan")
    in_specs = (
        rows, rows, P(None, "chan"), P(), P(None, "chan"),
        P("chan"), P("chan"), P("chan"), both, both,
    )
    return jax.shard_map(
        local(mesh.shape["seq"], mesh.shape["chan"]),
        mesh=mesh,
        in_specs=in_specs,
        out_specs=(both,) * 4,
        check_vma=False,
    )
```

```python
import jax
import jax.numpy as jnp
from jax import lax
from jax.experimental import pallas as pl
from jax.experimental.pallas import tpu as pltpu
from jax.sharding import PartitionSpec as P

BF = jnp.bfloat16
F32 = jnp.float32
LANES = 128


def mm(a, b, ca=1, cb=0):
    return lax.dot_general(a, b, (((ca,), (cb,)), ((), ())), preferred_element_type=F32)


def halves(x):
    high = x.astype(BF)
    return high, (x - high.astype(F32)).astype(BF)


def mm_exact(a, b, ca=1, cb=0):
    first, rest = b.astype(BF), None
    rest = b - first.astype(F32)
    second = rest.astype(BF)
    third = (rest - second.astype(F32)).astype(BF)
    return mm(a, first, ca, cb) + mm(a, second, ca, cb) + mm(a, third, ca, cb)


def iotas(rows, columns):
    return (
        lax.broadcasted_iota(jnp.int32, (rows, columns), 0),
        lax.broadcasted_iota(jnp.int32, (rows, columns), 1),
    )


def spread(weights, base, width, head_width):
    heads = weights[0].shape[1]
    row, channel = iotas(2 * heads, width)
    start = (jnp.where(row >= heads, row - heads, row) - base) * head_width
    pick = ((channel >= start) & (channel < start + head_width)).astype(BF)
    stacked = jnp.concatenate(weights, axis=0) if len(weights) > 1 else weights[0]
    out = mm(jnp.concatenate(halves(stacked), axis=1), pick)
    result, at = [], 0
    for w in weights:
        result.append(out[at : at + w.shape[0]])
        at += w.shape[0]
    return result


def spread_rows(rows, base, width, head_width):
    heads = rows[0].shape[1]
    wide = spread([jnp.broadcast_to(r, (8, heads)) for r in rows], base, width, head_width)
    return [w[0:1] for w in wide]


def gather_heads(parts, base, head_width):
    width = parts[0].shape[1]
    channel, head = iotas(width, LANES)
    start = (head - base) * head_width
    pick = ((channel >= start) & (channel < start + head_width)).astype(BF)
    out = mm(jnp.concatenate([x.astype(BF) for x in parts], axis=0), pick)
    result, at = [], 0
    for x in parts:
        result.append(out[at : at + x.shape[0]])
        at += x.shape[0]
    return result


def reversal(size):
    i, j = iotas(size, size)
    return (i + j == size - 1).astype(BF)


def flip_block(size):
    return 256 if size % 256 == 0 else 128


def sds(shape, dtype=F32):
    return jax.ShapeDtypeStruct(shape, dtype)


class Block:
    def __init__(self, array, shape, index):
        self.array, self.shape, self.index = array, shape, index


class Near:
    def __init__(self, array):
        self.array = array


class Far:
    def __init__(self, array):
        self.array = array


def run(body, ins, outs, scratch=(), limit=24, near_outs=()):
    specs, arrays = [], []
    for item in ins:
        if isinstance(item, Block):
            specs.append(pl.BlockSpec(item.shape, lambda i, index=item.index: index))
            arrays.append(item.array)
        elif isinstance(item, Near):
            specs.append(pl.BlockSpec(memory_space=pltpu.VMEM))
            arrays.append(item.array)
        elif isinstance(item, Far):
            specs.append(pl.BlockSpec(memory_space=pl.ANY))
            arrays.append(item.array)
        elif item.dtype == jnp.int32:
            specs.append(pl.BlockSpec(memory_space=pltpu.SMEM))
            arrays.append(item)
        else:
            specs.append(pl.BlockSpec(item.shape, lambda i, n=item.ndim: (0,) * n))
            arrays.append(item)
    out_specs = [
        pl.BlockSpec(memory_space=pltpu.VMEM)
        if n in near_outs
        else pl.BlockSpec(o.shape, lambda i, n=len(o.shape): (0,) * n)
        for n, o in enumerate(outs)
    ]
    return pl.pallas_call(
        body,
        grid=(1,),
        in_specs=specs,
        out_specs=out_specs,
        out_shape=outs,
        scratch_shapes=list(scratch),
        compiler_params=pltpu.CompilerParams(vmem_limit_bytes=limit * 1024 * 1024),
        cost_estimate=pl.CostEstimate(flops=0, bytes_accessed=1024, transcendentals=0),
    )(*arrays)


def start_body(hidden, other, weight, select, step, bias, rate, cot, v_out, source, pack0, pack1, wide):
    length, width = hidden.shape
    heads = bias.shape[1]
    source[0:length, :] = hidden[...]
    block = flip_block(width)
    turn = reversal(block)
    for j in range(width // block):
        source[length : 2 * length, j * block : (j + 1) * block] = mm(
            other[:, width - (j + 1) * block : width - j * block], turn
        ).astype(BF)
    keys = mm(source[...], select[...]).astype(BF).astype(F32)
    state = keys.shape[1] // 2
    raw = mm(source[...], step[...], 1, 1) + bias[...]
    dt = jnp.maximum(raw, 0.0) + jnp.log1p(jnp.exp(-jnp.abs(raw)))
    rise = jax.nn.sigmoid(raw)
    i, j = iotas(length, length)
    lower = (i >= j).astype(BF)
    for s, pack in enumerate((pack0, pack1)):
        rows = slice(s * length, (s + 1) * length)
        drop = dt[rows] * rate[...]
        total = mm_exact(lower, drop)
        pack[...] = jnp.zeros(pack.shape, F32)
        pack[:, 0 : 2 * state] = keys[rows]
        at = 2 * state
        for part in (dt[rows], total, total - drop, rise[rows]):
            pack[:, at : at + heads] = part
            at += heads
    piece = mm(source[...], weight[...]).astype(BF)
    for s in range(2):
        v_out[s] = piece[s * length : (s + 1) * length]
    wide[0:length, :] = piece[0:length].astype(F32)
    wide[length : 2 * length, :] = cot[...].astype(F32)


def more_body(source, weight, v_out):
    length = v_out.shape[2]
    piece = mm(source[...], weight[...]).astype(BF)
    for s in range(2):
        v_out[0, s] = piece[s * length : (s + 1) * length]


class Pack:
    def __init__(self, ref, heads):
        state = LANES
        self.write = ref[:, 0:state]
        self.read = ref[:, state : 2 * state]
        at = 2 * state
        self.dt = ref[:, at : at + heads]
        self.total = ref[:, at + heads : at + 2 * heads]
        self.before = ref[:, at + 2 * heads : at + 3 * heads]
        self.rise = ref[:, at + 3 * heads : at + 4 * heads]
        last = self.total.shape[0]
        self.whole = self.total[last - 1 : last, :]
        self.from_start = jnp.exp(-self.total)
        self.from_end = jnp.exp(self.before - self.whole)
        self.to_end = jnp.exp(self.total - self.whole)
        self.to_start = jnp.exp(-self.before)
        self.through = jnp.exp(-self.whole)


def pair_body(base, heads, head_width):
    def body(place, v_own, g_own, x_far, own_ref, far_ref, token, up, down, near, keep):
        first = place[0] == 0
        own, far = Pack(own_ref, heads), Pack(far_ref, heads)
        length, width = g_own.shape
        own_row, far_row = own.through, far.through
        keep[...] = jnp.broadcast_to(
            spread_rows([own_row * far_row], base, width, head_width)[0], keep.shape
        )
        own_up, own_down = jnp.where(first, far_row, 1.0), jnp.where(first, 1.0, far_row)
        far_up, far_down = jnp.where(first, 1.0, own_row), jnp.where(first, own_row, 1.0)
        for kind in range(2):
            rows = slice(kind * LANES, (kind + 1) * LANES)
            if kind == 0:
                keys = (own.write, far.write)
                ups = (own.dt * own.to_end, far.dt * far.to_end)
                downs = (own.dt * own.to_start, far.dt * far.to_start)
            else:
                keys = (own.read, far.read)
                ups = (own.from_end, far.from_end)
                downs = (own.from_start, far.from_start)
            x_own = (v_own if kind == 0 else g_own)[...].reshape(length, width).astype(F32)
            x_other = x_far[kind * length : (kind + 1) * length, :]
            w = spread(
                [ups[0] * own_up, ups[1] * far_up, downs[0] * own_down, downs[1] * far_down,
                 jnp.where(first, downs[1], ups[1])],
                base, width, head_width,
            )
            key = jnp.concatenate(keys, axis=0).astype(BF)
            both = lambda a, b: jnp.concatenate([(a * x_own).astype(BF), (b * x_other).astype(BF)], axis=0)
            up[rows, :] = mm(key, both(w[0], w[1]), 0, 0)
            down[rows, :] = mm(key, both(w[2], w[3]), 0, 0)
            near[rows, :] = mm(keys[1].astype(BF), (w[4] * x_other).astype(BF), 0, 0)

    return body


def fetch_start(options, index, target, sem):
    for z, option in enumerate(options):
        if option is not None:

            @pl.when(index == z)
            def _():
                pltpu.make_async_copy(option, target, sem).start()


def fetch_wait(options, index, target, sem):
    for z, option in enumerate(options):
        if option is not None:

            @pl.when(index == z)
            def _():
                pltpu.make_async_copy(option, target, sem).wait()


def step_body(has, first_step, widen, tokens):
    pairs = len(has)

    def body(place, *rest):
        rest = list(rest)
        take = lambda n: [rest.pop(0) for _ in range(n)]
        sides = []
        for d in range(2):
            totals = [take(1)[0] if h else None for h in has]
            keeps = [take(1)[0] if h else None for h in has]
            sides.append((totals, keeps))
        got = None if first_step else take(2)
        if widen:
            v_ref, g_ref = take(2)
        take(tokens)
        sends = take(2)
        token = take(1)[0]
        wide = take(1)[0] if widen else None
        bufs, sems = take(2)
        spots = (place[1], pairs - 1 - place[1])
        for d, (totals, keeps) in enumerate(sides):
            fetch_start(totals, spots[d], bufs.at[d], sems.at[d])
        if widen:
            length, width = g_ref.shape
            wide[0:length, :] = v_ref[...].reshape(length, width).astype(F32)
            wide[length : 2 * length, :] = g_ref[...].astype(F32)
        token[...] = jnp.zeros(token.shape, F32)
        for d, (totals, keeps) in enumerate(sides):
            fetch_wait(totals, spots[d], bufs.at[d], sems.at[d])
            for n in range(pairs):
                z = n if d == 0 else pairs - 1 - n
                send = sends[(z + d) % 2]

                @pl.when(spots[d] == n)
                def _():
                    if not has[n]:
                        send[...] = jnp.zeros(send.shape, F32)
                    elif got is None or n == 0:
                        send[...] = bufs[d]
                    else:
                        send[...] = bufs[d] + keeps[n][0:1, :] * got[(z + 1 + d) % 2][...]

    return body


def within_body(base, heads, head_width):
    def body(own_ref, v_ref, g_ref, rate, token, y_out, x_out, keys_out, steps_out, cols_s):
        own = Pack(own_ref, heads)
        length, width = g_ref.shape
        write, read = own.write.astype(BF), own.read.astype(BF)
        scores = mm(read, write, 1, 1)
        i, j = iotas(length, length)
        low = i > j
        high = i < j
        doubled = jnp.where(i == j, 2.0, 1.0).astype(F32)
        scores2 = scores * doubled
        turned = own_ref[:, 2 * LANES : 3 * LANES].T
        lane = lax.broadcasted_iota(jnp.int32, (length, LANES), 1)
        d_scores = jnp.zeros((length, length), F32)
        out_low = jnp.zeros((length, LANES), F32)
        out_high = jnp.zeros((length, LANES), F32)
        cols_s[...] = jnp.zeros(cols_s.shape, F32)
        v_all = v_ref[...].reshape(length, width)
        per = LANES // head_width
        for n in range(width // LANES):
            at = slice(n * LANES, (n + 1) * LANES)
            v, g = v_all[:, at], g_ref[:, at]
            mine = [(lane >= m * head_width) & (lane < (m + 1) * head_width) for m in range(per)]
            v_heads = jnp.concatenate([jnp.where(x, v, jnp.zeros_like(v)) for x in mine], axis=0)
            g_heads = jnp.concatenate([jnp.where(x, g, jnp.zeros_like(g)) for x in mine], axis=0)
            products = mm(g_heads, v, 1, 1)
            plains, steppeds = [], []
            for m in range(per):
                h = base + n * per + m
                c_col = own.total[:, h : h + 1]
                e_col = own.before[:, h : h + 1]
                dt_row = turned[h : h + 1, :]
                c_row = turned[heads + h : heads + h + 1, :]
                e_row = turned[2 * heads + h : 2 * heads + h + 1, :]
                decay = jnp.exp(jnp.where(low, c_row - c_col, e_col - e_row))
                plain = decay * scores2
                plains.append(plain.astype(BF))
                steppeds.append((plain * dt_row).astype(BF))
                inner = decay * dt_row * products[m * length : (m + 1) * length]
                d_scores = d_scores + inner
                flow = inner * scores
                flow_low = jnp.where(low, flow, 0.0)
                flow_high = jnp.where(high, flow, 0.0)
                out_low = jnp.where(lane == h, jnp.sum(flow_low, 1, keepdims=True), out_low)
                out_high = jnp.where(lane == h, jnp.sum(flow_high, 1, keepdims=True), out_high)
                cols_s[0, h : h + 1, :] = jnp.sum(flow_low, 0, keepdims=True)
                cols_s[1, h : h + 1, :] = jnp.sum(flow_high, 0, keepdims=True)
            y_out[:, at] = mm(jnp.concatenate(steppeds, axis=1), v_heads)
            x_out[:, at] = mm(jnp.concatenate(plains, axis=0), g_heads, 0, 0)
        d_scores = (d_scores * doubled).astype(BF)
        keys_out[:, 0:LANES] = mm(d_scores, read, 0, 0)
        keys_out[:, LANES : 2 * LANES] = mm(d_scores, write)
        net_low = out_low - cols_s[0].T
        net_high = out_high - cols_s[1].T
        at_or_after = (j >= i).astype(BF)
        after = (j > i).astype(BF)
        steps_out[...] = -rate[...] * (mm_exact(at_or_after, net_low) - mm_exact(after, net_high))

    return body


def post_body(base, heads, head_width, ups, downs):
    def body(
        place, own_ref, far_ref, v_ref, g_ref, yw, xw, keys_w, steps_w, near, skip, rate, token, *rest
    ):
        up_in, down_in = rest[0:ups], rest[ups : ups + downs]
        mixed, dv_out, keys_out, steps_out, bufs, sems = rest[ups + downs :]
        up_spot, down_spot = place[1], len(up_in) - 1 - place[1]
        fetch_start(up_in, up_spot, bufs.at[0], sems.at[0])
        fetch_start(down_in, down_spot, bufs.at[1], sems.at[1])
        first = place[0] == 0
        own, far = Pack(own_ref, heads), Pack(far_ref, heads)
        length, width = g_ref.shape
        far_row, own_row, gain = spread_rows(
            [far.through, own.through, skip[...]], base, width, head_width
        )
        up_row = jnp.where(first, 1.0, far_row)
        down_row = jnp.where(first, far_row, 1.0)
        dt, from_start, from_end, to_end, to_start = spread(
            [own.dt, own.from_start, own.from_end, own.to_end, own.to_start],
            base, width, head_width,
        )
        write, read = own.write.astype(BF), own.read.astype(BF)
        v = v_ref[...].reshape(length, width).astype(F32)
        g = g_ref[...].astype(F32)
        fetch_wait(up_in, up_spot, bufs.at[0], sems.at[0])
        fetch_wait(down_in, down_spot, bufs.at[1], sems.at[1])
        up = up_row * bufs[0] + jnp.where(first, 0.0, near[...])
        down = down_row * bufs[1] + jnp.where(first, near[...], 0.0)
        p, ab = up[0:LANES], up[LANES : 2 * LANES]
        q, af = down[0:LANES], down[LANES : 2 * LANES]
        crossing = jnp.sum(p * af + q * ab, axis=0, keepdims=True)
        p, q, af, ab = p.astype(BF), q.astype(BF), af.astype(BF), ab.astype(BF)
        y_p = from_start * mm(read, p)
        y_q = from_end * mm(read, q)
        x_f = to_end * mm(write, af)
        x_b = to_start * mm(write, ab)
        mixed[...] = (yw[...] + y_p + y_q + gain * v).astype(BF)
        x = xw[...] + x_f + x_b
        dv_out[...] = (dt * x + gain * g).astype(BF)
        dtv = dt * v
        keys_out[:, 0:LANES] = (
            keys_w[:, 0:LANES]
            + mm((to_end * dtv).astype(BF), af, 1, 1)
            + mm((to_start * dtv).astype(BF), ab, 1, 1)
        )
        keys_out[:, LANES : 2 * LANES] = (
            keys_w[:, LANES : 2 * LANES]
            + mm((from_start * g).astype(BF), p, 1, 1)
            + mm((from_end * g).astype(BF), q, 1, 1)
        )
        lane = lax.broadcasted_iota(jnp.int32, (length, LANES), 1)
        steps = jnp.where(lane < heads, own_ref[:, 2 * LANES : 3 * LANES], 0.0)
        direct, a_p, a_q, b_f, b_b, through = gather_heads(
            [v * x, g * y_p, g * y_q, v * x_f, v * x_b, jnp.broadcast_to(crossing * own_row, (8, width))],
            base, head_width,
        )
        i, j = iotas(length, length)
        masks = jnp.concatenate([j >= i, j <= i, j < i, j > i], axis=1).astype(F32).astype(BF)
        high, low = halves(jnp.concatenate([a_p, a_q, b_f * steps, b_b * steps], axis=0))
        flow = mm(masks, high) + mm(masks, low) + through[0:1]
        steps_out[...] = steps_w[...] + direct - rate[...] * flow

    return body


def partial_body(groups):
    def body(token, *rest):
        dvs, weights, out = rest[0:groups], rest[groups : 2 * groups], rest[2 * groups]
        total = mm(dvs[0][...], weights[0][...], 1, 1)
        for k in range(1, groups):
            total = total + mm(dvs[k][...], weights[k][...], 1, 1)
        out[...] = total

    return body


def term_body(groups, tails, heads, parts, swap):
    def body(place, own_ref, select, step, before, *rest):
        dvs, weights = rest[0:tails], rest[tails : 2 * tails]
        rest = rest[2 * tails :]
        keys, steps = rest[0:groups], rest[groups : 2 * groups]
        outs = rest[2 * groups :]
        d_keys, d_steps = keys[0][...], steps[0][...]
        for a, b in zip(keys[1:], steps[1:]):
            d_keys = d_keys + a[...]
            d_steps = d_steps + b[...]
        d_raw = d_steps[:, 0:heads] * own_ref[:, 2 * LANES + 3 * heads : 2 * LANES + 4 * heads]
        keys_high, keys_low = halves(d_keys)
        raw_high, raw_low = halves(d_raw)
        width = select.shape[0]
        block = width // parts
        tiles = []
        for b in range(parts):
            rows = slice(b * block, (b + 1) * block)
            total = before[:, rows]
            total = total + mm(keys_high, select[rows, :], 1, 1) + mm(keys_low, select[rows, :], 1, 1)
            total = total + mm(raw_high, step[:, rows]) + mm(raw_low, step[:, rows])
            for k in range(tails):
                total = total + mm(dvs[k][...], weights[k][rows, :], 1, 1)
            tiles.append(total)
        if swap:
            tiles = tiles[::-1]
        if parts == 2:
            first = place[2] == 0
            outs[0][...] = jnp.where(first, tiles[0], tiles[1])
            outs[1][...] = jnp.where(first, tiles[1], tiles[0])
        else:
            for b in range(parts):
                outs[0][:, b * block : (b + 1) * block] = tiles[b]

    return body


def finish_body(flip):
    def body(a, b, out):
        total = (a[...] + b[...]).astype(BF)
        if not flip:
            out[...] = total
            return
        width = total.shape[1]
        block = flip_block(width)
        turn = reversal(block)
        for j in range(width // block):
            out[:, j * block : (j + 1) * block] = mm(
                total[:, width - (j + 1) * block : width - j * block], turn
            ).astype(BF)

    return body


def widen_body(tokens):
    def body(v_ref, g_ref, pack_in, *rest):
        wide, pack_out = rest[tokens:]
        pack_out[...] = pack_in[...]
        length, width = g_ref.shape
        wide[0:length, :] = v_ref[...].reshape(length, width).astype(F32)
        wide[length : 2 * length, :] = g_ref[...].astype(F32)

    return body


def local(shards, parts):
    pairs = shards // 2

    def body(
        hidden, complement, inner_weight, select_weight, step_weight, step_bias, decay_rate,
        skip_gain, cotangent, complement_cotangent,
    ):
        length, width = hidden.shape
        inner = inner_weight.shape[1]
        heads = step_bias.shape[0]
        head_width = inner // heads
        groups = 4
        chunk = inner // groups
        group_heads = heads // groups
        seq = lax.axis_index("seq")
        place = jnp.stack([seq % 2, seq // 2, lax.axis_index("chan")]).astype(jnp.int32)
        bias = step_bias.reshape(1, heads)
        rate = decay_rate.reshape(1, heads)
        rate_row = jnp.pad(rate, ((0, 0), (0, LANES - heads)))
        gain = skip_gain.reshape(1, heads)
        step_rows = step_weight.T
        cots = (cotangent, complement_cotangent)
        swap_pairs = [(a, a ^ 1) for a in range(shards)]
        edges = [
            [
                (2 * a + y, 2 * b + y)
                for z in range(start, pairs - 1, 2)
                for a, b in ((z, z + 1), (z + 1, z))
                for y in range(2)
            ]
            for start in range(2)
        ]
        swap = lambda x: lax.ppermute(x, "seq", swap_pairs)
        pack_shape = (length, 3 * LANES)
        pair_shape = (2 * LANES, chunk)
        wide_shape = (2 * length, chunk)
        token_shape = sds((8, LANES))
        work = lambda: [pltpu.VMEM((2,) + pair_shape, F32), pltpu.SemaphoreType.DMA((2,))]
        order = [(s, k) for s in range(2) for k in range(groups)]
        chunks = len(order)

        v_first, source, pack0, pack1, wide = run(
            start_body,
            [hidden, complement, Block(inner_weight, (width, chunk), (0, 0)), select_weight,
             step_rows, bias, rate, Block(cots[0], (length, chunk), (0, 0))],
            [sds((2, length, chunk), BF), sds((2 * length, width), BF), sds(pack_shape),
             sds(pack_shape), sds(wide_shape)],
            limit=60,
        )
        packs = (pack0, pack1)
        v_more = pl.pallas_call(
            more_body,
            grid=(groups - 1,),
            in_specs=[
                pl.BlockSpec((2 * length, width), lambda i: (0, 0)),
                pl.BlockSpec((width, chunk), lambda i: (0, i + 1)),
            ],
            out_specs=pl.BlockSpec((1, 2, length, chunk), lambda i: (i, 0, 0, 0)),
            out_shape=sds((groups - 1, 2, length, chunk), BF),
            compiler_params=pltpu.CompilerParams(vmem_limit_bytes=60 * 1024 * 1024),
            cost_estimate=pl.CostEstimate(flops=0, bytes_accessed=1024, transcendentals=0),
        )(source, inner_weight)

        def value_block(c):
            s, k = order[c]
            if k == 0:
                return Block(v_first, (1, length, chunk), (s, 0, 0))
            return Block(v_more, (1, 1, length, chunk), (k - 1, s, 0, 0))

        def cot_block(c):
            s, k = order[c]
            return Block(cots[s], (length, chunk), (0, k))

        def weight_block(c):
            return Block(inner_weight, (width, chunk), (0, order[c][1]))

        far_packs = [None, None]
        far = {}
        totals, within, post = {}, {}, {}
        got = ([], [])
        grads = [None, None]

        def do_pair(c, token):
            s, k = order[c]
            totals[c] = run(
                pair_body(k * group_heads, heads, head_width),
                [place, value_block(c), cot_block(c), far[c], packs[s], far_packs[s], token],
                [sds(pair_shape), sds(pair_shape), sds(pair_shape), sds((8, chunk))],
            )
            return totals[c][3]

        def do_within(c, token):
            s, k = order[c]
            within[c] = run(
                within_body(k * group_heads, heads, head_width),
                [packs[s], value_block(c), cot_block(c), rate_row, token],
                [sds((length, chunk)), sds((length, chunk)), sds((length, 2 * LANES)), sds((length, LANES))],
                scratch=[pltpu.VMEM((2, LANES, length), F32)],
            )
            return within[c][3]

        def do_post(c, token):
            s, k = order[c]
            last = pairs - 1
            ups = [got[(z + 1) % 2][max(c + z - 1, c)] for z in range(pairs)]
            downs = [got[(last - z) % 2][max(c + z - 1, c)] for z in range(pairs)]
            post[c] = run(
                post_body(k * group_heads, heads, head_width, len(ups), len(downs)),
                [place, packs[s], far_packs[s], value_block(c), cot_block(c), *within[c],
                 totals[c][2], gain, rate_row, token, *map(Far, ups), *map(Far, downs)],
                [sds((length, chunk), BF), sds((length, chunk), BF), sds((length, 2 * LANES)), sds((length, LANES))],
                scratch=work(),
            )
            return post[c][3]

        def do_partial(cs, token):
            return run(
                partial_body(len(cs)),
                [token, *[post[c][1] for c in cs], *[weight_block(c) for c in cs]],
                [sds((length, width))],
            )[0]

        def do_term(s, cs, before, token):
            mine = [c for c in range(chunks) if order[c][0] == s]
            shares = [sds((length, width // parts))] * 2 if parts == 2 else [sds((length, width))]
            term = run(
                term_body(len(mine), len(cs), heads, parts, s == 1),
                [place, packs[s], select_weight, step_rows, before,
                 *[post[c][1] for c in cs], *[weight_block(c) for c in cs],
                 *[post[c][2] for c in mine], *[post[c][3] for c in mine]],
                shares,
            )
            if parts == 2:
                return term[0], lax.ppermute(term[1], "chan", [(0, 1), (1, 0)])
            share = lax.psum_scatter(term[0], "chan", scatter_dimension=1, tiled=True)
            return share, jnp.zeros_like(share)

        def do_finish(s, share):
            return run(finish_body(s == 1), list(share), [sds((length, width // parts), BF)])[0]

        def do_step(k, widen, ends):
            steps = chunks + pairs - 2
            sending = 0 <= k < steps
            has = [sending and 0 <= k - z < chunks and z < pairs - 1 for z in range(pairs)]
            ins = [place]
            for d in range(2):
                ins += [Far(totals[k - z][d]) for z in range(pairs) if has[z]]
                ins += [totals[k - z][3] for z in range(pairs) if has[z]]
            if k > 0:
                ins += [Near(got[0][-1]), Near(got[1][-1])]
            if widen is not None:
                ins += [value_block(widen), cot_block(widen)]
            ins += [Far(e) for e in ends]
            outs = [sds(pair_shape), sds(pair_shape), token_shape]
            if widen is not None:
                outs.append(sds(wide_shape))
            return run(
                step_body(has, k <= 0, widen is not None, len(ends)), ins, outs, scratch=work(),
                near_outs=(0, 1, 3),
            )

        far[0] = swap(wide)
        far_packs[0] = swap(pack0)
        early = [do_within(c, Far(wide)) for c in range(groups)]
        wide1, pack_late = run(
            widen_body(2 + len(early)),
            [value_block(1), cot_block(1), pack1, *map(Far, [far[0], far_packs[0], *early])],
            [sds(wide_shape), sds(pack_shape)],
        )
        far[1] = swap(wide1)
        ends = [do_pair(0, Far(wide1)), wide1]
        steps = chunks + pairs - 2
        halfway = None
        share = [None, None]
        for k in range(steps):
            made = do_step(k, k + 2 if k + 2 < chunks else None, ends)
            token = Far(made[2])
            for d in range(2):
                got[d].append(lax.ppermute(made[d], "seq", edges[d]))
            ends = []
            if k + 2 < chunks:
                far[k + 2] = swap(made[3])
                ends.append(far[k + 2])
            if k == groups - 2:
                far_packs[1] = swap(pack_late)
                ends.append(far_packs[1])
            if k + 1 < chunks:
                ends.append(do_pair(k + 1, token))
            if k < groups:
                ends.append(do_within(groups + k, token))
            c = k - pairs + 1
            if c >= 0:
                ends.append(do_post(c, token))
                if c == groups:
                    halfway = do_partial(list(range(groups)), token)
                    share[0] = do_term(0, [], halfway, token)
                    ends.append(share[0][0])
                if c == groups + 2:
                    grads[0] = do_finish(0, share[0])
                    halfway = do_partial(list(range(groups, groups + 2)), token)
                    ends += [grads[0], halfway]
        for c in range(chunks):
            if c not in post:
                do_post(c, Far(post[c - 1][3]))
        grads[1] = do_finish(1, do_term(1, list(range(groups + 2, chunks)), halfway, None))
        outs = [
            jnp.concatenate([post[c][0] for c in range(s * groups, (s + 1) * groups)], axis=1)
            for s in range(2)
        ]
        return (outs[0], outs[1], grads[0], grads[1])

    return body


def solution(mesh):
    rows = P(("dp", "seq"), None)
    both = P(("dp", "seq"), "chan")
    in_specs = (
        rows, rows, P(None, "chan"), P(), P(None, "chan"),
        P("chan"), P("chan"), P("chan"), both, both,
    )
    return jax.shard_map(
        local(mesh.shape["seq"], mesh.shape["chan"]),
        mesh=mesh,
        in_specs=in_specs,
        out_specs=(both,) * 4,
        check_vma=False,
    )
```

```python
import jax
import jax.numpy as jnp
from jax import lax
from jax.experimental import pallas as pl
from jax.experimental.pallas import tpu as pltpu
from jax.sharding import PartitionSpec as P

BF = jnp.bfloat16
F32 = jnp.float32
LANES = 128


def mm(a, b, ca=1, cb=0):
    return lax.dot_general(a, b, (((ca,), (cb,)), ((), ())), preferred_element_type=F32)


def halves(x):
    high = x.astype(BF)
    return high, (x - high.astype(F32)).astype(BF)


def mm_exact(a, b, ca=1, cb=0):
    first, rest = b.astype(BF), None
    rest = b - first.astype(F32)
    second = rest.astype(BF)
    third = (rest - second.astype(F32)).astype(BF)
    return mm(a, first, ca, cb) + mm(a, second, ca, cb) + mm(a, third, ca, cb)


def iotas(rows, columns):
    return (
        lax.broadcasted_iota(jnp.int32, (rows, columns), 0),
        lax.broadcasted_iota(jnp.int32, (rows, columns), 1),
    )


def spread(weights, base, width, head_width):
    heads = weights[0].shape[1]
    row, channel = iotas(2 * heads, width)
    start = (jnp.where(row >= heads, row - heads, row) - base) * head_width
    pick = ((channel >= start) & (channel < start + head_width)).astype(BF)
    stacked = jnp.concatenate(weights, axis=0) if len(weights) > 1 else weights[0]
    out = mm(jnp.concatenate(halves(stacked), axis=1), pick)
    result, at = [], 0
    for w in weights:
        result.append(out[at : at + w.shape[0]])
        at += w.shape[0]
    return result


def spread_rows(rows, base, width, head_width):
    heads = rows[0].shape[1]
    wide = spread([jnp.broadcast_to(r, (8, heads)) for r in rows], base, width, head_width)
    return [w[0:1] for w in wide]


def gather_heads(parts, base, head_width):
    width = parts[0].shape[1]
    channel, head = iotas(width, LANES)
    start = (head - base) * head_width
    pick = ((channel >= start) & (channel < start + head_width)).astype(BF)
    out = mm(jnp.concatenate([x.astype(BF) for x in parts], axis=0), pick)
    result, at = [], 0
    for x in parts:
        result.append(out[at : at + x.shape[0]])
        at += x.shape[0]
    return result


def reversal(size):
    i, j = iotas(size, size)
    return (i + j == size - 1).astype(BF)


def flip_block(size):
    return 256 if size % 256 == 0 else 128


def sds(shape, dtype=F32):
    return jax.ShapeDtypeStruct(shape, dtype)


class Block:
    def __init__(self, array, shape, index):
        self.array, self.shape, self.index = array, shape, index


class Late:
    def __init__(self, item):
        self.item = item


class Near:
    def __init__(self, array):
        self.array = array


class Pin:
    def __init__(self, array):
        self.array = array


class Far:
    def __init__(self, array):
        self.array = array


def run(body, ins, outs, scratch=(), limit=24, near_outs=()):
    specs, arrays, plan = [], [], []
    for item in ins:
        late = isinstance(item, Late)
        item = item.item if late else item
        if isinstance(item, (Near, Pin, Far)):
            space = {Near: pltpu.VMEM, Pin: pltpu.HBM, Far: pl.ANY}[type(item)]
            specs.append(pl.BlockSpec(memory_space=space))
            arrays.append(item.array)
            plan.append(None)
        elif not isinstance(item, Block) and item.dtype == jnp.int32:
            specs.append(pl.BlockSpec(memory_space=pltpu.SMEM))
            arrays.append(item)
            plan.append(None)
        else:
            if not isinstance(item, Block):
                item = Block(item, item.shape, (0,) * item.ndim)
            specs.append(pl.BlockSpec(memory_space=pltpu.HBM))
            arrays.append(item.array)
            plan.append((item, late))
    out_specs = [
        pl.BlockSpec(memory_space=pltpu.VMEM if n in near_outs else pltpu.HBM)
        for n in range(len(outs))
    ]
    copied = [q for q in plan if q is not None]
    stored = [o for n, o in enumerate(outs) if n not in near_outs]
    holds = [pltpu.VMEM(q[0].shape, q[0].array.dtype) for q in copied]
    holds += [pltpu.VMEM(o.shape, o.dtype) for o in stored]
    sems = [pltpu.SemaphoreType.DMA((max(len(copied), 1),)), pltpu.SemaphoreType.DMA((max(len(stored), 1),))]

    def kernel(*refs):
        refs = list(refs)
        take = lambda n: [refs.pop(0) for _ in range(n)]
        sources, targets = take(len(ins)), take(len(outs))
        in_holds, out_holds = take(len(copied)), take(len(stored))
        in_sems, out_sems = take(2)
        args, first, later, n = [], [], [], 0
        for ref, q in zip(sources, plan):
            if q is None:
                args.append(ref)
                continue
            item, late = q
            if item.shape != item.array.shape:
                ref = ref.at[tuple(pl.ds(i * b, b) for i, b in zip(item.index, item.shape))]
            copy = pltpu.make_async_copy(ref, in_holds[n], in_sems.at[n])
            copy.start()
            (later if late else first).append(copy)
            args.append(in_holds[n])
            n += 1
        for copy in first:
            copy.wait()
        results, back, n = [], [], 0
        for k, ref in enumerate(targets):
            if k in near_outs:
                results.append(ref)
            else:
                back.append(pltpu.make_async_copy(out_holds[n], ref, out_sems.at[n]))
                results.append(out_holds[n])
                n += 1

        def wait_late():
            for copy in later:
                copy.wait()

        body(*args, *results, *refs, **({"wait_late": wait_late} if later else {}))
        for copy in back:
            copy.start()
        for copy in back:
            copy.wait()

    return pl.pallas_call(
        kernel,
        in_specs=specs,
        out_specs=out_specs,
        out_shape=outs,
        scratch_shapes=holds + sems + list(scratch),
        compiler_params=pltpu.CompilerParams(vmem_limit_bytes=limit * 1024 * 1024),
        cost_estimate=pl.CostEstimate(flops=0, bytes_accessed=1024, transcendentals=0),
    )(*arrays)


def start_body(hidden, other, weight, select, step, bias, rate, cot, v_out, source, pack0, pack1, wide):
    length, width = hidden.shape
    heads = bias.shape[1]
    source[0:length, :] = hidden[...]
    block = flip_block(width)
    turn = reversal(block)
    for j in range(width // block):
        source[length : 2 * length, j * block : (j + 1) * block] = mm(
            other[:, width - (j + 1) * block : width - j * block], turn
        ).astype(BF)
    keys = mm(source[...], select[...]).astype(BF).astype(F32)
    state = keys.shape[1] // 2
    raw = mm(source[...], step[...], 1, 1) + bias[...]
    dt = jnp.maximum(raw, 0.0) + jnp.log1p(jnp.exp(-jnp.abs(raw)))
    rise = jax.nn.sigmoid(raw)
    i, j = iotas(length, length)
    lower = (i >= j).astype(BF)
    for s, pack in enumerate((pack0, pack1)):
        rows = slice(s * length, (s + 1) * length)
        drop = dt[rows] * rate[...]
        total = mm_exact(lower, drop)
        pack[...] = jnp.zeros(pack.shape, F32)
        pack[:, 0 : 2 * state] = keys[rows]
        at = 2 * state
        for part in (dt[rows], total, total - drop, rise[rows]):
            pack[:, at : at + heads] = part
            at += heads
    piece = mm(source[...], weight[...]).astype(BF)
    for s in range(2):
        v_out[s] = piece[s * length : (s + 1) * length]
    wide[0:length, :] = piece[0:length].astype(F32)
    wide[length : 2 * length, :] = cot[...].astype(F32)
    for n in range(3):
        row = 2 * length + n * piece_rows(length, wide.shape[1])
        put_piece(wide, row, pack0[:, n * LANES : (n + 1) * LANES])


def more_body(source, weight, v_out):
    length = v_out.shape[2]
    piece = mm(source[...], weight[...]).astype(BF)
    for s in range(2):
        v_out[0, s] = piece[s * length : (s + 1) * length]


class Pack:
    def __init__(self, write, read, stats, heads):
        self.write, self.read = write, read
        self.dt = stats[:, 0:heads]
        self.total = stats[:, heads : 2 * heads]
        self.before = stats[:, 2 * heads : 3 * heads]
        last = self.total.shape[0]
        self.whole = self.total[last - 1 : last, :]
        self.from_start = jnp.exp(-self.total)
        self.from_end = jnp.exp(self.before - self.whole)
        self.to_end = jnp.exp(self.total - self.whole)
        self.to_start = jnp.exp(-self.before)
        self.through = jnp.exp(-self.whole)


def own_pack(ref, heads):
    return Pack(*[ref[:, n * LANES : (n + 1) * LANES] for n in range(3)], heads)


def piece_rows(length, width):
    return length // (width // LANES)


def put_piece(ref, row, piece):
    count = piece_rows(piece.shape[0], ref.shape[1])
    for b in range(ref.shape[1] // LANES):
        ref[row : row + count, b * LANES : (b + 1) * LANES] = piece[b * count : (b + 1) * count]


def get_piece(ref, row, length):
    count = piece_rows(length, ref.shape[1])
    return jnp.concatenate(
        [
            ref[row : row + count, b * LANES : (b + 1) * LANES]
            for b in range(ref.shape[1] // LANES)
        ],
        axis=0,
    )


def pair_body(base, heads, head_width, piece_at):
    def body(place, v_own, g_own, x_far, far0, far1, far2, own_ref, token, up, down, near, keep):
        first = place[0] == 0
        length, width = g_own.shape
        own = own_pack(own_ref, heads)
        far = Pack(*[get_piece(f, at, length) for f, at in zip((far0, far1, far2), piece_at)], heads)
        own_row, far_row = own.through, far.through
        rows = spread_rows([own_row * far_row, far_row], base, width, head_width)
        keep[...] = jnp.zeros(keep.shape, F32)
        keep[0:1, :] = rows[0]
        keep[1:2, :] = rows[1]
        own_up, own_down = jnp.where(first, far_row, 1.0), jnp.where(first, 1.0, far_row)
        far_up, far_down = jnp.where(first, 1.0, own_row), jnp.where(first, own_row, 1.0)
        for kind in range(2):
            rows = slice(kind * LANES, (kind + 1) * LANES)
            if kind == 0:
                keys = (own.write, far.write)
                ups = (own.dt * own.to_end, far.dt * far.to_end)
                downs = (own.dt * own.to_start, far.dt * far.to_start)
            else:
                keys = (own.read, far.read)
                ups = (own.from_end, far.from_end)
                downs = (own.from_start, far.from_start)
            x_own = (v_own if kind == 0 else g_own)[...].reshape(length, width).astype(F32)
            x_other = x_far[kind * length : (kind + 1) * length, :]
            w = spread(
                [ups[0] * own_up, ups[1] * far_up, downs[0] * own_down, downs[1] * far_down,
                 jnp.where(first, downs[1], ups[1])],
                base, width, head_width,
            )
            key = jnp.concatenate(keys, axis=0).astype(BF)
            both = lambda a, b: jnp.concatenate([(a * x_own).astype(BF), (b * x_other).astype(BF)], axis=0)
            up[rows, :] = mm(key, both(w[0], w[1]), 0, 0)
            down[rows, :] = mm(key, both(w[2], w[3]), 0, 0)
            near[rows, :] = mm(keys[1].astype(BF), (w[4] * x_other).astype(BF), 0, 0)

    return body


def fetch_start(options, index, target, sem):
    for z, option in enumerate(options):
        if option is not None:

            @pl.when(index == z)
            def _():
                pltpu.make_async_copy(option, target, sem).start()


def fetch_wait(options, index, target, sem):
    for z, option in enumerate(options):
        if option is not None:

            @pl.when(index == z)
            def _():
                pltpu.make_async_copy(option, target, sem).wait()


def step_body(has, first_step, widen, piece, tokens):
    pairs = len(has)

    def body(place, *rest):
        rest = list(rest)
        take = lambda n: [rest.pop(0) for _ in range(n)]
        sides = []
        for d in range(2):
            totals = [take(1)[0] if h else None for h in has]
            keeps = [take(1)[0] if h else None for h in has]
            sides.append((totals, keeps))
        got = None if first_step else take(2)
        if widen:
            v_ref, g_ref = take(2)
        piece_ref = take(1)[0] if piece else None
        take(tokens)
        sends = take(2)
        token = take(1)[0]
        wide = take(1)[0] if widen else None
        bufs, sems = take(2)
        spots = (place[1], pairs - 1 - place[1])
        for d, (totals, keeps) in enumerate(sides):
            fetch_start(totals, spots[d], bufs.at[d], sems.at[d])
        if widen:
            length, width = g_ref.shape
            wide[0:length, :] = v_ref[...].reshape(length, width).astype(F32)
            wide[length : 2 * length, :] = g_ref[...].astype(F32)
            if piece:
                put_piece(wide, 2 * length, piece_ref[...])
        token[...] = jnp.zeros(token.shape, F32)
        for d, (totals, keeps) in enumerate(sides):
            fetch_wait(totals, spots[d], bufs.at[d], sems.at[d])
            for n in range(pairs):
                z = n if d == 0 else pairs - 1 - n
                send = sends[(z + d) % 2]

                @pl.when(spots[d] == n)
                def _():
                    if not has[n]:
                        send[...] = jnp.zeros(send.shape, F32)
                    elif got is None or n == 0:
                        send[...] = bufs[d]
                    else:
                        send[...] = bufs[d] + keeps[n][0:1, :] * got[(z + 1 + d) % 2][...]

    return body


def within_body(base, heads, head_width):
    def body(own_ref, v_ref, g_ref, rate, token, y_out, x_out, keys_out, steps_out, cols_s):
        own = own_pack(own_ref, heads)
        length, width = g_ref.shape
        write, read = own.write.astype(BF), own.read.astype(BF)
        scores = mm(read, write, 1, 1)
        i, j = iotas(length, length)
        low = i > j
        high = i < j
        doubled = jnp.where(i == j, 2.0, 1.0).astype(F32)
        scores2 = scores * doubled
        turned = own_ref[:, 2 * LANES : 3 * LANES].T
        lane = lax.broadcasted_iota(jnp.int32, (length, LANES), 1)
        d_scores = jnp.zeros((length, length), F32)
        out_low = jnp.zeros((length, LANES), F32)
        out_high = jnp.zeros((length, LANES), F32)
        cols_s[...] = jnp.zeros(cols_s.shape, F32)
        v_all = v_ref[...].reshape(length, width)
        per = LANES // head_width
        for n in range(width // LANES):
            at = slice(n * LANES, (n + 1) * LANES)
            v, g = v_all[:, at], g_ref[:, at]
            mine = [(lane >= m * head_width) & (lane < (m + 1) * head_width) for m in range(per)]
            v_heads = jnp.concatenate([jnp.where(x, v, jnp.zeros_like(v)) for x in mine], axis=0)
            g_heads = jnp.concatenate([jnp.where(x, g, jnp.zeros_like(g)) for x in mine], axis=0)
            products = mm(g_heads, v, 1, 1)
            plains, steppeds = [], []
            for m in range(per):
                h = base + n * per + m
                c_col = own.total[:, h : h + 1]
                e_col = own.before[:, h : h + 1]
                dt_row = turned[h : h + 1, :]
                c_row = turned[heads + h : heads + h + 1, :]
                e_row = turned[2 * heads + h : 2 * heads + h + 1, :]
                decay = jnp.exp(jnp.where(low, c_row - c_col, e_col - e_row))
                plain = decay * scores2
                plains.append(plain.astype(BF))
                steppeds.append((plain * dt_row).astype(BF))
                inner = decay * dt_row * products[m * length : (m + 1) * length]
                d_scores = d_scores + inner
                flow = inner * scores
                flow_low = jnp.where(low, flow, 0.0)
                flow_high = jnp.where(high, flow, 0.0)
                out_low = jnp.where(lane == h, jnp.sum(flow_low, 1, keepdims=True), out_low)
                out_high = jnp.where(lane == h, jnp.sum(flow_high, 1, keepdims=True), out_high)
                cols_s[0, h : h + 1, :] = jnp.sum(flow_low, 0, keepdims=True)
                cols_s[1, h : h + 1, :] = jnp.sum(flow_high, 0, keepdims=True)
            y_out[:, at] = mm(jnp.concatenate(steppeds, axis=1), v_heads)
            x_out[:, at] = mm(jnp.concatenate(plains, axis=0), g_heads, 0, 0)
        d_scores = (d_scores * doubled).astype(BF)
        keys_out[:, 0:LANES] = mm(d_scores, read, 0, 0)
        keys_out[:, LANES : 2 * LANES] = mm(d_scores, write)
        net_low = out_low - cols_s[0].T
        net_high = out_high - cols_s[1].T
        at_or_after = (j >= i).astype(BF)
        after = (j > i).astype(BF)
        steps_out[...] = -rate[...] * (mm_exact(at_or_after, net_low) - mm_exact(after, net_high))

    return body


def post_body(base, heads, head_width, ups, downs):
    def body(
        place, own_ref, v_ref, g_ref, yw, xw, keys_w, steps_w, near, keep, skip, rate, token, *rest
    ):
        up_in, down_in = rest[0:ups], rest[ups : ups + downs]
        mixed, dv_out, keys_out, steps_out, bufs, sems = rest[ups + downs :]
        up_spot, down_spot = place[1], len(up_in) - 1 - place[1]
        fetch_start(up_in, up_spot, bufs.at[0], sems.at[0])
        fetch_start(down_in, down_spot, bufs.at[1], sems.at[1])
        first = place[0] == 0
        own = own_pack(own_ref, heads)
        length, width = g_ref.shape
        far_row = keep[1:2, :]
        own_row, gain = spread_rows([own.through, skip[...]], base, width, head_width)
        up_row = jnp.where(first, 1.0, far_row)
        down_row = jnp.where(first, far_row, 1.0)
        dt, from_start, from_end, to_end, to_start = spread(
            [own.dt, own.from_start, own.from_end, own.to_end, own.to_start],
            base, width, head_width,
        )
        write, read = own.write.astype(BF), own.read.astype(BF)
        v = v_ref[...].reshape(length, width).astype(F32)
        g = g_ref[...].astype(F32)
        fetch_wait(up_in, up_spot, bufs.at[0], sems.at[0])
        fetch_wait(down_in, down_spot, bufs.at[1], sems.at[1])
        up = up_row * bufs[0] + jnp.where(first, 0.0, near[...])
        down = down_row * bufs[1] + jnp.where(first, near[...], 0.0)
        p, ab = up[0:LANES], up[LANES : 2 * LANES]
        q, af = down[0:LANES], down[LANES : 2 * LANES]
        crossing = jnp.sum(p * af + q * ab, axis=0, keepdims=True)
        p, q, af, ab = p.astype(BF), q.astype(BF), af.astype(BF), ab.astype(BF)
        y_p = from_start * mm(read, p)
        y_q = from_end * mm(read, q)
        x_f = to_end * mm(write, af)
        x_b = to_start * mm(write, ab)
        mixed[...] = (yw[...] + y_p + y_q + gain * v).astype(BF)
        x = xw[...] + x_f + x_b
        dv_out[...] = (dt * x + gain * g).astype(BF)
        dtv = dt * v
        keys_out[:, 0:LANES] = (
            keys_w[:, 0:LANES]
            + mm((to_end * dtv).astype(BF), af, 1, 1)
            + mm((to_start * dtv).astype(BF), ab, 1, 1)
        )
        keys_out[:, LANES : 2 * LANES] = (
            keys_w[:, LANES : 2 * LANES]
            + mm((from_start * g).astype(BF), p, 1, 1)
            + mm((from_end * g).astype(BF), q, 1, 1)
        )
        lane = lax.broadcasted_iota(jnp.int32, (length, LANES), 1)
        steps = jnp.where(lane < heads, own_ref[:, 2 * LANES : 3 * LANES], 0.0)
        direct, a_p, a_q, b_f, b_b, through = gather_heads(
            [v * x, g * y_p, g * y_q, v * x_f, v * x_b, jnp.broadcast_to(crossing * own_row, (8, width))],
            base, head_width,
        )
        i, j = iotas(length, length)
        masks = jnp.concatenate([j >= i, j <= i, j < i, j > i], axis=1).astype(F32).astype(BF)
        high, low = halves(jnp.concatenate([a_p, a_q, b_f * steps, b_b * steps], axis=0))
        flow = mm(masks, high) + mm(masks, low) + through[0:1]
        steps_out[...] = steps_w[...] + direct - rate[...] * flow

    return body


def partial_body(groups, more):
    def body(token, *rest):
        dvs, weights, rest = rest[0:groups], rest[groups : 2 * groups], rest[2 * groups :]
        out = rest[-1]
        total = mm(dvs[0][...], weights[0][...], 1, 1)
        for k in range(1, groups):
            total = total + mm(dvs[k][...], weights[k][...], 1, 1)
        out[...] = total + rest[0][...] if more else total

    return body


def term_body(groups, tails, heads, parts, swap):
    def body(place, own_ref, select, step, before, *rest, wait_late=None):
        dvs, weights = rest[0:tails], rest[tails : 2 * tails]
        rest = rest[2 * tails :]
        keys, steps = rest[0:groups], rest[groups : 2 * groups]
        outs = rest[2 * groups :]
        if wait_late is not None:
            wait_late()
        d_keys, d_steps = keys[0][...], steps[0][...]
        for a, b in zip(keys[1:], steps[1:]):
            d_keys = d_keys + a[...]
            d_steps = d_steps + b[...]
        d_raw = d_steps[:, 0:heads] * own_ref[:, 2 * LANES + 3 * heads : 2 * LANES + 4 * heads]
        keys_high, keys_low = halves(d_keys)
        raw_high, raw_low = halves(d_raw)
        width = select.shape[0]
        block = width // parts
        tiles = []
        for b in range(parts):
            rows = slice(b * block, (b + 1) * block)
            total = before[:, rows]
            total = total + mm(keys_high, select[rows, :], 1, 1) + mm(keys_low, select[rows, :], 1, 1)
            total = total + mm(raw_high, step[:, rows]) + mm(raw_low, step[:, rows])
            for k in range(tails):
                total = total + mm(dvs[k][...], weights[k][rows, :], 1, 1)
            tiles.append(total)
        if swap:
            tiles = tiles[::-1]
        if parts == 2:
            first = place[2] == 0
            outs[0][...] = jnp.where(first, tiles[0], tiles[1])
            outs[1][...] = jnp.where(first, tiles[1], tiles[0])
        else:
            for b in range(parts):
                outs[0][:, b * block : (b + 1) * block] = tiles[b]

    return body


def last_body(post, term, post_ins, shares):
    def body(place, *rest, wait_late):
        rest = list(rest)
        take = lambda n: [rest.pop(0) for _ in range(n)]
        for_post = take(post_ins)
        select, step, before, weight = take(4)
        others = take(len(rest) - 1 - shares - 5)
        half = len(others) // 2
        mixed, *outs = take(1 + shares)
        bufs, sems, dv, keys, steps = take(5)
        post(place, *for_post, mixed, dv, keys, steps, bufs, sems)
        wait_late()
        term(
            place, for_post[0], select, step, before, dv, weight,
            *others[:half], keys, *others[half:], steps, *outs,
        )

    return body


def finish_body(flip):
    def body(a, b, out):
        total = (a[...] + b[...]).astype(BF)
        if not flip:
            out[...] = total
            return
        width = total.shape[1]
        block = flip_block(width)
        turn = reversal(block)
        for j in range(width // block):
            out[:, j * block : (j + 1) * block] = mm(
                total[:, width - (j + 1) * block : width - j * block], turn
            ).astype(BF)

    return body


def widen_body(tokens):
    def body(v_ref, g_ref, *rest):
        wide = rest[tokens]
        length, width = g_ref.shape
        wide[0:length, :] = v_ref[...].reshape(length, width).astype(F32)
        wide[length : 2 * length, :] = g_ref[...].astype(F32)

    return body


def local(shards, parts):
    pairs = shards // 2

    def body(
        hidden, complement, inner_weight, select_weight, step_weight, step_bias, decay_rate,
        skip_gain, cotangent, complement_cotangent,
    ):
        length, width = hidden.shape
        inner = inner_weight.shape[1]
        heads = step_bias.shape[0]
        head_width = inner // heads
        groups = 4
        chunk = inner // groups
        group_heads = heads // groups
        seq = lax.axis_index("seq")
        place = jnp.stack([seq % 2, seq // 2, lax.axis_index("chan")]).astype(jnp.int32)
        bias = step_bias.reshape(1, heads)
        rate = decay_rate.reshape(1, heads)
        rate_row = jnp.pad(rate, ((0, 0), (0, LANES - heads)))
        gain = skip_gain.reshape(1, heads)
        step_rows = step_weight.T
        cots = (cotangent, complement_cotangent)
        swap_pairs = [(a, a ^ 1) for a in range(shards)]
        edges = []
        for start in range(2):
            meets = [(z, z + 1) for z in range(start, pairs - 1, 2)]
            paired = sum(meets, ())
            meets += [(b, a) for a, b in meets] + [(z, z) for z in range(pairs) if z not in paired]
            edges.append([(2 * a + y, 2 * b + y) for a, b in meets for y in range(2)])
        swap = lambda x: lax.ppermute(x, "seq", swap_pairs)
        pack_shape = (length, 3 * LANES)
        pair_shape = (2 * LANES, chunk)
        wide_shape = lambda pieces: sds((2 * length + pieces * piece_rows(length, chunk), chunk))
        token_shape = sds((8, LANES))
        work = lambda: [pltpu.VMEM((2,) + pair_shape, F32), pltpu.SemaphoreType.DMA((2,))]
        order = [(s, k) for s in range(2) for k in range(groups)]
        chunks = len(order)

        v_first, source, pack0, pack1, wide = run(
            start_body,
            [hidden, complement, Block(inner_weight, (width, chunk), (0, 0)), select_weight,
             step_rows, bias, rate, Block(cots[0], (length, chunk), (0, 0))],
            [sds((2, length, chunk), BF), sds((2 * length, width), BF), sds(pack_shape),
             sds(pack_shape), wide_shape(3)],
            near_outs=(4,),
            limit=60,
        )
        packs = (pack0, pack1)
        v_more = pl.pallas_call(
            more_body,
            grid=(groups - 1,),
            in_specs=[
                pl.BlockSpec((2 * length, width), lambda i: (0, 0)),
                pl.BlockSpec((width, chunk), lambda i: (0, i + 1)),
            ],
            out_specs=pl.BlockSpec((1, 2, length, chunk), lambda i: (i, 0, 0, 0)),
            out_shape=sds((groups - 1, 2, length, chunk), BF),
            compiler_params=pltpu.CompilerParams(vmem_limit_bytes=62 * 1024 * 1024),
            cost_estimate=pl.CostEstimate(flops=0, bytes_accessed=1024, transcendentals=0),
        )(source, inner_weight)

        def value_block(c):
            s, k = order[c]
            if k == 0:
                return Block(v_first, (1, length, chunk), (s, 0, 0))
            return Block(v_more, (1, 1, length, chunk), (k - 1, s, 0, 0))

        def cot_block(c):
            s, k = order[c]
            return Block(cots[s], (length, chunk), (0, k))

        def weight_block(c):
            return Block(inner_weight, (width, chunk), (0, order[c][1]))

        far = {}
        totals, within, post = {}, {}, {}
        got = ([], [])
        grads = [None, None]
        riders = {2 + n: n for n in range(3)}
        steps = chunks + pairs - 2

        def do_pair(c, token):
            s, k = order[c]
            rows = piece_rows(length, chunk)
            if s == 0:
                pieces, piece_at = [far[0]] * 3, [2 * length + n * rows for n in range(3)]
            else:
                pieces, piece_at = [far[r] for r in riders], [2 * length] * 3
            totals[c] = run(
                pair_body(k * group_heads, heads, head_width, piece_at),
                [place, value_block(c), cot_block(c), Near(far[c]), *map(Near, pieces), packs[s], token],
                [sds(pair_shape), sds(pair_shape), sds(pair_shape), sds((8, chunk))],
            )
            return Pin(totals[c][3])

        def do_within(c, token):
            s, k = order[c]
            within[c] = run(
                within_body(k * group_heads, heads, head_width),
                [packs[s], value_block(c), cot_block(c), rate_row, token],
                [sds((length, chunk)), sds((length, chunk)), sds((length, 2 * LANES)), sds((length, LANES))],
                scratch=[pltpu.VMEM((2, LANES, length), F32)],
            )
            return Pin(within[c][3])

        def post_parts(c, token):
            s, k = order[c]
            last = pairs - 1
            ups = [got[(z + 1) % 2][max(c + z - 1, c)] for z in range(pairs)]
            downs = [got[(last - z) % 2][max(c + z - 1, c)] for z in range(pairs)]
            body = post_body(k * group_heads, heads, head_width, len(ups), len(downs))
            ins = [packs[s], value_block(c), cot_block(c), *within[c], totals[c][2], totals[c][3],
                   gain, rate_row, token, *map(Far, ups), *map(Far, downs)]
            return body, ins

        post_shapes = [
            sds((length, chunk), BF), sds((length, chunk), BF), sds((length, 2 * LANES)), sds((length, LANES))
        ]

        def do_post(c, token):
            body, ins = post_parts(c, token)
            post[c] = run(body, [place, *ins], post_shapes, scratch=work())
            return Pin(post[c][3])

        def do_partial(cs, token, before=None):
            return run(
                partial_body(len(cs), before is not None),
                [token, *[post[c][1] for c in cs], *[weight_block(c) for c in cs]]
                + ([] if before is None else [before]),
                [sds((length, width))],
            )[0]

        shares = [sds((length, width // parts))] * 2 if parts == 2 else [sds((length, width))]
        near_share = (1,) if parts == 2 else ()

        def send_share(term):
            if parts == 2:
                return term[0], lax.ppermute(term[1], "chan", [(0, 1), (1, 0)])
            share = lax.psum_scatter(term[0], "chan", scatter_dimension=1, tiled=True)
            return share, jnp.zeros_like(share)

        def do_term(s, before):
            mine = [c for c in range(chunks) if order[c][0] == s]
            return send_share(run(
                term_body(len(mine), 0, heads, parts, s == 1),
                [place, packs[s], select_weight, step_rows, before,
                 *[post[c][2] for c in mine], *[post[c][3] for c in mine]],
                shares,
                near_outs=near_share,
            ))

        def do_last(c, before, token):
            s = order[c][0]
            mine = [n for n in range(chunks) if order[n][0] == s and n != c]
            body, ins = post_parts(c, token)
            late = [select_weight, step_rows, before, weight_block(c),
                    *[post[n][2] for n in mine], *[post[n][3] for n in mine]]
            out = run(
                last_body(
                    body, term_body(len(mine) + 1, 1, heads, parts, s == 1), len(ins), len(shares)
                ),
                [place, *ins, *map(Late, late)],
                [post_shapes[0], *shares],
                scratch=work() + [pltpu.VMEM(o.shape, o.dtype) for o in post_shapes[1:]],
                near_outs=tuple(n + 1 for n in near_share),
            )
            post[c] = (out[0],)
            return send_share(out[1:])

        def do_finish(s, share):
            mine, other = share
            return run(
                finish_body(s == 1), [mine, Near(other)], [sds((length, width // parts), BF)]
            )[0]

        def do_step(k, widen, ends):
            has = [0 <= k - z < chunks and z < pairs - 1 for z in range(pairs)]
            ins = [place]
            for d in range(2):
                ins += [Pin(totals[k - z][d]) for z in range(pairs) if has[z]]
                ins += [totals[k - z][3] for z in range(pairs) if has[z]]
            if k > 0:
                ins += [Near(got[0][-1]), Near(got[1][-1])]
            outs = [sds(pair_shape), sds(pair_shape), token_shape]
            if widen is not None:
                ins += [value_block(widen), cot_block(widen)]
                outs.append(wide_shape(1 if widen in riders else 0))
            if widen in riders:
                ins.append(Block(packs[1], (length, LANES), (0, riders[widen])))
            return run(
                step_body(has, k == 0, widen is not None, widen in riders, len(ends)),
                ins + ends, outs, scratch=work(), near_outs=(0, 1, 3),
            )

        far[0] = swap(wide)
        early = [do_within(c, Pin(pack0)) for c in range(groups)]
        wide1 = run(
            widen_body(1 + len(early)),
            [value_block(1), cot_block(1), Far(far[0]), *early],
            [wide_shape(0)],
            near_outs=(0,),
        )[0]
        far[1] = swap(wide1)
        ends = [do_pair(0, Far(wide1)), Far(wide1)]
        halfway = None
        share = None
        for k in range(steps):
            made = do_step(k, k + 2 if k + 2 < chunks else None, ends)
            token = Pin(made[2])
            for d in range(2):
                got[d].append(lax.ppermute(made[d], "seq", edges[d]))
            ends = []
            if k + 2 < chunks:
                far[k + 2] = swap(made[3])
            if k + 1 < chunks:
                ends.append(do_pair(k + 1, token))
            if k < groups:
                ends.append(do_within(groups + k, token))
            c = k - pairs + 1
            if c >= 0:
                ends.append(do_post(c, token))
            if c == groups:
                share = do_term(0, do_partial(list(range(groups)), token))
                ends.append(Pin(share[0]))
            if c == groups + 1:
                halfway = do_partial([groups, groups + 1], token)
                ends.append(Pin(halfway))
            if c == groups + 2:
                grads[0] = do_finish(0, share)
                halfway = do_partial([groups + 2], token, halfway)
        grads[1] = do_finish(1, do_last(chunks - 1, halfway, Pin(halfway)))
        outs = [
            jnp.concatenate([post[c][0] for c in range(s * groups, (s + 1) * groups)], axis=1)
            for s in range(2)
        ]
        return (outs[0], outs[1], grads[0], grads[1])

    return body


def solution(mesh):
    rows = P(("dp", "seq"), None)
    both = P(("dp", "seq"), "chan")
    in_specs = (
        rows, rows, P(None, "chan"), P(), P(None, "chan"),
        P("chan"), P("chan"), P("chan"), both, both,
    )
    return jax.shard_map(
        local(mesh.shape["seq"], mesh.shape["chan"]),
        mesh=mesh,
        in_specs=in_specs,
        out_specs=(both,) * 4,
        check_vma=False,
    )
```

```python
import jax
import jax.numpy as jnp
from jax import lax
from jax.experimental import pallas as pl
from jax.experimental.pallas import tpu as pltpu
from jax.sharding import PartitionSpec as P

BF = jnp.bfloat16
F32 = jnp.float32
LANES = 128


def mm(a, b, ca=1, cb=0):
    return lax.dot_general(a, b, (((ca,), (cb,)), ((), ())), preferred_element_type=F32)


def halves(x):
    high = x.astype(BF)
    return high, (x - high.astype(F32)).astype(BF)


def mm_exact(a, b, ca=1, cb=0):
    first, rest = b.astype(BF), None
    rest = b - first.astype(F32)
    second = rest.astype(BF)
    third = (rest - second.astype(F32)).astype(BF)
    return mm(a, first, ca, cb) + mm(a, second, ca, cb) + mm(a, third, ca, cb)


def iotas(rows, columns):
    return (
        lax.broadcasted_iota(jnp.int32, (rows, columns), 0),
        lax.broadcasted_iota(jnp.int32, (rows, columns), 1),
    )


def spread(weights, base, width, head_width):
    heads = weights[0].shape[1]
    row, channel = iotas(2 * heads, width)
    start = (jnp.where(row >= heads, row - heads, row) - base) * head_width
    pick = ((channel >= start) & (channel < start + head_width)).astype(BF)
    stacked = jnp.concatenate(weights, axis=0) if len(weights) > 1 else weights[0]
    out = mm(jnp.concatenate(halves(stacked), axis=1), pick)
    result, at = [], 0
    for w in weights:
        result.append(out[at : at + w.shape[0]])
        at += w.shape[0]
    return result


def spread_rows(rows, base, width, head_width):
    heads = rows[0].shape[1]
    wide = spread([jnp.broadcast_to(r, (8, heads)) for r in rows], base, width, head_width)
    return [w[0:1] for w in wide]


def gather_heads(parts, base, head_width):
    width = parts[0].shape[1]
    channel, head = iotas(width, LANES)
    start = (head - base) * head_width
    pick = ((channel >= start) & (channel < start + head_width)).astype(BF)
    out = mm(jnp.concatenate([x.astype(BF) for x in parts], axis=0), pick)
    result, at = [], 0
    for x in parts:
        result.append(out[at : at + x.shape[0]])
        at += x.shape[0]
    return result


def reversal(size):
    i, j = iotas(size, size)
    return (i + j == size - 1).astype(BF)


def flip_block(size):
    return 256 if size % 256 == 0 else 128


def sds(shape, dtype=F32):
    return jax.ShapeDtypeStruct(shape, dtype)


class Block:
    def __init__(self, array, shape, index):
        self.array, self.shape, self.index = array, shape, index

    def view(self, ref):
        if self.shape == self.array.shape:
            return ref
        return ref.at[tuple(pl.ds(i * b, b) for i, b in zip(self.index, self.shape))]


class Copied:
    def __init__(self, item):
        self.item = item if isinstance(item, Block) else Block(item, item.shape, (0,) * item.ndim)


class Far:
    def __init__(self, array):
        self.array = array


def run(body, ins, outs, scratch=(), limit=16, stored=()):
    specs, arrays, copied = [], [], []
    for item in ins:
        if isinstance(item, Far):
            specs.append(pl.BlockSpec(memory_space=pl.ANY))
            arrays.append(item.array)
        elif isinstance(item, Copied):
            specs.append(pl.BlockSpec(memory_space=pltpu.HBM))
            arrays.append(item.item.array)
            copied.append(item.item)
        elif isinstance(item, Block):
            specs.append(pl.BlockSpec(memory_space=pltpu.VMEM))
            arrays.append(item.array)
        else:
            space = pltpu.SMEM if item.dtype == jnp.int32 else pltpu.VMEM
            specs.append(pl.BlockSpec(memory_space=space))
            arrays.append(item)
    out_specs = [
        pl.BlockSpec(memory_space=pltpu.HBM if n in stored else pltpu.VMEM)
        for n in range(len(outs))
    ]
    holds = [pltpu.VMEM(q.shape, q.array.dtype) for q in copied]
    holds += [pltpu.VMEM(outs[n].shape, outs[n].dtype) for n in stored]
    sems = [pltpu.SemaphoreType.DMA((max(len(holds), 1),))]

    def kernel(*refs):
        refs = list(refs)
        take = lambda n: [refs.pop(0) for _ in range(n)]
        sources, targets = take(len(ins)), take(len(outs))
        held, (sem,) = take(len(holds)), take(1)
        args, copies = [], []
        for ref, item in zip(sources, ins):
            if isinstance(item, Copied):
                n = len(copies)
                copies.append(pltpu.make_async_copy(item.item.view(ref), held[n], sem.at[n]))
                copies[-1].start()
                ref = held[n]
            elif isinstance(item, Block):
                ref = item.view(ref)
            args.append(ref)
        back = []
        for n, ref in enumerate(targets):
            if n in stored:
                k = len(copied) + stored.index(n)
                back.append(pltpu.make_async_copy(held[k], ref, sem.at[k]))
                ref = held[k]
            args.append(ref)
        waits = {"waits": [c.wait for c in copies]} if copies else {}
        body(*args, *refs, **waits)
        for copy in back:
            copy.start()
        for copy in back:
            copy.wait()

    return pl.pallas_call(
        kernel,
        in_specs=specs,
        out_specs=out_specs,
        out_shape=outs,
        scratch_shapes=holds + sems + list(scratch),
        compiler_params=pltpu.CompilerParams(vmem_limit_bytes=limit * 1024 * 1024),
        cost_estimate=pl.CostEstimate(flops=0, bytes_accessed=1024, transcendentals=0),
    )(*arrays)


def start_body(
    hidden, other, select, step, bias, rate, weight, cot, v_out, source, pack0, pack1, wide, waits
):
    for wait in waits[0:2]:
        wait()
    length, width = hidden.shape
    heads = bias.shape[1]
    source[0:length, :] = hidden[...]
    block = flip_block(width)
    turn = reversal(block)
    for j in range(width // block):
        source[length : 2 * length, j * block : (j + 1) * block] = mm(
            other[:, width - (j + 1) * block : width - j * block], turn
        ).astype(BF)
    for wait in waits[2:6]:
        wait()
    keys = mm(source[...], select[...]).astype(BF).astype(F32)
    state = keys.shape[1] // 2
    raw = mm(source[...], step[...], 1, 1) + bias[...]
    dt = jnp.maximum(raw, 0.0) + jnp.log1p(jnp.exp(-jnp.abs(raw)))
    rise = jax.nn.sigmoid(raw)
    i, j = iotas(length, length)
    lower = (i >= j).astype(BF)
    for s, pack in enumerate((pack0, pack1)):
        rows = slice(s * length, (s + 1) * length)
        drop = dt[rows] * rate[...]
        total = mm_exact(lower, drop)
        pack[...] = jnp.zeros(pack.shape, F32)
        pack[:, 0 : 2 * state] = keys[rows]
        at = 2 * state
        for part in (dt[rows], total, total - drop, rise[rows]):
            pack[:, at : at + heads] = part
            at += heads
    for wait in waits[6:]:
        wait()
    piece = mm(source[...], weight[...]).astype(BF)
    for s in range(2):
        v_out[s] = piece[s * length : (s + 1) * length]
    wide[0:length, :] = piece[0:length].astype(F32)
    wide[length : 2 * length, :] = cot[...].astype(F32)
    for n in range(3):
        row = 2 * length + n * piece_rows(length, wide.shape[1])
        put_piece(wide, row, pack0[:, n * LANES : (n + 1) * LANES])


def more_body(source, weight, v_out):
    length = v_out.shape[2]
    piece = mm(source[...], weight[...]).astype(BF)
    for s in range(2):
        v_out[0, s] = piece[s * length : (s + 1) * length]


class Pack:
    def __init__(self, write, read, stats, heads):
        self.write, self.read = write, read
        self.dt = stats[:, 0:heads]
        self.total = stats[:, heads : 2 * heads]
        self.before = stats[:, 2 * heads : 3 * heads]
        last = self.total.shape[0]
        self.whole = self.total[last - 1 : last, :]
        self.from_start = jnp.exp(-self.total)
        self.from_end = jnp.exp(self.before - self.whole)
        self.to_end = jnp.exp(self.total - self.whole)
        self.to_start = jnp.exp(-self.before)
        self.through = jnp.exp(-self.whole)


def own_pack(ref, heads):
    return Pack(*[ref[:, n * LANES : (n + 1) * LANES] for n in range(3)], heads)


def piece_rows(length, width):
    return length // (width // LANES)


def put_piece(ref, row, piece):
    count = piece_rows(piece.shape[0], ref.shape[1])
    for b in range(ref.shape[1] // LANES):
        ref[row : row + count, b * LANES : (b + 1) * LANES] = piece[b * count : (b + 1) * count]


def get_piece(ref, row, length):
    count = piece_rows(length, ref.shape[1])
    return jnp.concatenate(
        [
            ref[row : row + count, b * LANES : (b + 1) * LANES]
            for b in range(ref.shape[1] // LANES)
        ],
        axis=0,
    )


def pair_body(base, heads, head_width, piece_at):
    def body(place, v_own, g_own, x_far, far0, far1, far2, own_ref, token, up, down, near, keep):
        first = place[0] == 0
        length, width = g_own.shape
        own = own_pack(own_ref, heads)
        far = Pack(*[get_piece(f, at, length) for f, at in zip((far0, far1, far2), piece_at)], heads)
        own_row, far_row = own.through, far.through
        rows = spread_rows([own_row * far_row, far_row], base, width, head_width)
        keep[...] = jnp.zeros(keep.shape, F32)
        keep[0:1, :] = rows[0]
        keep[1:2, :] = rows[1]
        own_up, own_down = jnp.where(first, far_row, 1.0), jnp.where(first, 1.0, far_row)
        far_up, far_down = jnp.where(first, 1.0, own_row), jnp.where(first, own_row, 1.0)
        for kind in range(2):
            rows = slice(kind * LANES, (kind + 1) * LANES)
            if kind == 0:
                keys = (own.write, far.write)
                ups = (own.dt * own.to_end, far.dt * far.to_end)
                downs = (own.dt * own.to_start, far.dt * far.to_start)
            else:
                keys = (own.read, far.read)
                ups = (own.from_end, far.from_end)
                downs = (own.from_start, far.from_start)
            x_own = (v_own if kind == 0 else g_own)[...].reshape(length, width).astype(F32)
            x_other = x_far[kind * length : (kind + 1) * length, :]
            w = spread(
                [ups[0] * own_up, ups[1] * far_up, downs[0] * own_down, downs[1] * far_down,
                 jnp.where(first, downs[1], ups[1])],
                base, width, head_width,
            )
            key = jnp.concatenate(keys, axis=0).astype(BF)
            both = lambda a, b: jnp.concatenate([(a * x_own).astype(BF), (b * x_other).astype(BF)], axis=0)
            up[rows, :] = mm(key, both(w[0], w[1]), 0, 0)
            down[rows, :] = mm(key, both(w[2], w[3]), 0, 0)
            near[rows, :] = mm(keys[1].astype(BF), (w[4] * x_other).astype(BF), 0, 0)

    return body


def fetch_start(options, index, target, sem):
    for z, option in enumerate(options):
        if option is not None:

            @pl.when(index == z)
            def _():
                pltpu.make_async_copy(option, target, sem).start()


def fetch_wait(options, index, target, sem):
    for z, option in enumerate(options):
        if option is not None:

            @pl.when(index == z)
            def _():
                pltpu.make_async_copy(option, target, sem).wait()


def step_body(has, first_step, widen, piece, tokens):
    pairs = len(has)

    def body(place, *rest):
        rest = list(rest)
        take = lambda n: [rest.pop(0) for _ in range(n)]
        sides = []
        for d in range(2):
            totals = [take(1)[0] if h else None for h in has]
            keeps = [take(1)[0] if h else None for h in has]
            sides.append((totals, keeps))
        got = None if first_step else take(2)
        if widen:
            v_ref, g_ref = take(2)
        piece_ref = take(1)[0] if piece else None
        take(tokens)
        sends = take(2)
        token = take(1)[0]
        wide = take(1)[0] if widen else None
        spots = (place[1], pairs - 1 - place[1])
        for d, (totals, keeps) in enumerate(sides):
            for n in range(pairs):
                z = n if d == 0 else pairs - 1 - n
                send = sends[(z + d) % 2]

                @pl.when(spots[d] == n)
                def _():
                    if not has[n]:
                        send[...] = jnp.zeros(send.shape, F32)
                    elif got is None or n == 0:
                        send[...] = totals[n][...]
                    else:
                        send[...] = totals[n][...] + keeps[n][0:1, :] * got[(z + 1 + d) % 2][...]

        token[...] = jnp.zeros(token.shape, F32)
        if widen:
            length, width = g_ref.shape
            wide[0:length, :] = v_ref[...].reshape(length, width).astype(F32)
            wide[length : 2 * length, :] = g_ref[...].astype(F32)
            if piece:
                put_piece(wide, 2 * length, piece_ref[...])

    return body


def within_body(base, heads, head_width):
    def body(own_ref, v_ref, g_ref, rate, y_out, x_out, keys_out, steps_out, cols_s):
        own = own_pack(own_ref, heads)
        length, width = g_ref.shape
        write, read = own.write.astype(BF), own.read.astype(BF)
        scores = mm(read, write, 1, 1)
        i, j = iotas(length, length)
        low = i > j
        high = i < j
        doubled = jnp.where(i == j, 2.0, 1.0).astype(F32)
        scores2 = scores * doubled
        turned = own_ref[:, 2 * LANES : 3 * LANES].T
        lane = lax.broadcasted_iota(jnp.int32, (length, LANES), 1)
        d_scores = jnp.zeros((length, length), F32)
        out_low = jnp.zeros((length, LANES), F32)
        out_high = jnp.zeros((length, LANES), F32)
        cols_s[...] = jnp.zeros(cols_s.shape, F32)
        v_all = v_ref[...].reshape(length, width)
        per = LANES // head_width
        for n in range(width // LANES):
            at = slice(n * LANES, (n + 1) * LANES)
            v, g = v_all[:, at], g_ref[:, at]
            mine = [(lane >= m * head_width) & (lane < (m + 1) * head_width) for m in range(per)]
            v_heads = jnp.concatenate([jnp.where(x, v, jnp.zeros_like(v)) for x in mine], axis=0)
            g_heads = jnp.concatenate([jnp.where(x, g, jnp.zeros_like(g)) for x in mine], axis=0)
            products = mm(g_heads, v, 1, 1)
            plains, steppeds = [], []
            for m in range(per):
                h = base + n * per + m
                c_col = own.total[:, h : h + 1]
                e_col = own.before[:, h : h + 1]
                dt_row = turned[h : h + 1, :]
                c_row = turned[heads + h : heads + h + 1, :]
                e_row = turned[2 * heads + h : 2 * heads + h + 1, :]
                decay = jnp.exp(jnp.where(low, c_row - c_col, e_col - e_row))
                plain = decay * scores2
                plains.append(plain.astype(BF))
                steppeds.append((plain * dt_row).astype(BF))
                inner = decay * dt_row * products[m * length : (m + 1) * length]
                d_scores = d_scores + inner
                flow = inner * scores
                flow_low = jnp.where(low, flow, 0.0)
                flow_high = jnp.where(high, flow, 0.0)
                out_low = jnp.where(lane == h, jnp.sum(flow_low, 1, keepdims=True), out_low)
                out_high = jnp.where(lane == h, jnp.sum(flow_high, 1, keepdims=True), out_high)
                cols_s[0, h : h + 1, :] = jnp.sum(flow_low, 0, keepdims=True)
                cols_s[1, h : h + 1, :] = jnp.sum(flow_high, 0, keepdims=True)
            y_out[:, at] = mm(jnp.concatenate(steppeds, axis=1), v_heads)
            x_out[:, at] = mm(jnp.concatenate(plains, axis=0), g_heads, 0, 0)
        d_scores = (d_scores * doubled).astype(BF)
        keys_out[:, 0:LANES] = mm(d_scores, read, 0, 0)
        keys_out[:, LANES : 2 * LANES] = mm(d_scores, write)
        net_low = out_low - cols_s[0].T
        net_high = out_high - cols_s[1].T
        at_or_after = (j >= i).astype(BF)
        after = (j > i).astype(BF)
        steps_out[...] = -rate[...] * (mm_exact(at_or_after, net_low) - mm_exact(after, net_high))

    return body


def post_body(base, heads, head_width, ups, downs):
    def body(
        place, own_ref, v_ref, g_ref, yw, xw, keys_w, steps_w, near, keep, skip, rate, token, *rest
    ):
        up_in, down_in = rest[0:ups], rest[ups : ups + downs]
        mixed, dv_out, keys_out, steps_out, bufs, sems = rest[ups + downs :]
        up_spot, down_spot = place[1], len(up_in) - 1 - place[1]
        fetch_start(up_in, up_spot, bufs.at[0], sems.at[0])
        fetch_start(down_in, down_spot, bufs.at[1], sems.at[1])
        first = place[0] == 0
        own = own_pack(own_ref, heads)
        length, width = g_ref.shape
        far_row = keep[1:2, :]
        own_row, gain = spread_rows([own.through, skip[...]], base, width, head_width)
        up_row = jnp.where(first, 1.0, far_row)
        down_row = jnp.where(first, far_row, 1.0)
        dt, from_start, from_end, to_end, to_start = spread(
            [own.dt, own.from_start, own.from_end, own.to_end, own.to_start],
            base, width, head_width,
        )
        write, read = own.write.astype(BF), own.read.astype(BF)
        v = v_ref[...].reshape(length, width).astype(F32)
        g = g_ref[...].astype(F32)
        fetch_wait(up_in, up_spot, bufs.at[0], sems.at[0])
        fetch_wait(down_in, down_spot, bufs.at[1], sems.at[1])
        up = up_row * bufs[0] + jnp.where(first, 0.0, near[...])
        down = down_row * bufs[1] + jnp.where(first, near[...], 0.0)
        p, ab = up[0:LANES], up[LANES : 2 * LANES]
        q, af = down[0:LANES], down[LANES : 2 * LANES]
        crossing = jnp.sum(p * af + q * ab, axis=0, keepdims=True)
        p, q, af, ab = p.astype(BF), q.astype(BF), af.astype(BF), ab.astype(BF)
        y_p = from_start * mm(read, p)
        y_q = from_end * mm(read, q)
        x_f = to_end * mm(write, af)
        x_b = to_start * mm(write, ab)
        mixed[...] = (yw[...] + y_p + y_q + gain * v).astype(BF)
        x = xw[...] + x_f + x_b
        dv_out[...] = (dt * x + gain * g).astype(BF)
        dtv = dt * v
        keys_out[:, 0:LANES] = (
            keys_w[:, 0:LANES]
            + mm((to_end * dtv).astype(BF), af, 1, 1)
            + mm((to_start * dtv).astype(BF), ab, 1, 1)
        )
        keys_out[:, LANES : 2 * LANES] = (
            keys_w[:, LANES : 2 * LANES]
            + mm((from_start * g).astype(BF), p, 1, 1)
            + mm((from_end * g).astype(BF), q, 1, 1)
        )
        lane = lax.broadcasted_iota(jnp.int32, (length, LANES), 1)
        steps = jnp.where(lane < heads, own_ref[:, 2 * LANES : 3 * LANES], 0.0)
        direct, a_p, a_q, b_f, b_b, through = gather_heads(
            [v * x, g * y_p, g * y_q, v * x_f, v * x_b, jnp.broadcast_to(crossing * own_row, (8, width))],
            base, head_width,
        )
        i, j = iotas(length, length)
        masks = jnp.concatenate([j >= i, j <= i, j < i, j > i], axis=1).astype(F32).astype(BF)
        high, low = halves(jnp.concatenate([a_p, a_q, b_f * steps, b_b * steps], axis=0))
        flow = mm(masks, high) + mm(masks, low) + through[0:1]
        steps_out[...] = steps_w[...] + direct - rate[...] * flow

    return body


def chunk_body(within, post):
    def body(place, own_ref, v_ref, g_ref, near, keep, skip, rate, token, *rest):
        bufs, sems, yw, xw, keys_w, steps_w, cols_s = rest[-7:]
        within(own_ref, v_ref, g_ref, rate, yw, xw, keys_w, steps_w, cols_s)
        post(
            place, own_ref, v_ref, g_ref, yw, xw, keys_w, steps_w, near, keep, skip, rate, token,
            *rest[:-5],
        )

    return body


def partial_body(groups, more):
    def body(token, *rest, waits):
        dvs, weights, rest = rest[0:groups], rest[groups : 2 * groups], rest[2 * groups :]
        out = rest[-1]
        for wait in waits:
            wait()
        total = mm(dvs[0][...], weights[0][...], 1, 1)
        for k in range(1, groups):
            total = total + mm(dvs[k][...], weights[k][...], 1, 1)
        out[...] = total + rest[0][...] if more else total

    return body


def term_body(groups, tails, heads, parts, swap):
    def body(place, own_ref, select, step, before, *rest, waits=()):
        dvs, weights = rest[0:tails], rest[tails : 2 * tails]
        rest = rest[2 * tails :]
        keys, steps = rest[0:groups], rest[groups : 2 * groups]
        outs = rest[2 * groups :]
        for wait in waits:
            wait()
        d_keys, d_steps = keys[0][...], steps[0][...]
        for a, b in zip(keys[1:], steps[1:]):
            d_keys = d_keys + a[...]
            d_steps = d_steps + b[...]
        d_raw = d_steps[:, 0:heads] * own_ref[:, 2 * LANES + 3 * heads : 2 * LANES + 4 * heads]
        keys_high, keys_low = halves(d_keys)
        raw_high, raw_low = halves(d_raw)
        width = select.shape[0]
        block = width // parts
        tiles = []
        for b in range(parts):
            rows = slice(b * block, (b + 1) * block)
            total = before[:, rows]
            total = total + mm(keys_high, select[rows, :], 1, 1) + mm(keys_low, select[rows, :], 1, 1)
            total = total + mm(raw_high, step[:, rows]) + mm(raw_low, step[:, rows])
            for k in range(tails):
                total = total + mm(dvs[k][...], weights[k][rows, :], 1, 1)
            tiles.append(total)
        if swap:
            tiles = tiles[::-1]
        if parts == 2:
            first = place[2] == 0
            outs[0][...] = jnp.where(first, tiles[0], tiles[1])
            outs[1][...] = jnp.where(first, tiles[1], tiles[0])
        else:
            for b in range(parts):
                outs[0][:, b * block : (b + 1) * block] = tiles[b]

    return body


def last_body(work, term, work_ins, shares):
    def body(place, *rest, waits):
        rest = list(rest)
        take = lambda n: [rest.pop(0) for _ in range(n)]
        for_work = take(work_ins)
        select, step, before, weight = take(4)
        others = take(len(rest) - 1 - shares - 5)
        half = len(others) // 2
        mixed, *outs = take(1 + shares)
        bufs, sems, dv, keys, steps = take(5)
        work(place, *for_work, mixed, dv, keys, steps, bufs, sems)
        term(
            place, for_work[0], select, step, before, dv, weight,
            *others[:half], keys, *others[half:], steps, *outs, waits=waits,
        )

    return body


def finish_body(flip):
    def body(a, b, out):
        total = (a[...] + b[...]).astype(BF)
        if not flip:
            out[...] = total
            return
        width = total.shape[1]
        block = flip_block(width)
        turn = reversal(block)
        for j in range(width // block):
            out[:, j * block : (j + 1) * block] = mm(
                total[:, width - (j + 1) * block : width - j * block], turn
            ).astype(BF)

    return body


def widen_body(tokens):
    def body(v_ref, g_ref, *rest):
        wide = rest[tokens]
        length, width = g_ref.shape
        wide[0:length, :] = v_ref[...].reshape(length, width).astype(F32)
        wide[length : 2 * length, :] = g_ref[...].astype(F32)

    return body


def local(shards, parts):
    pairs = shards // 2

    def body(
        hidden, complement, inner_weight, select_weight, step_weight, step_bias, decay_rate,
        skip_gain, cotangent, complement_cotangent,
    ):
        length, width = hidden.shape
        inner = inner_weight.shape[1]
        heads = step_bias.shape[0]
        head_width = inner // heads
        groups = 4
        chunk = inner // groups
        group_heads = heads // groups
        seq = lax.axis_index("seq")
        place = jnp.stack([seq % 2, seq // 2, lax.axis_index("chan")]).astype(jnp.int32)
        bias = step_bias.reshape(1, heads)
        rate = decay_rate.reshape(1, heads)
        rate_row = jnp.pad(rate, ((0, 0), (0, LANES - heads)))
        gain = skip_gain.reshape(1, heads)
        step_rows = step_weight.T
        cots = (cotangent, complement_cotangent)
        swap_pairs = [(a, a ^ 1) for a in range(shards)]
        edges = []
        for start in range(2):
            meets = [(z, z + 1) for z in range(start, pairs - 1, 2)]
            paired = sum(meets, ())
            meets += [(b, a) for a, b in meets] + [(z, z) for z in range(pairs) if z not in paired]
            edges.append([(2 * a + y, 2 * b + y) for a, b in meets for y in range(2)])
        swap = lambda x: lax.ppermute(x, "seq", swap_pairs)
        pack_shape = (length, 3 * LANES)
        pair_shape = (2 * LANES, chunk)
        wide_shape = lambda pieces: sds((2 * length + pieces * piece_rows(length, chunk), chunk))
        token_shape = sds((8, LANES))
        work = lambda: [pltpu.VMEM((2,) + pair_shape, F32), pltpu.SemaphoreType.DMA((2,))]
        order = [(s, k) for s in range(2) for k in range(groups)]
        chunks = len(order)

        v_first, source, pack0, pack1, wide = run(
            start_body,
            [*map(Copied, (hidden, complement, select_weight, step_rows, bias, rate)),
             Copied(Block(inner_weight, (width, chunk), (0, 0))),
             Copied(Block(cots[0], (length, chunk), (0, 0)))],
            [sds((2, length, chunk), BF), sds((2 * length, width), BF), sds(pack_shape),
             sds(pack_shape), wide_shape(3)],
            limit=54,
        )
        packs = (pack0, pack1)
        v_more = pl.pallas_call(
            more_body,
            grid=(groups - 1,),
            in_specs=[
                pl.BlockSpec((2 * length, width), lambda i: (0, 0)),
                pl.BlockSpec((width, chunk), lambda i: (0, i + 1)),
            ],
            out_specs=pl.BlockSpec((1, 2, length, chunk), lambda i: (i, 0, 0, 0)),
            out_shape=sds((groups - 1, 2, length, chunk), BF),
            compiler_params=pltpu.CompilerParams(vmem_limit_bytes=62 * 1024 * 1024),
            cost_estimate=pl.CostEstimate(flops=0, bytes_accessed=1024, transcendentals=0),
        )(source, inner_weight)

        def value_block(c):
            s, k = order[c]
            if k == 0:
                return Block(v_first, (1, length, chunk), (s, 0, 0))
            return Block(v_more, (1, 1, length, chunk), (k - 1, s, 0, 0))

        def cot_block(c):
            s, k = order[c]
            return Block(cots[s], (length, chunk), (0, k))

        def weight_block(c):
            return Copied(Block(inner_weight, (width, chunk), (0, order[c][1])))

        far = {}
        totals, within, post = {}, {}, {}
        got = ([], [])
        grads = [None, None]
        riders = {2 + n: n for n in range(3)}
        steps = chunks + pairs - 2

        def do_pair(c, token):
            s, k = order[c]
            rows = piece_rows(length, chunk)
            if s == 0:
                pieces, piece_at = [far[0]] * 3, [2 * length + n * rows for n in range(3)]
            else:
                pieces, piece_at = [far[r] for r in riders], [2 * length] * 3
            totals[c] = run(
                pair_body(k * group_heads, heads, head_width, piece_at),
                [place, value_block(c), cot_block(c), far[c], *pieces, packs[s], Far(token)],
                [sds(pair_shape), sds(pair_shape), sds(pair_shape), sds((8, chunk))],
            )
            return totals[c][3]

        within_shapes = [
            sds((length, chunk)), sds((length, chunk)), sds((length, 2 * LANES)), sds((length, LANES))
        ]
        post_shapes = [
            sds((length, chunk), BF), sds((length, chunk), BF), sds((length, 2 * LANES)), sds((length, LANES))
        ]
        flows = lambda: [pltpu.VMEM((2, LANES, length), F32)]

        def do_within(c):
            s, k = order[c]
            within[c] = run(
                within_body(k * group_heads, heads, head_width),
                [packs[s], value_block(c), cot_block(c), rate_row],
                within_shapes,
                scratch=flows(),
            )
            return within[c][3]

        def post_parts(c, token, fused):
            s, k = order[c]
            last = pairs - 1
            ups = [got[(z + 1) % 2][max(c + z - 1, c)] for z in range(pairs)]
            downs = [got[(last - z) % 2][max(c + z - 1, c)] for z in range(pairs)]
            body = post_body(k * group_heads, heads, head_width, len(ups), len(downs))
            if fused:
                body = chunk_body(within_body(k * group_heads, heads, head_width), body)
            ins = [packs[s], value_block(c), cot_block(c), *([] if fused else within[c]),
                   totals[c][2], totals[c][3], gain, rate_row, Far(token),
                   *map(Far, ups), *map(Far, downs)]
            return body, ins

        def do_chunk(c, token):
            body, ins = post_parts(c, token, True)
            post[c] = run(
                body, [place, *ins], post_shapes, stored=(0,),
                scratch=work() + [pltpu.VMEM(o.shape, o.dtype) for o in within_shapes] + flows(),
            )
            return post[c][3]

        def do_partial(cs, token, before=None):
            return run(
                partial_body(len(cs), before is not None),
                [Far(token), *[post[c][1] for c in cs], *[weight_block(c) for c in cs]]
                + ([] if before is None else [before]),
                [sds((length, width))],
            )[0]

        shares = [sds((length, width // parts))] * 2 if parts == 2 else [sds((length, width))]

        def send_share(term):
            if parts == 2:
                return term[0], lax.ppermute(term[1], "chan", [(0, 1), (1, 0)])
            share = lax.psum_scatter(term[0], "chan", scatter_dimension=1, tiled=True)
            return share, jnp.zeros_like(share)

        def do_term(s, before):
            mine = [c for c in range(chunks) if order[c][0] == s]
            return send_share(run(
                term_body(len(mine), 0, heads, parts, s == 1),
                [place, packs[s], Copied(select_weight), Copied(step_rows), before,
                 *[post[c][2] for c in mine], *[post[c][3] for c in mine]],
                shares,
            ))

        def do_last(c, before, token):
            s = order[c][0]
            mine = [n for n in range(chunks) if order[n][0] == s and n != c]
            body, ins = post_parts(c, token, False)
            out = run(
                last_body(
                    body, term_body(len(mine) + 1, 1, heads, parts, s == 1), len(ins), len(shares)
                ),
                [place, *ins, Copied(select_weight), Copied(step_rows), before, weight_block(c),
                 *[post[n][2] for n in mine], *[post[n][3] for n in mine]],
                [post_shapes[0], *shares],
                scratch=work() + [pltpu.VMEM(o.shape, o.dtype) for o in post_shapes[1:]],
                stored=(0,),
            )
            post[c] = (out[0],)
            return send_share(out[1:])

        def do_finish(s, share):
            return run(
                finish_body(s == 1), list(share), [sds((length, width // parts), BF)], stored=(0,)
            )[0]

        def do_step(k, widen, ends):
            has = [0 <= k - z < chunks and z < pairs - 1 for z in range(pairs)]
            ins = [place]
            for d in range(2):
                ins += [totals[k - z][d] for z in range(pairs) if has[z]]
                ins += [totals[k - z][3] for z in range(pairs) if has[z]]
            if k > 0:
                ins += [got[0][-1], got[1][-1]]
            outs = [sds(pair_shape), sds(pair_shape), token_shape]
            if widen is not None:
                ins += [value_block(widen), cot_block(widen)]
                outs.append(wide_shape(1 if widen in riders else 0))
            if widen in riders:
                ins.append(Block(packs[1], (length, LANES), (0, riders[widen])))
            return run(
                step_body(has, k == 0, widen is not None, widen in riders, len(ends)),
                ins + [Far(e) for e in ends], outs,
            )

        far[0] = swap(wide)
        wide1 = run(
            widen_body(1), [value_block(1), cot_block(1), Far(far[0])], [wide_shape(0)]
        )[0]
        far[1] = swap(wide1)
        ends = [do_pair(0, wide1), wide1]
        halfway = None
        share = None
        for k in range(steps):
            made = do_step(k, k + 2 if k + 2 < chunks else None, ends)
            token = made[2]
            arrived = [lax.ppermute(made[d], "seq", edges[d]) for d in (1, 0)]
            for d in range(2):
                got[d].append(arrived[1 - d])
            ends = []
            if k + 2 < chunks:
                far[k + 2] = swap(made[3])
            if k + 1 < chunks:
                ends.append(do_pair(k + 1, token))
            c = k - pairs + 1
            if c >= 0:
                ends.append(do_chunk(c, token))
            if c == groups:
                share = do_term(0, do_partial(list(range(groups)), token))
                ends.append(share[0])
            if c == groups + 1:
                halfway = do_partial([groups, groups + 1], token)
                ends.append(halfway)
            if c == groups + 2:
                grads[0] = do_finish(0, share)
                halfway = do_partial([groups + 2], token, halfway)
        do_within(chunks - 1)
        grads[1] = do_finish(1, do_last(chunks - 1, halfway, halfway))
        outs = [
            jnp.concatenate([post[c][0] for c in range(s * groups, (s + 1) * groups)], axis=1)
            for s in range(2)
        ]
        return (outs[0], outs[1], grads[0], grads[1])

    return body


def solution(mesh):
    rows = P(("dp", "seq"), None)
    both = P(("dp", "seq"), "chan")
    in_specs = (
        rows, rows, P(None, "chan"), P(), P(None, "chan"),
        P("chan"), P("chan"), P("chan"), both, both,
    )
    return jax.shard_map(
        local(mesh.shape["seq"], mesh.shape["chan"]),
        mesh=mesh,
        in_specs=in_specs,
        out_specs=(both,) * 4,
        check_vma=False,
    )
```

```python
import jax
import jax.numpy as jnp
from jax import lax
from jax.experimental import pallas as pl
from jax.experimental.pallas import tpu as pltpu
from jax.sharding import PartitionSpec as P

BF = jnp.bfloat16
F32 = jnp.float32
LANES = 128


def mm(a, b, ca=1, cb=0):
    return lax.dot_general(a, b, (((ca,), (cb,)), ((), ())), preferred_element_type=F32)


def halves(x):
    high = x.astype(BF)
    return high, (x - high.astype(F32)).astype(BF)


def mm_exact(a, b, ca=1, cb=0):
    first, rest = b.astype(BF), None
    rest = b - first.astype(F32)
    second = rest.astype(BF)
    third = (rest - second.astype(F32)).astype(BF)
    return mm(a, first, ca, cb) + mm(a, second, ca, cb) + mm(a, third, ca, cb)


def iotas(rows, columns):
    return (
        lax.broadcasted_iota(jnp.int32, (rows, columns), 0),
        lax.broadcasted_iota(jnp.int32, (rows, columns), 1),
    )


def spread(weights, base, width, head_width):
    heads = weights[0].shape[1]
    row, channel = iotas(2 * heads, width)
    start = (jnp.where(row >= heads, row - heads, row) - base) * head_width
    pick = ((channel >= start) & (channel < start + head_width)).astype(BF)
    stacked = jnp.concatenate(weights, axis=0) if len(weights) > 1 else weights[0]
    out = mm(jnp.concatenate(halves(stacked), axis=1), pick)
    result, at = [], 0
    for w in weights:
        result.append(out[at : at + w.shape[0]])
        at += w.shape[0]
    return result


def spread_rows(rows, base, width, head_width):
    heads = rows[0].shape[1]
    wide = spread([jnp.broadcast_to(r, (8, heads)) for r in rows], base, width, head_width)
    return [w[0:1] for w in wide]


def gather_heads(parts, base, head_width):
    width = parts[0].shape[1]
    channel, head = iotas(width, LANES)
    start = (head - base) * head_width
    pick = ((channel >= start) & (channel < start + head_width)).astype(BF)
    out = mm(jnp.concatenate([x.astype(BF) for x in parts], axis=0), pick)
    result, at = [], 0
    for x in parts:
        result.append(out[at : at + x.shape[0]])
        at += x.shape[0]
    return result


def reversal(size):
    i, j = iotas(size, size)
    return (i + j == size - 1).astype(BF)


def flip_block(size):
    return 256 if size % 256 == 0 else 128


def sds(shape, dtype=F32):
    return jax.ShapeDtypeStruct(shape, dtype)


class Block:
    def __init__(self, array, shape, index):
        self.array, self.shape, self.index = array, shape, index

    def view(self, ref):
        if self.shape == self.array.shape:
            return ref
        return ref.at[tuple(pl.ds(i * b, b) for i, b in zip(self.index, self.shape))]


class Copied:
    def __init__(self, item):
        self.item = item if isinstance(item, Block) else Block(item, item.shape, (0,) * item.ndim)


class Far:
    def __init__(self, array):
        self.array = array


def run(body, ins, outs, scratch=(), limit=16, stored=()):
    specs, arrays, copied = [], [], []
    for item in ins:
        if isinstance(item, Far):
            specs.append(pl.BlockSpec(memory_space=pl.ANY))
            arrays.append(item.array)
        elif isinstance(item, Copied):
            specs.append(pl.BlockSpec(memory_space=pltpu.HBM))
            arrays.append(item.item.array)
            copied.append(item.item)
        elif isinstance(item, Block):
            specs.append(pl.BlockSpec(memory_space=pltpu.VMEM))
            arrays.append(item.array)
        else:
            space = pltpu.SMEM if item.dtype == jnp.int32 else pltpu.VMEM
            specs.append(pl.BlockSpec(memory_space=space))
            arrays.append(item)
    out_specs = [
        pl.BlockSpec(memory_space=pltpu.HBM if n in stored else pltpu.VMEM)
        for n in range(len(outs))
    ]
    holds = [pltpu.VMEM(q.shape, q.array.dtype) for q in copied]
    holds += [pltpu.VMEM(outs[n].shape, outs[n].dtype) for n in stored]
    sems = [pltpu.SemaphoreType.DMA((max(len(holds), 1),))]

    def kernel(*refs):
        refs = list(refs)
        take = lambda n: [refs.pop(0) for _ in range(n)]
        sources, targets = take(len(ins)), take(len(outs))
        held, (sem,) = take(len(holds)), take(1)
        args, copies = [], []
        for ref, item in zip(sources, ins):
            if isinstance(item, Copied):
                n = len(copies)
                copies.append(pltpu.make_async_copy(item.item.view(ref), held[n], sem.at[n]))
                copies[-1].start()
                ref = held[n]
            elif isinstance(item, Block):
                ref = item.view(ref)
            args.append(ref)
        back = []
        for n, ref in enumerate(targets):
            if n in stored:
                k = len(copied) + stored.index(n)
                back.append(pltpu.make_async_copy(held[k], ref, sem.at[k]))
                ref = held[k]
            args.append(ref)
        waits = {"waits": [c.wait for c in copies]} if copies else {}
        body(*args, *refs, **waits)
        for copy in back:
            copy.start()
        for copy in back:
            copy.wait()

    return pl.pallas_call(
        kernel,
        in_specs=specs,
        out_specs=out_specs,
        out_shape=outs,
        scratch_shapes=holds + sems + list(scratch),
        compiler_params=pltpu.CompilerParams(vmem_limit_bytes=limit * 1024 * 1024),
        cost_estimate=pl.CostEstimate(flops=0, bytes_accessed=1024, transcendentals=0),
    )(*arrays)


def start_body(
    hidden, other, select, step, bias, rate, weight0, weight1, cot,
    v_out, source, pack0, pack1, row, wide, waits,
):
    for wait in waits[0:2]:
        wait()
    length, width = hidden.shape
    heads = bias.shape[1]
    source[0:length, :] = hidden[...]
    block = flip_block(width)
    turn = reversal(block)
    for j in range(width // block):
        source[length : 2 * length, j * block : (j + 1) * block] = mm(
            other[:, width - (j + 1) * block : width - j * block], turn
        ).astype(BF)
    for wait in waits[2:6]:
        wait()
    keys = mm(source[...], select[...]).astype(BF).astype(F32)
    state = keys.shape[1] // 2
    raw = mm(source[...], step[...], 1, 1) + bias[...]
    dt = jnp.maximum(raw, 0.0) + jnp.log1p(jnp.exp(-jnp.abs(raw)))
    rise = jax.nn.sigmoid(raw)
    i, j = iotas(length, length)
    lower = (i >= j).astype(BF)
    for s, pack in enumerate((pack0, pack1)):
        rows = slice(s * length, (s + 1) * length)
        drop = dt[rows] * rate[...]
        total = mm_exact(lower, drop)
        pack[...] = jnp.zeros(pack.shape, F32)
        pack[:, 0 : 2 * state] = keys[rows]
        at = 2 * state
        for part in (dt[rows], total, total - drop, rise[rows]):
            pack[:, at : at + heads] = part
            at += heads
    for wait in waits[6:]:
        wait()
    row[...] = jnp.zeros(row.shape, F32)
    row[0:1, 0:heads] = jnp.exp(
        -pack1[length - 1 : length, 2 * state + heads : 2 * state + 2 * heads]
    )
    for n, weight in enumerate((weight0, weight1)):
        piece = mm(source[...], weight[...]).astype(BF)
        for s in range(2):
            v_out[n, s] = piece[s * length : (s + 1) * length]
    wide[0:length, :] = v_out[0, 0].astype(F32)
    wide[length : 2 * length, :] = cot[...].astype(F32)
    for n in range(3):
        at = 2 * length + n * piece_rows(length, wide.shape[1])
        put_piece(wide, at, pack0[:, n * LANES : (n + 1) * LANES])


def more_body(source, *rest, waits):
    weights, v_out = rest[:-1], rest[-1]
    length = v_out.shape[2]
    for n, weight in enumerate(weights):
        waits[n]()
        piece = mm(source[...], weight[...]).astype(BF)
        for s in range(2):
            v_out[n, s] = piece[s * length : (s + 1) * length]


class Pack:
    def __init__(self, write, read, stats, heads):
        self.write, self.read = write, read
        self.dt = stats[:, 0:heads]
        self.total = stats[:, heads : 2 * heads]
        self.before = stats[:, 2 * heads : 3 * heads]
        last = self.total.shape[0]
        self.whole = self.total[last - 1 : last, :]
        self.from_start = jnp.exp(-self.total)
        self.from_end = jnp.exp(self.before - self.whole)
        self.to_end = jnp.exp(self.total - self.whole)
        self.to_start = jnp.exp(-self.before)
        self.through = jnp.exp(-self.whole)


def own_pack(ref, heads):
    return Pack(*[ref[:, n * LANES : (n + 1) * LANES] for n in range(3)], heads)


def piece_rows(length, width):
    return length // (width // LANES)


def put_piece(ref, row, piece):
    count = piece_rows(piece.shape[0], ref.shape[1])
    for b in range(ref.shape[1] // LANES):
        ref[row : row + count, b * LANES : (b + 1) * LANES] = piece[b * count : (b + 1) * count]


def get_piece(ref, row, length):
    count = piece_rows(length, ref.shape[1])
    return jnp.concatenate(
        [
            ref[row : row + count, b * LANES : (b + 1) * LANES]
            for b in range(ref.shape[1] // LANES)
        ],
        axis=0,
    )


def pair_body(base, heads, head_width, piece_at):
    def body(place, v_own, g_own, x_far, far0, far1, far2, own_ref, token, up, down, near, keep):
        first = place[0] == 0
        length, width = g_own.shape
        own = own_pack(own_ref, heads)
        far = Pack(*[get_piece(f, at, length) for f, at in zip((far0, far1, far2), piece_at)], heads)
        own_row, far_row = own.through, far.through
        rows = spread_rows([own_row * far_row, far_row], base, width, head_width)
        keep[...] = jnp.zeros(keep.shape, F32)
        keep[0:1, :] = rows[0]
        keep[1:2, :] = rows[1]
        own_up, own_down = jnp.where(first, far_row, 1.0), jnp.where(first, 1.0, far_row)
        far_up, far_down = jnp.where(first, 1.0, own_row), jnp.where(first, own_row, 1.0)
        for kind in range(2):
            rows = slice(kind * LANES, (kind + 1) * LANES)
            if kind == 0:
                keys = (own.write, far.write)
                ups = (own.dt * own.to_end, far.dt * far.to_end)
                downs = (own.dt * own.to_start, far.dt * far.to_start)
            else:
                keys = (own.read, far.read)
                ups = (own.from_end, far.from_end)
                downs = (own.from_start, far.from_start)
            x_own = (v_own if kind == 0 else g_own)[...].reshape(length, width).astype(F32)
            x_other = x_far[kind * length : (kind + 1) * length, :]
            w = spread(
                [ups[0] * own_up, ups[1] * far_up, downs[0] * own_down, downs[1] * far_down,
                 jnp.where(first, downs[1], ups[1])],
                base, width, head_width,
            )
            key = jnp.concatenate(keys, axis=0).astype(BF)
            both = lambda a, b: jnp.concatenate([(a * x_own).astype(BF), (b * x_other).astype(BF)], axis=0)
            up[rows, :] = mm(key, both(w[0], w[1]), 0, 0)
            down[rows, :] = mm(key, both(w[2], w[3]), 0, 0)
            near[rows, :] = mm(keys[1].astype(BF), (w[4] * x_other).astype(BF), 0, 0)

    return body


def column_body(base, heads, head_width):
    def body(place, v_own, g_own, own_ref, far_row_ref, up, down, own_up, own_down, keep):
        first = place[0] == 0
        length, width = g_own.shape
        own = own_pack(own_ref, heads)
        far_row = far_row_ref[0:1, 0:heads]
        rows = spread_rows([own.through * far_row, far_row, own.through], base, width, head_width)
        keep[...] = jnp.zeros(keep.shape, F32)
        for n, row in enumerate(rows):
            keep[n : n + 1, :] = row
        up_row = jnp.where(first, rows[1], 1.0)
        down_row = jnp.where(first, 1.0, rows[1])
        for kind in range(2):
            at = slice(kind * LANES, (kind + 1) * LANES)
            if kind == 0:
                key, weights = own.write, [own.dt * own.to_end, own.dt * own.to_start]
            else:
                key, weights = own.read, [own.from_end, own.from_start]
            key = key.astype(BF)
            x = (v_own if kind == 0 else g_own)[...].reshape(length, width).astype(F32)
            w = spread(weights, base, width, head_width)
            state_up = mm(key, (w[0] * x).astype(BF), 0, 0)
            state_down = mm(key, (w[1] * x).astype(BF), 0, 0)
            own_up[at, :] = state_up
            own_down[at, :] = state_down
            up[at, :] = up_row * state_up
            down[at, :] = down_row * state_down

    return body


def exchange_body(ups, downs):
    def body(place, own_up, own_down, keep, token, *rest):
        up_in, down_in = rest[0:ups], rest[ups : ups + downs]
        up_out, down_out, bufs, sems = rest[ups + downs :]
        up_spot, down_spot = place[1], len(up_in) - 1 - place[1]
        fetch_start(up_in, up_spot, bufs.at[0], sems.at[0])
        fetch_start(down_in, down_spot, bufs.at[1], sems.at[1])
        fetch_wait(up_in, up_spot, bufs.at[0], sems.at[0])
        fetch_wait(down_in, down_spot, bufs.at[1], sems.at[1])
        first = place[0] == 0
        row = keep[2:3, :]
        up_out[...] = jnp.where(first, row * bufs[0] + own_up[...], bufs[0])
        down_out[...] = jnp.where(first, bufs[1], row * bufs[1] + own_down[...])

    return body


def fetch_start(options, index, target, sem):
    for z, option in enumerate(options):
        if option is not None:

            @pl.when(index == z)
            def _():
                pltpu.make_async_copy(option, target, sem).start()


def fetch_wait(options, index, target, sem):
    for z, option in enumerate(options):
        if option is not None:

            @pl.when(index == z)
            def _():
                pltpu.make_async_copy(option, target, sem).wait()


def step_body(has, first_step, tokens):
    pairs = len(has)

    def body(place, *rest):
        rest = list(rest)
        take = lambda n: [rest.pop(0) for _ in range(n)]
        sides = []
        for d in range(2):
            totals = [take(1)[0] if h else None for h in has]
            keeps = [take(1)[0] if h else None for h in has]
            sides.append((totals, keeps))
        got = None if first_step else take(2)
        take(tokens)
        sends = take(2)
        token = take(1)[0]
        spots = (place[1], pairs - 1 - place[1])
        for d, (totals, keeps) in enumerate(sides):
            for n in range(pairs):
                z = n if d == 0 else pairs - 1 - n
                send = sends[(z + d) % 2]

                @pl.when(spots[d] == n)
                def _():
                    if not has[n]:
                        send[...] = jnp.zeros(send.shape, F32)
                    elif got is None or n == 0:
                        send[...] = totals[n][...]
                    else:
                        send[...] = totals[n][...] + keeps[n][0:1, :] * got[(z + 1 + d) % 2][...]

        token[...] = jnp.zeros(token.shape, F32)

    return body


def within_body(base, heads, head_width):
    def body(own_ref, v_ref, g_ref, rate, y_out, x_out, keys_out, steps_out, cols_s):
        own = own_pack(own_ref, heads)
        length, width = g_ref.shape
        write, read = own.write.astype(BF), own.read.astype(BF)
        scores = mm(read, write, 1, 1)
        i, j = iotas(length, length)
        low = i > j
        high = i < j
        doubled = jnp.where(i == j, 2.0, 1.0).astype(F32)
        scores2 = scores * doubled
        turned = own_ref[:, 2 * LANES : 3 * LANES].T
        lane = lax.broadcasted_iota(jnp.int32, (length, LANES), 1)
        d_scores = jnp.zeros((length, length), F32)
        out_low = jnp.zeros((length, LANES), F32)
        out_high = jnp.zeros((length, LANES), F32)
        cols_s[...] = jnp.zeros(cols_s.shape, F32)
        v_all = v_ref[...].reshape(length, width)
        per = LANES // head_width
        for n in range(width // LANES):
            at = slice(n * LANES, (n + 1) * LANES)
            v, g = v_all[:, at], g_ref[:, at]
            mine = [(lane >= m * head_width) & (lane < (m + 1) * head_width) for m in range(per)]
            v_heads = jnp.concatenate([jnp.where(x, v, jnp.zeros_like(v)) for x in mine], axis=0)
            g_heads = jnp.concatenate([jnp.where(x, g, jnp.zeros_like(g)) for x in mine], axis=0)
            products = mm(g_heads, v, 1, 1)
            plains, steppeds = [], []
            for m in range(per):
                h = base + n * per + m
                c_col = own.total[:, h : h + 1]
                e_col = own.before[:, h : h + 1]
                dt_row = turned[h : h + 1, :]
                c_row = turned[heads + h : heads + h + 1, :]
                e_row = turned[2 * heads + h : 2 * heads + h + 1, :]
                decay = jnp.exp(jnp.where(low, c_row - c_col, e_col - e_row))
                plain = decay * scores2
                plains.append(plain.astype(BF))
                steppeds.append((plain * dt_row).astype(BF))
                inner = decay * dt_row * products[m * length : (m + 1) * length]
                d_scores = d_scores + inner
                flow = inner * scores
                flow_low = jnp.where(low, flow, 0.0)
                flow_high = jnp.where(high, flow, 0.0)
                out_low = jnp.where(lane == h, jnp.sum(flow_low, 1, keepdims=True), out_low)
                out_high = jnp.where(lane == h, jnp.sum(flow_high, 1, keepdims=True), out_high)
                cols_s[0, h : h + 1, :] = jnp.sum(flow_low, 0, keepdims=True)
                cols_s[1, h : h + 1, :] = jnp.sum(flow_high, 0, keepdims=True)
            y_out[:, at] = mm(jnp.concatenate(steppeds, axis=1), v_heads)
            x_out[:, at] = mm(jnp.concatenate(plains, axis=0), g_heads, 0, 0)
        d_scores = (d_scores * doubled).astype(BF)
        keys_out[:, 0:LANES] = mm(d_scores, read, 0, 0)
        keys_out[:, LANES : 2 * LANES] = mm(d_scores, write)
        net_low = out_low - cols_s[0].T
        net_high = out_high - cols_s[1].T
        at_or_after = (j >= i).astype(BF)
        after = (j > i).astype(BF)
        steps_out[...] = -rate[...] * (mm_exact(at_or_after, net_low) - mm_exact(after, net_high))

    return body


def post_body(base, heads, head_width, ups, downs, columns=False):
    def body(
        place, own_ref, v_ref, g_ref, yw, xw, keys_w, steps_w, near, keep, skip, rate, token, *rest
    ):
        up_in, down_in = rest[0:ups], rest[ups : ups + downs]
        mixed, dv_out, keys_out, steps_out, bufs, sems = rest[ups + downs :]
        up_spot, down_spot = place[1], len(up_in) - 1 - place[1]
        fetch_start(up_in, up_spot, bufs.at[0], sems.at[0])
        fetch_start(down_in, down_spot, bufs.at[1], sems.at[1])
        first = place[0] == 0
        own = own_pack(own_ref, heads)
        length, width = g_ref.shape
        far_row = keep[1:2, :]
        own_row, gain = spread_rows([own.through, skip[...]], base, width, head_width)
        up_row = jnp.where(first, 1.0, far_row)
        down_row = jnp.where(first, far_row, 1.0)
        dt, from_start, from_end, to_end, to_start = spread(
            [own.dt, own.from_start, own.from_end, own.to_end, own.to_start],
            base, width, head_width,
        )
        write, read = own.write.astype(BF), own.read.astype(BF)
        v = v_ref[...].reshape(length, width).astype(F32)
        g = g_ref[...].astype(F32)
        fetch_wait(up_in, up_spot, bufs.at[0], sems.at[0])
        fetch_wait(down_in, down_spot, bufs.at[1], sems.at[1])
        if columns:
            up = up_row * bufs[0] + near[0][...]
            down = down_row * bufs[1] + near[1][...]
        else:
            up = up_row * bufs[0] + jnp.where(first, 0.0, near[...])
            down = down_row * bufs[1] + jnp.where(first, near[...], 0.0)
        p, ab = up[0:LANES], up[LANES : 2 * LANES]
        q, af = down[0:LANES], down[LANES : 2 * LANES]
        crossing = jnp.sum(p * af + q * ab, axis=0, keepdims=True)
        p, q, af, ab = p.astype(BF), q.astype(BF), af.astype(BF), ab.astype(BF)
        y_p = from_start * mm(read, p)
        y_q = from_end * mm(read, q)
        x_f = to_end * mm(write, af)
        x_b = to_start * mm(write, ab)
        mixed[...] = (yw[...] + y_p + y_q + gain * v).astype(BF)
        x = xw[...] + x_f + x_b
        dv_out[...] = (dt * x + gain * g).astype(BF)
        dtv = dt * v
        keys_out[:, 0:LANES] = (
            keys_w[:, 0:LANES]
            + mm((to_end * dtv).astype(BF), af, 1, 1)
            + mm((to_start * dtv).astype(BF), ab, 1, 1)
        )
        keys_out[:, LANES : 2 * LANES] = (
            keys_w[:, LANES : 2 * LANES]
            + mm((from_start * g).astype(BF), p, 1, 1)
            + mm((from_end * g).astype(BF), q, 1, 1)
        )
        lane = lax.broadcasted_iota(jnp.int32, (length, LANES), 1)
        steps = jnp.where(lane < heads, own_ref[:, 2 * LANES : 3 * LANES], 0.0)
        direct, a_p, a_q, b_f, b_b, through = gather_heads(
            [v * x, g * y_p, g * y_q, v * x_f, v * x_b, jnp.broadcast_to(crossing * own_row, (8, width))],
            base, head_width,
        )
        i, j = iotas(length, length)
        masks = jnp.concatenate([j >= i, j <= i, j < i, j > i], axis=1).astype(F32).astype(BF)
        high, low = halves(jnp.concatenate([a_p, a_q, b_f * steps, b_b * steps], axis=0))
        flow = mm(masks, high) + mm(masks, low) + through[0:1]
        steps_out[...] = steps_w[...] + direct - rate[...] * flow

    return body


def chunk_body(within, post, columns):
    def body(place, own_ref, v_ref, g_ref, *rest):
        nears = 2 if columns else 1
        near = rest[0:2] if columns else rest[0]
        keep, skip, rate, token, *rest = rest[nears:]
        bufs, sems, yw, xw, keys_w, steps_w, cols_s = rest[-7:]
        within(own_ref, v_ref, g_ref, rate, yw, xw, keys_w, steps_w, cols_s)
        post(
            place, own_ref, v_ref, g_ref, yw, xw, keys_w, steps_w, near, keep, skip, rate, token,
            *rest[:-5],
        )

    return body


def partial_body(groups, more):
    def body(token, *rest, waits):
        dvs, weights, rest = rest[0:groups], rest[groups : 2 * groups], rest[2 * groups :]
        out = rest[-1]
        for wait in waits:
            wait()
        total = mm(dvs[0][...], weights[0][...], 1, 1)
        for k in range(1, groups):
            total = total + mm(dvs[k][...], weights[k][...], 1, 1)
        out[...] = total + rest[0][...] if more else total

    return body


def term_body(groups, tails, heads, parts, swap):
    def body(place, own_ref, select, step, before, *rest, waits=()):
        dvs, weights = rest[0:tails], rest[tails : 2 * tails]
        rest = rest[2 * tails :]
        keys, steps = rest[0:groups], rest[groups : 2 * groups]
        outs = rest[2 * groups :]
        for wait in waits:
            wait()
        d_keys, d_steps = keys[0][...], steps[0][...]
        for a, b in zip(keys[1:], steps[1:]):
            d_keys = d_keys + a[...]
            d_steps = d_steps + b[...]
        d_raw = d_steps[:, 0:heads] * own_ref[:, 2 * LANES + 3 * heads : 2 * LANES + 4 * heads]
        keys_high, keys_low = halves(d_keys)
        raw_high, raw_low = halves(d_raw)
        width = select.shape[0]
        block = width // parts
        tiles = []
        for b in range(parts):
            rows = slice(b * block, (b + 1) * block)
            total = before[:, rows]
            total = total + mm(keys_high, select[rows, :], 1, 1) + mm(keys_low, select[rows, :], 1, 1)
            total = total + mm(raw_high, step[:, rows]) + mm(raw_low, step[:, rows])
            for k in range(tails):
                total = total + mm(dvs[k][...], weights[k][rows, :], 1, 1)
            tiles.append(total)
        if swap:
            tiles = tiles[::-1]
        if parts == 2:
            first = place[2] == 0
            outs[0][...] = jnp.where(first, tiles[0], tiles[1])
            outs[1][...] = jnp.where(first, tiles[1], tiles[0])
        else:
            for b in range(parts):
                outs[0][:, b * block : (b + 1) * block] = tiles[b]

    return body


def last_body(work, term, work_ins, shares):
    def body(place, *rest, waits):
        rest = list(rest)
        take = lambda n: [rest.pop(0) for _ in range(n)]
        for_work = take(work_ins)
        select, step, before, weight = take(4)
        others = take(len(rest) - 1 - shares - 5)
        half = len(others) // 2
        mixed, *outs = take(1 + shares)
        bufs, sems, dv, keys, steps = take(5)
        work(place, *for_work, mixed, dv, keys, steps, bufs, sems)
        term(
            place, for_work[0], select, step, before, dv, weight,
            *others[:half], keys, *others[half:], steps, *outs, waits=waits,
        )

    return body


def finish_body(flip):
    def body(a, b, out):
        total = (a[...] + b[...]).astype(BF)
        if not flip:
            out[...] = total
            return
        width = total.shape[1]
        block = flip_block(width)
        turn = reversal(block)
        for j in range(width // block):
            out[:, j * block : (j + 1) * block] = mm(
                total[:, width - (j + 1) * block : width - j * block], turn
            ).astype(BF)

    return body


def widen_body(piece):
    def body(v_ref, g_ref, token, *rest):
        wide = rest[-1]
        length, width = g_ref.shape
        wide[0:length, :] = v_ref[...].reshape(length, width).astype(F32)
        wide[length : 2 * length, :] = g_ref[...].astype(F32)
        if piece:
            put_piece(wide, 2 * length, rest[0][...])

    return body


def local(shards, parts):
    pairs = shards // 2

    def body(
        hidden, complement, inner_weight, select_weight, step_weight, step_bias, decay_rate,
        skip_gain, cotangent, complement_cotangent,
    ):
        length, width = hidden.shape
        inner = inner_weight.shape[1]
        heads = step_bias.shape[0]
        head_width = inner // heads
        groups = 4
        chunk = inner // groups
        group_heads = heads // groups
        seq = lax.axis_index("seq")
        place = jnp.stack([seq % 2, seq // 2, lax.axis_index("chan")]).astype(jnp.int32)
        bias = step_bias.reshape(1, heads)
        rate = decay_rate.reshape(1, heads)
        rate_row = jnp.pad(rate, ((0, 0), (0, LANES - heads)))
        gain = skip_gain.reshape(1, heads)
        step_rows = step_weight.T
        cots = (cotangent, complement_cotangent)
        swap_pairs = [(a, a ^ 1) for a in range(shards)]
        edges = []
        for start in range(2):
            meets = [(z, z + 1) for z in range(start, pairs - 1, 2)]
            paired = sum(meets, ())
            meets += [(b, a) for a, b in meets] + [(z, z) for z in range(pairs) if z not in paired]
            edges.append([(2 * a + y, 2 * b + y) for a, b in meets for y in range(2)])
        swap = lambda x: lax.ppermute(x, "seq", swap_pairs)
        pack_shape = (length, 3 * LANES)
        pair_shape = (2 * LANES, chunk)
        wide_shape = lambda pieces: sds((2 * length + pieces * piece_rows(length, chunk), chunk))
        token_shape = sds((8, LANES))
        work = lambda: [pltpu.VMEM((2,) + pair_shape, F32), pltpu.SemaphoreType.DMA((2,))]
        order = [(1, groups - 1)] + [(0, k) for k in range(groups)] + [(1, k) for k in range(groups - 1)]
        chunks = len(order)

        v_first, source, pack0, pack1, row, wide = run(
            start_body,
            [*map(Copied, (hidden, complement, select_weight, step_rows, bias, rate)),
             Copied(Block(inner_weight, (width, chunk), (0, 0))),
             Copied(Block(inner_weight, (width, chunk), (0, groups - 1))),
             Copied(Block(cots[0], (length, chunk), (0, 0)))],
            [sds((2, 2, length, chunk), BF), sds((2 * length, width), BF), sds(pack_shape),
             sds(pack_shape), token_shape, wide_shape(3)],
            limit=60,
        )
        packs = (pack0, pack1)
        far_row = swap(row)
        v_more = run(
            more_body,
            [source] + [Copied(Block(inner_weight, (width, chunk), (0, k))) for k in range(1, groups - 1)],
            [sds((groups - 2, 2, length, chunk), BF)],
        )[0]

        def value_block(c):
            s, k = order[c]
            array, n = (v_first, k // (groups - 1)) if k in (0, groups - 1) else (v_more, k - 1)
            return Block(array, (1, 1, length, chunk), (n, s, 0, 0))

        def cot_block(c):
            s, k = order[c]
            return Block(cots[s], (length, chunk), (0, k))

        def weight_block(c):
            return Copied(Block(inner_weight, (width, chunk), (0, order[c][1])))

        far = {}
        totals, within, post = {}, {}, {}
        got = ([], [])
        grads = [None, None]
        riders = {2 + n: n for n in range(3)}
        columns = {}
        steps = chunks + pairs - 2

        def do_pair(c, token):
            s, k = order[c]
            rows = piece_rows(length, chunk)
            if s == 0:
                pieces, piece_at = [far[1]] * 3, [2 * length + n * rows for n in range(3)]
            else:
                pieces, piece_at = [far[r] for r in riders], [2 * length] * 3
            totals[c] = run(
                pair_body(k * group_heads, heads, head_width, piece_at),
                [place, value_block(c), cot_block(c), far[c], *pieces, packs[s], Far(token)],
                [sds(pair_shape), sds(pair_shape), sds(pair_shape), sds((8, chunk))],
            )
            return totals[c][3]

        within_shapes = [
            sds((length, chunk)), sds((length, chunk)), sds((length, 2 * LANES)), sds((length, LANES))
        ]
        post_shapes = [
            sds((length, chunk), BF), sds((length, chunk), BF), sds((length, 2 * LANES)), sds((length, LANES))
        ]
        flows = lambda: [pltpu.VMEM((2, LANES, length), F32)]

        def do_within(c):
            s, k = order[c]
            within[c] = run(
                within_body(k * group_heads, heads, head_width),
                [packs[s], value_block(c), cot_block(c), rate_row],
                within_shapes,
                scratch=flows(),
            )
            return within[c][3]

        def post_parts(c, token, fused):
            s, k = order[c]
            last = pairs - 1
            ups = [got[(z + 1) % 2][max(c + z - 1, c)] for z in range(pairs)]
            downs = [got[(last - z) % 2][max(c + z - 1, c)] for z in range(pairs)]
            body = post_body(k * group_heads, heads, head_width, len(ups), len(downs), c == 0)
            if fused:
                body = chunk_body(within_body(k * group_heads, heads, head_width), body, c == 0)
            near = columns["far"] if c == 0 else [totals[c][2]]
            ins = [packs[s], value_block(c), cot_block(c), *([] if fused else within[c]),
                   *near, totals[c][3], gain, rate_row, Far(token),
                   *map(Far, ups), *map(Far, downs)]
            return body, ins

        def do_chunk(c, token):
            body, ins = post_parts(c, token, True)
            post[c] = run(
                body, [place, *ins], post_shapes, stored=(0,),
                scratch=work() + [pltpu.VMEM(o.shape, o.dtype) for o in within_shapes] + flows(),
            )
            return post[c][3]

        def do_partial(cs, token, before=None):
            return run(
                partial_body(len(cs), before is not None),
                [Far(token), *[post[c][1] for c in cs], *[weight_block(c) for c in cs]]
                + ([] if before is None else [before]),
                [sds((length, width))],
            )[0]

        shares = [sds((length, width // parts))] * 2 if parts == 2 else [sds((length, width))]

        def send_share(term):
            if parts == 2:
                return term[0], lax.ppermute(term[1], "chan", [(0, 1), (1, 0)])
            share = lax.psum_scatter(term[0], "chan", scatter_dimension=1, tiled=True)
            return share, jnp.zeros_like(share)

        def do_term(s, before):
            mine = [c for c in range(chunks) if order[c][0] == s]
            return send_share(run(
                term_body(len(mine), 0, heads, parts, s == 1),
                [place, packs[s], Copied(select_weight), Copied(step_rows), before,
                 *[post[c][2] for c in mine], *[post[c][3] for c in mine]],
                shares,
            ))

        def do_last(c, before, token):
            s = order[c][0]
            mine = [n for n in range(chunks) if order[n][0] == s and n != c]
            body, ins = post_parts(c, token, False)
            out = run(
                last_body(
                    body, term_body(len(mine) + 1, 1, heads, parts, s == 1), len(ins), len(shares)
                ),
                [place, *ins, Copied(select_weight), Copied(step_rows), before, weight_block(c),
                 *[post[n][2] for n in mine], *[post[n][3] for n in mine]],
                [post_shapes[0], *shares],
                scratch=work() + [pltpu.VMEM(o.shape, o.dtype) for o in post_shapes[1:]],
                stored=(0,),
            )
            post[c] = (out[0],)
            return send_share(out[1:])

        def do_finish(s, share):
            return run(
                finish_body(s == 1), list(share), [sds((length, width // parts), BF)], stored=(0,)
            )[0]

        def do_step(k, ends):
            has = [0 <= k - z < chunks and z < pairs - 1 for z in range(pairs)]
            ins = [place]
            for d in range(2):
                ins += [totals[k - z][d] for z in range(pairs) if has[z]]
                ins += [totals[k - z][3] for z in range(pairs) if has[z]]
            if k > 0:
                ins += [got[0][-1], got[1][-1]]
            return run(
                step_body(has, k == 0, len(ends)),
                ins + [Far(e) for e in ends],
                [sds(pair_shape), sds(pair_shape), token_shape],
            )

        def do_columns():
            s, k = order[0]
            out = run(
                column_body(k * group_heads, heads, head_width),
                [place, value_block(0), cot_block(0), packs[s], far_row],
                [sds(pair_shape)] * 4 + [sds((8, chunk))],
            )
            totals[0] = (out[0], out[1], None, out[4])
            columns["own"] = (out[2], out[3])
            return out[4]

        def do_exchange(token):
            last = pairs - 1
            ups = [got[(z + 1) % 2][max(z - 1, 0)] for z in range(pairs)]
            downs = [got[(last - z) % 2][max(z - 1, 0)] for z in range(pairs)]
            sends = run(
                exchange_body(len(ups), len(downs)),
                [place, *columns["own"], totals[0][3], Far(token), *map(Far, ups), *map(Far, downs)],
                [sds(pair_shape), sds(pair_shape)],
                scratch=work(),
            )
            columns["far"] = [swap(x) for x in sends]

        def do_widen(c):
            ins = [value_block(c), cot_block(c), Far(far[c - 1])]
            if c in riders:
                ins.append(Block(packs[1], (length, LANES), (0, riders[c])))
            return run(
                widen_body(c in riders), ins, [wide_shape(1 if c in riders else 0)]
            )[0]

        far[1] = swap(wide)
        ends = [do_columns()]
        halfway = None
        share = None
        for k in range(steps):
            made = do_step(k, ends)
            token = made[2]
            for d in range(2):
                got[d].append(lax.ppermute(made[d], "seq", edges[d]))
            ends = []
            if k + 2 < chunks:
                far[k + 2] = swap(do_widen(k + 2))
            if k + 1 < chunks:
                ends.append(do_pair(k + 1, token))
            if k == max(chunks - 2, pairs - 1):
                do_exchange(far[chunks - 1])
            if k == steps - 3:
                ends.append(columns["far"][0])
            c = k - pairs + 1
            if c > 0:
                ends.append(do_chunk(c, token))
            if c == groups:
                share = do_term(0, do_partial(list(range(1, groups + 1)), token))
                ends.append(share[0])
            if c == groups + 1:
                halfway = do_partial([groups + 1], token)
                ends.append(halfway)
            if c == groups + 2:
                grads[0] = do_finish(0, share)
                do_chunk(0, token)
                halfway = do_partial([groups + 2, 0], token, halfway)
        do_within(chunks - 1)
        grads[1] = do_finish(1, do_last(chunks - 1, halfway, halfway))
        outs = [
            jnp.concatenate([post[order.index((s, k))][0] for k in range(groups)], axis=1)
            for s in range(2)
        ]
        return (outs[0], outs[1], grads[0], grads[1])

    return body


def solution(mesh):
    rows = P(("dp", "seq"), None)
    both = P(("dp", "seq"), "chan")
    in_specs = (
        rows, rows, P(None, "chan"), P(), P(None, "chan"),
        P("chan"), P("chan"), P("chan"), both, both,
    )
    return jax.shard_map(
        local(mesh.shape["seq"], mesh.shape["chan"]),
        mesh=mesh,
        in_specs=in_specs,
        out_specs=(both,) * 4,
        check_vma=False,
    )
```

```python
import jax
import jax.numpy as jnp
from jax import lax
from jax.experimental import pallas as pl
from jax.experimental.pallas import tpu as pltpu
from jax.sharding import PartitionSpec as P

BF = jnp.bfloat16
F32 = jnp.float32
LANES = 128


def mm(a, b, ca=1, cb=0):
    return lax.dot_general(a, b, (((ca,), (cb,)), ((), ())), preferred_element_type=F32)


def halves(x):
    high = x.astype(BF)
    return high, (x - high.astype(F32)).astype(BF)


def mm_exact(a, b, ca=1, cb=0):
    first, rest = b.astype(BF), None
    rest = b - first.astype(F32)
    second = rest.astype(BF)
    third = (rest - second.astype(F32)).astype(BF)
    return mm(a, first, ca, cb) + mm(a, second, ca, cb) + mm(a, third, ca, cb)


def iotas(rows, columns):
    return (
        lax.broadcasted_iota(jnp.int32, (rows, columns), 0),
        lax.broadcasted_iota(jnp.int32, (rows, columns), 1),
    )


def spread(weights, base, width, head_width):
    heads = weights[0].shape[1]
    row, channel = iotas(2 * heads, width)
    start = (jnp.where(row >= heads, row - heads, row) - base) * head_width
    pick = ((channel >= start) & (channel < start + head_width)).astype(BF)
    stacked = jnp.concatenate(weights, axis=0) if len(weights) > 1 else weights[0]
    out = mm(jnp.concatenate(halves(stacked), axis=1), pick)
    result, at = [], 0
    for w in weights:
        result.append(out[at : at + w.shape[0]])
        at += w.shape[0]
    return result


def spread_rows(rows, base, width, head_width):
    heads = rows[0].shape[1]
    wide = spread([jnp.broadcast_to(r, (8, heads)) for r in rows], base, width, head_width)
    return [w[0:1] for w in wide]


def gather_heads(parts, base, head_width):
    width = parts[0].shape[1]
    channel, head = iotas(width, LANES)
    start = (head - base) * head_width
    pick = ((channel >= start) & (channel < start + head_width)).astype(BF)
    out = mm(jnp.concatenate([x.astype(BF) for x in parts], axis=0), pick)
    result, at = [], 0
    for x in parts:
        result.append(out[at : at + x.shape[0]])
        at += x.shape[0]
    return result


def reversal(size):
    i, j = iotas(size, size)
    return (i + j == size - 1).astype(BF)


def flip_block(size):
    return 256 if size % 256 == 0 else 128


def sds(shape, dtype=F32):
    return jax.ShapeDtypeStruct(shape, dtype)


class Block:
    def __init__(self, array, shape, index):
        self.array, self.shape, self.index = array, shape, index

    def view(self, ref):
        if self.shape == self.array.shape:
            return ref
        return ref.at[tuple(pl.ds(i * b, b) for i, b in zip(self.index, self.shape))]


class Copied:
    def __init__(self, item):
        self.item = item if isinstance(item, Block) else Block(item, item.shape, (0,) * item.ndim)


class Far:
    def __init__(self, array):
        self.array = array


def run(body, ins, outs, scratch=(), limit=16, stored=()):
    specs, arrays, copied = [], [], []
    for item in ins:
        if isinstance(item, Far):
            specs.append(pl.BlockSpec(memory_space=pl.ANY))
            arrays.append(item.array)
        elif isinstance(item, Copied):
            specs.append(pl.BlockSpec(memory_space=pltpu.HBM))
            arrays.append(item.item.array)
            copied.append(item.item)
        elif isinstance(item, Block):
            specs.append(pl.BlockSpec(memory_space=pltpu.VMEM))
            arrays.append(item.array)
        else:
            space = pltpu.SMEM if item.dtype == jnp.int32 else pltpu.VMEM
            specs.append(pl.BlockSpec(memory_space=space))
            arrays.append(item)
    out_specs = [
        pl.BlockSpec(memory_space=pltpu.HBM if n in stored else pltpu.VMEM)
        for n in range(len(outs))
    ]
    holds = [pltpu.VMEM(q.shape, q.array.dtype) for q in copied]
    holds += [pltpu.VMEM(outs[n].shape, outs[n].dtype) for n in stored]
    sems = [pltpu.SemaphoreType.DMA((max(len(holds), 1),))]

    def kernel(*refs):
        refs = list(refs)
        take = lambda n: [refs.pop(0) for _ in range(n)]
        sources, targets = take(len(ins)), take(len(outs))
        held, (sem,) = take(len(holds)), take(1)
        args, copies = [], []
        for ref, item in zip(sources, ins):
            if isinstance(item, Copied):
                n = len(copies)
                copies.append(pltpu.make_async_copy(item.item.view(ref), held[n], sem.at[n]))
                copies[-1].start()
                ref = held[n]
            elif isinstance(item, Block):
                ref = item.view(ref)
            args.append(ref)
        back = []
        for n, ref in enumerate(targets):
            if n in stored:
                k = len(copied) + stored.index(n)
                back.append(pltpu.make_async_copy(held[k], ref, sem.at[k]))
                ref = held[k]
            args.append(ref)
        waits = {"waits": [c.wait for c in copies]} if copies else {}
        body(*args, *refs, **waits)
        for copy in back:
            copy.start()
        for copy in back:
            copy.wait()

    return pl.pallas_call(
        kernel,
        in_specs=specs,
        out_specs=out_specs,
        out_shape=outs,
        scratch_shapes=holds + sems + list(scratch),
        compiler_params=pltpu.CompilerParams(vmem_limit_bytes=limit * 1024 * 1024),
        cost_estimate=pl.CostEstimate(flops=0, bytes_accessed=1024, transcendentals=0),
    )(*arrays)


def start_body(
    hidden, other, select, step, bias, rate, weight, cot,
    source, pack0, pack1, row, v_out, wide, waits,
):
    for wait in waits[0:2]:
        wait()
    length, width = hidden.shape
    heads = bias.shape[1]
    source[0:length, :] = hidden[...]
    block = flip_block(width)
    turn = reversal(block)
    for j in range(width // block):
        source[length : 2 * length, j * block : (j + 1) * block] = mm(
            other[:, width - (j + 1) * block : width - j * block], turn
        ).astype(BF)
    for wait in waits[2:6]:
        wait()
    keys = mm(source[...], select[...]).astype(BF).astype(F32)
    state = keys.shape[1] // 2
    raw = mm(source[...], step[...], 1, 1) + bias[...]
    dt = jnp.maximum(raw, 0.0) + jnp.log1p(jnp.exp(-jnp.abs(raw)))
    rise = jax.nn.sigmoid(raw)
    i, j = iotas(length, length)
    lower = (i >= j).astype(BF)
    for s, pack in enumerate((pack0, pack1)):
        rows = slice(s * length, (s + 1) * length)
        drop = dt[rows] * rate[...]
        total = mm_exact(lower, drop)
        pack[...] = jnp.zeros(pack.shape, F32)
        pack[:, 0 : 2 * state] = keys[rows]
        at = 2 * state
        for part in (dt[rows], total, total - drop, rise[rows]):
            pack[:, at : at + heads] = part
            at += heads
    row[...] = jnp.zeros(row.shape, F32)
    row[0:1, 0:heads] = jnp.exp(
        -pack1[length - 1 : length, 2 * state + heads : 2 * state + 2 * heads]
    )
    for wait in waits[6:]:
        wait()
    piece = mm(source[...], weight[...]).astype(BF)
    for s in range(2):
        v_out[0, s] = piece[s * length : (s + 1) * length]
    wide[0:length, :] = piece[0:length].astype(F32)
    wide[length : 2 * length, :] = cot[...].astype(F32)
    for n in range(3):
        at = 2 * length + n * piece_rows(length, wide.shape[1])
        put_piece(wide, at, pack0[:, n * LANES : (n + 1) * LANES])


def gate_body(wide, token0, token1, out):
    pass


def values_body(source, token, *rest, waits):
    weights, v_out = rest[:-1], rest[-1]
    length = v_out.shape[2]
    for n, weight in enumerate(weights):
        waits[n]()
        piece = mm(source[...], weight[...]).astype(BF)
        for s in range(2):
            v_out[n, s] = piece[s * length : (s + 1) * length]


class Pack:
    def __init__(self, write, read, stats, heads):
        self.write, self.read = write, read
        self.dt = stats[:, 0:heads]
        self.total = stats[:, heads : 2 * heads]
        self.before = stats[:, 2 * heads : 3 * heads]
        last = self.total.shape[0]
        self.whole = self.total[last - 1 : last, :]
        self.from_start = jnp.exp(-self.total)
        self.from_end = jnp.exp(self.before - self.whole)
        self.to_end = jnp.exp(self.total - self.whole)
        self.to_start = jnp.exp(-self.before)
        self.through = jnp.exp(-self.whole)


def own_pack(ref, heads):
    return Pack(*[ref[:, n * LANES : (n + 1) * LANES] for n in range(3)], heads)


def piece_rows(length, width):
    return length // (width // LANES)


def put_piece(ref, row, piece):
    count = piece_rows(piece.shape[0], ref.shape[1])
    for b in range(ref.shape[1] // LANES):
        ref[row : row + count, b * LANES : (b + 1) * LANES] = piece[b * count : (b + 1) * count]


def get_piece(ref, row, length):
    count = piece_rows(length, ref.shape[1])
    return jnp.concatenate(
        [
            ref[row : row + count, b * LANES : (b + 1) * LANES]
            for b in range(ref.shape[1] // LANES)
        ],
        axis=0,
    )


def pair_body(base, heads, head_width, piece_at):
    def body(place, v_own, g_own, x_far, far0, far1, far2, own_ref, token, up, down, near, keep):
        first = place[0] == 0
        length, width = g_own.shape
        own = own_pack(own_ref, heads)
        far = Pack(*[get_piece(f, at, length) for f, at in zip((far0, far1, far2), piece_at)], heads)
        own_row, far_row = own.through, far.through
        rows = spread_rows([own_row * far_row, far_row], base, width, head_width)
        keep[...] = jnp.zeros(keep.shape, F32)
        keep[0:1, :] = rows[0]
        keep[1:2, :] = rows[1]
        own_up, own_down = jnp.where(first, far_row, 1.0), jnp.where(first, 1.0, far_row)
        far_up, far_down = jnp.where(first, 1.0, own_row), jnp.where(first, own_row, 1.0)
        for kind in range(2):
            rows = slice(kind * LANES, (kind + 1) * LANES)
            if kind == 0:
                keys = (own.write, far.write)
                ups = (own.dt * own.to_end, far.dt * far.to_end)
                downs = (own.dt * own.to_start, far.dt * far.to_start)
            else:
                keys = (own.read, far.read)
                ups = (own.from_end, far.from_end)
                downs = (own.from_start, far.from_start)
            x_own = (v_own if kind == 0 else g_own)[...].reshape(length, width).astype(F32)
            x_other = x_far[kind * length : (kind + 1) * length, :]
            w = spread(
                [ups[0] * own_up, ups[1] * far_up, downs[0] * own_down, downs[1] * far_down,
                 jnp.where(first, downs[1], ups[1])],
                base, width, head_width,
            )
            key = jnp.concatenate(keys, axis=0).astype(BF)
            both = lambda a, b: jnp.concatenate([(a * x_own).astype(BF), (b * x_other).astype(BF)], axis=0)
            up[rows, :] = mm(key, both(w[0], w[1]), 0, 0)
            down[rows, :] = mm(key, both(w[2], w[3]), 0, 0)
            near[rows, :] = mm(keys[1].astype(BF), (w[4] * x_other).astype(BF), 0, 0)

    return body


def column_body(base, heads, head_width):
    def body(place, v_own, g_own, own_ref, far_row_ref, up, down, own_up, own_down, keep):
        first = place[0] == 0
        length, width = g_own.shape
        own = own_pack(own_ref, heads)
        far_row = far_row_ref[0:1, 0:heads]
        rows = spread_rows([own.through * far_row, far_row, own.through], base, width, head_width)
        keep[...] = jnp.zeros(keep.shape, F32)
        for n, row in enumerate(rows):
            keep[n : n + 1, :] = row
        up_row = jnp.where(first, rows[1], 1.0)
        down_row = jnp.where(first, 1.0, rows[1])
        for kind in range(2):
            at = slice(kind * LANES, (kind + 1) * LANES)
            if kind == 0:
                key, weights = own.write, [own.dt * own.to_end, own.dt * own.to_start]
            else:
                key, weights = own.read, [own.from_end, own.from_start]
            key = key.astype(BF)
            x = (v_own if kind == 0 else g_own)[...].reshape(length, width).astype(F32)
            w = spread(weights, base, width, head_width)
            state_up = mm(key, (w[0] * x).astype(BF), 0, 0)
            state_down = mm(key, (w[1] * x).astype(BF), 0, 0)
            own_up[at, :] = state_up
            own_down[at, :] = state_down
            up[at, :] = up_row * state_up
            down[at, :] = down_row * state_down

    return body


def exchange_body(ups, downs):
    def body(place, own_up, own_down, keep, token, *rest):
        up_in, down_in = rest[0:ups], rest[ups : ups + downs]
        up_out, down_out, bufs, sems = rest[ups + downs :]
        up_spot, down_spot = place[1], len(up_in) - 1 - place[1]
        fetch_start(up_in, up_spot, bufs.at[0], sems.at[0])
        fetch_start(down_in, down_spot, bufs.at[1], sems.at[1])
        fetch_wait(up_in, up_spot, bufs.at[0], sems.at[0])
        fetch_wait(down_in, down_spot, bufs.at[1], sems.at[1])
        first = place[0] == 0
        row = keep[2:3, :]
        up_out[...] = jnp.where(first, row * bufs[0] + own_up[...], bufs[0])
        down_out[...] = jnp.where(first, bufs[1], row * bufs[1] + own_down[...])

    return body


def fetch_start(options, index, target, sem):
    for z, option in enumerate(options):
        if option is not None:

            @pl.when(index == z)
            def _():
                pltpu.make_async_copy(option, target, sem).start()


def fetch_wait(options, index, target, sem):
    for z, option in enumerate(options):
        if option is not None:

            @pl.when(index == z)
            def _():
                pltpu.make_async_copy(option, target, sem).wait()


def step_body(has, first_step, widen, pieces, tokens):
    pairs = len(has)

    def body(place, *rest):
        rest = list(rest)
        take = lambda n: [rest.pop(0) for _ in range(n)]
        sides = []
        for d in range(2):
            totals = [take(1)[0] if h else None for h in has]
            keeps = [take(1)[0] if h else None for h in has]
            sides.append((totals, keeps))
        got = None if first_step else take(2)
        chunk = take(2) if widen else None
        piece_refs = take(pieces)
        take(tokens)
        sends = take(2)
        token = take(1)[0]
        spots = (place[1], pairs - 1 - place[1])
        for d, (totals, keeps) in enumerate(sides):
            for n in range(pairs):
                z = n if d == 0 else pairs - 1 - n
                send = sends[(z + d) % 2]

                @pl.when(spots[d] == n)
                def _():
                    if not has[n]:
                        send[...] = jnp.zeros(send.shape, F32)
                    elif got is None or n == 0:
                        send[...] = totals[n][...]
                    else:
                        send[...] = totals[n][...] + keeps[n][0:1, :] * got[(z + 1 + d) % 2][...]

        token[...] = jnp.zeros(token.shape, F32)
        if widen:
            put_chunk(take(1)[0], *chunk, piece_refs)

    return body


def within_body(base, heads, head_width):
    def body(own_ref, v_ref, g_ref, rate, y_out, x_out, keys_out, steps_out, cols_s):
        own = own_pack(own_ref, heads)
        length, width = g_ref.shape
        write, read = own.write.astype(BF), own.read.astype(BF)
        scores = mm(read, write, 1, 1)
        i, j = iotas(length, length)
        low = i > j
        high = i < j
        doubled = jnp.where(i == j, 2.0, 1.0).astype(F32)
        scores2 = scores * doubled
        turned = own_ref[:, 2 * LANES : 3 * LANES].T
        lane = lax.broadcasted_iota(jnp.int32, (length, LANES), 1)
        d_scores = jnp.zeros((length, length), F32)
        out_low = jnp.zeros((length, LANES), F32)
        out_high = jnp.zeros((length, LANES), F32)
        cols_s[...] = jnp.zeros(cols_s.shape, F32)
        v_all = v_ref[...].reshape(length, width)
        per = LANES // head_width
        for n in range(width // LANES):
            at = slice(n * LANES, (n + 1) * LANES)
            v, g = v_all[:, at], g_ref[:, at]
            mine = [(lane >= m * head_width) & (lane < (m + 1) * head_width) for m in range(per)]
            v_heads = jnp.concatenate([jnp.where(x, v, jnp.zeros_like(v)) for x in mine], axis=0)
            g_heads = jnp.concatenate([jnp.where(x, g, jnp.zeros_like(g)) for x in mine], axis=0)
            products = mm(g_heads, v, 1, 1)
            plains, steppeds = [], []
            for m in range(per):
                h = base + n * per + m
                c_col = own.total[:, h : h + 1]
                e_col = own.before[:, h : h + 1]
                dt_row = turned[h : h + 1, :]
                c_row = turned[heads + h : heads + h + 1, :]
                e_row = turned[2 * heads + h : 2 * heads + h + 1, :]
                decay = jnp.exp(jnp.where(low, c_row - c_col, e_col - e_row))
                plain = decay * scores2
                plains.append(plain.astype(BF))
                steppeds.append((plain * dt_row).astype(BF))
                inner = decay * dt_row * products[m * length : (m + 1) * length]
                d_scores = d_scores + inner
                flow = inner * scores
                flow_low = jnp.where(low, flow, 0.0)
                flow_high = jnp.where(high, flow, 0.0)
                out_low = jnp.where(lane == h, jnp.sum(flow_low, 1, keepdims=True), out_low)
                out_high = jnp.where(lane == h, jnp.sum(flow_high, 1, keepdims=True), out_high)
                cols_s[0, h : h + 1, :] = jnp.sum(flow_low, 0, keepdims=True)
                cols_s[1, h : h + 1, :] = jnp.sum(flow_high, 0, keepdims=True)
            y_out[:, at] = mm(jnp.concatenate(steppeds, axis=1), v_heads)
            x_out[:, at] = mm(jnp.concatenate(plains, axis=0), g_heads, 0, 0)
        d_scores = (d_scores * doubled).astype(BF)
        keys_out[:, 0:LANES] = mm(d_scores, read, 0, 0)
        keys_out[:, LANES : 2 * LANES] = mm(d_scores, write)
        net_low = out_low - cols_s[0].T
        net_high = out_high - cols_s[1].T
        at_or_after = (j >= i).astype(BF)
        after = (j > i).astype(BF)
        steps_out[...] = -rate[...] * (mm_exact(at_or_after, net_low) - mm_exact(after, net_high))

    return body


def post_body(base, heads, head_width, ups, downs, columns=False):
    def body(
        place, own_ref, v_ref, g_ref, yw, xw, keys_w, steps_w, near, keep, skip, rate, token, *rest
    ):
        up_in, down_in = rest[0:ups], rest[ups : ups + downs]
        mixed, dv_out, keys_out, steps_out, bufs, sems = rest[ups + downs :]
        up_spot, down_spot = place[1], len(up_in) - 1 - place[1]
        fetch_start(up_in, up_spot, bufs.at[0], sems.at[0])
        fetch_start(down_in, down_spot, bufs.at[1], sems.at[1])
        first = place[0] == 0
        own = own_pack(own_ref, heads)
        length, width = g_ref.shape
        far_row = keep[1:2, :]
        own_row, gain = spread_rows([own.through, skip[...]], base, width, head_width)
        up_row = jnp.where(first, 1.0, far_row)
        down_row = jnp.where(first, far_row, 1.0)
        dt, from_start, from_end, to_end, to_start = spread(
            [own.dt, own.from_start, own.from_end, own.to_end, own.to_start],
            base, width, head_width,
        )
        write, read = own.write.astype(BF), own.read.astype(BF)
        v = v_ref[...].reshape(length, width).astype(F32)
        g = g_ref[...].astype(F32)
        fetch_wait(up_in, up_spot, bufs.at[0], sems.at[0])
        fetch_wait(down_in, down_spot, bufs.at[1], sems.at[1])
        if columns:
            up = up_row * bufs[0] + near[0][...]
            down = down_row * bufs[1] + near[1][...]
        else:
            up = up_row * bufs[0] + jnp.where(first, 0.0, near[...])
            down = down_row * bufs[1] + jnp.where(first, near[...], 0.0)
        p, ab = up[0:LANES], up[LANES : 2 * LANES]
        q, af = down[0:LANES], down[LANES : 2 * LANES]
        crossing = jnp.sum(p * af + q * ab, axis=0, keepdims=True)
        p, q, af, ab = p.astype(BF), q.astype(BF), af.astype(BF), ab.astype(BF)
        y_p = from_start * mm(read, p)
        y_q = from_end * mm(read, q)
        x_f = to_end * mm(write, af)
        x_b = to_start * mm(write, ab)
        mixed[...] = (yw[...] + y_p + y_q + gain * v).astype(BF)
        x = xw[...] + x_f + x_b
        dv_out[...] = (dt * x + gain * g).astype(BF)
        dtv = dt * v
        keys_out[:, 0:LANES] = (
            keys_w[:, 0:LANES]
            + mm((to_end * dtv).astype(BF), af, 1, 1)
            + mm((to_start * dtv).astype(BF), ab, 1, 1)
        )
        keys_out[:, LANES : 2 * LANES] = (
            keys_w[:, LANES : 2 * LANES]
            + mm((from_start * g).astype(BF), p, 1, 1)
            + mm((from_end * g).astype(BF), q, 1, 1)
        )
        lane = lax.broadcasted_iota(jnp.int32, (length, LANES), 1)
        steps = jnp.where(lane < heads, own_ref[:, 2 * LANES : 3 * LANES], 0.0)
        direct, a_p, a_q, b_f, b_b, through = gather_heads(
            [v * x, g * y_p, g * y_q, v * x_f, v * x_b, jnp.broadcast_to(crossing * own_row, (8, width))],
            base, head_width,
        )
        i, j = iotas(length, length)
        masks = jnp.concatenate([j >= i, j <= i, j < i, j > i], axis=1).astype(F32).astype(BF)
        high, low = halves(jnp.concatenate([a_p, a_q, b_f * steps, b_b * steps], axis=0))
        flow = mm(masks, high) + mm(masks, low) + through[0:1]
        steps_out[...] = steps_w[...] + direct - rate[...] * flow

    return body


def chunk_body(within, post, columns):
    def body(place, own_ref, v_ref, g_ref, *rest):
        nears = 2 if columns else 1
        near = rest[0:2] if columns else rest[0]
        keep, skip, rate, token, *rest = rest[nears:]
        bufs, sems, yw, xw, keys_w, steps_w, cols_s = rest[-7:]
        within(own_ref, v_ref, g_ref, rate, yw, xw, keys_w, steps_w, cols_s)
        post(
            place, own_ref, v_ref, g_ref, yw, xw, keys_w, steps_w, near, keep, skip, rate, token,
            *rest[:-5],
        )

    return body


def partial_body(groups, more):
    def body(token, *rest, waits):
        dvs, weights, rest = rest[0:groups], rest[groups : 2 * groups], rest[2 * groups :]
        out = rest[-1]
        for wait in waits:
            wait()
        total = mm(dvs[0][...], weights[0][...], 1, 1)
        for k in range(1, groups):
            total = total + mm(dvs[k][...], weights[k][...], 1, 1)
        out[...] = total + rest[0][...] if more else total

    return body


def term_body(groups, tails, heads, parts, swap):
    def body(place, own_ref, select, step, before, *rest, waits=()):
        dvs, weights = rest[0:tails], rest[tails : 2 * tails]
        rest = rest[2 * tails :]
        keys, steps = rest[0:groups], rest[groups : 2 * groups]
        outs = rest[2 * groups :]
        for wait in waits:
            wait()
        d_keys, d_steps = keys[0][...], steps[0][...]
        for a, b in zip(keys[1:], steps[1:]):
            d_keys = d_keys + a[...]
            d_steps = d_steps + b[...]
        d_raw = d_steps[:, 0:heads] * own_ref[:, 2 * LANES + 3 * heads : 2 * LANES + 4 * heads]
        keys_high, keys_low = halves(d_keys)
        raw_high, raw_low = halves(d_raw)
        width = select.shape[0]
        block = width // parts
        tiles = []
        for b in range(parts):
            rows = slice(b * block, (b + 1) * block)
            total = before[:, rows]
            total = total + mm(keys_high, select[rows, :], 1, 1) + mm(keys_low, select[rows, :], 1, 1)
            total = total + mm(raw_high, step[:, rows]) + mm(raw_low, step[:, rows])
            for k in range(tails):
                total = total + mm(dvs[k][...], weights[k][rows, :], 1, 1)
            tiles.append(total)
        if swap:
            tiles = tiles[::-1]
        if parts == 2:
            first = place[2] == 0
            outs[0][...] = jnp.where(first, tiles[0], tiles[1])
            outs[1][...] = jnp.where(first, tiles[1], tiles[0])
        else:
            for b in range(parts):
                outs[0][:, b * block : (b + 1) * block] = tiles[b]

    return body


def last_body(work, term, work_ins, shares):
    def body(place, *rest, waits):
        rest = list(rest)
        take = lambda n: [rest.pop(0) for _ in range(n)]
        for_work = take(work_ins)
        select, step, before, weight = take(4)
        others = take(len(rest) - 1 - shares - 5)
        half = len(others) // 2
        mixed, *outs = take(1 + shares)
        bufs, sems, dv, keys, steps = take(5)
        work(place, *for_work, mixed, dv, keys, steps, bufs, sems)
        term(
            place, for_work[0], select, step, before, dv, weight,
            *others[:half], keys, *others[half:], steps, *outs, waits=waits,
        )

    return body


def finish_body(flip):
    def body(a, b, out):
        total = (a[...] + b[...]).astype(BF)
        if not flip:
            out[...] = total
            return
        width = total.shape[1]
        block = flip_block(width)
        turn = reversal(block)
        for j in range(width // block):
            out[:, j * block : (j + 1) * block] = mm(
                total[:, width - (j + 1) * block : width - j * block], turn
            ).astype(BF)

    return body


def put_chunk(wide, v_ref, g_ref, pieces):
    length, width = g_ref.shape
    wide[0:length, :] = v_ref[...].reshape(length, width).astype(F32)
    wide[length : 2 * length, :] = g_ref[...].astype(F32)
    for n, piece in enumerate(pieces):
        put_piece(wide, 2 * length + n * piece_rows(length, width), piece[...])


def widen_body(v_ref, g_ref, token, *rest):
    put_chunk(rest[-1], v_ref, g_ref, rest[:-1])


def local(shards, parts):
    pairs = shards // 2

    def body(
        hidden, complement, inner_weight, select_weight, step_weight, step_bias, decay_rate,
        skip_gain, cotangent, complement_cotangent,
    ):
        length, width = hidden.shape
        inner = inner_weight.shape[1]
        heads = step_bias.shape[0]
        head_width = inner // heads
        groups = 4
        chunk = inner // groups
        group_heads = heads // groups
        seq = lax.axis_index("seq")
        place = jnp.stack([seq % 2, seq // 2, lax.axis_index("chan")]).astype(jnp.int32)
        bias = step_bias.reshape(1, heads)
        rate = decay_rate.reshape(1, heads)
        rate_row = jnp.pad(rate, ((0, 0), (0, LANES - heads)))
        gain = skip_gain.reshape(1, heads)
        step_rows = step_weight.T
        cots = (cotangent, complement_cotangent)
        swap_pairs = [(a, a ^ 1) for a in range(shards)]
        edges = []
        for start in range(2):
            meets = [(z, z + 1) for z in range(start, pairs - 1, 2)]
            paired = sum(meets, ())
            meets += [(b, a) for a, b in meets] + [(z, z) for z in range(pairs) if z not in paired]
            edges.append([(2 * a + y, 2 * b + y) for a, b in meets for y in range(2)])
        swap = lambda x: lax.ppermute(x, "seq", swap_pairs)
        pack_shape = (length, 3 * LANES)
        pair_shape = (2 * LANES, chunk)
        wide_shape = lambda pieces: sds((2 * length + pieces * piece_rows(length, chunk), chunk))
        token_shape = sds((8, LANES))
        work = lambda: [pltpu.VMEM((2,) + pair_shape, F32), pltpu.SemaphoreType.DMA((2,))]
        order = [(1, groups - 1)] + [(0, k) for k in range(groups)] + [(1, k) for k in range(groups - 1)]
        chunks = len(order)

        source, pack0, pack1, row, v_zero, wide = run(
            start_body,
            [*map(Copied, (hidden, complement, select_weight, step_rows, bias, rate)),
             Copied(Block(inner_weight, (width, chunk), (0, 0))),
             Copied(Block(cots[0], (length, chunk), (0, 0)))],
            [sds((2 * length, width), BF), sds(pack_shape), sds(pack_shape), token_shape,
             sds((1, 2, length, chunk), BF), wide_shape(3)],
            limit=57,
        )
        packs = (pack0, pack1)
        far_row = swap(row)

        def do_values(ks, token):
            return run(
                values_body,
                [source, Far(token)] + [Copied(Block(inner_weight, (width, chunk), (0, k))) for k in ks],
                [sds((len(ks), 2, length, chunk), BF)],
                limit=57,
            )[0]

        v_last = do_values([groups - 1], row)
        v_more = None

        def value_block(c):
            s, k = order[c]
            array, n = {0: (v_zero, 0), groups - 1: (v_last, 0)}.get(k, (v_more, k - 1))
            return Block(array, (1, 1, length, chunk), (n, s, 0, 0))

        def cot_block(c):
            s, k = order[c]
            return Block(cots[s], (length, chunk), (0, k))

        def weight_block(c):
            return Copied(Block(inner_weight, (width, chunk), (0, order[c][1])))

        far = {}
        totals, within, post = {}, {}, {}
        got = ([], [])
        grads = [None, None]
        riders = {2 + n: n for n in range(3)}
        columns = {}
        steps = chunks + pairs - 2

        def do_pair(c, token):
            s, k = order[c]
            rows = piece_rows(length, chunk)
            if s == 0:
                pieces, piece_at = [far[1]] * 3, [2 * length + n * rows for n in range(3)]
            else:
                pieces, piece_at = [far[r] for r in riders], [2 * length] * 3
            totals[c] = run(
                pair_body(k * group_heads, heads, head_width, piece_at),
                [place, value_block(c), cot_block(c), far[c], *pieces, packs[s], Far(token)],
                [sds(pair_shape), sds(pair_shape), sds(pair_shape), sds((8, chunk))],
            )
            return totals[c][3]

        within_shapes = [
            sds((length, chunk)), sds((length, chunk)), sds((length, 2 * LANES)), sds((length, LANES))
        ]
        post_shapes = [
            sds((length, chunk), BF), sds((length, chunk), BF), sds((length, 2 * LANES)), sds((length, LANES))
        ]
        flows = lambda: [pltpu.VMEM((2, LANES, length), F32)]

        def do_within(c):
            s, k = order[c]
            within[c] = run(
                within_body(k * group_heads, heads, head_width),
                [packs[s], value_block(c), cot_block(c), rate_row],
                within_shapes,
                scratch=flows(),
            )
            return within[c][3]

        def post_parts(c, token, fused):
            s, k = order[c]
            last = pairs - 1
            ups = [got[(z + 1) % 2][max(c + z - 1, c)] for z in range(pairs)]
            downs = [got[(last - z) % 2][max(c + z - 1, c)] for z in range(pairs)]
            body = post_body(k * group_heads, heads, head_width, len(ups), len(downs), c == 0)
            if fused:
                body = chunk_body(within_body(k * group_heads, heads, head_width), body, c == 0)
            near = columns["far"] if c == 0 else [totals[c][2]]
            ins = [packs[s], value_block(c), cot_block(c), *([] if fused else within[c]),
                   *near, totals[c][3], gain, rate_row, Far(token),
                   *map(Far, ups), *map(Far, downs)]
            return body, ins

        def do_chunk(c, token):
            body, ins = post_parts(c, token, True)
            post[c] = run(
                body, [place, *ins], post_shapes, stored=(0,),
                scratch=work() + [pltpu.VMEM(o.shape, o.dtype) for o in within_shapes] + flows(),
            )
            return post[c][3]

        def do_partial(cs, token, before=None):
            return run(
                partial_body(len(cs), before is not None),
                [Far(token), *[post[c][1] for c in cs], *[weight_block(c) for c in cs]]
                + ([] if before is None else [before]),
                [sds((length, width))],
            )[0]

        shares = [sds((length, width // parts))] * 2 if parts == 2 else [sds((length, width))]

        def send_share(term):
            if parts == 2:
                return term[0], lax.ppermute(term[1], "chan", [(0, 1), (1, 0)])
            share = lax.psum_scatter(term[0], "chan", scatter_dimension=1, tiled=True)
            return share, jnp.zeros_like(share)

        def do_term(s, before):
            mine = [c for c in range(chunks) if order[c][0] == s]
            return send_share(run(
                term_body(len(mine), 0, heads, parts, s == 1),
                [place, packs[s], Copied(select_weight), Copied(step_rows), before,
                 *[post[c][2] for c in mine], *[post[c][3] for c in mine]],
                shares,
            ))

        def do_last(c, before, token):
            s = order[c][0]
            mine = [n for n in range(chunks) if order[n][0] == s and n != c]
            body, ins = post_parts(c, token, False)
            out = run(
                last_body(
                    body, term_body(len(mine) + 1, 1, heads, parts, s == 1), len(ins), len(shares)
                ),
                [place, *ins, Copied(select_weight), Copied(step_rows), before, weight_block(c),
                 *[post[n][2] for n in mine], *[post[n][3] for n in mine]],
                [post_shapes[0], *shares],
                scratch=work() + [pltpu.VMEM(o.shape, o.dtype) for o in post_shapes[1:]],
                stored=(0,),
            )
            post[c] = (out[0],)
            return send_share(out[1:])

        def do_finish(s, share):
            return run(
                finish_body(s == 1), list(share), [sds((length, width // parts), BF)], stored=(0,)
            )[0]

        def do_step(k, widen, ends):
            has = [0 <= k - z < chunks and z < pairs - 1 for z in range(pairs)]
            ins = [place]
            for d in range(2):
                ins += [totals[k - z][d] for z in range(pairs) if has[z]]
                ins += [totals[k - z][3] for z in range(pairs) if has[z]]
            if k > 0:
                ins += [got[0][-1], got[1][-1]]
            outs = [sds(pair_shape), sds(pair_shape), token_shape]
            pieces = [] if widen is None else pieces_of(widen)
            if widen is not None:
                ins += [value_block(widen), cot_block(widen), *pieces]
                outs.append(wide_shape(len(pieces)))
            return run(
                step_body(has, k == 0, widen is not None, len(pieces), len(ends)),
                ins + [Far(e) for e in ends],
                outs,
            )

        def do_columns():
            s, k = order[0]
            out = run(
                column_body(k * group_heads, heads, head_width),
                [place, value_block(0), cot_block(0), packs[s], far_row],
                [sds(pair_shape)] * 4 + [sds((8, chunk))],
            )
            totals[0] = (out[0], out[1], None, out[4])
            columns["own"] = (out[2], out[3])
            return out[4]

        def do_exchange(token):
            last = pairs - 1
            ups = [got[(z + 1) % 2][max(z - 1, 0)] for z in range(pairs)]
            downs = [got[(last - z) % 2][max(z - 1, 0)] for z in range(pairs)]
            sends = run(
                exchange_body(len(ups), len(downs)),
                [place, *columns["own"], totals[0][3], Far(token), *map(Far, ups), *map(Far, downs)],
                [sds(pair_shape), sds(pair_shape)],
                scratch=work(),
            )
            columns["far"] = [swap(x) for x in sends]

        def pieces_of(c):
            return [Block(packs[1], (length, LANES), (0, riders[c]))] if c in riders else []

        def do_widen(c, token):
            pieces = pieces_of(c)
            return run(
                widen_body, [value_block(c), cot_block(c), Far(token), *pieces], [wide_shape(len(pieces))]
            )[0]

        far[1] = swap(pl.pallas_call(
            gate_body,
            in_specs=[pl.BlockSpec(memory_space=pl.ANY)] * 3,
            out_specs=pl.BlockSpec(memory_space=pl.ANY),
            out_shape=wide_shape(3),
            input_output_aliases={0: 0},
            cost_estimate=pl.CostEstimate(flops=0, bytes_accessed=1024, transcendentals=0),
        )(wide, far_row, v_last))
        ends = [do_columns()]
        halfway = None
        share = None
        for k in range(steps):
            queue = k + 2 if 0 < k < chunks - 2 else None
            made = do_step(k, queue, ends)
            token = made[2]
            for d in range(2):
                got[d].append(lax.ppermute(made[d], "seq", edges[d]))
            ends = []
            if k == 0:
                v_more = do_values(list(range(1, groups - 1)), token)
                far[2] = swap(do_widen(2, token))
            if queue is not None:
                far[queue] = swap(made[3])
            if k + 1 < chunks:
                ends.append(do_pair(k + 1, token))
            if k == max(chunks - 2, pairs - 1):
                do_exchange(far[chunks - 1])
            if k == steps - 3:
                ends += columns["far"]
            c = k - pairs + 1
            if c > 0:
                ends.append(do_chunk(c, token))
            if c == groups:
                share = do_term(0, do_partial(list(range(1, groups + 1)), token))
                ends.append(share[0])
            if c == groups + 1:
                do_chunk(0, token)
                halfway = do_partial([groups + 1, 0], token)
                ends.append(halfway)
            if c == groups + 2:
                grads[0] = do_finish(0, share)
                halfway = do_partial([groups + 2], token, halfway)
        do_within(chunks - 1)
        grads[1] = do_finish(1, do_last(chunks - 1, halfway, halfway))
        outs = [
            jnp.concatenate([post[order.index((s, k))][0] for k in range(groups)], axis=1)
            for s in range(2)
        ]
        return (outs[0], outs[1], grads[0], grads[1])

    return body


def solution(mesh):
    rows = P(("dp", "seq"), None)
    both = P(("dp", "seq"), "chan")
    in_specs = (
        rows, rows, P(None, "chan"), P(), P(None, "chan"),
        P("chan"), P("chan"), P("chan"), both, both,
    )
    return jax.shard_map(
        local(mesh.shape["seq"], mesh.shape["chan"]),
        mesh=mesh,
        in_specs=in_specs,
        out_specs=(both,) * 4,
        check_vma=False,
    )
```

```python
import jax
import jax.numpy as jnp
from jax import lax
from jax.experimental import pallas as pl
from jax.experimental.pallas import tpu as pltpu
from jax.sharding import PartitionSpec as P

BF = jnp.bfloat16
F32 = jnp.float32
LANES = 128


def mm(a, b, ca=1, cb=0):
    return lax.dot_general(a, b, (((ca,), (cb,)), ((), ())), preferred_element_type=F32)


def halves(x):
    high = x.astype(BF)
    return high, (x - high.astype(F32)).astype(BF)


def mm_exact(a, b, ca=1, cb=0):
    first, rest = b.astype(BF), None
    rest = b - first.astype(F32)
    second = rest.astype(BF)
    third = (rest - second.astype(F32)).astype(BF)
    return mm(a, first, ca, cb) + mm(a, second, ca, cb) + mm(a, third, ca, cb)


def iotas(rows, columns):
    return (
        lax.broadcasted_iota(jnp.int32, (rows, columns), 0),
        lax.broadcasted_iota(jnp.int32, (rows, columns), 1),
    )


def spread(weights, base, width, head_width):
    heads = weights[0].shape[1]
    row, channel = iotas(2 * heads, width)
    start = (jnp.where(row >= heads, row - heads, row) - base) * head_width
    pick = ((channel >= start) & (channel < start + head_width)).astype(BF)
    stacked = jnp.concatenate(weights, axis=0) if len(weights) > 1 else weights[0]
    out = mm(jnp.concatenate(halves(stacked), axis=1), pick)
    result, at = [], 0
    for w in weights:
        result.append(out[at : at + w.shape[0]])
        at += w.shape[0]
    return result


def spread_rows(rows, base, width, head_width):
    heads = rows[0].shape[1]
    wide = spread([jnp.broadcast_to(r, (8, heads)) for r in rows], base, width, head_width)
    return [w[0:1] for w in wide]


def gather_heads(parts, base, head_width):
    width = parts[0].shape[1]
    channel, head = iotas(width, LANES)
    start = (head - base) * head_width
    pick = ((channel >= start) & (channel < start + head_width)).astype(BF)
    out = mm(jnp.concatenate([x.astype(BF) for x in parts], axis=0), pick)
    result, at = [], 0
    for x in parts:
        result.append(out[at : at + x.shape[0]])
        at += x.shape[0]
    return result


def reversal(size):
    i, j = iotas(size, size)
    return (i + j == size - 1).astype(BF)


def flip_block(size):
    return 256 if size % 256 == 0 else 128


def sds(shape, dtype=F32):
    return jax.ShapeDtypeStruct(shape, dtype)


class Block:
    def __init__(self, array, shape, index):
        self.array, self.shape, self.index = array, shape, index

    def view(self, ref):
        if self.shape == self.array.shape:
            return ref
        return ref.at[tuple(pl.ds(i * b, b) for i, b in zip(self.index, self.shape))]


class Copied:
    def __init__(self, item):
        self.item = item if isinstance(item, Block) else Block(item, item.shape, (0,) * item.ndim)


class Far:
    def __init__(self, array):
        self.array = array


def run(body, ins, outs, scratch=(), limit=16, stored=()):
    specs, arrays, copied = [], [], []
    for item in ins:
        if isinstance(item, Far):
            specs.append(pl.BlockSpec(memory_space=pl.ANY))
            arrays.append(item.array)
        elif isinstance(item, Copied):
            specs.append(pl.BlockSpec(memory_space=pltpu.HBM))
            arrays.append(item.item.array)
            copied.append(item.item)
        elif isinstance(item, Block):
            specs.append(pl.BlockSpec(memory_space=pltpu.VMEM))
            arrays.append(item.array)
        else:
            space = pltpu.SMEM if item.dtype == jnp.int32 else pltpu.VMEM
            specs.append(pl.BlockSpec(memory_space=space))
            arrays.append(item)
    out_specs = [
        pl.BlockSpec(memory_space=pltpu.HBM if n in stored else pltpu.VMEM)
        for n in range(len(outs))
    ]
    holds = [pltpu.VMEM(q.shape, q.array.dtype) for q in copied]
    holds += [pltpu.VMEM(outs[n].shape, outs[n].dtype) for n in stored]
    sems = [pltpu.SemaphoreType.DMA((max(len(holds), 1),))]

    def kernel(*refs):
        refs = list(refs)
        take = lambda n: [refs.pop(0) for _ in range(n)]
        sources, targets = take(len(ins)), take(len(outs))
        held, (sem,) = take(len(holds)), take(1)
        args, copies = [], []
        for ref, item in zip(sources, ins):
            if isinstance(item, Copied):
                n = len(copies)
                copies.append(pltpu.make_async_copy(item.item.view(ref), held[n], sem.at[n]))
                copies[-1].start()
                ref = held[n]
            elif isinstance(item, Block):
                ref = item.view(ref)
            args.append(ref)
        back = []
        for n, ref in enumerate(targets):
            if n in stored:
                k = len(copied) + stored.index(n)
                back.append(pltpu.make_async_copy(held[k], ref, sem.at[k]))
                ref = held[k]
            args.append(ref)
        waits = {"waits": [c.wait for c in copies]} if copies else {}
        body(*args, *refs, **waits)
        for copy in back:
            copy.start()
        for copy in back:
            copy.wait()

    return pl.pallas_call(
        kernel,
        in_specs=specs,
        out_specs=out_specs,
        out_shape=outs,
        scratch_shapes=holds + sems + list(scratch),
        compiler_params=pltpu.CompilerParams(vmem_limit_bytes=limit * 1024 * 1024),
        cost_estimate=pl.CostEstimate(flops=0, bytes_accessed=1024, transcendentals=0),
    )(*arrays)


def start_body(
    hidden, other, select, step, bias, rate, weight, cot,
    source, pack0, pack1, row, v_out, wide, waits,
):
    for wait in waits[0:2]:
        wait()
    length, width = hidden.shape
    heads = bias.shape[1]
    source[0:length, :] = hidden[...]
    block = flip_block(width)
    turn = reversal(block)
    for j in range(width // block):
        source[length : 2 * length, j * block : (j + 1) * block] = mm(
            other[:, width - (j + 1) * block : width - j * block], turn
        ).astype(BF)
    for wait in waits[2:6]:
        wait()
    keys = mm(source[...], select[...]).astype(BF).astype(F32)
    state = keys.shape[1] // 2
    raw = mm(source[...], step[...], 1, 1) + bias[...]
    dt = jnp.maximum(raw, 0.0) + jnp.log1p(jnp.exp(-jnp.abs(raw)))
    rise = jax.nn.sigmoid(raw)
    i, j = iotas(length, length)
    lower = (i >= j).astype(BF)
    for s, pack in enumerate((pack0, pack1)):
        rows = slice(s * length, (s + 1) * length)
        drop = dt[rows] * rate[...]
        total = mm_exact(lower, drop)
        pack[...] = jnp.zeros(pack.shape, F32)
        pack[:, 0 : 2 * state] = keys[rows]
        at = 2 * state
        for part in (dt[rows], total, total - drop, rise[rows]):
            pack[:, at : at + heads] = part
            at += heads
    row[...] = jnp.zeros(row.shape, F32)
    row[0:1, 0:heads] = jnp.exp(
        -pack1[length - 1 : length, 2 * state + heads : 2 * state + 2 * heads]
    )
    for wait in waits[6:]:
        wait()
    for at in columns_of(weight.shape[1]):
        piece = mm(source[...], weight[:, at]).astype(BF)
        for s in range(2):
            v_out[0, s, :, at] = piece[s * length : (s + 1) * length]
        wide[0:length, at] = piece[0:length].astype(F32)
    wide[length : 2 * length, :] = cot[...].astype(F32)
    for n in range(3):
        at = 2 * length + n * piece_rows(length, wide.shape[1])
        put_piece(wide, at, pack0[:, n * LANES : (n + 1) * LANES])


def columns_of(width):
    block = min(256, width)
    return [slice(k * block, (k + 1) * block) for k in range(width // block)]


def gate_body(wide, token0, token1, out):
    pass


def values_body(source, token, *rest):
    weights, v_out = rest[:-1], rest[-1]
    length = v_out.shape[2]
    for n, weight in enumerate(weights):
        for at in columns_of(weight.shape[1]):
            piece = mm(source[...], weight[:, at]).astype(BF)
            for s in range(2):
                v_out[n, s, :, at] = piece[s * length : (s + 1) * length]


class Pack:
    def __init__(self, write, read, stats, heads):
        self.write, self.read = write, read
        self.dt = stats[:, 0:heads]
        self.total = stats[:, heads : 2 * heads]
        self.before = stats[:, 2 * heads : 3 * heads]
        last = self.total.shape[0]
        self.whole = self.total[last - 1 : last, :]
        self.from_start = jnp.exp(-self.total)
        self.from_end = jnp.exp(self.before - self.whole)
        self.to_end = jnp.exp(self.total - self.whole)
        self.to_start = jnp.exp(-self.before)
        self.through = jnp.exp(-self.whole)


def own_pack(ref, heads):
    return Pack(*[ref[:, n * LANES : (n + 1) * LANES] for n in range(3)], heads)


def piece_rows(length, width):
    return length // (width // LANES)


def put_piece(ref, row, piece):
    count = piece_rows(piece.shape[0], ref.shape[1])
    for b in range(ref.shape[1] // LANES):
        ref[row : row + count, b * LANES : (b + 1) * LANES] = piece[b * count : (b + 1) * count]


def get_piece(ref, row, length):
    count = piece_rows(length, ref.shape[1])
    return jnp.concatenate(
        [
            ref[row : row + count, b * LANES : (b + 1) * LANES]
            for b in range(ref.shape[1] // LANES)
        ],
        axis=0,
    )


def pair_body(base, heads, head_width, piece_at):
    def body(place, v_own, g_own, x_far, far0, far1, far2, own_ref, token, up, down, near, keep):
        first = place[0] == 0
        length, width = g_own.shape
        own = own_pack(own_ref, heads)
        far = Pack(*[get_piece(f, at, length) for f, at in zip((far0, far1, far2), piece_at)], heads)
        own_row, far_row = own.through, far.through
        rows = spread_rows([own_row * far_row, far_row], base, width, head_width)
        keep[...] = jnp.zeros(keep.shape, F32)
        keep[0:1, :] = rows[0]
        keep[1:2, :] = rows[1]
        own_up, own_down = jnp.where(first, far_row, 1.0), jnp.where(first, 1.0, far_row)
        far_up, far_down = jnp.where(first, 1.0, own_row), jnp.where(first, own_row, 1.0)
        for kind in range(2):
            rows = slice(kind * LANES, (kind + 1) * LANES)
            if kind == 0:
                keys = (own.write, far.write)
                ups = (own.dt * own.to_end, far.dt * far.to_end)
                downs = (own.dt * own.to_start, far.dt * far.to_start)
            else:
                keys = (own.read, far.read)
                ups = (own.from_end, far.from_end)
                downs = (own.from_start, far.from_start)
            x_own = (v_own if kind == 0 else g_own)[...].reshape(length, width).astype(F32)
            x_other = x_far[kind * length : (kind + 1) * length, :]
            w = spread(
                [ups[0] * own_up, ups[1] * far_up, downs[0] * own_down, downs[1] * far_down,
                 jnp.where(first, downs[1], ups[1])],
                base, width, head_width,
            )
            key = jnp.concatenate(keys, axis=0).astype(BF)
            both = lambda a, b: jnp.concatenate([(a * x_own).astype(BF), (b * x_other).astype(BF)], axis=0)
            up[rows, :] = mm(key, both(w[0], w[1]), 0, 0)
            down[rows, :] = mm(key, both(w[2], w[3]), 0, 0)
            near[rows, :] = mm(keys[1].astype(BF), (w[4] * x_other).astype(BF), 0, 0)

    return body


def column_body(base, heads, head_width):
    def body(own_ref, source, weight, g_own, v_out, own_up, own_down):
        length, width = g_own.shape
        own = own_pack(own_ref, heads)
        w_values = spread([own.dt * own.to_end, own.dt * own.to_start], base, width, head_width)
        w_grads = spread([own.from_end, own.from_start], base, width, head_width)
        write, read = own.write.astype(BF), own.read.astype(BF)
        for at in columns_of(width):
            piece = mm(source[...], weight[:, at]).astype(BF)
            for s in range(2):
                v_out[0, s, :, at] = piece[s * length : (s + 1) * length]
            v, g = piece[length:].astype(F32), g_own[:, at].astype(F32)
            for out, n in ((own_up, 0), (own_down, 1)):
                out[0:LANES, at] = mm(write, (w_values[n][:, at] * v).astype(BF), 0, 0)
                out[LANES : 2 * LANES, at] = mm(read, (w_grads[n][:, at] * g).astype(BF), 0, 0)

    return body


def column_totals(place, own_ref, far_row_ref, base, heads, head_width, owns, totals, keep):
    first = place[0] == 0
    width = keep.shape[1]
    own = own_pack(own_ref, heads)
    far_row = far_row_ref[0:1, 0:heads]
    rows = spread_rows([own.through * far_row, far_row, own.through], base, width, head_width)
    keep[...] = jnp.zeros(keep.shape, F32)
    for n, row in enumerate(rows):
        keep[n : n + 1, :] = row
    totals[0][...] = jnp.where(first, rows[1], 1.0) * owns[0][...]
    totals[1][...] = jnp.where(first, 1.0, rows[1]) * owns[1][...]


def first_step_body(pairs, base, heads, head_width, tokens):
    def body(place, own_ref, far_row_ref, own_up, own_down, *rest):
        send_a, send_b, token, up, down, keep = rest[tokens:]
        column_totals(
            place, own_ref, far_row_ref, base, heads, head_width, (own_up, own_down), (up, down), keep
        )
        token[...] = jnp.zeros(token.shape, F32)
        sends = (send_a, send_b)
        for d, total in enumerate((up, down)):
            spot = place[1] if d == 0 else pairs - 1 - place[1]
            for n in range(pairs):
                z = n if d == 0 else pairs - 1 - n
                send = sends[(z + d) % 2]

                @pl.when(spot == n)
                def _():
                    send[...] = total[...] if n == 0 else jnp.zeros(send.shape, F32)

    return body


def exchange_body(ups, downs):
    def body(place, own_up, own_down, keep, token, *rest):
        up_in, down_in = rest[0:ups], rest[ups : ups + downs]
        up_out, down_out, bufs, sems = rest[ups + downs :]
        up_spot, down_spot = place[1], len(up_in) - 1 - place[1]
        fetch_start(up_in, up_spot, bufs.at[0], sems.at[0])
        fetch_start(down_in, down_spot, bufs.at[1], sems.at[1])
        fetch_wait(up_in, up_spot, bufs.at[0], sems.at[0])
        fetch_wait(down_in, down_spot, bufs.at[1], sems.at[1])
        first = place[0] == 0
        row = keep[2:3, :]
        up_out[...] = jnp.where(first, row * bufs[0] + own_up[...], bufs[0])
        down_out[...] = jnp.where(first, bufs[1], row * bufs[1] + own_down[...])

    return body


def fetch_start(options, index, target, sem):
    for z, option in enumerate(options):
        if option is not None:

            @pl.when(index == z)
            def _():
                pltpu.make_async_copy(option, target, sem).start()


def fetch_wait(options, index, target, sem):
    for z, option in enumerate(options):
        if option is not None:

            @pl.when(index == z)
            def _():
                pltpu.make_async_copy(option, target, sem).wait()


def step_body(has, first_step, widen, pieces, tokens):
    pairs = len(has)

    def body(place, *rest):
        rest = list(rest)
        take = lambda n: [rest.pop(0) for _ in range(n)]
        sides = []
        for d in range(2):
            totals = [take(1)[0] if h else None for h in has]
            keeps = [take(1)[0] if h else None for h in has]
            sides.append((totals, keeps))
        got = None if first_step else take(2)
        chunk = take(2) if widen else None
        piece_refs = take(pieces)
        take(tokens)
        sends = take(2)
        token = take(1)[0]
        spots = (place[1], pairs - 1 - place[1])
        for d, (totals, keeps) in enumerate(sides):
            for n in range(pairs):
                z = n if d == 0 else pairs - 1 - n
                send = sends[(z + d) % 2]

                @pl.when(spots[d] == n)
                def _():
                    if not has[n]:
                        send[...] = jnp.zeros(send.shape, F32)
                    elif got is None or n == 0:
                        send[...] = totals[n][...]
                    else:
                        send[...] = totals[n][...] + keeps[n][0:1, :] * got[(z + 1 + d) % 2][...]

        token[...] = jnp.zeros(token.shape, F32)
        if widen:
            put_chunk(take(1)[0], *chunk, piece_refs)

    return body


def within_body(base, heads, head_width):
    def body(own_ref, v_ref, g_ref, rate, y_out, x_out, keys_out, steps_out, cols_s):
        own = own_pack(own_ref, heads)
        length, width = g_ref.shape
        write, read = own.write.astype(BF), own.read.astype(BF)
        scores = mm(read, write, 1, 1)
        i, j = iotas(length, length)
        low = i > j
        high = i < j
        doubled = jnp.where(i == j, 2.0, 1.0).astype(F32)
        scores2 = scores * doubled
        turned = own_ref[:, 2 * LANES : 3 * LANES].T
        lane = lax.broadcasted_iota(jnp.int32, (length, LANES), 1)
        d_scores = jnp.zeros((length, length), F32)
        out_low = jnp.zeros((length, LANES), F32)
        out_high = jnp.zeros((length, LANES), F32)
        cols_s[...] = jnp.zeros(cols_s.shape, F32)
        v_all = v_ref[...].reshape(length, width)
        per = LANES // head_width
        for n in range(width // LANES):
            at = slice(n * LANES, (n + 1) * LANES)
            v, g = v_all[:, at], g_ref[:, at]
            mine = [(lane >= m * head_width) & (lane < (m + 1) * head_width) for m in range(per)]
            v_heads = jnp.concatenate([jnp.where(x, v, jnp.zeros_like(v)) for x in mine], axis=0)
            g_heads = jnp.concatenate([jnp.where(x, g, jnp.zeros_like(g)) for x in mine], axis=0)
            products = mm(g_heads, v, 1, 1)
            plains, steppeds = [], []
            for m in range(per):
                h = base + n * per + m
                c_col = own.total[:, h : h + 1]
                e_col = own.before[:, h : h + 1]
                dt_row = turned[h : h + 1, :]
                c_row = turned[heads + h : heads + h + 1, :]
                e_row = turned[2 * heads + h : 2 * heads + h + 1, :]
                decay = jnp.exp(jnp.where(low, c_row - c_col, e_col - e_row))
                plain = decay * scores2
                plains.append(plain.astype(BF))
                steppeds.append((plain * dt_row).astype(BF))
                inner = decay * dt_row * products[m * length : (m + 1) * length]
                d_scores = d_scores + inner
                flow = inner * scores
                flow_low = jnp.where(low, flow, 0.0)
                flow_high = jnp.where(high, flow, 0.0)
                out_low = jnp.where(lane == h, jnp.sum(flow_low, 1, keepdims=True), out_low)
                out_high = jnp.where(lane == h, jnp.sum(flow_high, 1, keepdims=True), out_high)
                cols_s[0, h : h + 1, :] = jnp.sum(flow_low, 0, keepdims=True)
                cols_s[1, h : h + 1, :] = jnp.sum(flow_high, 0, keepdims=True)
            y_out[:, at] = mm(jnp.concatenate(steppeds, axis=1), v_heads)
            x_out[:, at] = mm(jnp.concatenate(plains, axis=0), g_heads, 0, 0)
        d_scores = (d_scores * doubled).astype(BF)
        keys_out[:, 0:LANES] = mm(d_scores, read, 0, 0)
        keys_out[:, LANES : 2 * LANES] = mm(d_scores, write)
        net_low = out_low - cols_s[0].T
        net_high = out_high - cols_s[1].T
        at_or_after = (j >= i).astype(BF)
        after = (j > i).astype(BF)
        steps_out[...] = -rate[...] * (mm_exact(at_or_after, net_low) - mm_exact(after, net_high))

    return body


def post_body(base, heads, head_width, ups, downs, columns=False):
    def body(
        place, own_ref, v_ref, g_ref, yw, xw, keys_w, steps_w, near, keep, skip, rate, token, *rest
    ):
        up_in, down_in = rest[0:ups], rest[ups : ups + downs]
        mixed, dv_out, keys_out, steps_out, bufs, sems = rest[ups + downs :]
        up_spot, down_spot = place[1], len(up_in) - 1 - place[1]
        fetch_start(up_in, up_spot, bufs.at[0], sems.at[0])
        fetch_start(down_in, down_spot, bufs.at[1], sems.at[1])
        first = place[0] == 0
        own = own_pack(own_ref, heads)
        length, width = g_ref.shape
        far_row = keep[1:2, :]
        own_row, gain = spread_rows([own.through, skip[...]], base, width, head_width)
        up_row = jnp.where(first, 1.0, far_row)
        down_row = jnp.where(first, far_row, 1.0)
        dt, from_start, from_end, to_end, to_start = spread(
            [own.dt, own.from_start, own.from_end, own.to_end, own.to_start],
            base, width, head_width,
        )
        write, read = own.write.astype(BF), own.read.astype(BF)
        v = v_ref[...].reshape(length, width).astype(F32)
        g = g_ref[...].astype(F32)
        fetch_wait(up_in, up_spot, bufs.at[0], sems.at[0])
        fetch_wait(down_in, down_spot, bufs.at[1], sems.at[1])
        if columns:
            up = up_row * bufs[0] + near[0][...]
            down = down_row * bufs[1] + near[1][...]
        else:
            up = up_row * bufs[0] + jnp.where(first, 0.0, near[...])
            down = down_row * bufs[1] + jnp.where(first, near[...], 0.0)
        p, ab = up[0:LANES], up[LANES : 2 * LANES]
        q, af = down[0:LANES], down[LANES : 2 * LANES]
        crossing = jnp.sum(p * af + q * ab, axis=0, keepdims=True)
        p, q, af, ab = p.astype(BF), q.astype(BF), af.astype(BF), ab.astype(BF)
        y_p = from_start * mm(read, p)
        y_q = from_end * mm(read, q)
        x_f = to_end * mm(write, af)
        x_b = to_start * mm(write, ab)
        mixed[...] = (yw[...] + y_p + y_q + gain * v).astype(BF)
        x = xw[...] + x_f + x_b
        dv_out[...] = (dt * x + gain * g).astype(BF)
        dtv = dt * v
        keys_out[:, 0:LANES] = (
            keys_w[:, 0:LANES]
            + mm((to_end * dtv).astype(BF), af, 1, 1)
            + mm((to_start * dtv).astype(BF), ab, 1, 1)
        )
        keys_out[:, LANES : 2 * LANES] = (
            keys_w[:, LANES : 2 * LANES]
            + mm((from_start * g).astype(BF), p, 1, 1)
            + mm((from_end * g).astype(BF), q, 1, 1)
        )
        lane = lax.broadcasted_iota(jnp.int32, (length, LANES), 1)
        steps = jnp.where(lane < heads, own_ref[:, 2 * LANES : 3 * LANES], 0.0)
        direct, a_p, a_q, b_f, b_b, through = gather_heads(
            [v * x, g * y_p, g * y_q, v * x_f, v * x_b, jnp.broadcast_to(crossing * own_row, (8, width))],
            base, head_width,
        )
        i, j = iotas(length, length)
        masks = jnp.concatenate([j >= i, j <= i, j < i, j > i], axis=1).astype(F32).astype(BF)
        high, low = halves(jnp.concatenate([a_p, a_q, b_f * steps, b_b * steps], axis=0))
        flow = mm(masks, high) + mm(masks, low) + through[0:1]
        steps_out[...] = steps_w[...] + direct - rate[...] * flow

    return body


def chunk_body(within, post, columns):
    def body(place, own_ref, v_ref, g_ref, *rest):
        nears = 2 if columns else 1
        near = rest[0:2] if columns else rest[0]
        keep, skip, rate, token, *rest = rest[nears:]
        bufs, sems, yw, xw, keys_w, steps_w, cols_s = rest[-7:]
        within(own_ref, v_ref, g_ref, rate, yw, xw, keys_w, steps_w, cols_s)
        post(
            place, own_ref, v_ref, g_ref, yw, xw, keys_w, steps_w, near, keep, skip, rate, token,
            *rest[:-5],
        )

    return body


def partial_body(groups, more):
    def body(token, *rest):
        dvs, weights, rest = rest[0:groups], rest[groups : 2 * groups], rest[2 * groups :]
        out = rest[-1]
        for at in columns_of(out.shape[1]):
            total = rest[0][:, at] if more else 0.0
            for dv, weight in zip(dvs, weights):
                total = total + mm(dv[...], weight[at, :], 1, 1)
            out[:, at] = total

    return body


def term_body(groups, tails, heads, parts, swap):
    def body(place, own_ref, select, step, before, *rest, waits=()):
        dvs, weights = rest[0:tails], rest[tails : 2 * tails]
        rest = rest[2 * tails :]
        keys, steps = rest[0:groups], rest[groups : 2 * groups]
        outs = rest[2 * groups :]
        for wait in waits:
            wait()
        d_keys, d_steps = keys[0][...], steps[0][...]
        for a, b in zip(keys[1:], steps[1:]):
            d_keys = d_keys + a[...]
            d_steps = d_steps + b[...]
        d_raw = d_steps[:, 0:heads] * own_ref[:, 2 * LANES + 3 * heads : 2 * LANES + 4 * heads]
        keys_high, keys_low = halves(d_keys)
        raw_high, raw_low = halves(d_raw)
        width = select.shape[0]
        block = width // parts
        tiles = []
        for b in range(parts):
            rows = slice(b * block, (b + 1) * block)
            total = before[:, rows]
            total = total + mm(keys_high, select[rows, :], 1, 1) + mm(keys_low, select[rows, :], 1, 1)
            total = total + mm(raw_high, step[:, rows]) + mm(raw_low, step[:, rows])
            for k in range(tails):
                total = total + mm(dvs[k][...], weights[k][rows, :], 1, 1)
            tiles.append(total)
        if swap:
            tiles = tiles[::-1]
        if parts == 2:
            first = place[2] == 0
            outs[0][...] = jnp.where(first, tiles[0], tiles[1])
            outs[1][...] = jnp.where(first, tiles[1], tiles[0])
        else:
            for b in range(parts):
                outs[0][:, b * block : (b + 1) * block] = tiles[b]

    return body


def last_body(work, term, work_ins, shares):
    def body(place, *rest, waits):
        rest = list(rest)
        take = lambda n: [rest.pop(0) for _ in range(n)]
        for_work = take(work_ins)
        select, step, before, weight = take(4)
        others = take(len(rest) - 1 - shares - 5)
        half = len(others) // 2
        mixed, *outs = take(1 + shares)
        bufs, sems, dv, keys, steps = take(5)
        work(place, *for_work, mixed, dv, keys, steps, bufs, sems)
        term(
            place, for_work[0], select, step, before, dv, weight,
            *others[:half], keys, *others[half:], steps, *outs, waits=waits,
        )

    return body


def finish_body(flip):
    def body(a, b, out):
        total = (a[...] + b[...]).astype(BF)
        if not flip:
            out[...] = total
            return
        width = total.shape[1]
        block = flip_block(width)
        turn = reversal(block)
        for j in range(width // block):
            out[:, j * block : (j + 1) * block] = mm(
                total[:, width - (j + 1) * block : width - j * block], turn
            ).astype(BF)

    return body


def put_chunk(wide, v_ref, g_ref, pieces):
    length, width = g_ref.shape
    wide[0:length, :] = v_ref[...].reshape(length, width).astype(F32)
    wide[length : 2 * length, :] = g_ref[...].astype(F32)
    for n, piece in enumerate(pieces):
        put_piece(wide, 2 * length + n * piece_rows(length, width), piece[...])


def widen_body(v_ref, g_ref, token, *rest):
    put_chunk(rest[-1], v_ref, g_ref, rest[:-1])


def local(shards, parts):
    pairs = shards // 2

    def body(
        hidden, complement, inner_weight, select_weight, step_weight, step_bias, decay_rate,
        skip_gain, cotangent, complement_cotangent,
    ):
        length, width = hidden.shape
        inner = inner_weight.shape[1]
        heads = step_bias.shape[0]
        head_width = inner // heads
        groups = 4
        chunk = inner // groups
        group_heads = heads // groups
        seq = lax.axis_index("seq")
        place = jnp.stack([seq % 2, seq // 2, lax.axis_index("chan")]).astype(jnp.int32)
        bias = step_bias.reshape(1, heads)
        rate = decay_rate.reshape(1, heads)
        rate_row = jnp.pad(rate, ((0, 0), (0, LANES - heads)))
        gain = skip_gain.reshape(1, heads)
        step_rows = step_weight.T
        cots = (cotangent, complement_cotangent)
        swap_pairs = [(a, a ^ 1) for a in range(shards)]
        edges = []
        for start in range(2):
            meets = [(z, z + 1) for z in range(start, pairs - 1, 2)]
            paired = sum(meets, ())
            meets += [(b, a) for a, b in meets] + [(z, z) for z in range(pairs) if z not in paired]
            edges.append([(2 * a + y, 2 * b + y) for a, b in meets for y in range(2)])
        swap = lambda x: lax.ppermute(x, "seq", swap_pairs)
        pack_shape = (length, 3 * LANES)
        pair_shape = (2 * LANES, chunk)
        wide_shape = lambda pieces: sds((2 * length + pieces * piece_rows(length, chunk), chunk))
        token_shape = sds((8, LANES))
        work = lambda: [pltpu.VMEM((2,) + pair_shape, F32), pltpu.SemaphoreType.DMA((2,))]
        order = [(1, groups - 1)] + [(0, k) for k in range(groups)] + [(1, k) for k in range(groups - 1)]
        chunks = len(order)

        source, pack0, pack1, row, v_zero, wide = run(
            start_body,
            [*map(Copied, (hidden, complement, select_weight, step_rows, bias, rate)),
             Copied(Block(inner_weight, (width, chunk), (0, 0))),
             Copied(Block(cots[0], (length, chunk), (0, 0)))],
            [sds((2 * length, width), BF), sds(pack_shape), sds(pack_shape), token_shape,
             sds((1, 2, length, chunk), BF), wide_shape(3)],
            limit=54,
        )
        packs = (pack0, pack1)
        far_row = swap(row)

        def weight_of(k):
            return Block(inner_weight, (width, chunk), (0, k))

        def do_values(ks, token):
            return run(
                values_body,
                [source, Far(token), *map(weight_of, ks)],
                [sds((len(ks), 2, length, chunk), BF)],
            )[0]

        v_last, *own_states = run(
            column_body((groups - 1) * group_heads, heads, head_width),
            [pack1, source, weight_of(groups - 1),
             Block(cots[1], (length, chunk), (0, groups - 1))],
            [sds((1, 2, length, chunk), BF), sds(pair_shape), sds(pair_shape)],
        )
        v_more = None

        def value_block(c):
            s, k = order[c]
            array, n = {0: (v_zero, 0), groups - 1: (v_last, 0)}.get(k, (v_more, k - 1))
            return Block(array, (1, 1, length, chunk), (n, s, 0, 0))

        def cot_block(c):
            s, k = order[c]
            return Block(cots[s], (length, chunk), (0, k))

        def weight_block(c):
            return weight_of(order[c][1])

        far = {}
        totals, within, post = {}, {}, {}
        got = ([], [])
        grads = [None, None]
        riders = {2 + n: n for n in range(3)}
        columns = {}
        steps = chunks + pairs - 2

        def do_pair(c, token):
            s, k = order[c]
            rows = piece_rows(length, chunk)
            if s == 0:
                pieces, piece_at = [far[1]] * 3, [2 * length + n * rows for n in range(3)]
            else:
                pieces, piece_at = [far[r] for r in riders], [2 * length] * 3
            totals[c] = run(
                pair_body(k * group_heads, heads, head_width, piece_at),
                [place, value_block(c), cot_block(c), far[c], *pieces, packs[s], Far(token)],
                [sds(pair_shape), sds(pair_shape), sds(pair_shape), sds((8, chunk))],
            )
            return totals[c][3]

        within_shapes = [
            sds((length, chunk)), sds((length, chunk)), sds((length, 2 * LANES)), sds((length, LANES))
        ]
        post_shapes = [
            sds((length, chunk), BF), sds((length, chunk), BF), sds((length, 2 * LANES)), sds((length, LANES))
        ]
        flows = lambda: [pltpu.VMEM((2, LANES, length), F32)]

        def do_within(c):
            s, k = order[c]
            within[c] = run(
                within_body(k * group_heads, heads, head_width),
                [packs[s], value_block(c), cot_block(c), rate_row],
                within_shapes,
                scratch=flows(),
            )
            return within[c][3]

        def post_parts(c, token, fused):
            s, k = order[c]
            last = pairs - 1
            ups = [got[(z + 1) % 2][max(c + z - 1, c)] for z in range(pairs)]
            downs = [got[(last - z) % 2][max(c + z - 1, c)] for z in range(pairs)]
            body = post_body(k * group_heads, heads, head_width, len(ups), len(downs), c == 0)
            if fused:
                body = chunk_body(within_body(k * group_heads, heads, head_width), body, c == 0)
            near = columns["far"] if c == 0 else [totals[c][2]]
            ins = [packs[s], value_block(c), cot_block(c), *([] if fused else within[c]),
                   *near, totals[c][3], gain, rate_row, Far(token),
                   *map(Far, ups), *map(Far, downs)]
            return body, ins

        def do_chunk(c, token):
            body, ins = post_parts(c, token, True)
            post[c] = run(
                body, [place, *ins], post_shapes, stored=(0,),
                scratch=work() + [pltpu.VMEM(o.shape, o.dtype) for o in within_shapes] + flows(),
            )
            return post[c][3]

        def do_partial(cs, token, before=None):
            return run(
                partial_body(len(cs), before is not None),
                [Far(token), *[post[c][1] for c in cs], *[weight_block(c) for c in cs]]
                + ([] if before is None else [before]),
                [sds((length, width))],
            )[0]

        shares = [sds((length, width // parts))] * 2 if parts == 2 else [sds((length, width))]

        def send_share(term):
            if parts == 2:
                return term[0], lax.ppermute(term[1], "chan", [(0, 1), (1, 0)])
            share = lax.psum_scatter(term[0], "chan", scatter_dimension=1, tiled=True)
            return share, jnp.zeros_like(share)

        def do_term(s, before):
            mine = [c for c in range(chunks) if order[c][0] == s]
            return send_share(run(
                term_body(len(mine), 0, heads, parts, s == 1),
                [place, packs[s], Copied(select_weight), Copied(step_rows), before,
                 *[post[c][2] for c in mine], *[post[c][3] for c in mine]],
                shares,
            ))

        def do_last(c, before, token):
            s = order[c][0]
            mine = [n for n in range(chunks) if order[n][0] == s and n != c]
            body, ins = post_parts(c, token, False)
            out = run(
                last_body(
                    body, term_body(len(mine) + 1, 1, heads, parts, s == 1), len(ins), len(shares)
                ),
                [place, *ins, Copied(select_weight), Copied(step_rows), before, weight_block(c),
                 *[post[n][2] for n in mine], *[post[n][3] for n in mine]],
                [post_shapes[0], *shares],
                scratch=work() + [pltpu.VMEM(o.shape, o.dtype) for o in post_shapes[1:]],
                stored=(0,),
            )
            post[c] = (out[0],)
            return send_share(out[1:])

        def do_finish(s, share):
            return run(
                finish_body(s == 1), list(share), [sds((length, width // parts), BF)], stored=(0,)
            )[0]

        def do_step(k, widen, ends):
            has = [0 <= k - z < chunks and z < pairs - 1 for z in range(pairs)]
            ins = [place]
            for d in range(2):
                ins += [totals[k - z][d] for z in range(pairs) if has[z]]
                ins += [totals[k - z][3] for z in range(pairs) if has[z]]
            if k > 0:
                ins += [got[0][-1], got[1][-1]]
            outs = [sds(pair_shape), sds(pair_shape), token_shape]
            pieces = [] if widen is None else pieces_of(widen)
            if widen is not None:
                ins += [value_block(widen), cot_block(widen), *pieces]
                outs.append(wide_shape(len(pieces)))
            return run(
                step_body(has, k == 0, widen is not None, len(pieces), len(ends)),
                ins + [Far(e) for e in ends],
                outs,
            )

        def do_first_step(ends):
            s, k = order[0]
            out = run(
                first_step_body(pairs, k * group_heads, heads, head_width, len(ends)),
                [place, packs[s], far_row, *own_states, *map(Far, ends)],
                [sds(pair_shape), sds(pair_shape), token_shape, sds(pair_shape), sds(pair_shape),
                 sds((8, chunk))],
            )
            totals[0] = (out[3], out[4], None, out[5])
            columns["own"] = own_states
            return out

        def do_exchange(token):
            last = pairs - 1
            ups = [got[(z + 1) % 2][max(z - 1, 0)] for z in range(pairs)]
            downs = [got[(last - z) % 2][max(z - 1, 0)] for z in range(pairs)]
            sends = run(
                exchange_body(len(ups), len(downs)),
                [place, *columns["own"], totals[0][3], Far(token), *map(Far, ups), *map(Far, downs)],
                [sds(pair_shape), sds(pair_shape)],
                scratch=work(),
            )
            columns["far"] = [swap(x) for x in sends]

        def pieces_of(c):
            return [Block(packs[1], (length, LANES), (0, riders[c]))] if c in riders else []

        def do_widen(c, token):
            pieces = pieces_of(c)
            return run(
                widen_body, [value_block(c), cot_block(c), Far(token), *pieces], [wide_shape(len(pieces))]
            )[0]

        far[1] = swap(pl.pallas_call(
            gate_body,
            in_specs=[pl.BlockSpec(memory_space=pl.ANY)] * 3,
            out_specs=pl.BlockSpec(memory_space=pl.ANY),
            out_shape=wide_shape(3),
            input_output_aliases={0: 0},
            cost_estimate=pl.CostEstimate(flops=0, bytes_accessed=1024, transcendentals=0),
        )(wide, far_row, v_last))
        ends = []
        halfway = None
        share = None
        for k in range(steps):
            queue = k + 2 if 0 < k < chunks - 2 else None
            made = do_first_step(ends) if k == 0 else do_step(k, queue, ends)
            token = made[2]
            for d in range(2):
                got[d].append(lax.ppermute(made[d], "seq", edges[d]))
            ends = []
            if k == 0:
                v_more = do_values(list(range(1, groups - 1)), token)
                far[2] = swap(do_widen(2, token))
            if queue is not None:
                far[queue] = swap(made[3])
            if k + 1 < chunks:
                ends.append(do_pair(k + 1, token))
            if k == max(chunks - 2, pairs - 1):
                do_exchange(far[chunks - 1])
            if k == steps - 3:
                ends += columns["far"]
            c = k - pairs + 1
            if c > 0:
                ends.append(do_chunk(c, token))
            if c == groups - 2:
                halfway = do_partial(list(range(1, groups - 1)), token)
                ends.append(halfway)
            if c == groups:
                share = do_term(0, do_partial([groups - 1, groups], token, halfway))
                ends.append(share[0])
            if c == groups + 1:
                ends.append(do_chunk(0, token))
            if c == groups + 2:
                grads[0] = do_finish(0, share)
                halfway = do_partial([groups + 1, 0, groups + 2], token)
        do_within(chunks - 1)
        grads[1] = do_finish(1, do_last(chunks - 1, halfway, halfway))
        outs = [
            jnp.concatenate([post[order.index((s, k))][0] for k in range(groups)], axis=1)
            for s in range(2)
        ]
        return (outs[0], outs[1], grads[0], grads[1])

    return body


def solution(mesh):
    rows = P(("dp", "seq"), None)
    both = P(("dp", "seq"), "chan")
    in_specs = (
        rows, rows, P(None, "chan"), P(), P(None, "chan"),
        P("chan"), P("chan"), P("chan"), both, both,
    )
    return jax.shard_map(
        local(mesh.shape["seq"], mesh.shape["chan"]),
        mesh=mesh,
        in_specs=in_specs,
        out_specs=(both,) * 4,
        check_vma=False,
    )
```

```python
import jax
import jax.numpy as jnp
from jax import lax
from jax.experimental import pallas as pl
from jax.experimental.pallas import tpu as pltpu
from jax.sharding import PartitionSpec as P

BF = jnp.bfloat16
F32 = jnp.float32
LANES = 128


def mm(a, b, ca=1, cb=0):
    return lax.dot_general(a, b, (((ca,), (cb,)), ((), ())), preferred_element_type=F32)


def halves(x):
    high = x.astype(BF)
    return high, (x - high.astype(F32)).astype(BF)


def mm_exact(a, b, ca=1, cb=0):
    first, rest = b.astype(BF), None
    rest = b - first.astype(F32)
    second = rest.astype(BF)
    third = (rest - second.astype(F32)).astype(BF)
    return mm(a, first, ca, cb) + mm(a, second, ca, cb) + mm(a, third, ca, cb)


def iotas(rows, columns):
    return (
        lax.broadcasted_iota(jnp.int32, (rows, columns), 0),
        lax.broadcasted_iota(jnp.int32, (rows, columns), 1),
    )


def spread(weights, base, width, head_width):
    heads = weights[0].shape[1]
    row, channel = iotas(2 * heads, width)
    start = (jnp.where(row >= heads, row - heads, row) - base) * head_width
    pick = ((channel >= start) & (channel < start + head_width)).astype(BF)
    stacked = jnp.concatenate(weights, axis=0) if len(weights) > 1 else weights[0]
    out = mm(jnp.concatenate(halves(stacked), axis=1), pick)
    result, at = [], 0
    for w in weights:
        result.append(out[at : at + w.shape[0]])
        at += w.shape[0]
    return result


def spread_rows(rows, base, width, head_width):
    heads = rows[0].shape[1]
    wide = spread([jnp.broadcast_to(r, (8, heads)) for r in rows], base, width, head_width)
    return [w[0:1] for w in wide]


def gather_heads(parts, base, head_width):
    width = parts[0].shape[1]
    channel, head = iotas(width, LANES)
    start = (head - base) * head_width
    pick = ((channel >= start) & (channel < start + head_width)).astype(BF)
    out = mm(jnp.concatenate([x.astype(BF) for x in parts], axis=0), pick)
    result, at = [], 0
    for x in parts:
        result.append(out[at : at + x.shape[0]])
        at += x.shape[0]
    return result


def reversal(size):
    i, j = iotas(size, size)
    return (i + j == size - 1).astype(BF)


def flip_block(size):
    return 256 if size % 256 == 0 else 128


def sds(shape, dtype=F32):
    return jax.ShapeDtypeStruct(shape, dtype)


class Block:
    def __init__(self, array, shape, index):
        self.array, self.shape, self.index = array, shape, index

    def view(self, ref):
        if self.shape == self.array.shape:
            return ref
        return ref.at[tuple(pl.ds(i * b, b) for i, b in zip(self.index, self.shape))]


class Copied:
    def __init__(self, item):
        self.item = item if isinstance(item, Block) else Block(item, item.shape, (0,) * item.ndim)


class Far:
    def __init__(self, array):
        self.array = array


def run(body, ins, outs, scratch=(), limit=16, stored=()):
    specs, arrays, copied = [], [], []
    for item in ins:
        if isinstance(item, Far):
            specs.append(pl.BlockSpec(memory_space=pl.ANY))
            arrays.append(item.array)
        elif isinstance(item, Copied):
            specs.append(pl.BlockSpec(memory_space=pltpu.HBM))
            arrays.append(item.item.array)
            copied.append(item.item)
        elif isinstance(item, Block):
            specs.append(pl.BlockSpec(memory_space=pltpu.VMEM))
            arrays.append(item.array)
        else:
            space = pltpu.SMEM if item.dtype == jnp.int32 else pltpu.VMEM
            specs.append(pl.BlockSpec(memory_space=space))
            arrays.append(item)
    out_specs = [
        pl.BlockSpec(memory_space=pltpu.HBM if n in stored else pltpu.VMEM)
        for n in range(len(outs))
    ]
    holds = [pltpu.VMEM(q.shape, q.array.dtype) for q in copied]
    holds += [pltpu.VMEM(outs[n].shape, outs[n].dtype) for n in stored]
    sems = [pltpu.SemaphoreType.DMA((max(len(holds), 1),))]

    def kernel(*refs):
        refs = list(refs)
        take = lambda n: [refs.pop(0) for _ in range(n)]
        sources, targets = take(len(ins)), take(len(outs))
        held, (sem,) = take(len(holds)), take(1)
        args, copies = [], []
        for ref, item in zip(sources, ins):
            if isinstance(item, Copied):
                n = len(copies)
                copies.append(pltpu.make_async_copy(item.item.view(ref), held[n], sem.at[n]))
                copies[-1].start()
                ref = held[n]
            elif isinstance(item, Block):
                ref = item.view(ref)
            args.append(ref)
        back = []
        for n, ref in enumerate(targets):
            if n in stored:
                k = len(copied) + stored.index(n)
                back.append(pltpu.make_async_copy(held[k], ref, sem.at[k]))
                ref = held[k]
            args.append(ref)
        waits = {"waits": [c.wait for c in copies]} if copies else {}
        body(*args, *refs, **waits)
        for copy in back:
            copy.start()
        for copy in back:
            copy.wait()

    return pl.pallas_call(
        kernel,
        in_specs=specs,
        out_specs=out_specs,
        out_shape=outs,
        scratch_shapes=holds + sems + list(scratch),
        compiler_params=pltpu.CompilerParams(vmem_limit_bytes=limit * 1024 * 1024),
        cost_estimate=pl.CostEstimate(flops=0, bytes_accessed=1024, transcendentals=0),
    )(*arrays)


def start_body(
    hidden, other, select, step, bias, rate, weight, cot,
    source, pack0, pack1, row, v_out, wide, waits,
):
    for wait in waits[0:2]:
        wait()
    length, width = hidden.shape
    heads = bias.shape[1]
    source[0:length, :] = hidden[...]
    block = flip_block(width)
    turn = reversal(block)
    for j in range(width // block):
        source[length : 2 * length, j * block : (j + 1) * block] = mm(
            other[:, width - (j + 1) * block : width - j * block], turn
        ).astype(BF)
    for wait in waits[2:6]:
        wait()
    keys = mm(source[...], select[...]).astype(BF).astype(F32)
    state = keys.shape[1] // 2
    raw = mm(source[...], step[...], 1, 1) + bias[...]
    dt = jnp.maximum(raw, 0.0) + jnp.log1p(jnp.exp(-jnp.abs(raw)))
    rise = jax.nn.sigmoid(raw)
    i, j = iotas(length, length)
    lower = (i >= j).astype(BF)
    for s, pack in enumerate((pack0, pack1)):
        rows = slice(s * length, (s + 1) * length)
        drop = dt[rows] * rate[...]
        total = mm_exact(lower, drop)
        pack[...] = jnp.zeros(pack.shape, F32)
        pack[:, 0 : 2 * state] = keys[rows]
        at = 2 * state
        for part in (dt[rows], total, total - drop, rise[rows]):
            pack[:, at : at + heads] = part
            at += heads
    row[...] = jnp.zeros(row.shape, F32)
    row[0:1, 0:heads] = jnp.exp(
        -pack1[length - 1 : length, 2 * state + heads : 2 * state + 2 * heads]
    )
    for wait in waits[6:]:
        wait()
    for at in columns_of(weight.shape[1]):
        piece = mm(source[...], weight[:, at]).astype(BF)
        for s in range(2):
            v_out[0, s, :, at] = piece[s * length : (s + 1) * length]
        wide[0:length, at] = piece[0:length].astype(F32)
    wide[length : 2 * length, :] = cot[...].astype(F32)
    for n in range(3):
        at = 2 * length + n * piece_rows(length, wide.shape[1])
        put_piece(wide, at, pack0[:, n * LANES : (n + 1) * LANES])


def columns_of(width):
    block = min(256, width)
    return [slice(k * block, (k + 1) * block) for k in range(width // block)]


def values_body(source, token, *rest):
    weights, v_out = rest[:-1], rest[-1]
    length = v_out.shape[2]
    for n, weight in enumerate(weights):
        for at in columns_of(weight.shape[1]):
            piece = mm(source[...], weight[:, at]).astype(BF)
            for s in range(2):
                v_out[n, s, :, at] = piece[s * length : (s + 1) * length]


class Pack:
    def __init__(self, write, read, stats, heads):
        self.write, self.read = write, read
        self.dt = stats[:, 0:heads]
        self.total = stats[:, heads : 2 * heads]
        self.before = stats[:, 2 * heads : 3 * heads]
        last = self.total.shape[0]
        self.whole = self.total[last - 1 : last, :]
        self.from_start = jnp.exp(-self.total)
        self.from_end = jnp.exp(self.before - self.whole)
        self.to_end = jnp.exp(self.total - self.whole)
        self.to_start = jnp.exp(-self.before)
        self.through = jnp.exp(-self.whole)


def own_pack(ref, heads):
    return Pack(*[ref[:, n * LANES : (n + 1) * LANES] for n in range(3)], heads)


def piece_rows(length, width):
    return length // (width // LANES)


def put_piece(ref, row, piece):
    count = piece_rows(piece.shape[0], ref.shape[1])
    for b in range(ref.shape[1] // LANES):
        ref[row : row + count, b * LANES : (b + 1) * LANES] = piece[b * count : (b + 1) * count]


def get_piece(ref, row, length):
    count = piece_rows(length, ref.shape[1])
    return jnp.concatenate(
        [
            ref[row : row + count, b * LANES : (b + 1) * LANES]
            for b in range(ref.shape[1] // LANES)
        ],
        axis=0,
    )


def pair_body(base, heads, head_width, piece_at):
    def body(place, v_own, g_own, x_far, far0, far1, far2, own_ref, token, up, down, near, keep):
        first = place[0] == 0
        length, width = g_own.shape
        own = own_pack(own_ref, heads)
        far = Pack(*[get_piece(f, at, length) for f, at in zip((far0, far1, far2), piece_at)], heads)
        own_row, far_row = own.through, far.through
        rows = spread_rows([own_row * far_row, far_row], base, width, head_width)
        keep[...] = jnp.zeros(keep.shape, F32)
        keep[0:1, :] = rows[0]
        keep[1:2, :] = rows[1]
        own_up, own_down = jnp.where(first, far_row, 1.0), jnp.where(first, 1.0, far_row)
        far_up, far_down = jnp.where(first, 1.0, own_row), jnp.where(first, own_row, 1.0)
        for kind in range(2):
            rows = slice(kind * LANES, (kind + 1) * LANES)
            if kind == 0:
                keys = (own.write, far.write)
                ups = (own.dt * own.to_end, far.dt * far.to_end)
                downs = (own.dt * own.to_start, far.dt * far.to_start)
            else:
                keys = (own.read, far.read)
                ups = (own.from_end, far.from_end)
                downs = (own.from_start, far.from_start)
            x_own = (v_own if kind == 0 else g_own)[...].reshape(length, width).astype(F32)
            x_other = x_far[kind * length : (kind + 1) * length, :]
            w = spread(
                [ups[0] * own_up, ups[1] * far_up, downs[0] * own_down, downs[1] * far_down,
                 jnp.where(first, downs[1], ups[1])],
                base, width, head_width,
            )
            key = jnp.concatenate(keys, axis=0).astype(BF)
            both = lambda a, b: jnp.concatenate([(a * x_own).astype(BF), (b * x_other).astype(BF)], axis=0)
            up[rows, :] = mm(key, both(w[0], w[1]), 0, 0)
            down[rows, :] = mm(key, both(w[2], w[3]), 0, 0)
            near[rows, :] = mm(keys[1].astype(BF), (w[4] * x_other).astype(BF), 0, 0)

    return body


def column_body(base, heads, head_width):
    def body(own_ref, source, weight, g_own, v_out, own_up, own_down):
        length, width = g_own.shape
        own = own_pack(own_ref, heads)
        w_values = spread([own.dt * own.to_end, own.dt * own.to_start], base, width, head_width)
        w_grads = spread([own.from_end, own.from_start], base, width, head_width)
        write, read = own.write.astype(BF), own.read.astype(BF)
        for at in columns_of(width):
            piece = mm(source[...], weight[:, at]).astype(BF)
            for s in range(2):
                v_out[0, s, :, at] = piece[s * length : (s + 1) * length]
            v, g = piece[length:].astype(F32), g_own[:, at].astype(F32)
            for out, n in ((own_up, 0), (own_down, 1)):
                out[0:LANES, at] = mm(write, (w_values[n][:, at] * v).astype(BF), 0, 0)
                out[LANES : 2 * LANES, at] = mm(read, (w_grads[n][:, at] * g).astype(BF), 0, 0)

    return body


def column_totals(place, own_ref, far_row_ref, base, heads, head_width, owns, totals, keep):
    first = place[0] == 0
    width = keep.shape[1]
    own = own_pack(own_ref, heads)
    far_row = far_row_ref[0:1, 0:heads]
    rows = spread_rows([own.through * far_row, far_row, own.through], base, width, head_width)
    keep[...] = jnp.zeros(keep.shape, F32)
    for n, row in enumerate(rows):
        keep[n : n + 1, :] = row
    totals[0][...] = jnp.where(first, rows[1], 1.0) * owns[0][...]
    totals[1][...] = jnp.where(first, 1.0, rows[1]) * owns[1][...]


def first_step_body(pairs, base, heads, head_width, tokens):
    def body(place, own_ref, far_row_ref, own_up, own_down, *rest):
        send_a, send_b, token, up, down, keep = rest[tokens:]
        column_totals(
            place, own_ref, far_row_ref, base, heads, head_width, (own_up, own_down), (up, down), keep
        )
        token[...] = jnp.zeros(token.shape, F32)
        sends = (send_a, send_b)
        for d, total in enumerate((up, down)):
            spot = place[1] if d == 0 else pairs - 1 - place[1]
            for n in range(pairs):
                z = n if d == 0 else pairs - 1 - n
                send = sends[(z + d) % 2]

                @pl.when(spot == n)
                def _():
                    send[...] = total[...] if n == 0 else jnp.zeros(send.shape, F32)

    return body


def exchange_body(ups, downs):
    def body(place, own_up, own_down, keep, token, *rest):
        up_in, down_in = rest[0:ups], rest[ups : ups + downs]
        up_out, down_out, bufs, sems = rest[ups + downs :]
        up_spot, down_spot = place[1], len(up_in) - 1 - place[1]
        fetch_start(up_in, up_spot, bufs.at[0], sems.at[0])
        fetch_start(down_in, down_spot, bufs.at[1], sems.at[1])
        fetch_wait(up_in, up_spot, bufs.at[0], sems.at[0])
        fetch_wait(down_in, down_spot, bufs.at[1], sems.at[1])
        first = place[0] == 0
        row = keep[2:3, :]
        up_out[...] = jnp.where(first, row * bufs[0] + own_up[...], bufs[0])
        down_out[...] = jnp.where(first, bufs[1], row * bufs[1] + own_down[...])

    return body


def fetch_start(options, index, target, sem):
    for z, option in enumerate(options):
        if option is not None:

            @pl.when(index == z)
            def _():
                pltpu.make_async_copy(option, target, sem).start()


def fetch_wait(options, index, target, sem):
    for z, option in enumerate(options):
        if option is not None:

            @pl.when(index == z)
            def _():
                pltpu.make_async_copy(option, target, sem).wait()


def step_body(has, first_step, widen, pieces, tokens):
    pairs = len(has)

    def body(place, *rest):
        rest = list(rest)
        take = lambda n: [rest.pop(0) for _ in range(n)]
        sides = []
        for d in range(2):
            totals = [take(1)[0] if h else None for h in has]
            keeps = [take(1)[0] if h else None for h in has]
            sides.append((totals, keeps))
        got = None if first_step else take(2)
        chunk = take(2) if widen else None
        piece_refs = take(pieces)
        take(tokens)
        sends = take(2)
        token = take(1)[0]
        spots = (place[1], pairs - 1 - place[1])
        for d, (totals, keeps) in enumerate(sides):
            for n in range(pairs):
                z = n if d == 0 else pairs - 1 - n
                send = sends[(z + d) % 2]

                @pl.when(spots[d] == n)
                def _():
                    if not has[n]:
                        send[...] = jnp.zeros(send.shape, F32)
                    elif got is None or n == 0:
                        send[...] = totals[n][...]
                    else:
                        send[...] = totals[n][...] + keeps[n][0:1, :] * got[(z + 1 + d) % 2][...]

        token[...] = jnp.zeros(token.shape, F32)
        if widen:
            put_chunk(take(1)[0], *chunk, piece_refs)

    return body


def within_body(base, heads, head_width):
    def body(own_ref, v_ref, g_ref, rate, token, y_out, x_out, keys_out, steps_out, cols_s):
        own = own_pack(own_ref, heads)
        length, width = g_ref.shape
        write, read = own.write.astype(BF), own.read.astype(BF)
        scores = mm(read, write, 1, 1)
        i, j = iotas(length, length)
        low = i > j
        high = i < j
        doubled = jnp.where(i == j, 2.0, 1.0).astype(F32)
        scores2 = scores * doubled
        turned = own_ref[:, 2 * LANES : 3 * LANES].T
        lane = lax.broadcasted_iota(jnp.int32, (length, LANES), 1)
        d_scores = jnp.zeros((length, length), F32)
        out_low = jnp.zeros((length, LANES), F32)
        out_high = jnp.zeros((length, LANES), F32)
        cols_s[...] = jnp.zeros(cols_s.shape, F32)
        v_all = v_ref[...].reshape(length, width)
        per = LANES // head_width
        for n in range(width // LANES):
            at = slice(n * LANES, (n + 1) * LANES)
            v, g = v_all[:, at], g_ref[:, at]
            mine = [(lane >= m * head_width) & (lane < (m + 1) * head_width) for m in range(per)]
            v_heads = jnp.concatenate([jnp.where(x, v, jnp.zeros_like(v)) for x in mine], axis=0)
            g_heads = jnp.concatenate([jnp.where(x, g, jnp.zeros_like(g)) for x in mine], axis=0)
            products = mm(g_heads, v, 1, 1)
            plains, steppeds = [], []
            for m in range(per):
                h = base + n * per + m
                c_col = own.total[:, h : h + 1]
                e_col = own.before[:, h : h + 1]
                dt_row = turned[h : h + 1, :]
                c_row = turned[heads + h : heads + h + 1, :]
                e_row = turned[2 * heads + h : 2 * heads + h + 1, :]
                decay = jnp.exp(jnp.where(low, c_row - c_col, e_col - e_row))
                plain = decay * scores2
                plains.append(plain.astype(BF))
                steppeds.append((plain * dt_row).astype(BF))
                inner = decay * dt_row * products[m * length : (m + 1) * length]
                d_scores = d_scores + inner
                flow = inner * scores
                flow_low = jnp.where(low, flow, 0.0)
                flow_high = jnp.where(high, flow, 0.0)
                out_low = jnp.where(lane == h, jnp.sum(flow_low, 1, keepdims=True), out_low)
                out_high = jnp.where(lane == h, jnp.sum(flow_high, 1, keepdims=True), out_high)
                cols_s[0, h : h + 1, :] = jnp.sum(flow_low, 0, keepdims=True)
                cols_s[1, h : h + 1, :] = jnp.sum(flow_high, 0, keepdims=True)
            y_out[:, at] = mm(jnp.concatenate(steppeds, axis=1), v_heads)
            x_out[:, at] = mm(jnp.concatenate(plains, axis=0), g_heads, 0, 0)
        d_scores = (d_scores * doubled).astype(BF)
        keys_out[:, 0:LANES] = mm(d_scores, read, 0, 0)
        keys_out[:, LANES : 2 * LANES] = mm(d_scores, write)
        net_low = out_low - cols_s[0].T
        net_high = out_high - cols_s[1].T
        at_or_after = (j >= i).astype(BF)
        after = (j > i).astype(BF)
        steps_out[...] = -rate[...] * (mm_exact(at_or_after, net_low) - mm_exact(after, net_high))

    return body


def post_body(base, heads, head_width, ups, downs, columns=False):
    def body(
        place, own_ref, v_ref, g_ref, yw, xw, keys_w, steps_w, near, keep, skip, rate, token, *rest
    ):
        up_in, down_in = rest[0:ups], rest[ups : ups + downs]
        mixed, dv_out, keys_out, steps_out, bufs, sems = rest[ups + downs :]
        up_spot, down_spot = place[1], len(up_in) - 1 - place[1]
        fetch_start(up_in, up_spot, bufs.at[0], sems.at[0])
        fetch_start(down_in, down_spot, bufs.at[1], sems.at[1])
        first = place[0] == 0
        own = own_pack(own_ref, heads)
        length, width = g_ref.shape
        far_row = keep[1:2, :]
        own_row, gain = spread_rows([own.through, skip[...]], base, width, head_width)
        up_row = jnp.where(first, 1.0, far_row)
        down_row = jnp.where(first, far_row, 1.0)
        dt, from_start, from_end, to_end, to_start = spread(
            [own.dt, own.from_start, own.from_end, own.to_end, own.to_start],
            base, width, head_width,
        )
        write, read = own.write.astype(BF), own.read.astype(BF)
        v = v_ref[...].reshape(length, width).astype(F32)
        g = g_ref[...].astype(F32)
        fetch_wait(up_in, up_spot, bufs.at[0], sems.at[0])
        fetch_wait(down_in, down_spot, bufs.at[1], sems.at[1])
        if columns:
            up = up_row * bufs[0] + near[0][...]
            down = down_row * bufs[1] + near[1][...]
        else:
            up = up_row * bufs[0] + jnp.where(first, 0.0, near[...])
            down = down_row * bufs[1] + jnp.where(first, near[...], 0.0)
        p, ab = up[0:LANES], up[LANES : 2 * LANES]
        q, af = down[0:LANES], down[LANES : 2 * LANES]
        crossing = jnp.sum(p * af + q * ab, axis=0, keepdims=True)
        p, q, af, ab = p.astype(BF), q.astype(BF), af.astype(BF), ab.astype(BF)
        y_p = from_start * mm(read, p)
        y_q = from_end * mm(read, q)
        x_f = to_end * mm(write, af)
        x_b = to_start * mm(write, ab)
        mixed[...] = (yw[...] + y_p + y_q + gain * v).astype(BF)
        x = xw[...] + x_f + x_b
        dv_out[...] = (dt * x + gain * g).astype(BF)
        dtv = dt * v
        keys_out[:, 0:LANES] = (
            keys_w[:, 0:LANES]
            + mm((to_end * dtv).astype(BF), af, 1, 1)
            + mm((to_start * dtv).astype(BF), ab, 1, 1)
        )
        keys_out[:, LANES : 2 * LANES] = (
            keys_w[:, LANES : 2 * LANES]
            + mm((from_start * g).astype(BF), p, 1, 1)
            + mm((from_end * g).astype(BF), q, 1, 1)
        )
        lane = lax.broadcasted_iota(jnp.int32, (length, LANES), 1)
        steps = jnp.where(lane < heads, own_ref[:, 2 * LANES : 3 * LANES], 0.0)
        direct, a_p, a_q, b_f, b_b, through = gather_heads(
            [v * x, g * y_p, g * y_q, v * x_f, v * x_b, jnp.broadcast_to(crossing * own_row, (8, width))],
            base, head_width,
        )
        i, j = iotas(length, length)
        masks = jnp.concatenate([j >= i, j <= i, j < i, j > i], axis=1).astype(F32).astype(BF)
        high, low = halves(jnp.concatenate([a_p, a_q, b_f * steps, b_b * steps], axis=0))
        flow = mm(masks, high) + mm(masks, low) + through[0:1]
        steps_out[...] = steps_w[...] + direct - rate[...] * flow

    return body


def paired_near(post):
    def body(place, own_ref, v_ref, g_ref, yw, xw, keys_w, steps_w, near_up, near_down, *rest):
        post(place, own_ref, v_ref, g_ref, yw, xw, keys_w, steps_w, (near_up, near_down), *rest)

    return body


def chunk_body(within, post, columns):
    def body(place, own_ref, v_ref, g_ref, *rest):
        nears = 2 if columns else 1
        near = rest[0:2] if columns else rest[0]
        keep, skip, rate, token, *rest = rest[nears:]
        bufs, sems, yw, xw, keys_w, steps_w, cols_s = rest[-7:]
        within(own_ref, v_ref, g_ref, rate, token, yw, xw, keys_w, steps_w, cols_s)
        post(
            place, own_ref, v_ref, g_ref, yw, xw, keys_w, steps_w, near, keep, skip, rate, token,
            *rest[:-5],
        )

    return body


def partial_body(groups, more):
    def body(token, *rest):
        dvs, weights, rest = rest[0:groups], rest[groups : 2 * groups], rest[2 * groups :]
        out = rest[-1]
        for at in columns_of(out.shape[1]):
            total = rest[0][:, at] if more else 0.0
            for dv, weight in zip(dvs, weights):
                total = total + mm(dv[...], weight[at, :], 1, 1)
            out[:, at] = total

    return body


def term_body(groups, tails, heads, parts, swap):
    def body(place, own_ref, select, step, before, *rest):
        dvs, weights = rest[0:tails], rest[tails : 2 * tails]
        rest = rest[2 * tails :]
        keys, steps = rest[0:groups], rest[groups : 2 * groups]
        outs = rest[2 * groups :]
        d_keys, d_steps = keys[0][...], steps[0][...]
        for a, b in zip(keys[1:], steps[1:]):
            d_keys = d_keys + a[...]
            d_steps = d_steps + b[...]
        d_raw = d_steps[:, 0:heads] * own_ref[:, 2 * LANES + 3 * heads : 2 * LANES + 4 * heads]
        keys_high, keys_low = halves(d_keys)
        raw_high, raw_low = halves(d_raw)
        width = select.shape[0]
        block = width // parts
        tiles = []
        for b in range(parts):
            rows = slice(b * block, (b + 1) * block)
            total = before[:, rows]
            total = total + mm(keys_high, select[rows, :], 1, 1) + mm(keys_low, select[rows, :], 1, 1)
            total = total + mm(raw_high, step[:, rows]) + mm(raw_low, step[:, rows])
            for k in range(tails):
                total = total + mm(dvs[k][...], weights[k][rows, :], 1, 1)
            tiles.append(total)
        if swap:
            tiles = tiles[::-1]
        if parts == 2:
            first = place[2] == 0
            outs[0][...] = jnp.where(first, tiles[0], tiles[1])
            outs[1][...] = jnp.where(first, tiles[1], tiles[0])
        else:
            for b in range(parts):
                outs[0][:, b * block : (b + 1) * block] = tiles[b]

    return body


def tile_body(groups, tails, heads, swap, keep):
    def body(place, own_ref, select, step, before, *rest):
        dvs, weights = rest[0:tails], rest[tails : 2 * tails]
        rest = rest[2 * tails :]
        keys, steps, out = rest[0:groups], rest[groups : 2 * groups], rest[-1]
        d_keys, d_steps = keys[0][...], steps[0][...]
        for a, b in zip(keys[1:], steps[1:]):
            d_keys = d_keys + a[...]
            d_steps = d_steps + b[...]
        d_raw = d_steps[:, 0:heads] * own_ref[:, 2 * LANES + 3 * heads : 2 * LANES + 4 * heads]
        keys_high, keys_low = halves(d_keys)
        raw_high, raw_low = halves(d_raw)
        block = out.shape[1]
        mine = place[2] if keep != swap else 1 - place[2]
        rows = pl.ds(pl.multiple_of(mine * block, block), block)
        total = before[:, rows]
        total = total + mm(keys_high, select[rows, :], 1, 1) + mm(keys_low, select[rows, :], 1, 1)
        total = total + mm(raw_high, step[:, rows]) + mm(raw_low, step[:, rows])
        for dv, weight in zip(dvs, weights):
            total = total + mm(dv[...], weight[rows, :], 1, 1)
        out[...] = total

    return body


def last_body(work, term, work_ins):
    def body(place, *rest):
        rest = list(rest)
        take = lambda n: [rest.pop(0) for _ in range(n)]
        for_work = take(work_ins)
        select, step, before, weight = take(4)
        others = take(len(rest) - 7)
        half = len(others) // 2
        mixed, dv, keys, steps, out = take(5)
        bufs, sems = take(2)
        work(place, *for_work, mixed, dv, keys, steps, bufs, sems)
        term(
            place, for_work[0], select, step, before, dv, weight,
            *others[:half], keys, *others[half:], steps, out,
        )

    return body


def finish_body(flip):
    def body(a, b, out):
        total = (a[...] + b[...]).astype(BF)
        if not flip:
            out[...] = total
            return
        width = total.shape[1]
        block = flip_block(width)
        turn = reversal(block)
        for j in range(width // block):
            out[:, j * block : (j + 1) * block] = mm(
                total[:, width - (j + 1) * block : width - j * block], turn
            ).astype(BF)

    return body


def put_chunk(wide, v_ref, g_ref, pieces):
    length, width = g_ref.shape
    wide[0:length, :] = v_ref[...].reshape(length, width).astype(F32)
    wide[length : 2 * length, :] = g_ref[...].astype(F32)
    for n, piece in enumerate(pieces):
        put_piece(wide, 2 * length + n * piece_rows(length, width), piece[...])


def widen_body(v_ref, g_ref, token, *rest):
    put_chunk(rest[-1], v_ref, g_ref, rest[:-1])


def local(shards, parts):
    pairs = shards // 2

    def body(
        hidden, complement, inner_weight, select_weight, step_weight, step_bias, decay_rate,
        skip_gain, cotangent, complement_cotangent,
    ):
        length, width = hidden.shape
        inner = inner_weight.shape[1]
        heads = step_bias.shape[0]
        head_width = inner // heads
        groups = 4
        chunk = inner // groups
        group_heads = heads // groups
        seq = lax.axis_index("seq")
        place = jnp.stack([seq % 2, seq // 2, lax.axis_index("chan")]).astype(jnp.int32)
        bias = step_bias.reshape(1, heads)
        rate = decay_rate.reshape(1, heads)
        rate_row = jnp.pad(rate, ((0, 0), (0, LANES - heads)))
        gain = skip_gain.reshape(1, heads)
        step_rows = step_weight.T
        cots = (cotangent, complement_cotangent)
        swap_pairs = [(a, a ^ 1) for a in range(shards)]
        edges = []
        for start in range(2):
            meets = [(z, z + 1) for z in range(start, pairs - 1, 2)]
            paired = sum(meets, ())
            meets += [(b, a) for a, b in meets] + [(z, z) for z in range(pairs) if z not in paired]
            edges.append([(2 * a + y, 2 * b + y) for a, b in meets for y in range(2)])
        swap = lambda x: lax.ppermute(x, "seq", swap_pairs)
        pack_shape = (length, 3 * LANES)
        pair_shape = (2 * LANES, chunk)
        wide_shape = lambda pieces: sds((2 * length + pieces * piece_rows(length, chunk), chunk))
        token_shape = sds((8, LANES))
        work = lambda: [pltpu.VMEM((2,) + pair_shape, F32), pltpu.SemaphoreType.DMA((2,))]
        order = [(1, groups - 1)] + [(0, k) for k in range(groups)] + [(1, k) for k in range(groups - 1)]
        chunks = len(order)

        source, pack0, pack1, row, v_zero, wide = run(
            start_body,
            [*map(Copied, (hidden, complement, select_weight, step_rows, bias, rate)),
             Copied(Block(inner_weight, (width, chunk), (0, 0))),
             Copied(Block(cots[0], (length, chunk), (0, 0)))],
            [sds((2 * length, width), BF), sds(pack_shape), sds(pack_shape), token_shape,
             sds((1, 2, length, chunk), BF), wide_shape(3)],
            limit=54,
        )
        packs = (pack0, pack1)
        far_row = swap(row)

        def weight_of(k):
            return Block(inner_weight, (width, chunk), (0, k))

        def do_values(ks, token):
            return run(
                values_body,
                [source, Far(token), *map(weight_of, ks)],
                [sds((len(ks), 2, length, chunk), BF)],
            )[0]

        v_last, *own_states = run(
            column_body((groups - 1) * group_heads, heads, head_width),
            [pack1, source, weight_of(groups - 1),
             Block(cots[1], (length, chunk), (0, groups - 1))],
            [sds((1, 2, length, chunk), BF), sds(pair_shape), sds(pair_shape)],
        )
        v_more = None

        def value_block(c):
            s, k = order[c]
            array, n = {0: (v_zero, 0), groups - 1: (v_last, 0)}.get(k, (v_more, k - 1))
            return Block(array, (1, 1, length, chunk), (n, s, 0, 0))

        def cot_block(c):
            s, k = order[c]
            return Block(cots[s], (length, chunk), (0, k))

        def weight_block(c):
            return weight_of(order[c][1])

        far = {}
        totals, within, post = {}, {}, {}
        got = ([], [])
        grads = [None, None]
        riders = {2 + n: n for n in range(3)}
        columns = {}
        steps = chunks + pairs - 2

        def do_pair(c, token):
            s, k = order[c]
            rows = piece_rows(length, chunk)
            if s == 0:
                pieces, piece_at = [far[1]] * 3, [2 * length + n * rows for n in range(3)]
            else:
                pieces, piece_at = [far[r] for r in riders], [2 * length] * 3
            totals[c] = run(
                pair_body(k * group_heads, heads, head_width, piece_at),
                [place, value_block(c), cot_block(c), far[c], *pieces, packs[s], Far(token)],
                [sds(pair_shape), sds(pair_shape), sds(pair_shape), sds((8, chunk))],
            )
            return totals[c][3]

        within_shapes = [
            sds((length, chunk)), sds((length, chunk)), sds((length, 2 * LANES)), sds((length, LANES))
        ]
        post_shapes = [
            sds((length, chunk), BF), sds((length, chunk), BF), sds((length, 2 * LANES)), sds((length, LANES))
        ]
        flows = lambda: [pltpu.VMEM((2, LANES, length), F32)]

        def do_within(c, token):
            s, k = order[c]
            within[c] = run(
                within_body(k * group_heads, heads, head_width),
                [packs[s], value_block(c), cot_block(c), rate_row, Far(token)],
                within_shapes,
                scratch=flows(),
            )
            return within[c][3]

        def post_parts(c, token, fused):
            s, k = order[c]
            fused = fused and c not in within
            last = pairs - 1
            ups = [got[(z + 1) % 2][max(c + z - 1, c)] for z in range(pairs)]
            downs = [got[(last - z) % 2][max(c + z - 1, c)] for z in range(pairs)]
            body = post_body(k * group_heads, heads, head_width, len(ups), len(downs), c == 0)
            if not fused and c == 0:
                body = paired_near(body)
            if fused:
                body = chunk_body(within_body(k * group_heads, heads, head_width), body, c == 0)
            near = columns["far"] if c == 0 else [totals[c][2]]
            ins = [packs[s], value_block(c), cot_block(c), *([] if fused else within[c]),
                   *near, totals[c][3], gain, rate_row, Far(token),
                   *map(Far, ups), *map(Far, downs)]
            return body, ins

        def do_chunk(c, token):
            body, ins = post_parts(c, token, True)
            more = [] if c in within else [pltpu.VMEM(o.shape, o.dtype) for o in within_shapes] + flows()
            post[c] = run(body, [place, *ins], post_shapes, stored=(0,), scratch=work() + more)
            return post[c][3]

        def do_partial(cs, token, before=None):
            return run(
                partial_body(len(cs), before is not None),
                [Far(token), *[post[c][1] for c in cs], *[weight_block(c) for c in cs]]
                + ([] if before is None else [before]),
                [sds((length, width))],
            )[0]

        shares = [sds((length, width // parts))] * 2 if parts == 2 else [sds((length, width))]

        def send_share(term):
            if parts == 2:
                return term[0], lax.ppermute(term[1], "chan", [(0, 1), (1, 0)])
            share = lax.psum_scatter(term[0], "chan", scatter_dimension=1, tiled=True)
            return share, jnp.zeros_like(share)

        def do_term(s, before):
            mine = [c for c in range(chunks) if order[c][0] == s]
            return send_share(run(
                term_body(len(mine), 0, heads, parts, s == 1),
                [place, packs[s], select_weight, step_rows, before,
                 *[post[c][2] for c in mine], *[post[c][3] for c in mine]],
                shares,
            ))

        def do_last(c, before, token):
            s = order[c][0]
            mine = [n for n in range(chunks) if order[n][0] == s and n != c]
            body, ins = post_parts(c, token, False)
            sums = [select_weight, step_rows, before]
            others = [[post[n][k] for n in mine] for k in (2, 3)]
            if parts == 2:
                term = tile_body(len(mine) + 1, 1, heads, s == 1, False)
            else:
                term = term_body(len(mine) + 1, 1, heads, parts, s == 1)
            post[c] = run(
                last_body(body, term, len(ins)),
                [place, *ins, *sums, weight_block(c), *others[0], *others[1]],
                [*post_shapes, shares[0]],
                scratch=work(),
                stored=(0,),
            )
            if parts != 2:
                return send_share(post[c][4:])
            arriving = lax.ppermute(post[c][4], "chan", [(0, 1), (1, 0)])
            kept = run(
                tile_body(len(mine) + 1, 1, heads, s == 1, True),
                [place, packs[s], *sums, post[c][1], weight_block(c),
                 *others[0], post[c][2], *others[1], post[c][3]],
                [shares[0]],
            )[0]
            return kept, arriving

        def do_finish(s, share):
            return run(
                finish_body(s == 1), list(share), [sds((length, width // parts), BF)], stored=(0,)
            )[0]

        def do_step(k, widen, ends):
            has = [0 <= k - z < chunks and z < pairs - 1 for z in range(pairs)]
            ins = [place]
            for d in range(2):
                ins += [totals[k - z][d] for z in range(pairs) if has[z]]
                ins += [totals[k - z][3] for z in range(pairs) if has[z]]
            if k > 0:
                ins += [got[0][-1], got[1][-1]]
            outs = [sds(pair_shape), sds(pair_shape), token_shape]
            pieces = [] if widen is None else pieces_of(widen)
            if widen is not None:
                ins += [value_block(widen), cot_block(widen), *pieces]
                outs.append(wide_shape(len(pieces)))
            return run(
                step_body(has, k == 0, widen is not None, len(pieces), len(ends)),
                ins + [Far(e) for e in ends],
                outs,
            )

        def do_first_step(ends):
            s, k = order[0]
            out = run(
                first_step_body(pairs, k * group_heads, heads, head_width, len(ends)),
                [place, packs[s], far_row, *own_states, *map(Far, ends)],
                [sds(pair_shape), sds(pair_shape), token_shape, sds(pair_shape), sds(pair_shape),
                 sds((8, chunk))],
            )
            totals[0] = (out[3], out[4], None, out[5])
            columns["own"] = own_states
            return out

        def do_exchange(token):
            last = pairs - 1
            ups = [got[(z + 1) % 2][max(z - 1, 0)] for z in range(pairs)]
            downs = [got[(last - z) % 2][max(z - 1, 0)] for z in range(pairs)]
            sends = run(
                exchange_body(len(ups), len(downs)),
                [place, *columns["own"], totals[0][3], Far(token), *map(Far, ups), *map(Far, downs)],
                [sds(pair_shape), sds(pair_shape)],
                scratch=work(),
            )
            columns["far"] = [swap(x) for x in sends]

        def pieces_of(c):
            return [Block(packs[1], (length, LANES), (0, riders[c]))] if c in riders else []

        def do_widen(c, token):
            pieces = pieces_of(c)
            return run(
                widen_body, [value_block(c), cot_block(c), Far(token), *pieces], [wide_shape(len(pieces))]
            )[0]

        far[1] = swap(lax.optimization_barrier((wide, far_row))[0])
        ends = []
        halfway = None
        share = None
        for k in range(steps):
            queue = k + 2 if 0 < k < chunks - 2 else None
            made = do_first_step(ends) if k == 0 else do_step(k, queue, ends)
            token = made[2]
            for d in range(2):
                got[d].append(lax.ppermute(made[d], "seq", edges[d]))
            ends = []
            if k == 0:
                v_more = do_values(list(range(1, groups - 1)), token)
                far[2] = swap(do_widen(2, token))
            if queue is not None:
                far[queue] = swap(made[3])
            if k + 1 < chunks:
                ends.append(do_pair(k + 1, token))
            if k == max(chunks - 2, pairs - 1):
                do_exchange(far[chunks - 1])
            if k == steps - 3:
                ends += columns["far"]
            for c in {1: (2, 5), 2: (3, 6, 0), 3: (4, 7)}.get(k, ()):
                ends.append(do_within(c, token))
            c = k - pairs + 1
            if c > 0:
                ends.append(do_chunk(c, token))
            if c == groups - 2:
                halfway = do_partial(list(range(1, groups - 1)), token)
                ends.append(halfway)
            if c == groups:
                share = do_term(0, do_partial([groups - 1, groups], token, halfway))
                ends.append(share[0])
            if c == groups + 1:
                ends.append(do_chunk(0, token))
            if c == groups + 2:
                grads[0] = do_finish(0, share)
                halfway = do_partial([groups + 1, 0, groups + 2], token)
        grads[1] = do_finish(1, do_last(chunks - 1, halfway, halfway))
        outs = [
            jnp.concatenate([post[order.index((s, k))][0] for k in range(groups)], axis=1)
            for s in range(2)
        ]
        return (outs[0], outs[1], grads[0], grads[1])

    return body


def solution(mesh):
    rows = P(("dp", "seq"), None)
    both = P(("dp", "seq"), "chan")
    in_specs = (
        rows, rows, P(None, "chan"), P(), P(None, "chan"),
        P("chan"), P("chan"), P("chan"), both, both,
    )
    return jax.shard_map(
        local(mesh.shape["seq"], mesh.shape["chan"]),
        mesh=mesh,
        in_specs=in_specs,
        out_specs=(both,) * 4,
        check_vma=False,
    )
```

```python
import jax
import jax.numpy as jnp
from jax import lax
from jax.experimental import pallas as pl
from jax.experimental.pallas import tpu as pltpu
from jax.sharding import PartitionSpec as P

BF = jnp.bfloat16
F32 = jnp.float32
LANES = 128


def mm(a, b, ca=1, cb=0):
    return lax.dot_general(a, b, (((ca,), (cb,)), ((), ())), preferred_element_type=F32)


def halves(x):
    high = x.astype(BF)
    return high, (x - high.astype(F32)).astype(BF)


def mm_exact(a, b, ca=1, cb=0):
    first, rest = b.astype(BF), None
    rest = b - first.astype(F32)
    second = rest.astype(BF)
    third = (rest - second.astype(F32)).astype(BF)
    return mm(a, first, ca, cb) + mm(a, second, ca, cb) + mm(a, third, ca, cb)


def iotas(rows, columns):
    return (
        lax.broadcasted_iota(jnp.int32, (rows, columns), 0),
        lax.broadcasted_iota(jnp.int32, (rows, columns), 1),
    )


def spread(weights, base, width, head_width):
    heads = weights[0].shape[1]
    row, channel = iotas(2 * heads, width)
    start = (jnp.where(row >= heads, row - heads, row) - base) * head_width
    pick = ((channel >= start) & (channel < start + head_width)).astype(BF)
    stacked = jnp.concatenate(weights, axis=0) if len(weights) > 1 else weights[0]
    out = mm(jnp.concatenate(halves(stacked), axis=1), pick)
    result, at = [], 0
    for w in weights:
        result.append(out[at : at + w.shape[0]])
        at += w.shape[0]
    return result


def spread_rows(rows, base, width, head_width):
    heads = rows[0].shape[1]
    wide = spread([jnp.broadcast_to(r, (8, heads)) for r in rows], base, width, head_width)
    return [w[0:1] for w in wide]


def gather_heads(parts, base, head_width):
    width = parts[0].shape[1]
    channel, head = iotas(width, LANES)
    start = (head - base) * head_width
    pick = ((channel >= start) & (channel < start + head_width)).astype(BF)
    out = mm(jnp.concatenate([x.astype(BF) for x in parts], axis=0), pick)
    result, at = [], 0
    for x in parts:
        result.append(out[at : at + x.shape[0]])
        at += x.shape[0]
    return result


def reversal(size):
    i, j = iotas(size, size)
    return (i + j == size - 1).astype(BF)


def flip_block(size):
    return 256 if size % 256 == 0 else 128


def sds(shape, dtype=F32):
    return jax.ShapeDtypeStruct(shape, dtype)


class Block:
    def __init__(self, array, shape, index):
        self.array, self.shape, self.index = array, shape, index

    def view(self, ref):
        if self.shape == self.array.shape:
            return ref
        return ref.at[tuple(pl.ds(i * b, b) for i, b in zip(self.index, self.shape))]


class Copied:
    def __init__(self, item):
        self.item = item if isinstance(item, Block) else Block(item, item.shape, (0,) * item.ndim)


class Far:
    def __init__(self, array):
        self.array = array


def run(body, ins, outs, scratch=(), limit=16, stored=()):
    specs, arrays, copied = [], [], []
    for item in ins:
        if isinstance(item, Far):
            specs.append(pl.BlockSpec(memory_space=pl.ANY))
            arrays.append(item.array)
        elif isinstance(item, Copied):
            specs.append(pl.BlockSpec(memory_space=pltpu.HBM))
            arrays.append(item.item.array)
            copied.append(item.item)
        elif isinstance(item, Block):
            specs.append(pl.BlockSpec(memory_space=pltpu.VMEM))
            arrays.append(item.array)
        else:
            space = pltpu.SMEM if item.dtype == jnp.int32 else pltpu.VMEM
            specs.append(pl.BlockSpec(memory_space=space))
            arrays.append(item)
    out_specs = [
        pl.BlockSpec(memory_space=pltpu.HBM if n in stored else pltpu.VMEM)
        for n in range(len(outs))
    ]
    holds = [pltpu.VMEM(q.shape, q.array.dtype) for q in copied]
    holds += [pltpu.VMEM(outs[n].shape, outs[n].dtype) for n in stored]
    sems = [pltpu.SemaphoreType.DMA((max(len(holds), 1),))]

    def kernel(*refs):
        refs = list(refs)
        take = lambda n: [refs.pop(0) for _ in range(n)]
        sources, targets = take(len(ins)), take(len(outs))
        held, (sem,) = take(len(holds)), take(1)
        args, copies = [], []
        for ref, item in zip(sources, ins):
            if isinstance(item, Copied):
                n = len(copies)
                copies.append(pltpu.make_async_copy(item.item.view(ref), held[n], sem.at[n]))
                copies[-1].start()
                ref = held[n]
            elif isinstance(item, Block):
                ref = item.view(ref)
            args.append(ref)
        back = []
        for n, ref in enumerate(targets):
            if n in stored:
                k = len(copied) + stored.index(n)
                back.append(pltpu.make_async_copy(held[k], ref, sem.at[k]))
                ref = held[k]
            args.append(ref)
        waits = {"waits": [c.wait for c in copies]} if copies else {}
        body(*args, *refs, **waits)
        for copy in back:
            copy.start()
        for copy in back:
            copy.wait()

    return pl.pallas_call(
        kernel,
        in_specs=specs,
        out_specs=out_specs,
        out_shape=outs,
        scratch_shapes=holds + sems + list(scratch),
        compiler_params=pltpu.CompilerParams(vmem_limit_bytes=limit * 1024 * 1024),
        cost_estimate=pl.CostEstimate(flops=0, bytes_accessed=1024, transcendentals=0),
    )(*arrays)


def start_body(
    hidden, other, select, step, bias, rate, weight, cot,
    source, pack0, pack1, row, v_out, wide, waits,
):
    for wait in waits[0:2]:
        wait()
    length, width = hidden.shape
    heads = bias.shape[1]
    source[0:length, :] = hidden[...]
    block = flip_block(width)
    turn = reversal(block)
    for j in range(width // block):
        source[length : 2 * length, j * block : (j + 1) * block] = mm(
            other[:, width - (j + 1) * block : width - j * block], turn
        ).astype(BF)
    for wait in waits[2:6]:
        wait()
    keys = mm(source[...], select[...]).astype(BF).astype(F32)
    state = keys.shape[1] // 2
    raw = mm(source[...], step[...], 1, 1) + bias[...]
    dt = jnp.maximum(raw, 0.0) + jnp.log1p(jnp.exp(-jnp.abs(raw)))
    rise = jax.nn.sigmoid(raw)
    i, j = iotas(length, length)
    lower = (i >= j).astype(BF)
    for s, pack in enumerate((pack0, pack1)):
        rows = slice(s * length, (s + 1) * length)
        drop = dt[rows] * rate[...]
        total = mm_exact(lower, drop)
        pack[...] = jnp.zeros(pack.shape, F32)
        pack[:, 0 : 2 * state] = keys[rows]
        at = 2 * state
        for part in (dt[rows], total, total - drop, rise[rows]):
            pack[:, at : at + heads] = part
            at += heads
    row[...] = jnp.zeros(row.shape, F32)
    row[0:1, 0:heads] = jnp.exp(
        -pack1[length - 1 : length, 2 * state + heads : 2 * state + 2 * heads]
    )
    for wait in waits[6:]:
        wait()
    for at in columns_of(weight.shape[1]):
        piece = mm(source[...], weight[:, at]).astype(BF)
        for s in range(2):
            v_out[0, s, :, at] = piece[s * length : (s + 1) * length]
        wide[0:length, at] = piece[0:length].astype(F32)
    wide[length : 2 * length, :] = cot[...].astype(F32)
    for n in range(3):
        at = 2 * length + n * piece_rows(length, wide.shape[1])
        put_piece(wide, at, pack0[:, n * LANES : (n + 1) * LANES])


def columns_of(width):
    block = min(256, width)
    return [slice(k * block, (k + 1) * block) for k in range(width // block)]


def values_body(source, token, *rest):
    weights, v_out = rest[:-1], rest[-1]
    length = v_out.shape[2]
    for n, weight in enumerate(weights):
        for at in columns_of(weight.shape[1]):
            piece = mm(source[...], weight[:, at]).astype(BF)
            for s in range(2):
                v_out[n, s, :, at] = piece[s * length : (s + 1) * length]


class Pack:
    def __init__(self, write, read, stats, heads):
        self.write, self.read = write, read
        self.dt = stats[:, 0:heads]
        self.total = stats[:, heads : 2 * heads]
        self.before = stats[:, 2 * heads : 3 * heads]
        last = self.total.shape[0]
        self.whole = self.total[last - 1 : last, :]
        self.from_start = jnp.exp(-self.total)
        self.from_end = jnp.exp(self.before - self.whole)
        self.to_end = jnp.exp(self.total - self.whole)
        self.to_start = jnp.exp(-self.before)
        self.through = jnp.exp(-self.whole)


def own_pack(ref, heads):
    return Pack(*[ref[:, n * LANES : (n + 1) * LANES] for n in range(3)], heads)


def piece_rows(length, width):
    return length // (width // LANES)


def put_piece(ref, row, piece):
    count = piece_rows(piece.shape[0], ref.shape[1])
    for b in range(ref.shape[1] // LANES):
        ref[row : row + count, b * LANES : (b + 1) * LANES] = piece[b * count : (b + 1) * count]


def get_piece(ref, row, length):
    count = piece_rows(length, ref.shape[1])
    return jnp.concatenate(
        [
            ref[row : row + count, b * LANES : (b + 1) * LANES]
            for b in range(ref.shape[1] // LANES)
        ],
        axis=0,
    )


def pair_body(base, heads, head_width, piece_at):
    def body(place, v_own, g_own, x_far, far0, far1, far2, own_ref, token, up, down, near, keep):
        first = place[0] == 0
        length, width = g_own.shape
        own = own_pack(own_ref, heads)
        far = Pack(*[get_piece(f, at, length) for f, at in zip((far0, far1, far2), piece_at)], heads)
        own_row, far_row = own.through, far.through
        rows = spread_rows([own_row * far_row, far_row], base, width, head_width)
        keep[...] = jnp.zeros(keep.shape, F32)
        keep[0:1, :] = rows[0]
        keep[1:2, :] = rows[1]
        own_up, own_down = jnp.where(first, far_row, 1.0), jnp.where(first, 1.0, far_row)
        far_up, far_down = jnp.where(first, 1.0, own_row), jnp.where(first, own_row, 1.0)
        for kind in range(2):
            rows = slice(kind * LANES, (kind + 1) * LANES)
            if kind == 0:
                keys = (own.write, far.write)
                ups = (own.dt * own.to_end, far.dt * far.to_end)
                downs = (own.dt * own.to_start, far.dt * far.to_start)
            else:
                keys = (own.read, far.read)
                ups = (own.from_end, far.from_end)
                downs = (own.from_start, far.from_start)
            x_own = (v_own if kind == 0 else g_own)[...].reshape(length, width).astype(F32)
            x_other = x_far[kind * length : (kind + 1) * length, :]
            w = spread(
                [ups[0] * own_up, ups[1] * far_up, downs[0] * own_down, downs[1] * far_down,
                 jnp.where(first, downs[1], ups[1])],
                base, width, head_width,
            )
            key = jnp.concatenate(keys, axis=0).astype(BF)
            both = lambda a, b: jnp.concatenate([(a * x_own).astype(BF), (b * x_other).astype(BF)], axis=0)
            up[rows, :] = mm(key, both(w[0], w[1]), 0, 0)
            down[rows, :] = mm(key, both(w[2], w[3]), 0, 0)
            near[rows, :] = mm(keys[1].astype(BF), (w[4] * x_other).astype(BF), 0, 0)

    return body


def column_body(base, heads, head_width):
    def body(own_ref, source, weight, g_own, v_out, own_up, own_down, waits):
        length, width = g_own.shape
        own = own_pack(own_ref, heads)
        w_values = spread([own.dt * own.to_end, own.dt * own.to_start], base, width, head_width)
        w_grads = spread([own.from_end, own.from_start], base, width, head_width)
        write, read = own.write.astype(BF), own.read.astype(BF)
        waits[0]()
        for at in columns_of(width):
            piece = mm(source[...], weight[:, at]).astype(BF)
            for s in range(2):
                v_out[0, s, :, at] = piece[s * length : (s + 1) * length]
            v, g = piece[length:].astype(F32), g_own[:, at].astype(F32)
            for out, n in ((own_up, 0), (own_down, 1)):
                out[0:LANES, at] = mm(write, (w_values[n][:, at] * v).astype(BF), 0, 0)
                out[LANES : 2 * LANES, at] = mm(read, (w_grads[n][:, at] * g).astype(BF), 0, 0)

    return body


def column_totals(place, own_ref, far_row_ref, base, heads, head_width, owns, totals, keep):
    first = place[0] == 0
    width = keep.shape[1]
    own = own_pack(own_ref, heads)
    far_row = far_row_ref[0:1, 0:heads]
    rows = spread_rows([own.through * far_row, far_row, own.through], base, width, head_width)
    keep[...] = jnp.zeros(keep.shape, F32)
    for n, row in enumerate(rows):
        keep[n : n + 1, :] = row
    totals[0][...] = jnp.where(first, rows[1], 1.0) * owns[0][...]
    totals[1][...] = jnp.where(first, 1.0, rows[1]) * owns[1][...]


def first_step_body(pairs, base, heads, head_width, tokens):
    def body(place, own_ref, far_row_ref, own_up, own_down, *rest):
        send_a, send_b, token, up, down, keep = rest[tokens:]
        column_totals(
            place, own_ref, far_row_ref, base, heads, head_width, (own_up, own_down), (up, down), keep
        )
        token[...] = jnp.zeros(token.shape, F32)
        sends = (send_a, send_b)
        for d, total in enumerate((up, down)):
            spot = place[1] if d == 0 else pairs - 1 - place[1]
            for n in range(pairs):
                z = n if d == 0 else pairs - 1 - n
                send = sends[(z + d) % 2]

                @pl.when(spot == n)
                def _():
                    send[...] = total[...] if n == 0 else jnp.zeros(send.shape, F32)

    return body


def exchange_body(ups, downs):
    def body(place, own_up, own_down, keep, token, *rest):
        up_in, down_in = rest[0:ups], rest[ups : ups + downs]
        up_out, down_out, bufs, sems = rest[ups + downs :]
        up_spot, down_spot = place[1], len(up_in) - 1 - place[1]
        fetch_start(up_in, up_spot, bufs.at[0], sems.at[0])
        fetch_start(down_in, down_spot, bufs.at[1], sems.at[1])
        fetch_wait(up_in, up_spot, bufs.at[0], sems.at[0])
        fetch_wait(down_in, down_spot, bufs.at[1], sems.at[1])
        first = place[0] == 0
        row = keep[2:3, :]
        up_out[...] = jnp.where(first, row * bufs[0] + own_up[...], bufs[0])
        down_out[...] = jnp.where(first, bufs[1], row * bufs[1] + own_down[...])

    return body


def fetch_start(options, index, target, sem):
    for z, option in enumerate(options):
        if option is not None:

            @pl.when(index == z)
            def _():
                pltpu.make_async_copy(option, target, sem).start()


def fetch_wait(options, index, target, sem):
    for z, option in enumerate(options):
        if option is not None:

            @pl.when(index == z)
            def _():
                pltpu.make_async_copy(option, target, sem).wait()


def step_body(has, first_step, widen, pieces, tokens):
    pairs = len(has)

    def body(place, *rest):
        rest = list(rest)
        take = lambda n: [rest.pop(0) for _ in range(n)]
        sides = []
        for d in range(2):
            totals = [take(1)[0] if h else None for h in has]
            keeps = [take(1)[0] if h else None for h in has]
            sides.append((totals, keeps))
        got = None if first_step else take(2)
        chunk = take(2) if widen else None
        piece_refs = take(pieces)
        take(tokens)
        sends = take(2)
        token = take(1)[0]
        spots = (place[1], pairs - 1 - place[1])
        for d, (totals, keeps) in enumerate(sides):
            for n in range(pairs):
                z = n if d == 0 else pairs - 1 - n
                send = sends[(z + d) % 2]

                @pl.when(spots[d] == n)
                def _():
                    if not has[n]:
                        send[...] = jnp.zeros(send.shape, F32)
                    elif got is None or n == 0:
                        send[...] = totals[n][...]
                    else:
                        send[...] = totals[n][...] + keeps[n][0:1, :] * got[(z + 1 + d) % 2][...]

        token[...] = jnp.zeros(token.shape, F32)
        if widen:
            put_chunk(take(1)[0], *chunk, piece_refs)

    return body


def within_body(base, heads, head_width):
    def body(own_ref, v_ref, g_ref, rate, token, y_out, x_out, keys_out, steps_out, cols_s):
        own = own_pack(own_ref, heads)
        length, width = g_ref.shape
        write, read = own.write.astype(BF), own.read.astype(BF)
        scores = mm(read, write, 1, 1)
        i, j = iotas(length, length)
        low = i > j
        high = i < j
        doubled = jnp.where(i == j, 2.0, 1.0).astype(F32)
        scores2 = scores * doubled
        turned = own_ref[:, 2 * LANES : 3 * LANES].T
        lane = lax.broadcasted_iota(jnp.int32, (length, LANES), 1)
        d_scores = jnp.zeros((length, length), F32)
        out_low = jnp.zeros((length, LANES), F32)
        out_high = jnp.zeros((length, LANES), F32)
        cols_s[...] = jnp.zeros(cols_s.shape, F32)
        v_all = v_ref[...].reshape(length, width)
        per = LANES // head_width
        for n in range(width // LANES):
            at = slice(n * LANES, (n + 1) * LANES)
            v, g = v_all[:, at], g_ref[:, at]
            mine = [(lane >= m * head_width) & (lane < (m + 1) * head_width) for m in range(per)]
            v_heads = jnp.concatenate([jnp.where(x, v, jnp.zeros_like(v)) for x in mine], axis=0)
            g_heads = jnp.concatenate([jnp.where(x, g, jnp.zeros_like(g)) for x in mine], axis=0)
            products = mm(g_heads, v, 1, 1)
            plains, steppeds = [], []
            for m in range(per):
                h = base + n * per + m
                c_col = own.total[:, h : h + 1]
                e_col = own.before[:, h : h + 1]
                dt_row = turned[h : h + 1, :]
                c_row = turned[heads + h : heads + h + 1, :]
                e_row = turned[2 * heads + h : 2 * heads + h + 1, :]
                decay = jnp.exp(jnp.where(low, c_row - c_col, e_col - e_row))
                plain = decay * scores2
                plains.append(plain.astype(BF))
                steppeds.append((plain * dt_row).astype(BF))
                inner = decay * dt_row * products[m * length : (m + 1) * length]
                d_scores = d_scores + inner
                flow = inner * scores
                flow_low = jnp.where(low, flow, 0.0)
                flow_high = jnp.where(high, flow, 0.0)
                out_low = jnp.where(lane == h, jnp.sum(flow_low, 1, keepdims=True), out_low)
                out_high = jnp.where(lane == h, jnp.sum(flow_high, 1, keepdims=True), out_high)
                cols_s[0, h : h + 1, :] = jnp.sum(flow_low, 0, keepdims=True)
                cols_s[1, h : h + 1, :] = jnp.sum(flow_high, 0, keepdims=True)
            y_out[:, at] = mm(jnp.concatenate(steppeds, axis=1), v_heads)
            x_out[:, at] = mm(jnp.concatenate(plains, axis=0), g_heads, 0, 0)
        d_scores = (d_scores * doubled).astype(BF)
        keys_out[:, 0:LANES] = mm(d_scores, read, 0, 0)
        keys_out[:, LANES : 2 * LANES] = mm(d_scores, write)
        net_low = out_low - cols_s[0].T
        net_high = out_high - cols_s[1].T
        at_or_after = (j >= i).astype(BF)
        after = (j > i).astype(BF)
        steps_out[...] = -rate[...] * (mm_exact(at_or_after, net_low) - mm_exact(after, net_high))

    return body


def post_body(base, heads, head_width, ups, downs, columns=False):
    def body(
        place, own_ref, v_ref, g_ref, yw, xw, keys_w, steps_w, near, keep, skip, rate, token, *rest
    ):
        up_in, down_in = rest[0:ups], rest[ups : ups + downs]
        mixed, dv_out, keys_out, steps_out, bufs, sems = rest[ups + downs :]
        up_spot, down_spot = place[1], len(up_in) - 1 - place[1]
        fetch_start(up_in, up_spot, bufs.at[0], sems.at[0])
        fetch_start(down_in, down_spot, bufs.at[1], sems.at[1])
        first = place[0] == 0
        own = own_pack(own_ref, heads)
        length, width = g_ref.shape
        far_row = keep[1:2, :]
        own_row, gain = spread_rows([own.through, skip[...]], base, width, head_width)
        up_row = jnp.where(first, 1.0, far_row)
        down_row = jnp.where(first, far_row, 1.0)
        dt, from_start, from_end, to_end, to_start = spread(
            [own.dt, own.from_start, own.from_end, own.to_end, own.to_start],
            base, width, head_width,
        )
        write, read = own.write.astype(BF), own.read.astype(BF)
        v = v_ref[...].reshape(length, width).astype(F32)
        g = g_ref[...].astype(F32)
        fetch_wait(up_in, up_spot, bufs.at[0], sems.at[0])
        fetch_wait(down_in, down_spot, bufs.at[1], sems.at[1])
        if columns:
            up = up_row * bufs[0] + near[0][...]
            down = down_row * bufs[1] + near[1][...]
        else:
            up = up_row * bufs[0] + jnp.where(first, 0.0, near[...])
            down = down_row * bufs[1] + jnp.where(first, near[...], 0.0)
        p, ab = up[0:LANES], up[LANES : 2 * LANES]
        q, af = down[0:LANES], down[LANES : 2 * LANES]
        crossing = jnp.sum(p * af + q * ab, axis=0, keepdims=True)
        p, q, af, ab = p.astype(BF), q.astype(BF), af.astype(BF), ab.astype(BF)
        y_p = from_start * mm(read, p)
        y_q = from_end * mm(read, q)
        x_f = to_end * mm(write, af)
        x_b = to_start * mm(write, ab)
        mixed[...] = (yw[...] + y_p + y_q + gain * v).astype(BF)
        x = xw[...] + x_f + x_b
        dv_out[...] = (dt * x + gain * g).astype(BF)
        dtv = dt * v
        keys_out[:, 0:LANES] = (
            keys_w[:, 0:LANES]
            + mm((to_end * dtv).astype(BF), af, 1, 1)
            + mm((to_start * dtv).astype(BF), ab, 1, 1)
        )
        keys_out[:, LANES : 2 * LANES] = (
            keys_w[:, LANES : 2 * LANES]
            + mm((from_start * g).astype(BF), p, 1, 1)
            + mm((from_end * g).astype(BF), q, 1, 1)
        )
        lane = lax.broadcasted_iota(jnp.int32, (length, LANES), 1)
        steps = jnp.where(lane < heads, own_ref[:, 2 * LANES : 3 * LANES], 0.0)
        direct, a_p, a_q, b_f, b_b, through = gather_heads(
            [v * x, g * y_p, g * y_q, v * x_f, v * x_b, jnp.broadcast_to(crossing * own_row, (8, width))],
            base, head_width,
        )
        i, j = iotas(length, length)
        masks = jnp.concatenate([j >= i, j <= i, j < i, j > i], axis=1).astype(F32).astype(BF)
        high, low = halves(jnp.concatenate([a_p, a_q, b_f * steps, b_b * steps], axis=0))
        flow = mm(masks, high) + mm(masks, low) + through[0:1]
        steps_out[...] = steps_w[...] + direct - rate[...] * flow

    return body


class Either:
    def __init__(self, choice, a, b):
        self.choice, self.a, self.b = choice, a, b

    def __getitem__(self, index):
        return jnp.where(self.choice, self.a[index], self.b[index])


def either_within(post):
    def body(place, own_ref, v_ref, g_ref, *rest):
        merged = [Either(place[3] == 0, a, b) for a, b in zip(rest[0:4], rest[4:8])]
        post(place, own_ref, v_ref, g_ref, *merged, *rest[8:])

    return body


def turn_body(works, strands, turn):
    def body(place, pack0, pack1, rate, *rest):
        count = len(works)
        blocks, token = rest[0 : 2 * count], rest[2 * count]
        outs, flows = rest[2 * count + 1 : -1], rest[-1]

        @pl.when(place[3] == turn)
        def _():
            for n, work in enumerate(works):
                work(
                    (pack0, pack1)[strands[n]], blocks[2 * n], blocks[2 * n + 1], rate, token,
                    *outs[4 * n : 4 * n + 4], flows,
                )

    return body


def paired_near(post):
    def body(place, own_ref, v_ref, g_ref, yw, xw, keys_w, steps_w, near_up, near_down, *rest):
        post(place, own_ref, v_ref, g_ref, yw, xw, keys_w, steps_w, (near_up, near_down), *rest)

    return body


def chunk_body(within, post, columns):
    def body(place, own_ref, v_ref, g_ref, *rest):
        nears = 2 if columns else 1
        near = rest[0:2] if columns else rest[0]
        keep, skip, rate, token, *rest = rest[nears:]
        bufs, sems, yw, xw, keys_w, steps_w, cols_s = rest[-7:]
        within(own_ref, v_ref, g_ref, rate, token, yw, xw, keys_w, steps_w, cols_s)
        post(
            place, own_ref, v_ref, g_ref, yw, xw, keys_w, steps_w, near, keep, skip, rate, token,
            *rest[:-5],
        )

    return body


def partial_body(groups, more):
    def body(token, *rest):
        dvs, weights, rest = rest[0:groups], rest[groups : 2 * groups], rest[2 * groups :]
        out = rest[-1]
        for at in columns_of(out.shape[1]):
            total = rest[0][:, at] if more else 0.0
            for dv, weight in zip(dvs, weights):
                total = total + mm(dv[...], weight[at, :], 1, 1)
            out[:, at] = total

    return body


def term_body(groups, tails, heads, parts, swap):
    def body(place, own_ref, select, step, before, *rest):
        dvs, weights = rest[0:tails], rest[tails : 2 * tails]
        rest = rest[2 * tails :]
        keys, steps = rest[0:groups], rest[groups : 2 * groups]
        outs = rest[2 * groups :]
        d_keys, d_steps = keys[0][...], steps[0][...]
        for a, b in zip(keys[1:], steps[1:]):
            d_keys = d_keys + a[...]
            d_steps = d_steps + b[...]
        d_raw = d_steps[:, 0:heads] * own_ref[:, 2 * LANES + 3 * heads : 2 * LANES + 4 * heads]
        keys_high, keys_low = halves(d_keys)
        raw_high, raw_low = halves(d_raw)
        width = select.shape[0]
        block = width // parts
        tiles = []
        for b in range(parts):
            rows = slice(b * block, (b + 1) * block)
            total = before[:, rows]
            total = total + mm(keys_high, select[rows, :], 1, 1) + mm(keys_low, select[rows, :], 1, 1)
            total = total + mm(raw_high, step[:, rows]) + mm(raw_low, step[:, rows])
            for k in range(tails):
                total = total + mm(dvs[k][...], weights[k][rows, :], 1, 1)
            tiles.append(total)
        if swap:
            tiles = tiles[::-1]
        if parts == 2:
            first = place[2] == 0
            outs[0][...] = jnp.where(first, tiles[0], tiles[1])
            outs[1][...] = jnp.where(first, tiles[1], tiles[0])
        else:
            for b in range(parts):
                outs[0][:, b * block : (b + 1) * block] = tiles[b]

    return body


def tile_body(groups, tails, heads, swap, keep):
    def body(place, own_ref, select, step, before, *rest):
        dvs, weights = rest[0:tails], rest[tails : 2 * tails]
        rest = rest[2 * tails :]
        keys, steps, out = rest[0:groups], rest[groups : 2 * groups], rest[-1]
        d_keys, d_steps = keys[0][...], steps[0][...]
        for a, b in zip(keys[1:], steps[1:]):
            d_keys = d_keys + a[...]
            d_steps = d_steps + b[...]
        d_raw = d_steps[:, 0:heads] * own_ref[:, 2 * LANES + 3 * heads : 2 * LANES + 4 * heads]
        keys_high, keys_low = halves(d_keys)
        raw_high, raw_low = halves(d_raw)
        block = out.shape[1]
        mine = place[2] if keep != swap else 1 - place[2]
        rows = pl.ds(pl.multiple_of(mine * block, block), block)
        total = before[:, rows]
        total = total + mm(keys_high, select[rows, :], 1, 1) + mm(keys_low, select[rows, :], 1, 1)
        total = total + mm(raw_high, step[:, rows]) + mm(raw_low, step[:, rows])
        for dv, weight in zip(dvs, weights):
            total = total + mm(dv[...], weight[rows, :], 1, 1)
        out[...] = total

    return body


def last_body(work, term, work_ins):
    def body(place, *rest):
        rest = list(rest)
        take = lambda n: [rest.pop(0) for _ in range(n)]
        for_work = take(work_ins)
        select, step, before, weight = take(4)
        others = take(len(rest) - 7)
        half = len(others) // 2
        mixed, dv, keys, steps, out = take(5)
        bufs, sems = take(2)
        work(place, *for_work, mixed, dv, keys, steps, bufs, sems)
        term(
            place, for_work[0], select, step, before, dv, weight,
            *others[:half], keys, *others[half:], steps, out,
        )

    return body


def finish_body(flip):
    def body(a, b, out):
        total = (a[...] + b[...]).astype(BF)
        if not flip:
            out[...] = total
            return
        width = total.shape[1]
        block = flip_block(width)
        turn = reversal(block)
        for j in range(width // block):
            out[:, j * block : (j + 1) * block] = mm(
                total[:, width - (j + 1) * block : width - j * block], turn
            ).astype(BF)

    return body


def put_chunk(wide, v_ref, g_ref, pieces):
    length, width = g_ref.shape
    wide[0:length, :] = v_ref[...].reshape(length, width).astype(F32)
    wide[length : 2 * length, :] = g_ref[...].astype(F32)
    for n, piece in enumerate(pieces):
        put_piece(wide, 2 * length + n * piece_rows(length, width), piece[...])


def widen_body(v_ref, g_ref, token, *rest):
    put_chunk(rest[-1], v_ref, g_ref, rest[:-1])


def local(shards, parts):
    pairs = shards // 2

    def body(
        hidden, complement, inner_weight, select_weight, step_weight, step_bias, decay_rate,
        skip_gain, cotangent, complement_cotangent,
    ):
        length, width = hidden.shape
        inner = inner_weight.shape[1]
        heads = step_bias.shape[0]
        head_width = inner // heads
        groups = 4
        chunk = inner // groups
        group_heads = heads // groups
        seq = lax.axis_index("seq")
        place = jnp.stack(
            [seq % 2, seq // 2, lax.axis_index("chan"), lax.axis_index("dp")]
        ).astype(jnp.int32)
        bias = step_bias.reshape(1, heads)
        rate = decay_rate.reshape(1, heads)
        rate_row = jnp.pad(rate, ((0, 0), (0, LANES - heads)))
        gain = skip_gain.reshape(1, heads)
        step_rows = step_weight.T
        cots = (cotangent, complement_cotangent)
        swap_pairs = [(a, a ^ 1) for a in range(shards)]
        edges = []
        for start in range(2):
            meets = [(z, z + 1) for z in range(start, pairs - 1, 2)]
            paired = sum(meets, ())
            meets += [(b, a) for a, b in meets] + [(z, z) for z in range(pairs) if z not in paired]
            edges.append([(2 * a + y, 2 * b + y) for a, b in meets for y in range(2)])
        swap = lambda x: lax.ppermute(x, "seq", swap_pairs)
        pack_shape = (length, 3 * LANES)
        pair_shape = (2 * LANES, chunk)
        wide_shape = lambda pieces: sds((2 * length + pieces * piece_rows(length, chunk), chunk))
        token_shape = sds((8, LANES))
        work = lambda: [pltpu.VMEM((2,) + pair_shape, F32), pltpu.SemaphoreType.DMA((2,))]
        order = [(1, groups - 1)] + [(0, k) for k in range(groups)] + [(1, k) for k in range(groups - 1)]
        chunks = len(order)

        source, pack0, pack1, row, v_zero, wide = run(
            start_body,
            [*map(Copied, (hidden, complement, select_weight, step_rows, bias, rate)),
             Copied(Block(inner_weight, (width, chunk), (0, 0))),
             Copied(Block(cots[0], (length, chunk), (0, 0)))],
            [sds((2 * length, width), BF), sds(pack_shape), sds(pack_shape), token_shape,
             sds((1, 2, length, chunk), BF), wide_shape(3)],
            limit=57,
        )
        packs = (pack0, pack1)
        far_row = swap(row)

        def weight_of(k):
            return Block(inner_weight, (width, chunk), (0, k))

        def do_values(ks, token):
            return run(
                values_body,
                [source, Far(token), *map(weight_of, ks)],
                [sds((len(ks), 2, length, chunk), BF)],
            )[0]

        v_last, *own_states = run(
            column_body((groups - 1) * group_heads, heads, head_width),
            [pack1, source, Copied(weight_of(groups - 1)),
             Block(cots[1], (length, chunk), (0, groups - 1))],
            [sds((1, 2, length, chunk), BF), sds(pair_shape), sds(pair_shape)],
            limit=48,
        )
        v_more = None

        def value_block(c):
            s, k = order[c]
            array, n = {0: (v_zero, 0), groups - 1: (v_last, 0)}.get(k, (v_more, k - 1))
            return Block(array, (1, 1, length, chunk), (n, s, 0, 0))

        def cot_block(c):
            s, k = order[c]
            return Block(cots[s], (length, chunk), (0, k))

        def weight_block(c):
            return weight_of(order[c][1])

        far = {}
        totals, within, post = {}, {}, {}
        got = ([], [])
        grads = [None, None]
        riders = {2 + n: n for n in range(3)}
        columns = {}
        steps = chunks + pairs - 2

        def do_pair(c, token):
            s, k = order[c]
            rows = piece_rows(length, chunk)
            if s == 0:
                pieces, piece_at = [far[1]] * 3, [2 * length + n * rows for n in range(3)]
            else:
                pieces, piece_at = [far[r] for r in riders], [2 * length] * 3
            totals[c] = run(
                pair_body(k * group_heads, heads, head_width, piece_at),
                [place, value_block(c), cot_block(c), far[c], *pieces, packs[s], Far(token)],
                [sds(pair_shape), sds(pair_shape), sds(pair_shape), sds((8, chunk))],
            )
            return totals[c][3]

        within_shapes = [
            sds((length, chunk)), sds((length, chunk)), sds((length, 2 * LANES)), sds((length, LANES))
        ]
        post_shapes = [
            sds((length, chunk), BF), sds((length, chunk), BF), sds((length, 2 * LANES)), sds((length, LANES))
        ]
        flows = lambda: [pltpu.VMEM((2, LANES, length), F32)]

        def do_within(c, token):
            s, k = order[c]
            within[c] = run(
                within_body(k * group_heads, heads, head_width),
                [packs[s], value_block(c), cot_block(c), rate_row, Far(token)],
                within_shapes,
                scratch=flows(),
            )
            return within[c][3]

        def do_turn(cs, turn, token):
            blocks = [b for c in cs for b in (value_block(c), cot_block(c))]
            works = [within_body(order[c][1] * group_heads, heads, head_width) for c in cs]
            out = run(
                turn_body(works, [order[c][0] for c in cs], turn),
                [place, *packs, rate_row, *blocks, Far(token)],
                within_shapes * len(cs),
                scratch=flows(),
            )
            for n, c in enumerate(cs):
                within[c] = within.get(c, []) + list(out[4 * n : 4 * n + 4])
            return out[3]

        def post_parts(c, token, fused):
            s, k = order[c]
            fused = fused and c not in within
            last = pairs - 1
            ups = [got[(z + 1) % 2][max(c + z - 1, c)] for z in range(pairs)]
            downs = [got[(last - z) % 2][max(c + z - 1, c)] for z in range(pairs)]
            body = post_body(k * group_heads, heads, head_width, len(ups), len(downs), c == 0)
            if not fused and c == 0:
                body = paired_near(body)
            if len(within.get(c, ())) == 8:
                body = either_within(body)
            if fused:
                body = chunk_body(within_body(k * group_heads, heads, head_width), body, c == 0)
            near = columns["far"] if c == 0 else [totals[c][2]]
            ins = [packs[s], value_block(c), cot_block(c), *([] if fused else within[c]),
                   *near, totals[c][3], gain, rate_row, Far(token),
                   *map(Far, ups), *map(Far, downs)]
            return body, ins

        def do_chunk(c, token):
            body, ins = post_parts(c, token, True)
            more = [] if c in within else [pltpu.VMEM(o.shape, o.dtype) for o in within_shapes] + flows()
            post[c] = run(body, [place, *ins], post_shapes, stored=(0,), scratch=work() + more)
            return post[c][3]

        def do_partial(cs, token, before=None):
            return run(
                partial_body(len(cs), before is not None),
                [Far(token), *[post[c][1] for c in cs], *[weight_block(c) for c in cs]]
                + ([] if before is None else [before]),
                [sds((length, width))],
            )[0]

        shares = [sds((length, width // parts))] * 2 if parts == 2 else [sds((length, width))]

        def send_share(term):
            if parts == 2:
                return term[0], lax.ppermute(term[1], "chan", [(0, 1), (1, 0)])
            share = lax.psum_scatter(term[0], "chan", scatter_dimension=1, tiled=True)
            return share, jnp.zeros_like(share)

        def do_term(s, before):
            mine = [c for c in range(chunks) if order[c][0] == s]
            return send_share(run(
                term_body(len(mine), 0, heads, parts, s == 1),
                [place, packs[s], select_weight, step_rows, before,
                 *[post[c][2] for c in mine], *[post[c][3] for c in mine]],
                shares,
            ))

        def do_last(c, before, token):
            s = order[c][0]
            mine = [n for n in range(chunks) if order[n][0] == s and n != c]
            body, ins = post_parts(c, token, False)
            sums = [select_weight, step_rows, before]
            others = [[post[n][k] for n in mine] for k in (2, 3)]
            if parts == 2:
                term = tile_body(len(mine) + 1, 1, heads, s == 1, False)
            else:
                term = term_body(len(mine) + 1, 1, heads, parts, s == 1)
            post[c] = run(
                last_body(body, term, len(ins)),
                [place, *ins, *sums, weight_block(c), *others[0], *others[1]],
                [*post_shapes, shares[0]],
                scratch=work(),
                stored=(0,),
            )
            if parts != 2:
                return send_share(post[c][4:])
            arriving = lax.ppermute(post[c][4], "chan", [(0, 1), (1, 0)])
            kept = run(
                tile_body(len(mine) + 1, 1, heads, s == 1, True),
                [place, packs[s], *sums, post[c][1], weight_block(c),
                 *others[0], post[c][2], *others[1], post[c][3]],
                [shares[0]],
            )[0]
            return kept, arriving

        def do_finish(s, share):
            return run(
                finish_body(s == 1), list(share), [sds((length, width // parts), BF)], stored=(0,)
            )[0]

        def do_step(k, widen, ends):
            has = [0 <= k - z < chunks and z < pairs - 1 for z in range(pairs)]
            ins = [place]
            for d in range(2):
                ins += [totals[k - z][d] for z in range(pairs) if has[z]]
                ins += [totals[k - z][3] for z in range(pairs) if has[z]]
            if k > 0:
                ins += [got[0][-1], got[1][-1]]
            outs = [sds(pair_shape), sds(pair_shape), token_shape]
            pieces = [] if widen is None else pieces_of(widen)
            if widen is not None:
                ins += [value_block(widen), cot_block(widen), *pieces]
                outs.append(wide_shape(len(pieces)))
            return run(
                step_body(has, k == 0, widen is not None, len(pieces), len(ends)),
                ins + [Far(e) for e in ends],
                outs,
            )

        def do_first_step(ends):
            s, k = order[0]
            out = run(
                first_step_body(pairs, k * group_heads, heads, head_width, len(ends)),
                [place, packs[s], far_row, *own_states, *map(Far, ends)],
                [sds(pair_shape), sds(pair_shape), token_shape, sds(pair_shape), sds(pair_shape),
                 sds((8, chunk))],
            )
            totals[0] = (out[3], out[4], None, out[5])
            columns["own"] = own_states
            return out

        def do_exchange(token):
            last = pairs - 1
            ups = [got[(z + 1) % 2][max(z - 1, 0)] for z in range(pairs)]
            downs = [got[(last - z) % 2][max(z - 1, 0)] for z in range(pairs)]
            sends = run(
                exchange_body(len(ups), len(downs)),
                [place, *columns["own"], totals[0][3], Far(token), *map(Far, ups), *map(Far, downs)],
                [sds(pair_shape), sds(pair_shape)],
                scratch=work(),
            )
            columns["far"] = [swap(x) for x in sends]

        def pieces_of(c):
            return [Block(packs[1], (length, LANES), (0, riders[c]))] if c in riders else []

        def do_widen(c, token):
            pieces = pieces_of(c)
            return run(
                widen_body, [value_block(c), cot_block(c), Far(token), *pieces], [wide_shape(len(pieces))]
            )[0]

        far[1] = swap(lax.optimization_barrier((wide, far_row))[0])
        turns = (0, 1, groups, groups + 1)
        ends = [do_turn(turns, 0, far_row)]
        halfway = None
        share = None
        for k in range(steps):
            queue = k + 2 if 0 < k < chunks - 2 else None
            made = do_first_step(ends) if k == 0 else do_step(k, queue, ends)
            token = made[2]
            for d in range(2):
                got[d].append(lax.ppermute(made[d], "seq", edges[d]))
            ends = []
            if k == 0:
                v_more = do_values(list(range(1, groups - 1)), token)
                far[2] = swap(do_widen(2, token))
            if queue is not None:
                far[queue] = swap(made[3])
            if k + 1 < chunks:
                ends.append(do_pair(k + 1, token))
            if k == max(chunks - 2, pairs - 1):
                do_exchange(far[chunks - 1])
            if k == steps - 3:
                ends += columns["far"]
            for cs in {1: [turns[1:3]], 2: [(turns[3], 0)]}.get(k, ()):
                ends.append(do_turn(cs, 1, token))
            for c in {2: (2,), 3: (3,), 4: (6,), 5: (7,)}.get(k, ()):
                ends.append(do_within(c, token))
            c = k - pairs + 1
            if c > 0:
                ends.append(do_chunk(c, token))
            if c == groups - 2:
                halfway = do_partial(list(range(1, groups - 1)), token)
                ends.append(halfway)
            if c == groups:
                share = do_term(0, do_partial([groups - 1, groups], token, halfway))
                ends.append(share[0])
            if c == groups + 1:
                ends.append(do_chunk(0, token))
            if c == groups + 2:
                grads[0] = do_finish(0, share)
                halfway = do_partial([groups + 1, 0, groups + 2], token)
        grads[1] = do_finish(1, do_last(chunks - 1, halfway, halfway))
        outs = [
            jnp.concatenate([post[order.index((s, k))][0] for k in range(groups)], axis=1)
            for s in range(2)
        ]
        return (outs[0], outs[1], grads[0], grads[1])

    return body


def solution(mesh):
    rows = P(("dp", "seq"), None)
    both = P(("dp", "seq"), "chan")
    in_specs = (
        rows, rows, P(None, "chan"), P(), P(None, "chan"),
        P("chan"), P("chan"), P("chan"), both, both,
    )
    return jax.shard_map(
        local(mesh.shape["seq"], mesh.shape["chan"]),
        mesh=mesh,
        in_specs=in_specs,
        out_specs=(both,) * 4,
        check_vma=False,
    )
```

```python
import jax
import jax.numpy as jnp
from jax import lax
from jax.experimental import pallas as pl
from jax.experimental.pallas import tpu as pltpu
from jax.sharding import PartitionSpec as P

BF = jnp.bfloat16
F32 = jnp.float32
LANES = 128


def mm(a, b, ca=1, cb=0):
    return lax.dot_general(a, b, (((ca,), (cb,)), ((), ())), preferred_element_type=F32)


def halves(x):
    high = x.astype(BF)
    return high, (x - high.astype(F32)).astype(BF)


def mm_exact(a, b, ca=1, cb=0):
    first, rest = b.astype(BF), None
    rest = b - first.astype(F32)
    second = rest.astype(BF)
    third = (rest - second.astype(F32)).astype(BF)
    return mm(a, first, ca, cb) + mm(a, second, ca, cb) + mm(a, third, ca, cb)


def iotas(rows, columns):
    return (
        lax.broadcasted_iota(jnp.int32, (rows, columns), 0),
        lax.broadcasted_iota(jnp.int32, (rows, columns), 1),
    )


def spread(weights, base, width, head_width):
    heads = weights[0].shape[1]
    row, channel = iotas(2 * heads, width)
    start = (jnp.where(row >= heads, row - heads, row) - base) * head_width
    pick = ((channel >= start) & (channel < start + head_width)).astype(BF)
    stacked = jnp.concatenate(weights, axis=0) if len(weights) > 1 else weights[0]
    out = mm(jnp.concatenate(halves(stacked), axis=1), pick)
    result, at = [], 0
    for w in weights:
        result.append(out[at : at + w.shape[0]])
        at += w.shape[0]
    return result


def spread_rows(rows, base, width, head_width):
    heads = rows[0].shape[1]
    wide = spread([jnp.broadcast_to(r, (8, heads)) for r in rows], base, width, head_width)
    return [w[0:1] for w in wide]


def gather_heads(parts, base, head_width):
    width = parts[0].shape[1]
    channel, head = iotas(width, LANES)
    start = (head - base) * head_width
    pick = ((channel >= start) & (channel < start + head_width)).astype(BF)
    out = mm(jnp.concatenate([x.astype(BF) for x in parts], axis=0), pick)
    result, at = [], 0
    for x in parts:
        result.append(out[at : at + x.shape[0]])
        at += x.shape[0]
    return result


def reversal(size):
    i, j = iotas(size, size)
    return (i + j == size - 1).astype(BF)


def flip_block(size):
    return 256 if size % 256 == 0 else 128


def sds(shape, dtype=F32):
    return jax.ShapeDtypeStruct(shape, dtype)


class Block:
    def __init__(self, array, shape, index):
        self.array, self.shape, self.index = array, shape, index

    def view(self, ref):
        if self.shape == self.array.shape:
            return ref
        return ref.at[tuple(pl.ds(i * b, b) for i, b in zip(self.index, self.shape))]


class Copied:
    def __init__(self, item):
        self.item = item if isinstance(item, Block) else Block(item, item.shape, (0,) * item.ndim)


class Far:
    def __init__(self, array):
        self.array = array


def run(body, ins, outs, scratch=(), limit=16, stored=()):
    specs, arrays, copied = [], [], []
    for item in ins:
        if isinstance(item, Far):
            specs.append(pl.BlockSpec(memory_space=pl.ANY))
            arrays.append(item.array)
        elif isinstance(item, Copied):
            specs.append(pl.BlockSpec(memory_space=pltpu.HBM))
            arrays.append(item.item.array)
            copied.append(item.item)
        elif isinstance(item, Block):
            specs.append(pl.BlockSpec(memory_space=pltpu.VMEM))
            arrays.append(item.array)
        else:
            space = pltpu.SMEM if item.dtype == jnp.int32 else pltpu.VMEM
            specs.append(pl.BlockSpec(memory_space=space))
            arrays.append(item)
    out_specs = [
        pl.BlockSpec(memory_space=pltpu.HBM if n in stored else pltpu.VMEM)
        for n in range(len(outs))
    ]
    holds = [pltpu.VMEM(q.shape, q.array.dtype) for q in copied]
    holds += [pltpu.VMEM(outs[n].shape, outs[n].dtype) for n in stored]
    sems = [pltpu.SemaphoreType.DMA((max(len(holds), 1),))]

    def kernel(*refs):
        refs = list(refs)
        take = lambda n: [refs.pop(0) for _ in range(n)]
        sources, targets = take(len(ins)), take(len(outs))
        held, (sem,) = take(len(holds)), take(1)
        args, copies = [], []
        for ref, item in zip(sources, ins):
            if isinstance(item, Copied):
                n = len(copies)
                copies.append(pltpu.make_async_copy(item.item.view(ref), held[n], sem.at[n]))
                copies[-1].start()
                ref = held[n]
            elif isinstance(item, Block):
                ref = item.view(ref)
            args.append(ref)
        back = []
        for n, ref in enumerate(targets):
            if n in stored:
                k = len(copied) + stored.index(n)
                back.append(pltpu.make_async_copy(held[k], ref, sem.at[k]))
                ref = held[k]
            args.append(ref)
        waits = {"waits": [c.wait for c in copies]} if copies else {}
        body(*args, *refs, **waits)
        for copy in back:
            copy.start()
        for copy in back:
            copy.wait()

    return pl.pallas_call(
        kernel,
        in_specs=specs,
        out_specs=out_specs,
        out_shape=outs,
        scratch_shapes=holds + sems + list(scratch),
        compiler_params=pltpu.CompilerParams(vmem_limit_bytes=limit * 1024 * 1024),
        cost_estimate=pl.CostEstimate(flops=0, bytes_accessed=1024, transcendentals=0),
    )(*arrays)


def start_body(
    hidden, other, select, step, bias, rate, weight, cot,
    source, pack0, pack1, row, v_out, wide, waits,
):
    for wait in waits[0:2]:
        wait()
    length, width = hidden.shape
    heads = bias.shape[1]
    source[0:length, :] = hidden[...]
    block = flip_block(width)
    turn = reversal(block)
    for j in range(width // block):
        source[length : 2 * length, j * block : (j + 1) * block] = mm(
            other[:, width - (j + 1) * block : width - j * block], turn
        ).astype(BF)
    for wait in waits[2:6]:
        wait()
    keys = mm(source[...], select[...]).astype(BF).astype(F32)
    state = keys.shape[1] // 2
    raw = mm(source[...], step[...], 1, 1) + bias[...]
    dt = jnp.maximum(raw, 0.0) + jnp.log1p(jnp.exp(-jnp.abs(raw)))
    rise = jax.nn.sigmoid(raw)
    i, j = iotas(length, length)
    lower = (i >= j).astype(BF)
    for s, pack in enumerate((pack0, pack1)):
        rows = slice(s * length, (s + 1) * length)
        drop = dt[rows] * rate[...]
        total = mm_exact(lower, drop)
        pack[...] = jnp.zeros(pack.shape, F32)
        pack[:, 0 : 2 * state] = keys[rows]
        at = 2 * state
        for part in (dt[rows], total, total - drop, rise[rows]):
            pack[:, at : at + heads] = part
            at += heads
    row[...] = jnp.zeros(row.shape, F32)
    row[0:1, 0:heads] = jnp.exp(
        -pack1[length - 1 : length, 2 * state + heads : 2 * state + 2 * heads]
    )
    for wait in waits[6:]:
        wait()
    for at in columns_of(weight.shape[1]):
        piece = mm(source[...], weight[:, at]).astype(BF)
        for s in range(2):
            v_out[0, s, :, at] = piece[s * length : (s + 1) * length]
        wide[0:length, at] = piece[0:length].astype(F32)
    wide[length : 2 * length, :] = cot[...].astype(F32)
    for n in range(3):
        at = 2 * length + n * piece_rows(length, wide.shape[1])
        put_piece(wide, at, pack0[:, n * LANES : (n + 1) * LANES])


def columns_of(width):
    block = min(256, width)
    return [slice(k * block, (k + 1) * block) for k in range(width // block)]


def values_body(source, token, *rest):
    weights, v_out = rest[:-1], rest[-1]
    length = v_out.shape[2]
    for n, weight in enumerate(weights):
        for at in columns_of(weight.shape[1]):
            piece = mm(source[...], weight[:, at]).astype(BF)
            for s in range(2):
                v_out[n, s, :, at] = piece[s * length : (s + 1) * length]


class Pack:
    def __init__(self, write, read, stats, heads):
        self.write, self.read = write, read
        self.dt = stats[:, 0:heads]
        self.total = stats[:, heads : 2 * heads]
        self.before = stats[:, 2 * heads : 3 * heads]
        last = self.total.shape[0]
        self.whole = self.total[last - 1 : last, :]
        self.from_start = jnp.exp(-self.total)
        self.from_end = jnp.exp(self.before - self.whole)
        self.to_end = jnp.exp(self.total - self.whole)
        self.to_start = jnp.exp(-self.before)
        self.through = jnp.exp(-self.whole)


def own_pack(ref, heads):
    return Pack(*[ref[:, n * LANES : (n + 1) * LANES] for n in range(3)], heads)


def piece_rows(length, width):
    return length // (width // LANES)


def put_piece(ref, row, piece):
    count = piece_rows(piece.shape[0], ref.shape[1])
    for b in range(ref.shape[1] // LANES):
        ref[row : row + count, b * LANES : (b + 1) * LANES] = piece[b * count : (b + 1) * count]


def get_piece(ref, row, length):
    count = piece_rows(length, ref.shape[1])
    return jnp.concatenate(
        [
            ref[row : row + count, b * LANES : (b + 1) * LANES]
            for b in range(ref.shape[1] // LANES)
        ],
        axis=0,
    )


def pair_body(base, heads, head_width, piece_at):
    def body(place, v_own, g_own, x_far, far0, far1, far2, own_ref, token, up, down, near, keep):
        first = place[0] == 0
        length, width = g_own.shape
        own = own_pack(own_ref, heads)
        far = Pack(*[get_piece(f, at, length) for f, at in zip((far0, far1, far2), piece_at)], heads)
        own_row, far_row = own.through, far.through
        rows = spread_rows([own_row * far_row, far_row], base, width, head_width)
        keep[...] = jnp.zeros(keep.shape, F32)
        keep[0:1, :] = rows[0]
        keep[1:2, :] = rows[1]
        own_up, own_down = jnp.where(first, far_row, 1.0), jnp.where(first, 1.0, far_row)
        far_up, far_down = jnp.where(first, 1.0, own_row), jnp.where(first, own_row, 1.0)
        for kind in range(2):
            rows = slice(kind * LANES, (kind + 1) * LANES)
            if kind == 0:
                keys = (own.write, far.write)
                ups = (own.dt * own.to_end, far.dt * far.to_end)
                downs = (own.dt * own.to_start, far.dt * far.to_start)
            else:
                keys = (own.read, far.read)
                ups = (own.from_end, far.from_end)
                downs = (own.from_start, far.from_start)
            x_own = (v_own if kind == 0 else g_own)[...].reshape(length, width).astype(F32)
            x_other = x_far[kind * length : (kind + 1) * length, :]
            w = spread(
                [ups[0] * own_up, ups[1] * far_up, downs[0] * own_down, downs[1] * far_down,
                 jnp.where(first, downs[1], ups[1])],
                base, width, head_width,
            )
            key = jnp.concatenate(keys, axis=0).astype(BF)
            both = lambda a, b: jnp.concatenate([(a * x_own).astype(BF), (b * x_other).astype(BF)], axis=0)
            up[rows, :] = mm(key, both(w[0], w[1]), 0, 0)
            down[rows, :] = mm(key, both(w[2], w[3]), 0, 0)
            near[rows, :] = mm(keys[1].astype(BF), (w[4] * x_other).astype(BF), 0, 0)

    return body


def column_body(base, heads, head_width):
    def body(own_ref, source, weight, g_own, v_out, own_up, own_down, waits):
        length, width = g_own.shape
        own = own_pack(own_ref, heads)
        w_values = spread([own.dt * own.to_end, own.dt * own.to_start], base, width, head_width)
        w_grads = spread([own.from_end, own.from_start], base, width, head_width)
        write, read = own.write.astype(BF), own.read.astype(BF)
        waits[0]()
        for at in columns_of(width):
            piece = mm(source[...], weight[:, at]).astype(BF)
            for s in range(2):
                v_out[0, s, :, at] = piece[s * length : (s + 1) * length]
            v, g = piece[length:].astype(F32), g_own[:, at].astype(F32)
            for out, n in ((own_up, 0), (own_down, 1)):
                out[0:LANES, at] = mm(write, (w_values[n][:, at] * v).astype(BF), 0, 0)
                out[LANES : 2 * LANES, at] = mm(read, (w_grads[n][:, at] * g).astype(BF), 0, 0)

    return body


def column_totals(place, own_ref, far_row_ref, base, heads, head_width, owns, totals, keep):
    first = place[0] == 0
    width = keep.shape[1]
    own = own_pack(own_ref, heads)
    far_row = far_row_ref[0:1, 0:heads]
    rows = spread_rows([own.through * far_row, far_row, own.through], base, width, head_width)
    keep[...] = jnp.zeros(keep.shape, F32)
    for n, row in enumerate(rows):
        keep[n : n + 1, :] = row
    totals[0][...] = jnp.where(first, rows[1], 1.0) * owns[0][...]
    totals[1][...] = jnp.where(first, 1.0, rows[1]) * owns[1][...]


def first_step_body(pairs, base, heads, head_width, tokens):
    def body(place, own_ref, far_row_ref, own_up, own_down, *rest):
        send_a, send_b, token, up, down, keep = rest[tokens:]
        column_totals(
            place, own_ref, far_row_ref, base, heads, head_width, (own_up, own_down), (up, down), keep
        )
        token[...] = jnp.zeros(token.shape, F32)
        sends = (send_a, send_b)
        for d, total in enumerate((up, down)):
            spot = place[1] if d == 0 else pairs - 1 - place[1]
            for n in range(pairs):
                z = n if d == 0 else pairs - 1 - n
                send = sends[(z + d) % 2]

                @pl.when(spot == n)
                def _():
                    send[...] = total[...] if n == 0 else jnp.zeros(send.shape, F32)

    return body


def exchange_body(ups, downs):
    def body(place, own_up, own_down, keep, token, *rest):
        up_in, down_in = rest[0:ups], rest[ups : ups + downs]
        up_out, down_out, bufs, sems = rest[ups + downs :]
        up_spot, down_spot = place[1], len(up_in) - 1 - place[1]
        fetch_start(up_in, up_spot, bufs.at[0], sems.at[0])
        fetch_start(down_in, down_spot, bufs.at[1], sems.at[1])
        fetch_wait(up_in, up_spot, bufs.at[0], sems.at[0])
        fetch_wait(down_in, down_spot, bufs.at[1], sems.at[1])
        first = place[0] == 0
        row = keep[2:3, :]
        up_out[...] = jnp.where(first, row * bufs[0] + own_up[...], bufs[0])
        down_out[...] = jnp.where(first, bufs[1], row * bufs[1] + own_down[...])

    return body


def fetch_start(options, index, target, sem):
    for z, option in enumerate(options):
        if option is not None:

            @pl.when(index == z)
            def _():
                pltpu.make_async_copy(option, target, sem).start()


def fetch_wait(options, index, target, sem):
    for z, option in enumerate(options):
        if option is not None:

            @pl.when(index == z)
            def _():
                pltpu.make_async_copy(option, target, sem).wait()


def step_body(has, first_step, widen, pieces, tokens):
    pairs = len(has)

    def body(place, *rest):
        rest = list(rest)
        take = lambda n: [rest.pop(0) for _ in range(n)]
        sides = []
        for d in range(2):
            totals = [take(1)[0] if h else None for h in has]
            keeps = [take(1)[0] if h else None for h in has]
            sides.append((totals, keeps))
        got = None if first_step else take(2)
        chunk = take(2) if widen else None
        piece_refs = take(pieces)
        take(tokens)
        sends = take(2)
        token = take(1)[0]
        spots = (place[1], pairs - 1 - place[1])
        for d, (totals, keeps) in enumerate(sides):
            for n in range(pairs):
                z = n if d == 0 else pairs - 1 - n
                send = sends[(z + d) % 2]

                @pl.when(spots[d] == n)
                def _():
                    if not has[n]:
                        send[...] = jnp.zeros(send.shape, F32)
                    elif got is None or n == 0:
                        send[...] = totals[n][...]
                    else:
                        send[...] = totals[n][...] + keeps[n][0:1, :] * got[(z + 1 + d) % 2][...]

        token[...] = jnp.zeros(token.shape, F32)
        if widen:
            put_chunk(take(1)[0], *chunk, piece_refs)

    return body


def within_body(base, heads, head_width):
    def body(own_ref, v_ref, g_ref, rate, token, y_out, x_out, keys_out, steps_out, cols_s):
        own = own_pack(own_ref, heads)
        length, width = g_ref.shape
        write, read = own.write.astype(BF), own.read.astype(BF)
        scores = mm(read, write, 1, 1)
        i, j = iotas(length, length)
        low = i > j
        high = i < j
        doubled = jnp.where(i == j, 2.0, 1.0).astype(F32)
        scores2 = scores * doubled
        turned = own_ref[:, 2 * LANES : 3 * LANES].T
        lane = lax.broadcasted_iota(jnp.int32, (length, LANES), 1)
        d_scores = jnp.zeros((length, length), F32)
        out_low = jnp.zeros((length, LANES), F32)
        out_high = jnp.zeros((length, LANES), F32)
        cols_s[...] = jnp.zeros(cols_s.shape, F32)
        v_all = v_ref[...].reshape(length, width)
        per = LANES // head_width
        for n in range(width // LANES):
            at = slice(n * LANES, (n + 1) * LANES)
            v, g = v_all[:, at], g_ref[:, at]
            mine = [(lane >= m * head_width) & (lane < (m + 1) * head_width) for m in range(per)]
            v_heads = jnp.concatenate([jnp.where(x, v, jnp.zeros_like(v)) for x in mine], axis=0)
            g_heads = jnp.concatenate([jnp.where(x, g, jnp.zeros_like(g)) for x in mine], axis=0)
            products = mm(g_heads, v, 1, 1)
            plains, steppeds = [], []
            for m in range(per):
                h = base + n * per + m
                c_col = own.total[:, h : h + 1]
                e_col = own.before[:, h : h + 1]
                dt_row = turned[h : h + 1, :]
                c_row = turned[heads + h : heads + h + 1, :]
                e_row = turned[2 * heads + h : 2 * heads + h + 1, :]
                decay = jnp.exp(jnp.where(low, c_row - c_col, e_col - e_row))
                plain = decay * scores2
                plains.append(plain.astype(BF))
                steppeds.append((plain * dt_row).astype(BF))
                inner = decay * dt_row * products[m * length : (m + 1) * length]
                d_scores = d_scores + inner
                flow = inner * scores
                flow_low = jnp.where(low, flow, 0.0)
                flow_high = jnp.where(high, flow, 0.0)
                out_low = jnp.where(lane == h, jnp.sum(flow_low, 1, keepdims=True), out_low)
                out_high = jnp.where(lane == h, jnp.sum(flow_high, 1, keepdims=True), out_high)
                cols_s[0, h : h + 1, :] = jnp.sum(flow_low, 0, keepdims=True)
                cols_s[1, h : h + 1, :] = jnp.sum(flow_high, 0, keepdims=True)
            y_out[:, at] = mm(jnp.concatenate(steppeds, axis=1), v_heads)
            x_out[:, at] = mm(jnp.concatenate(plains, axis=0), g_heads, 0, 0)
        d_scores = (d_scores * doubled).astype(BF)
        keys_out[:, 0:LANES] = mm(d_scores, read, 0, 0)
        keys_out[:, LANES : 2 * LANES] = mm(d_scores, write)
        net_low = out_low - cols_s[0].T
        net_high = out_high - cols_s[1].T
        at_or_after = (j >= i).astype(BF)
        after = (j > i).astype(BF)
        steps_out[...] = -rate[...] * (mm_exact(at_or_after, net_low) - mm_exact(after, net_high))

    return body


def post_body(base, heads, head_width, ups, downs, columns=False):
    def body(
        place, own_ref, v_ref, g_ref, yw, xw, keys_w, steps_w, near, keep, skip, rate, token, *rest
    ):
        up_in, down_in = rest[0:ups], rest[ups : ups + downs]
        mixed, dv_out, keys_out, steps_out, bufs, sems = rest[ups + downs :]
        up_spot, down_spot = place[1], len(up_in) - 1 - place[1]
        fetch_start(up_in, up_spot, bufs.at[0], sems.at[0])
        fetch_start(down_in, down_spot, bufs.at[1], sems.at[1])
        first = place[0] == 0
        own = own_pack(own_ref, heads)
        length, width = g_ref.shape
        far_row = keep[1:2, :]
        own_row, gain = spread_rows([own.through, skip[...]], base, width, head_width)
        up_row = jnp.where(first, 1.0, far_row)
        down_row = jnp.where(first, far_row, 1.0)
        dt, from_start, from_end, to_end, to_start = spread(
            [own.dt, own.from_start, own.from_end, own.to_end, own.to_start],
            base, width, head_width,
        )
        write, read = own.write.astype(BF), own.read.astype(BF)
        v = v_ref[...].reshape(length, width).astype(F32)
        g = g_ref[...].astype(F32)
        fetch_wait(up_in, up_spot, bufs.at[0], sems.at[0])
        fetch_wait(down_in, down_spot, bufs.at[1], sems.at[1])
        if columns:
            up = up_row * bufs[0] + near[0][...]
            down = down_row * bufs[1] + near[1][...]
        else:
            up = up_row * bufs[0] + jnp.where(first, 0.0, near[...])
            down = down_row * bufs[1] + jnp.where(first, near[...], 0.0)
        p, ab = up[0:LANES], up[LANES : 2 * LANES]
        q, af = down[0:LANES], down[LANES : 2 * LANES]
        crossing = jnp.sum(p * af + q * ab, axis=0, keepdims=True)
        p, q, af, ab = p.astype(BF), q.astype(BF), af.astype(BF), ab.astype(BF)
        y_p = from_start * mm(read, p)
        y_q = from_end * mm(read, q)
        x_f = to_end * mm(write, af)
        x_b = to_start * mm(write, ab)
        mixed[...] = (yw[...] + y_p + y_q + gain * v).astype(BF)
        x = xw[...] + x_f + x_b
        dv_out[...] = (dt * x + gain * g).astype(BF)
        dtv = dt * v
        keys_out[:, 0:LANES] = (
            keys_w[:, 0:LANES]
            + mm((to_end * dtv).astype(BF), af, 1, 1)
            + mm((to_start * dtv).astype(BF), ab, 1, 1)
        )
        keys_out[:, LANES : 2 * LANES] = (
            keys_w[:, LANES : 2 * LANES]
            + mm((from_start * g).astype(BF), p, 1, 1)
            + mm((from_end * g).astype(BF), q, 1, 1)
        )
        lane = lax.broadcasted_iota(jnp.int32, (length, LANES), 1)
        steps = jnp.where(lane < heads, own_ref[:, 2 * LANES : 3 * LANES], 0.0)
        direct, a_p, a_q, b_f, b_b, through = gather_heads(
            [v * x, g * y_p, g * y_q, v * x_f, v * x_b, jnp.broadcast_to(crossing * own_row, (8, width))],
            base, head_width,
        )
        i, j = iotas(length, length)
        masks = jnp.concatenate([j >= i, j <= i, j < i, j > i], axis=1).astype(F32).astype(BF)
        high, low = halves(jnp.concatenate([a_p, a_q, b_f * steps, b_b * steps], axis=0))
        flow = mm(masks, high) + mm(masks, low) + through[0:1]
        steps_out[...] = steps_w[...] + direct - rate[...] * flow

    return body


class Either:
    def __init__(self, choice, a, b):
        self.choice, self.a, self.b = choice, a, b

    def __getitem__(self, index):
        return jnp.where(self.choice, self.a[index], self.b[index])


def either_within(post):
    def body(place, own_ref, v_ref, g_ref, *rest):
        merged = [Either(place[3] == 0, a, b) for a, b in zip(rest[0:4], rest[4:8])]
        post(place, own_ref, v_ref, g_ref, *merged, *rest[8:])

    return body


def split_body(within, post, columns):
    def body(place, own_ref, v_ref, g_ref, *rest):
        bufs, sems, yw, xw, keys_w, steps_w, cols_s = rest[-7:]
        before, rest = rest[0:4], rest[4:]
        nears = 2 if columns else 1
        near = rest[0:2] if columns else rest[0]
        keep, skip, rate, token, *rest = rest[nears:]

        @pl.when(place[3] == 1)
        def _():
            within(own_ref, v_ref, g_ref, rate, token, yw, xw, keys_w, steps_w, cols_s)

        merged = [Either(place[3] == 0, a, b) for a, b in zip(before, (yw, xw, keys_w, steps_w))]
        post(place, own_ref, v_ref, g_ref, *merged, near, keep, skip, rate, token, *rest[:-5])

    return body


def turn_body(works, strands, turn):
    def body(place, pack0, pack1, rate, *rest):
        count = len(works)
        blocks, token = rest[0 : 2 * count], rest[2 * count]
        outs, flows = rest[2 * count + 1 : -1], rest[-1]

        @pl.when(place[3] == turn)
        def _():
            for n, work in enumerate(works):
                work(
                    (pack0, pack1)[strands[n]], blocks[2 * n], blocks[2 * n + 1], rate, token,
                    *outs[4 * n : 4 * n + 4], flows,
                )

    return body


def chunk_body(within, post, columns):
    def body(place, own_ref, v_ref, g_ref, *rest):
        nears = 2 if columns else 1
        near = rest[0:2] if columns else rest[0]
        keep, skip, rate, token, *rest = rest[nears:]
        bufs, sems, yw, xw, keys_w, steps_w, cols_s = rest[-7:]
        within(own_ref, v_ref, g_ref, rate, token, yw, xw, keys_w, steps_w, cols_s)
        post(
            place, own_ref, v_ref, g_ref, yw, xw, keys_w, steps_w, near, keep, skip, rate, token,
            *rest[:-5],
        )

    return body


def partial_body(groups, more):
    def body(token, *rest):
        dvs, weights, rest = rest[0:groups], rest[groups : 2 * groups], rest[2 * groups :]
        out = rest[-1]
        for at in columns_of(out.shape[1]):
            total = rest[0][:, at] if more else 0.0
            for dv, weight in zip(dvs, weights):
                total = total + mm(dv[...], weight[at, :], 1, 1)
            out[:, at] = total

    return body


def term_body(groups, tails, heads, parts, swap):
    def body(place, own_ref, select, step, before, *rest):
        dvs, weights = rest[0:tails], rest[tails : 2 * tails]
        rest = rest[2 * tails :]
        keys, steps = rest[0:groups], rest[groups : 2 * groups]
        outs = rest[2 * groups :]
        d_keys, d_steps = keys[0][...], steps[0][...]
        for a, b in zip(keys[1:], steps[1:]):
            d_keys = d_keys + a[...]
            d_steps = d_steps + b[...]
        d_raw = d_steps[:, 0:heads] * own_ref[:, 2 * LANES + 3 * heads : 2 * LANES + 4 * heads]
        keys_high, keys_low = halves(d_keys)
        raw_high, raw_low = halves(d_raw)
        width = select.shape[0]
        block = width // parts
        tiles = []
        for b in range(parts):
            rows = slice(b * block, (b + 1) * block)
            total = before[:, rows]
            total = total + mm(keys_high, select[rows, :], 1, 1) + mm(keys_low, select[rows, :], 1, 1)
            total = total + mm(raw_high, step[:, rows]) + mm(raw_low, step[:, rows])
            for k in range(tails):
                total = total + mm(dvs[k][...], weights[k][rows, :], 1, 1)
            tiles.append(total)
        if swap:
            tiles = tiles[::-1]
        if parts == 2:
            first = place[2] == 0
            outs[0][...] = jnp.where(first, tiles[0], tiles[1])
            outs[1][...] = jnp.where(first, tiles[1], tiles[0])
        else:
            for b in range(parts):
                outs[0][:, b * block : (b + 1) * block] = tiles[b]

    return body


def tile_body(groups, tails, heads, swap, keep):
    def body(place, own_ref, select, step, before, *rest):
        dvs, weights = rest[0:tails], rest[tails : 2 * tails]
        rest = rest[2 * tails :]
        keys, steps, out = rest[0:groups], rest[groups : 2 * groups], rest[-1]
        d_keys, d_steps = keys[0][...], steps[0][...]
        for a, b in zip(keys[1:], steps[1:]):
            d_keys = d_keys + a[...]
            d_steps = d_steps + b[...]
        d_raw = d_steps[:, 0:heads] * own_ref[:, 2 * LANES + 3 * heads : 2 * LANES + 4 * heads]
        keys_high, keys_low = halves(d_keys)
        raw_high, raw_low = halves(d_raw)
        block = out.shape[1]
        mine = place[2] if keep != swap else 1 - place[2]
        rows = pl.ds(pl.multiple_of(mine * block, block), block)
        total = before[:, rows]
        total = total + mm(keys_high, select[rows, :], 1, 1) + mm(keys_low, select[rows, :], 1, 1)
        total = total + mm(raw_high, step[:, rows]) + mm(raw_low, step[:, rows])
        for dv, weight in zip(dvs, weights):
            total = total + mm(dv[...], weight[rows, :], 1, 1)
        out[...] = total

    return body


def last_body(work, term, work_ins):
    def body(place, *rest):
        rest = list(rest)
        take = lambda n: [rest.pop(0) for _ in range(n)]
        for_work = take(work_ins)
        select, step, before, weight = take(4)
        others = take(len(rest) - 7)
        half = len(others) // 2
        mixed, dv, keys, steps, out = take(5)
        bufs, sems = take(2)
        work(place, *for_work, mixed, dv, keys, steps, bufs, sems)
        term(
            place, for_work[0], select, step, before, dv, weight,
            *others[:half], keys, *others[half:], steps, out,
        )

    return body


def finish_body(flip):
    def body(a, b, out):
        total = (a[...] + b[...]).astype(BF)
        if not flip:
            out[...] = total
            return
        width = total.shape[1]
        block = flip_block(width)
        turn = reversal(block)
        for j in range(width // block):
            out[:, j * block : (j + 1) * block] = mm(
                total[:, width - (j + 1) * block : width - j * block], turn
            ).astype(BF)

    return body


def put_chunk(wide, v_ref, g_ref, pieces):
    length, width = g_ref.shape
    wide[0:length, :] = v_ref[...].reshape(length, width).astype(F32)
    wide[length : 2 * length, :] = g_ref[...].astype(F32)
    for n, piece in enumerate(pieces):
        put_piece(wide, 2 * length + n * piece_rows(length, width), piece[...])


def widen_body(v_ref, g_ref, token, *rest):
    put_chunk(rest[-1], v_ref, g_ref, rest[:-1])


def local(shards, parts):
    pairs = shards // 2

    def body(
        hidden, complement, inner_weight, select_weight, step_weight, step_bias, decay_rate,
        skip_gain, cotangent, complement_cotangent,
    ):
        length, width = hidden.shape
        inner = inner_weight.shape[1]
        heads = step_bias.shape[0]
        head_width = inner // heads
        groups = 4
        chunk = inner // groups
        group_heads = heads // groups
        seq = lax.axis_index("seq")
        place = jnp.stack(
            [seq % 2, seq // 2, lax.axis_index("chan"), lax.axis_index("dp")]
        ).astype(jnp.int32)
        bias = step_bias.reshape(1, heads)
        rate = decay_rate.reshape(1, heads)
        rate_row = jnp.pad(rate, ((0, 0), (0, LANES - heads)))
        gain = skip_gain.reshape(1, heads)
        step_rows = step_weight.T
        cots = (cotangent, complement_cotangent)
        swap_pairs = [(a, a ^ 1) for a in range(shards)]
        edges = []
        for start in range(2):
            meets = [(z, z + 1) for z in range(start, pairs - 1, 2)]
            paired = sum(meets, ())
            meets += [(b, a) for a, b in meets] + [(z, z) for z in range(pairs) if z not in paired]
            edges.append([(2 * a + y, 2 * b + y) for a, b in meets for y in range(2)])
        swap = lambda x: lax.ppermute(x, "seq", swap_pairs)
        pack_shape = (length, 3 * LANES)
        pair_shape = (2 * LANES, chunk)
        wide_shape = lambda pieces: sds((2 * length + pieces * piece_rows(length, chunk), chunk))
        token_shape = sds((8, LANES))
        work = lambda: [pltpu.VMEM((2,) + pair_shape, F32), pltpu.SemaphoreType.DMA((2,))]
        order = [(1, groups - 1)] + [(0, k) for k in range(groups)] + [(1, k) for k in range(groups - 1)]
        chunks = len(order)

        source, pack0, pack1, row, v_zero, wide = run(
            start_body,
            [*map(Copied, (hidden, complement, select_weight, step_rows, bias, rate)),
             Copied(Block(inner_weight, (width, chunk), (0, 0))),
             Copied(Block(cots[0], (length, chunk), (0, 0)))],
            [sds((2 * length, width), BF), sds(pack_shape), sds(pack_shape), token_shape,
             sds((1, 2, length, chunk), BF), wide_shape(3)],
            limit=57,
        )
        packs = (pack0, pack1)
        far_row = swap(row)

        def weight_of(k):
            return Block(inner_weight, (width, chunk), (0, k))

        def do_values(ks, token):
            return run(
                values_body,
                [source, Far(token), *map(weight_of, ks)],
                [sds((len(ks), 2, length, chunk), BF)],
            )[0]

        v_last, *own_states = run(
            column_body((groups - 1) * group_heads, heads, head_width),
            [pack1, source, Copied(weight_of(groups - 1)),
             Block(cots[1], (length, chunk), (0, groups - 1))],
            [sds((1, 2, length, chunk), BF), sds(pair_shape), sds(pair_shape)],
            limit=48,
        )
        v_more = None

        def value_block(c):
            s, k = order[c]
            array, n = {0: (v_zero, 0), groups - 1: (v_last, 0)}.get(k, (v_more, k - 1))
            return Block(array, (1, 1, length, chunk), (n, s, 0, 0))

        def cot_block(c):
            s, k = order[c]
            return Block(cots[s], (length, chunk), (0, k))

        def weight_block(c):
            return weight_of(order[c][1])

        far = {}
        totals, within, post = {}, {}, {}
        got = ([], [])
        grads = [None, None]
        riders = {2 + n: n for n in range(3)}
        columns = {}
        steps = chunks + pairs - 2

        def do_pair(c, token):
            s, k = order[c]
            rows = piece_rows(length, chunk)
            if s == 0:
                pieces, piece_at = [far[1]] * 3, [2 * length + n * rows for n in range(3)]
            else:
                pieces, piece_at = [far[r] for r in riders], [2 * length] * 3
            totals[c] = run(
                pair_body(k * group_heads, heads, head_width, piece_at),
                [place, value_block(c), cot_block(c), far[c], *pieces, packs[s], Far(token)],
                [sds(pair_shape), sds(pair_shape), sds(pair_shape), sds((8, chunk))],
            )
            return totals[c][3]

        within_shapes = [
            sds((length, chunk)), sds((length, chunk)), sds((length, 2 * LANES)), sds((length, LANES))
        ]
        post_shapes = [
            sds((length, chunk), BF), sds((length, chunk), BF), sds((length, 2 * LANES)), sds((length, LANES))
        ]
        flows = lambda: [pltpu.VMEM((2, LANES, length), F32)]

        def do_within(c, token):
            s, k = order[c]
            within[c] = run(
                within_body(k * group_heads, heads, head_width),
                [packs[s], value_block(c), cot_block(c), rate_row, Far(token)],
                within_shapes,
                scratch=flows(),
            )
            return within[c][3]

        def do_turn(cs, turn, token):
            blocks = [b for c in cs for b in (value_block(c), cot_block(c))]
            works = [within_body(order[c][1] * group_heads, heads, head_width) for c in cs]
            out = run(
                turn_body(works, [order[c][0] for c in cs], turn),
                [place, *packs, rate_row, *blocks, Far(token)],
                within_shapes * len(cs),
                scratch=flows(),
            )
            for n, c in enumerate(cs):
                within[c] = within.get(c, []) + list(out[4 * n : 4 * n + 4])
            return out[3]

        def post_parts(c, token):
            s, k = order[c]
            last = pairs - 1
            ups = [got[(z + 1) % 2][max(c + z - 1, c, 1 - z)] for z in range(pairs)]
            downs = [got[(last - z) % 2][max(c + z - 1, c, 1 - z)] for z in range(pairs)]
            body = post_body(k * group_heads, heads, head_width, len(ups), len(downs), c == 0)
            work = within_body(k * group_heads, heads, head_width)
            if len(within.get(c, ())) == 8:
                body = either_within(body)
            elif c in within:
                body = split_body(work, body, c == 0)
            else:
                body = chunk_body(work, body, c == 0)
            near = columns["far"] if c == 0 else [totals[c][2]]
            ins = [packs[s], value_block(c), cot_block(c), *within.get(c, []),
                   *near, totals[c][3], gain, rate_row, Far(token),
                   *map(Far, ups), *map(Far, downs)]
            return body, ins

        def do_chunk(c, token):
            body, ins = post_parts(c, token)
            more = [pltpu.VMEM(o.shape, o.dtype) for o in within_shapes] + flows()
            post[c] = run(body, [place, *ins], post_shapes, stored=(0,), scratch=work() + more)
            return post[c][3]

        def do_partial(cs, token, before=None):
            return run(
                partial_body(len(cs), before is not None),
                [Far(token), *[post[c][1] for c in cs], *[weight_block(c) for c in cs]]
                + ([] if before is None else [before]),
                [sds((length, width))],
            )[0]

        shares = [sds((length, width // parts))] * 2 if parts == 2 else [sds((length, width))]

        def send_share(term):
            if parts == 2:
                return term[0], lax.ppermute(term[1], "chan", [(0, 1), (1, 0)])
            share = lax.psum_scatter(term[0], "chan", scatter_dimension=1, tiled=True)
            return share, jnp.zeros_like(share)

        def do_term(s, before):
            mine = [c for c in range(chunks) if order[c][0] == s]
            return send_share(run(
                term_body(len(mine), 0, heads, parts, s == 1),
                [place, packs[s], select_weight, step_rows, before,
                 *[post[c][2] for c in mine], *[post[c][3] for c in mine]],
                shares,
            ))

        def do_last(c, before, token):
            s = order[c][0]
            mine = [n for n in range(chunks) if order[n][0] == s and n != c]
            body, ins = post_parts(c, token)
            sums = [select_weight, step_rows, before]
            others = [[post[n][k] for n in mine] for k in (2, 3)]
            if parts == 2:
                term = tile_body(len(mine) + 1, 1, heads, s == 1, False)
            else:
                term = term_body(len(mine) + 1, 1, heads, parts, s == 1)
            post[c] = run(
                last_body(body, term, len(ins)),
                [place, *ins, *sums, weight_block(c), *others[0], *others[1]],
                [*post_shapes, shares[0]],
                scratch=work(),
                stored=(0,),
            )
            if parts != 2:
                return send_share(post[c][4:])
            arriving = lax.ppermute(post[c][4], "chan", [(0, 1), (1, 0)])
            kept = run(
                tile_body(len(mine) + 1, 1, heads, s == 1, True),
                [place, packs[s], *sums, post[c][1], weight_block(c),
                 *others[0], post[c][2], *others[1], post[c][3]],
                [shares[0]],
            )[0]
            return kept, arriving

        def do_finish(s, share):
            return run(
                finish_body(s == 1), list(share), [sds((length, width // parts), BF)], stored=(0,)
            )[0]

        def do_step(k, widen, ends):
            has = [0 <= k - z < chunks and z < pairs - 1 for z in range(pairs)]
            ins = [place]
            for d in range(2):
                ins += [totals[k - z][d] for z in range(pairs) if has[z]]
                ins += [totals[k - z][3] for z in range(pairs) if has[z]]
            if k > 0:
                ins += [got[0][-1], got[1][-1] if k > 1 else got[0][-1]]
            outs = [sds(pair_shape), sds(pair_shape), token_shape]
            pieces = [] if widen is None else pieces_of(widen)
            if widen is not None:
                ins += [value_block(widen), cot_block(widen), *pieces]
                outs.append(wide_shape(len(pieces)))
            return run(
                step_body(has, k == 0, widen is not None, len(pieces), len(ends)),
                ins + [Far(e) for e in ends],
                outs,
            )

        def do_first_step(ends):
            s, k = order[0]
            out = run(
                first_step_body(pairs, k * group_heads, heads, head_width, len(ends)),
                [place, packs[s], far_row, *own_states, *map(Far, ends)],
                [sds(pair_shape), sds(pair_shape), token_shape, sds(pair_shape), sds(pair_shape),
                 sds((8, chunk))],
            )
            totals[0] = (out[3], out[4], None, out[5])
            columns["own"] = own_states
            return out

        def do_exchange(token):
            last = pairs - 1
            ups = [got[(z + 1) % 2][max(z - 1, 1 - z)] for z in range(pairs)]
            downs = [got[(last - z) % 2][max(z - 1, 1 - z)] for z in range(pairs)]
            sends = run(
                exchange_body(len(ups), len(downs)),
                [place, *columns["own"], totals[0][3], Far(token), *map(Far, ups), *map(Far, downs)],
                [sds(pair_shape), sds(pair_shape)],
                scratch=work(),
            )
            columns["far"] = [swap(x) for x in sends]

        def pieces_of(c):
            return [Block(packs[1], (length, LANES), (0, riders[c]))] if c in riders else []

        def do_widen(c, token):
            pieces = pieces_of(c)
            return run(
                widen_body, [value_block(c), cot_block(c), Far(token), *pieces], [wide_shape(len(pieces))]
            )[0]

        far[1] = swap(lax.optimization_barrier((wide, far_row))[0])
        ends = []
        halfway = None
        share = None
        for k in range(steps):
            queue = k + 2 if 0 < k < chunks - 2 else None
            made = do_first_step(ends) if k == 0 else do_step(k, queue, ends)
            token = made[2]
            got[0].append(lax.ppermute(made[0], "seq", edges[0]))
            got[1].append(lax.ppermute(made[1], "seq", edges[1]) if 0 < k < steps - 1 else None)
            ends = []
            if k == 0:
                v_more = do_values(list(range(1, groups - 1)), token)
                far[2] = swap(do_widen(2, token))
            if queue is not None:
                far[queue] = swap(made[3])
            if k + 1 < chunks:
                ends.append(do_pair(k + 1, token))
            if k == max(chunks - 2, pairs - 1):
                do_exchange(far[chunks - 1])
            if k == steps - 3:
                ends += columns["far"]
            for cs in {1: [(2, 3)], 2: [(4, 5)], 3: [(6, 0)], 4: [(7,)]}.get(k, ()):
                ends.append(do_turn(cs, 0, token))
            if k == steps - 1:
                do_turn((7,), 1, token)
            c = k - pairs + 1
            if c > 0:
                ends.append(do_chunk(c, token))
            if c == groups - 2:
                halfway = do_partial(list(range(1, groups - 1)), token)
                ends.append(halfway)
            if c == groups:
                share = do_term(0, do_partial([groups - 1, groups], token, halfway))
                ends.append(share[0])
            if c == groups + 1:
                ends.append(do_chunk(0, token))
            if c == groups + 2:
                grads[0] = do_finish(0, share)
                halfway = do_partial([groups + 1, 0, groups + 2], token)
        grads[1] = do_finish(1, do_last(chunks - 1, halfway, halfway))
        outs = [
            jnp.concatenate([post[order.index((s, k))][0] for k in range(groups)], axis=1)
            for s in range(2)
        ]
        return (outs[0], outs[1], grads[0], grads[1])

    return body


def solution(mesh):
    rows = P(("dp", "seq"), None)
    both = P(("dp", "seq"), "chan")
    in_specs = (
        rows, rows, P(None, "chan"), P(), P(None, "chan"),
        P("chan"), P("chan"), P("chan"), both, both,
    )
    return jax.shard_map(
        local(mesh.shape["seq"], mesh.shape["chan"]),
        mesh=mesh,
        in_specs=in_specs,
        out_specs=(both,) * 4,
        check_vma=False,
    )
```

```python
import jax
import jax.numpy as jnp
from jax import lax
from jax.experimental import pallas as pl
from jax.experimental.pallas import tpu as pltpu
from jax.sharding import PartitionSpec as P

BF = jnp.bfloat16
F32 = jnp.float32
LANES = 128


def mm(a, b, ca=1, cb=0):
    return lax.dot_general(a, b, (((ca,), (cb,)), ((), ())), preferred_element_type=F32)


def halves(x):
    high = x.astype(BF)
    return high, (x - high.astype(F32)).astype(BF)


def mm_exact(a, b, ca=1, cb=0):
    first, rest = b.astype(BF), None
    rest = b - first.astype(F32)
    second = rest.astype(BF)
    third = (rest - second.astype(F32)).astype(BF)
    return mm(a, first, ca, cb) + mm(a, second, ca, cb) + mm(a, third, ca, cb)


def iotas(rows, columns):
    return (
        lax.broadcasted_iota(jnp.int32, (rows, columns), 0),
        lax.broadcasted_iota(jnp.int32, (rows, columns), 1),
    )


def spread(weights, base, width, head_width):
    heads = weights[0].shape[1]
    row, channel = iotas(2 * heads, width)
    start = (jnp.where(row >= heads, row - heads, row) - base) * head_width
    pick = ((channel >= start) & (channel < start + head_width)).astype(BF)
    stacked = jnp.concatenate(weights, axis=0) if len(weights) > 1 else weights[0]
    out = mm(jnp.concatenate(halves(stacked), axis=1), pick)
    result, at = [], 0
    for w in weights:
        result.append(out[at : at + w.shape[0]])
        at += w.shape[0]
    return result


def spread_rows(rows, base, width, head_width):
    heads = rows[0].shape[1]
    wide = spread([jnp.broadcast_to(r, (8, heads)) for r in rows], base, width, head_width)
    return [w[0:1] for w in wide]


def gather_heads(parts, base, head_width):
    width = parts[0].shape[1]
    channel, head = iotas(width, LANES)
    start = (head - base) * head_width
    pick = ((channel >= start) & (channel < start + head_width)).astype(BF)
    out = mm(jnp.concatenate([x.astype(BF) for x in parts], axis=0), pick)
    result, at = [], 0
    for x in parts:
        result.append(out[at : at + x.shape[0]])
        at += x.shape[0]
    return result


def reversal(size):
    i, j = iotas(size, size)
    return (i + j == size - 1).astype(BF)


def flip_block(size):
    return 256 if size % 256 == 0 else 128


def sds(shape, dtype=F32):
    return jax.ShapeDtypeStruct(shape, dtype)


class Block:
    def __init__(self, array, shape, index):
        self.array, self.shape, self.index = array, shape, index

    def view(self, ref):
        if self.shape == self.array.shape:
            return ref
        return ref.at[tuple(pl.ds(i * b, b) for i, b in zip(self.index, self.shape))]


class Copied:
    def __init__(self, item):
        self.item = item if isinstance(item, Block) else Block(item, item.shape, (0,) * item.ndim)


class Far:
    def __init__(self, array):
        self.array = array


def run(body, ins, outs, scratch=(), limit=16, stored=()):
    specs, arrays, copied = [], [], []
    for item in ins:
        if isinstance(item, Far):
            specs.append(pl.BlockSpec(memory_space=pl.ANY))
            arrays.append(item.array)
        elif isinstance(item, Copied):
            specs.append(pl.BlockSpec(memory_space=pltpu.HBM))
            arrays.append(item.item.array)
            copied.append(item.item)
        elif isinstance(item, Block):
            specs.append(pl.BlockSpec(memory_space=pltpu.VMEM))
            arrays.append(item.array)
        else:
            space = pltpu.SMEM if item.dtype == jnp.int32 else pltpu.VMEM
            specs.append(pl.BlockSpec(memory_space=space))
            arrays.append(item)
    out_specs = [
        pl.BlockSpec(memory_space=pltpu.HBM if n in stored else pltpu.VMEM)
        for n in range(len(outs))
    ]
    holds = [pltpu.VMEM(q.shape, q.array.dtype) for q in copied]
    holds += [pltpu.VMEM(outs[n].shape, outs[n].dtype) for n in stored]
    sems = [pltpu.SemaphoreType.DMA((max(len(holds), 1),))]

    def kernel(*refs):
        refs = list(refs)
        take = lambda n: [refs.pop(0) for _ in range(n)]
        sources, targets = take(len(ins)), take(len(outs))
        held, (sem,) = take(len(holds)), take(1)
        args, copies = [], []
        for ref, item in zip(sources, ins):
            if isinstance(item, Copied):
                n = len(copies)
                copies.append(pltpu.make_async_copy(item.item.view(ref), held[n], sem.at[n]))
                copies[-1].start()
                ref = held[n]
            elif isinstance(item, Block):
                ref = item.view(ref)
            args.append(ref)
        back = []
        for n, ref in enumerate(targets):
            if n in stored:
                k = len(copied) + stored.index(n)
                back.append(pltpu.make_async_copy(held[k], ref, sem.at[k]))
                ref = held[k]
            args.append(ref)
        waits = {"waits": [c.wait for c in copies]} if copies else {}
        body(*args, *refs, **waits)
        for copy in back:
            copy.start()
        for copy in back:
            copy.wait()

    return pl.pallas_call(
        kernel,
        in_specs=specs,
        out_specs=out_specs,
        out_shape=outs,
        scratch_shapes=holds + sems + list(scratch),
        compiler_params=pltpu.CompilerParams(vmem_limit_bytes=limit * 1024 * 1024),
        cost_estimate=pl.CostEstimate(flops=0, bytes_accessed=1024, transcendentals=0),
    )(*arrays)


def start_body(
    hidden, other, select, step, bias, rate, weight, cot,
    source, pack0, pack1, row, v_out, wide, waits,
):
    for wait in waits[0:2]:
        wait()
    length, width = hidden.shape
    heads = bias.shape[1]
    source[0:length, :] = hidden[...]
    block = flip_block(width)
    turn = reversal(block)
    for j in range(width // block):
        source[length : 2 * length, j * block : (j + 1) * block] = mm(
            other[:, width - (j + 1) * block : width - j * block], turn
        ).astype(BF)
    for wait in waits[2:6]:
        wait()
    keys = mm(source[...], select[...]).astype(BF).astype(F32)
    state = keys.shape[1] // 2
    raw = mm(source[...], step[...], 1, 1) + bias[...]
    dt = jnp.maximum(raw, 0.0) + jnp.log1p(jnp.exp(-jnp.abs(raw)))
    rise = jax.nn.sigmoid(raw)
    i, j = iotas(length, length)
    lower = (i >= j).astype(BF)
    for s, pack in enumerate((pack0, pack1)):
        rows = slice(s * length, (s + 1) * length)
        drop = dt[rows] * rate[...]
        total = mm_exact(lower, drop)
        pack[...] = jnp.zeros(pack.shape, F32)
        pack[:, 0 : 2 * state] = keys[rows]
        at = 2 * state
        for part in (dt[rows], total, total - drop, rise[rows]):
            pack[:, at : at + heads] = part
            at += heads
    row[...] = jnp.zeros(row.shape, F32)
    row[0:1, 0:heads] = jnp.exp(
        -pack1[length - 1 : length, 2 * state + heads : 2 * state + 2 * heads]
    )
    for wait in waits[6:]:
        wait()
    for at in columns_of(weight.shape[1]):
        piece = mm(source[...], weight[:, at]).astype(BF)
        for s in range(2):
            v_out[0, s, :, at] = piece[s * length : (s + 1) * length]
        wide[0:length, at] = piece[0:length].astype(F32)
    wide[length : 2 * length, :] = cot[...].astype(F32)
    for n in range(3):
        at = 2 * length + n * piece_rows(length, wide.shape[1])
        put_piece(wide, at, pack0[:, n * LANES : (n + 1) * LANES])


def columns_of(width):
    block = min(256, width)
    return [slice(k * block, (k + 1) * block) for k in range(width // block)]


def values_body(source, token, *rest):
    weights, v_out = rest[:-1], rest[-1]
    length = v_out.shape[2]
    for n, weight in enumerate(weights):
        for at in columns_of(weight.shape[1]):
            piece = mm(source[...], weight[:, at]).astype(BF)
            for s in range(2):
                v_out[n, s, :, at] = piece[s * length : (s + 1) * length]


class Pack:
    def __init__(self, write, read, stats, heads):
        self.write, self.read = write, read
        self.dt = stats[:, 0:heads]
        self.total = stats[:, heads : 2 * heads]
        self.before = stats[:, 2 * heads : 3 * heads]
        last = self.total.shape[0]
        self.whole = self.total[last - 1 : last, :]
        self.from_start = jnp.exp(-self.total)
        self.from_end = jnp.exp(self.before - self.whole)
        self.to_end = jnp.exp(self.total - self.whole)
        self.to_start = jnp.exp(-self.before)
        self.through = jnp.exp(-self.whole)


def own_pack(ref, heads):
    return Pack(*[ref[:, n * LANES : (n + 1) * LANES] for n in range(3)], heads)


def piece_rows(length, width):
    return length // (width // LANES)


def put_piece(ref, row, piece):
    count = piece_rows(piece.shape[0], ref.shape[1])
    for b in range(ref.shape[1] // LANES):
        ref[row : row + count, b * LANES : (b + 1) * LANES] = piece[b * count : (b + 1) * count]


def get_piece(ref, row, length):
    count = piece_rows(length, ref.shape[1])
    return jnp.concatenate(
        [
            ref[row : row + count, b * LANES : (b + 1) * LANES]
            for b in range(ref.shape[1] // LANES)
        ],
        axis=0,
    )


def pair_body(base, heads, head_width, piece_at):
    def body(place, v_own, g_own, x_far, far0, far1, far2, own_ref, token, up, down, near, keep):
        first = place[0] == 0
        length, width = g_own.shape
        own = own_pack(own_ref, heads)
        far = Pack(*[get_piece(f, at, length) for f, at in zip((far0, far1, far2), piece_at)], heads)
        own_row, far_row = own.through, far.through
        rows = spread_rows([own_row * far_row, far_row], base, width, head_width)
        keep[...] = jnp.zeros(keep.shape, F32)
        keep[0:1, :] = rows[0]
        keep[1:2, :] = rows[1]
        own_up, own_down = jnp.where(first, far_row, 1.0), jnp.where(first, 1.0, far_row)
        far_up, far_down = jnp.where(first, 1.0, own_row), jnp.where(first, own_row, 1.0)
        for kind in range(2):
            rows = slice(kind * LANES, (kind + 1) * LANES)
            if kind == 0:
                keys = (own.write, far.write)
                ups = (own.dt * own.to_end, far.dt * far.to_end)
                downs = (own.dt * own.to_start, far.dt * far.to_start)
            else:
                keys = (own.read, far.read)
                ups = (own.from_end, far.from_end)
                downs = (own.from_start, far.from_start)
            x_own = (v_own if kind == 0 else g_own)[...].reshape(length, width).astype(F32)
            x_other = x_far[kind * length : (kind + 1) * length, :]
            w = spread(
                [ups[0] * own_up, ups[1] * far_up, downs[0] * own_down, downs[1] * far_down,
                 jnp.where(first, downs[1], ups[1])],
                base, width, head_width,
            )
            key = jnp.concatenate(keys, axis=0).astype(BF)
            both = lambda a, b: jnp.concatenate([(a * x_own).astype(BF), (b * x_other).astype(BF)], axis=0)
            up[rows, :] = mm(key, both(w[0], w[1]), 0, 0)
            down[rows, :] = mm(key, both(w[2], w[3]), 0, 0)
            near[rows, :] = mm(keys[1].astype(BF), (w[4] * x_other).astype(BF), 0, 0)

    return body


def column_body(base, heads, head_width):
    def body(own_ref, source, weight, g_own, v_out, own_up, own_down, waits):
        length, width = g_own.shape
        own = own_pack(own_ref, heads)
        w_values = spread([own.dt * own.to_end, own.dt * own.to_start], base, width, head_width)
        w_grads = spread([own.from_end, own.from_start], base, width, head_width)
        write, read = own.write.astype(BF), own.read.astype(BF)
        waits[0]()
        for at in columns_of(width):
            piece = mm(source[...], weight[:, at]).astype(BF)
            for s in range(2):
                v_out[0, s, :, at] = piece[s * length : (s + 1) * length]
            v, g = piece[length:].astype(F32), g_own[:, at].astype(F32)
            for out, n in ((own_up, 0), (own_down, 1)):
                out[0:LANES, at] = mm(write, (w_values[n][:, at] * v).astype(BF), 0, 0)
                out[LANES : 2 * LANES, at] = mm(read, (w_grads[n][:, at] * g).astype(BF), 0, 0)

    return body


def column_totals(place, own_ref, far_row_ref, base, heads, head_width, owns, totals, keep):
    first = place[0] == 0
    width = keep.shape[1]
    own = own_pack(own_ref, heads)
    far_row = far_row_ref[0:1, 0:heads]
    rows = spread_rows([own.through * far_row, far_row, own.through], base, width, head_width)
    keep[...] = jnp.zeros(keep.shape, F32)
    for n, row in enumerate(rows):
        keep[n : n + 1, :] = row
    totals[0][...] = jnp.where(first, rows[1], 1.0) * owns[0][...]
    totals[1][...] = jnp.where(first, 1.0, rows[1]) * owns[1][...]


def first_step_body(pairs, base, heads, head_width, tokens):
    def body(place, own_ref, far_row_ref, own_up, own_down, *rest):
        send_a, send_b, token, up, down, keep = rest[tokens:]
        column_totals(
            place, own_ref, far_row_ref, base, heads, head_width, (own_up, own_down), (up, down), keep
        )
        token[...] = jnp.zeros(token.shape, F32)
        sends = (send_a, send_b)
        for d, total in enumerate((up, down)):
            spot = place[1] if d == 0 else pairs - 1 - place[1]
            for n in range(pairs):
                z = n if d == 0 else pairs - 1 - n
                send = sends[(z + d) % 2]

                @pl.when(spot == n)
                def _():
                    send[...] = total[...] if n == 0 else jnp.zeros(send.shape, F32)

    return body


def exchange_body(ups, downs):
    def body(place, own_up, own_down, keep, token, *rest):
        up_in, down_in = rest[0:ups], rest[ups : ups + downs]
        up_out, down_out, bufs, sems = rest[ups + downs :]
        up_spot, down_spot = place[1], len(up_in) - 1 - place[1]
        fetch_start(up_in, up_spot, bufs.at[0], sems.at[0])
        fetch_start(down_in, down_spot, bufs.at[1], sems.at[1])
        fetch_wait(up_in, up_spot, bufs.at[0], sems.at[0])
        fetch_wait(down_in, down_spot, bufs.at[1], sems.at[1])
        first = place[0] == 0
        row = keep[2:3, :]
        up_out[...] = jnp.where(first, row * bufs[0] + own_up[...], bufs[0])
        down_out[...] = jnp.where(first, bufs[1], row * bufs[1] + own_down[...])

    return body


def fetch_start(options, index, target, sem):
    for z, option in enumerate(options):
        if option is not None:

            @pl.when(index == z)
            def _():
                pltpu.make_async_copy(option, target, sem).start()


def fetch_wait(options, index, target, sem):
    for z, option in enumerate(options):
        if option is not None:

            @pl.when(index == z)
            def _():
                pltpu.make_async_copy(option, target, sem).wait()


def step_body(has, first_step, last_step, widen, pieces, tokens):
    pairs = len(has)

    def body(place, *rest):
        rest = list(rest)
        take = lambda n: [rest.pop(0) for _ in range(n)]
        sides = []
        for d in range(2):
            totals = [take(1)[0] if h else None for h in has]
            keeps = [take(1)[0] if h else None for h in has]
            sides.append((totals, keeps))
        got = None if first_step else take(2)
        chunk = take(2) if widen else None
        piece_refs = take(pieces)
        take(tokens)
        sends = take(2)
        token = take(1)[0]
        spots = (place[1], pairs - 1 - place[1])
        for d, (totals, keeps) in enumerate(sides):
            for n in range(pairs):
                z = n if d == 0 else pairs - 1 - n
                send = sends[(z + d) % 2]

                @pl.when(spots[d] == n)
                def _():
                    if not has[n] and last_step:
                        pass
                    elif not has[n]:
                        send[...] = jnp.zeros(send.shape, F32)
                    elif got is None or n == 0:
                        send[...] = totals[n][...]
                    else:
                        send[...] = totals[n][...] + keeps[n][0:1, :] * got[(z + 1 + d) % 2][...]

        token[...] = jnp.zeros(token.shape, F32)
        if widen:
            put_chunk(take(1)[0], *chunk, piece_refs)

    return body


def within_body(base, heads, head_width):
    def body(own_ref, v_ref, g_ref, rate, token, y_out, x_out, keys_out, steps_out, cols_s):
        own = own_pack(own_ref, heads)
        length, width = g_ref.shape
        write, read = own.write.astype(BF), own.read.astype(BF)
        scores = mm(read, write, 1, 1)
        i, j = iotas(length, length)
        low = i > j
        high = i < j
        doubled = jnp.where(i == j, 2.0, 1.0).astype(F32)
        scores2 = scores * doubled
        turned = own_ref[:, 2 * LANES : 3 * LANES].T
        lane = lax.broadcasted_iota(jnp.int32, (length, LANES), 1)
        d_scores = jnp.zeros((length, length), F32)
        out_low = jnp.zeros((length, LANES), F32)
        out_high = jnp.zeros((length, LANES), F32)
        cols_s[...] = jnp.zeros(cols_s.shape, F32)
        v_all = v_ref[...].reshape(length, width)
        per = LANES // head_width
        for n in range(width // LANES):
            at = slice(n * LANES, (n + 1) * LANES)
            v, g = v_all[:, at], g_ref[:, at]
            mine = [(lane >= m * head_width) & (lane < (m + 1) * head_width) for m in range(per)]
            v_heads = jnp.concatenate([jnp.where(x, v, jnp.zeros_like(v)) for x in mine], axis=0)
            g_heads = jnp.concatenate([jnp.where(x, g, jnp.zeros_like(g)) for x in mine], axis=0)
            products = mm(g_heads, v, 1, 1)
            plains, steppeds = [], []
            for m in range(per):
                h = base + n * per + m
                c_col = own.total[:, h : h + 1]
                e_col = own.before[:, h : h + 1]
                dt_row = turned[h : h + 1, :]
                c_row = turned[heads + h : heads + h + 1, :]
                e_row = turned[2 * heads + h : 2 * heads + h + 1, :]
                decay = jnp.exp(jnp.where(low, c_row - c_col, e_col - e_row))
                plain = decay * scores2
                plains.append(plain.astype(BF))
                steppeds.append((plain * dt_row).astype(BF))
                inner = decay * dt_row * products[m * length : (m + 1) * length]
                d_scores = d_scores + inner
                flow = inner * scores
                flow_low = jnp.where(low, flow, 0.0)
                flow_high = jnp.where(high, flow, 0.0)
                out_low = jnp.where(lane == h, jnp.sum(flow_low, 1, keepdims=True), out_low)
                out_high = jnp.where(lane == h, jnp.sum(flow_high, 1, keepdims=True), out_high)
                cols_s[0, h : h + 1, :] = jnp.sum(flow_low, 0, keepdims=True)
                cols_s[1, h : h + 1, :] = jnp.sum(flow_high, 0, keepdims=True)
            y_out[:, at] = mm(jnp.concatenate(steppeds, axis=1), v_heads)
            x_out[:, at] = mm(jnp.concatenate(plains, axis=0), g_heads, 0, 0)
        d_scores = (d_scores * doubled).astype(BF)
        keys_out[:, 0:LANES] = mm(d_scores, read, 0, 0)
        keys_out[:, LANES : 2 * LANES] = mm(d_scores, write)
        net_low = out_low - cols_s[0].T
        net_high = out_high - cols_s[1].T
        at_or_after = (j >= i).astype(BF)
        after = (j > i).astype(BF)
        steps_out[...] = -rate[...] * (mm_exact(at_or_after, net_low) - mm_exact(after, net_high))

    return body


def post_body(base, heads, head_width, ups, downs, columns=False):
    def body(
        place, own_ref, v_ref, g_ref, yw, xw, keys_w, steps_w, near, keep, skip, rate, token, *rest
    ):
        up_in, down_in = rest[0:ups], rest[ups : ups + downs]
        mixed, dv_out, keys_out, steps_out, bufs, sems = rest[ups + downs :]
        up_spot, down_spot = place[1], len(up_in) - 1 - place[1]
        fetch_start(up_in, up_spot, bufs.at[0], sems.at[0])
        fetch_start(down_in, down_spot, bufs.at[1], sems.at[1])
        first = place[0] == 0
        own = own_pack(own_ref, heads)
        length, width = g_ref.shape
        far_row = keep[1:2, :]
        own_row, gain = spread_rows([own.through, skip[...]], base, width, head_width)
        up_row = jnp.where(first, 1.0, far_row)
        down_row = jnp.where(first, far_row, 1.0)
        dt, from_start, from_end, to_end, to_start = spread(
            [own.dt, own.from_start, own.from_end, own.to_end, own.to_start],
            base, width, head_width,
        )
        write, read = own.write.astype(BF), own.read.astype(BF)
        v = v_ref[...].reshape(length, width).astype(F32)
        g = g_ref[...].astype(F32)
        fetch_wait(up_in, up_spot, bufs.at[0], sems.at[0])
        fetch_wait(down_in, down_spot, bufs.at[1], sems.at[1])
        if columns:
            up = up_row * bufs[0] + near[0][...]
            down = down_row * bufs[1] + near[1][...]
        else:
            up = up_row * bufs[0] + jnp.where(first, 0.0, near[...])
            down = down_row * bufs[1] + jnp.where(first, near[...], 0.0)
        p, ab = up[0:LANES], up[LANES : 2 * LANES]
        q, af = down[0:LANES], down[LANES : 2 * LANES]
        crossing = jnp.sum(p * af + q * ab, axis=0, keepdims=True)
        p, q, af, ab = p.astype(BF), q.astype(BF), af.astype(BF), ab.astype(BF)
        y_p = from_start * mm(read, p)
        y_q = from_end * mm(read, q)
        x_f = to_end * mm(write, af)
        x_b = to_start * mm(write, ab)
        mixed[...] = (yw[...] + y_p + y_q + gain * v).astype(BF)
        x = xw[...] + x_f + x_b
        dv_out[...] = (dt * x + gain * g).astype(BF)
        dtv = dt * v
        keys_out[:, 0:LANES] = (
            keys_w[:, 0:LANES]
            + mm((to_end * dtv).astype(BF), af, 1, 1)
            + mm((to_start * dtv).astype(BF), ab, 1, 1)
        )
        keys_out[:, LANES : 2 * LANES] = (
            keys_w[:, LANES : 2 * LANES]
            + mm((from_start * g).astype(BF), p, 1, 1)
            + mm((from_end * g).astype(BF), q, 1, 1)
        )
        lane = lax.broadcasted_iota(jnp.int32, (length, LANES), 1)
        steps = jnp.where(lane < heads, own_ref[:, 2 * LANES : 3 * LANES], 0.0)
        direct, a_p, a_q, b_f, b_b, through = gather_heads(
            [v * x, g * y_p, g * y_q, v * x_f, v * x_b, jnp.broadcast_to(crossing * own_row, (8, width))],
            base, head_width,
        )
        i, j = iotas(length, length)
        masks = jnp.concatenate([j >= i, j <= i, j < i, j > i], axis=1).astype(F32).astype(BF)
        high, low = halves(jnp.concatenate([a_p, a_q, b_f * steps, b_b * steps], axis=0))
        flow = mm(masks, high) + mm(masks, low) + through[0:1]
        steps_out[...] = steps_w[...] + direct - rate[...] * flow

    return body


class Either:
    def __init__(self, choice, a, b):
        self.choice, self.a, self.b = choice, a, b

    def __getitem__(self, index):
        return jnp.where(self.choice, self.a[index], self.b[index])


def either_within(post):
    def body(place, own_ref, v_ref, g_ref, *rest):
        merged = [Either(place[3] == 0, a, b) for a, b in zip(rest[0:4], rest[4:8])]
        post(place, own_ref, v_ref, g_ref, *merged, *rest[8:])

    return body


def split_body(within, post, columns):
    def body(place, own_ref, v_ref, g_ref, *rest):
        bufs, sems, yw, xw, keys_w, steps_w, cols_s = rest[-7:]
        before, rest = rest[0:4], rest[4:]
        nears = 2 if columns else 1
        near = rest[0:2] if columns else rest[0]
        keep, skip, rate, token, *rest = rest[nears:]

        @pl.when(place[3] == 1)
        def _():
            within(own_ref, v_ref, g_ref, rate, token, yw, xw, keys_w, steps_w, cols_s)

        merged = [Either(place[3] == 0, a, b) for a, b in zip(before, (yw, xw, keys_w, steps_w))]
        post(place, own_ref, v_ref, g_ref, *merged, near, keep, skip, rate, token, *rest[:-5])

    return body


def turn_body(works, strands, turns):
    def body(place, pack0, pack1, rate, *rest):
        count = len(works)
        blocks, token = rest[0 : 2 * count], rest[2 * count]
        outs, flows = rest[2 * count + 1 : -1], rest[-1]

        for n, work in enumerate(works):

            @pl.when(place[3] == turns[n])
            def _():
                work(
                    (pack0, pack1)[strands[n]], blocks[2 * n], blocks[2 * n + 1], rate, token,
                    *outs[4 * n : 4 * n + 4], flows,
                )

    return body


def chunk_body(within, post, columns):
    def body(place, own_ref, v_ref, g_ref, *rest):
        nears = 2 if columns else 1
        near = rest[0:2] if columns else rest[0]
        keep, skip, rate, token, *rest = rest[nears:]
        bufs, sems, yw, xw, keys_w, steps_w, cols_s = rest[-7:]
        within(own_ref, v_ref, g_ref, rate, token, yw, xw, keys_w, steps_w, cols_s)
        post(
            place, own_ref, v_ref, g_ref, yw, xw, keys_w, steps_w, near, keep, skip, rate, token,
            *rest[:-5],
        )

    return body


def partial_body(groups, more):
    def body(token, *rest):
        dvs, weights, rest = rest[0:groups], rest[groups : 2 * groups], rest[2 * groups :]
        out = rest[-1]
        for at in columns_of(out.shape[1]):
            total = rest[0][:, at] if more else 0.0
            for dv, weight in zip(dvs, weights):
                total = total + mm(dv[...], weight[at, :], 1, 1)
            out[:, at] = total

    return body


def term_body(groups, tails, heads, parts, swap):
    def body(place, own_ref, select, step, before, *rest):
        dvs, weights = rest[0:tails], rest[tails : 2 * tails]
        rest = rest[2 * tails :]
        keys, steps = rest[0:groups], rest[groups : 2 * groups]
        outs = rest[2 * groups :]
        d_keys, d_steps = keys[0][...], steps[0][...]
        for a, b in zip(keys[1:], steps[1:]):
            d_keys = d_keys + a[...]
            d_steps = d_steps + b[...]
        d_raw = d_steps[:, 0:heads] * own_ref[:, 2 * LANES + 3 * heads : 2 * LANES + 4 * heads]
        keys_high, keys_low = halves(d_keys)
        raw_high, raw_low = halves(d_raw)
        width = select.shape[0]
        block = width // parts
        tiles = []
        for b in range(parts):
            rows = slice(b * block, (b + 1) * block)
            total = before[:, rows]
            total = total + mm(keys_high, select[rows, :], 1, 1) + mm(keys_low, select[rows, :], 1, 1)
            total = total + mm(raw_high, step[:, rows]) + mm(raw_low, step[:, rows])
            for k in range(tails):
                total = total + mm(dvs[k][...], weights[k][rows, :], 1, 1)
            tiles.append(total)
        if swap:
            tiles = tiles[::-1]
        if parts == 2:
            first = place[2] == 0
            outs[0][...] = jnp.where(first, tiles[0], tiles[1])
            outs[1][...] = jnp.where(first, tiles[1], tiles[0])
        else:
            for b in range(parts):
                outs[0][:, b * block : (b + 1) * block] = tiles[b]

    return body


def tile_body(groups, tails, heads, swap, keep):
    def body(place, own_ref, select, step, before, *rest):
        dvs, weights = rest[0:tails], rest[tails : 2 * tails]
        rest = rest[2 * tails :]
        keys, steps, out = rest[0:groups], rest[groups : 2 * groups], rest[-1]
        d_keys, d_steps = keys[0][...], steps[0][...]
        for a, b in zip(keys[1:], steps[1:]):
            d_keys = d_keys + a[...]
            d_steps = d_steps + b[...]
        d_raw = d_steps[:, 0:heads] * own_ref[:, 2 * LANES + 3 * heads : 2 * LANES + 4 * heads]
        keys_high, keys_low = halves(d_keys)
        raw_high, raw_low = halves(d_raw)
        block = out.shape[1]
        mine = place[2] if keep != swap else 1 - place[2]
        rows = pl.ds(pl.multiple_of(mine * block, block), block)
        total = before[:, rows]
        total = total + mm(keys_high, select[rows, :], 1, 1) + mm(keys_low, select[rows, :], 1, 1)
        total = total + mm(raw_high, step[:, rows]) + mm(raw_low, step[:, rows])
        for dv, weight in zip(dvs, weights):
            total = total + mm(dv[...], weight[rows, :], 1, 1)
        out[...] = total

    return body


def last_body(work, term, work_ins):
    def body(place, *rest):
        rest = list(rest)
        take = lambda n: [rest.pop(0) for _ in range(n)]
        for_work = take(work_ins)
        select, step, before, weight = take(4)
        others = take(len(rest) - 7)
        half = len(others) // 2
        mixed, dv, keys, steps, out = take(5)
        bufs, sems = take(2)
        work(place, *for_work, mixed, dv, keys, steps, bufs, sems)
        term(
            place, for_work[0], select, step, before, dv, weight,
            *others[:half], keys, *others[half:], steps, out,
        )

    return body


def finish_body(flip):
    def body(a, b, out):
        total = (a[...] + b[...]).astype(BF)
        if not flip:
            out[...] = total
            return
        width = total.shape[1]
        block = flip_block(width)
        turn = reversal(block)
        for j in range(width // block):
            out[:, j * block : (j + 1) * block] = mm(
                total[:, width - (j + 1) * block : width - j * block], turn
            ).astype(BF)

    return body


def put_chunk(wide, v_ref, g_ref, pieces):
    length, width = g_ref.shape
    wide[0:length, :] = v_ref[...].reshape(length, width).astype(F32)
    wide[length : 2 * length, :] = g_ref[...].astype(F32)
    for n, piece in enumerate(pieces):
        put_piece(wide, 2 * length + n * piece_rows(length, width), piece[...])


def widen_body(v_ref, g_ref, token, *rest):
    put_chunk(rest[-1], v_ref, g_ref, rest[:-1])


def local(shards, parts):
    pairs = shards // 2

    def body(
        hidden, complement, inner_weight, select_weight, step_weight, step_bias, decay_rate,
        skip_gain, cotangent, complement_cotangent,
    ):
        length, width = hidden.shape
        inner = inner_weight.shape[1]
        heads = step_bias.shape[0]
        head_width = inner // heads
        groups = 4
        chunk = inner // groups
        group_heads = heads // groups
        seq = lax.axis_index("seq")
        place = jnp.stack(
            [seq % 2, seq // 2, lax.axis_index("chan"), lax.axis_index("dp")]
        ).astype(jnp.int32)
        bias = step_bias.reshape(1, heads)
        rate = decay_rate.reshape(1, heads)
        rate_row = jnp.pad(rate, ((0, 0), (0, LANES - heads)))
        gain = skip_gain.reshape(1, heads)
        step_rows = step_weight.T
        cots = (cotangent, complement_cotangent)
        swap_pairs = [(a, a ^ 1) for a in range(shards)]
        edges = []
        for start in range(2):
            meets = [(z, z + 1) for z in range(start, pairs - 1, 2)]
            paired = sum(meets, ())
            meets += [(b, a) for a, b in meets] + [(z, z) for z in range(pairs) if z not in paired]
            edges.append([(2 * a + y, 2 * b + y) for a, b in meets for y in range(2)])
        swap = lambda x: lax.ppermute(x, "seq", swap_pairs)
        pack_shape = (length, 3 * LANES)
        pair_shape = (2 * LANES, chunk)
        wide_shape = lambda pieces: sds((2 * length + pieces * piece_rows(length, chunk), chunk))
        token_shape = sds((8, LANES))
        work = lambda: [pltpu.VMEM((2,) + pair_shape, F32), pltpu.SemaphoreType.DMA((2,))]
        order = [(1, groups - 1)] + [(0, k) for k in range(groups)] + [(1, k) for k in range(groups - 1)]
        chunks = len(order)

        source, pack0, pack1, row, v_zero, wide = run(
            start_body,
            [*map(Copied, (hidden, complement, select_weight, step_rows, bias, rate)),
             Copied(Block(inner_weight, (width, chunk), (0, 0))),
             Copied(Block(cots[0], (length, chunk), (0, 0)))],
            [sds((2 * length, width), BF), sds(pack_shape), sds(pack_shape), token_shape,
             sds((1, 2, length, chunk), BF), wide_shape(3)],
            limit=57,
        )
        packs = (pack0, pack1)
        far_row = swap(row)

        def weight_of(k):
            return Block(inner_weight, (width, chunk), (0, k))

        def do_values(ks, token):
            return run(
                values_body,
                [source, Far(token), *map(weight_of, ks)],
                [sds((len(ks), 2, length, chunk), BF)],
            )[0]

        v_last, *own_states = run(
            column_body((groups - 1) * group_heads, heads, head_width),
            [pack1, source, Copied(weight_of(groups - 1)),
             Block(cots[1], (length, chunk), (0, groups - 1))],
            [sds((1, 2, length, chunk), BF), sds(pair_shape), sds(pair_shape)],
            limit=48,
        )
        v_more = None

        def value_block(c):
            s, k = order[c]
            array, n = {0: (v_zero, 0), groups - 1: (v_last, 0)}.get(k, (v_more, k - 1))
            return Block(array, (1, 1, length, chunk), (n, s, 0, 0))

        def cot_block(c):
            s, k = order[c]
            return Block(cots[s], (length, chunk), (0, k))

        def weight_block(c):
            return weight_of(order[c][1])

        far = {}
        totals, within, post = {}, {}, {}
        got = ([], [])
        grads = [None, None]
        riders = {2 + n: n for n in range(3)}
        columns = {}
        steps = chunks + pairs - 2

        def do_pair(c, token):
            s, k = order[c]
            rows = piece_rows(length, chunk)
            if s == 0:
                pieces, piece_at = [far[1]] * 3, [2 * length + n * rows for n in range(3)]
            else:
                pieces, piece_at = [far[r] for r in riders], [2 * length] * 3
            totals[c] = run(
                pair_body(k * group_heads, heads, head_width, piece_at),
                [place, value_block(c), cot_block(c), far[c], *pieces, packs[s], Far(token)],
                [sds(pair_shape), sds(pair_shape), sds(pair_shape), sds((8, chunk))],
            )
            return totals[c][3]

        within_shapes = [
            sds((length, chunk)), sds((length, chunk)), sds((length, 2 * LANES)), sds((length, LANES))
        ]
        post_shapes = [
            sds((length, chunk), BF), sds((length, chunk), BF), sds((length, 2 * LANES)), sds((length, LANES))
        ]
        flows = lambda: [pltpu.VMEM((2, LANES, length), F32)]

        def do_within(c, token):
            s, k = order[c]
            within[c] = run(
                within_body(k * group_heads, heads, head_width),
                [packs[s], value_block(c), cot_block(c), rate_row, Far(token)],
                within_shapes,
                scratch=flows(),
            )
            return within[c][3]

        def do_turn(cs, turns, token):
            blocks = [b for c in cs for b in (value_block(c), cot_block(c))]
            works = [within_body(order[c][1] * group_heads, heads, head_width) for c in cs]
            out = run(
                turn_body(works, [order[c][0] for c in cs], turns),
                [place, *packs, rate_row, *blocks, Far(token)],
                within_shapes * len(cs),
                scratch=flows(),
            )
            for n, c in enumerate(cs):
                within[c] = within.get(c, []) + list(out[4 * n : 4 * n + 4])
            return out[3]

        def post_parts(c, token):
            s, k = order[c]
            last = pairs - 1
            ups = [got[(z + 1) % 2][max(c + z - 1, c, 1 - z)] for z in range(pairs)]
            downs = [got[(last - z) % 2][max(c + z - 1, c, 1 - z)] for z in range(pairs)]
            body = post_body(k * group_heads, heads, head_width, len(ups), len(downs), c == 0)
            work = within_body(k * group_heads, heads, head_width)
            if len(within.get(c, ())) == 8:
                body = either_within(body)
            elif c in within:
                body = split_body(work, body, c == 0)
            else:
                body = chunk_body(work, body, c == 0)
            near = columns["far"] if c == 0 else [totals[c][2]]
            ins = [packs[s], value_block(c), cot_block(c), *within.get(c, []),
                   *near, totals[c][3], gain, rate_row, Far(token),
                   *map(Far, ups), *map(Far, downs)]
            return body, ins

        def do_chunk(c, token):
            body, ins = post_parts(c, token)
            more = [pltpu.VMEM(o.shape, o.dtype) for o in within_shapes] + flows()
            more = [] if len(within.get(c, ())) == 8 else more
            post[c] = run(body, [place, *ins], post_shapes, stored=(0,), scratch=work() + more)
            return post[c][3]

        def do_partial(cs, token, before=None):
            return run(
                partial_body(len(cs), before is not None),
                [Far(token), *[post[c][1] for c in cs], *[weight_block(c) for c in cs]]
                + ([] if before is None else [before]),
                [sds((length, width))],
            )[0]

        shares = [sds((length, width // parts))] * 2 if parts == 2 else [sds((length, width))]

        def send_share(term):
            if parts == 2:
                return term[0], lax.ppermute(term[1], "chan", [(0, 1), (1, 0)])
            share = lax.psum_scatter(term[0], "chan", scatter_dimension=1, tiled=True)
            return share, jnp.zeros_like(share)

        def do_term(s, before):
            mine = [c for c in range(chunks) if order[c][0] == s]
            return send_share(run(
                term_body(len(mine), 0, heads, parts, s == 1),
                [place, packs[s], select_weight, step_rows, before,
                 *[post[c][2] for c in mine], *[post[c][3] for c in mine]],
                shares,
            ))

        def do_last(c, before, token):
            s = order[c][0]
            mine = [n for n in range(chunks) if order[n][0] == s and n != c]
            body, ins = post_parts(c, token)
            sums = [select_weight, step_rows, before]
            others = [[post[n][k] for n in mine] for k in (2, 3)]
            if parts == 2:
                term = tile_body(len(mine) + 1, 1, heads, s == 1, False)
            else:
                term = term_body(len(mine) + 1, 1, heads, parts, s == 1)
            post[c] = run(
                last_body(body, term, len(ins)),
                [place, *ins, *sums, weight_block(c), *others[0], *others[1]],
                [*post_shapes, shares[0]],
                scratch=work(),
                stored=(0,),
            )
            if parts != 2:
                return send_share(post[c][4:])
            arriving = lax.ppermute(post[c][4], "chan", [(0, 1), (1, 0)])
            kept = run(
                tile_body(len(mine) + 1, 1, heads, s == 1, True),
                [place, packs[s], *sums, post[c][1], weight_block(c),
                 *others[0], post[c][2], *others[1], post[c][3]],
                [shares[0]],
            )[0]
            return kept, arriving

        def do_finish(s, share):
            return run(
                finish_body(s == 1), list(share), [sds((length, width // parts), BF)], stored=(0,)
            )[0]

        def do_step(k, widen, ends):
            has = [0 <= k - z < chunks and z < pairs - 1 for z in range(pairs)]
            ins = [place]
            for d in range(2):
                ins += [totals[k - z][d] for z in range(pairs) if has[z]]
                ins += [totals[k - z][3] for z in range(pairs) if has[z]]
            if k > 0:
                ins += [got[0][-1], got[1][-1] if k > 1 else got[0][-1]]
            outs = [sds(pair_shape), sds(pair_shape), token_shape]
            pieces = [] if widen is None else pieces_of(widen)
            if widen is not None:
                ins += [value_block(widen), cot_block(widen), *pieces]
                outs.append(wide_shape(len(pieces)))
            return run(
                step_body(has, k == 0, k == steps - 1, widen is not None, len(pieces), len(ends)),
                ins + [Far(e) for e in ends],
                outs,
            )

        def do_first_step(ends):
            s, k = order[0]
            out = run(
                first_step_body(pairs, k * group_heads, heads, head_width, len(ends)),
                [place, packs[s], far_row, *own_states, *map(Far, ends)],
                [sds(pair_shape), sds(pair_shape), token_shape, sds(pair_shape), sds(pair_shape),
                 sds((8, chunk))],
            )
            totals[0] = (out[3], out[4], None, out[5])
            columns["own"] = own_states
            return out

        def do_exchange(token):
            last = pairs - 1
            ups = [got[(z + 1) % 2][max(z - 1, 1 - z)] for z in range(pairs)]
            downs = [got[(last - z) % 2][max(z - 1, 1 - z)] for z in range(pairs)]
            sends = run(
                exchange_body(len(ups), len(downs)),
                [place, *columns["own"], totals[0][3], Far(token), *map(Far, ups), *map(Far, downs)],
                [sds(pair_shape), sds(pair_shape)],
                scratch=work(),
            )
            columns["far"] = [swap(x) for x in sends]

        def pieces_of(c):
            return [Block(packs[1], (length, LANES), (0, riders[c]))] if c in riders else []

        def do_widen(c, token):
            pieces = pieces_of(c)
            return run(
                widen_body, [value_block(c), cot_block(c), Far(token), *pieces], [wide_shape(len(pieces))]
            )[0]

        far[1] = swap(lax.optimization_barrier((wide, far_row))[0])
        ends = []
        halfway = None
        share = None
        for k in range(steps):
            queue = k + 2 if 0 < k < chunks - 2 else None
            made = do_first_step(ends) if k == 0 else do_step(k, queue, ends)
            token = made[2]
            got[0].append(lax.ppermute(made[0], "seq", edges[0]))
            got[1].append(lax.ppermute(made[1], "seq", edges[1]) if 0 < k < steps - 1 else None)
            ends = []
            if k == 0:
                v_more = do_values(list(range(1, groups - 1)), token)
                far[2] = swap(do_widen(2, token))
            if queue is not None:
                far[queue] = swap(made[3])
            if k + 1 < chunks:
                ends.append(do_pair(k + 1, token))
            if k == max(chunks - 2, pairs - 1):
                do_exchange(far[chunks - 1])
            if k == steps - 3:
                ends += columns["far"]
            moment = {0: ((1, 7), (0, 0)), 1: ((2, 3), (0, 0)), 2: ((4, 5), (0, 0)),
                      3: ((6, 0, 5), (0, 0, 1)), steps - 1: ((7,), (1,))}.get(k)
            if moment is not None:
                done = do_turn(*moment, token)
                ends += [done] if k < steps - 1 else []
            c = k - pairs + 1
            if c > 0:
                ends.append(do_chunk(c, token))
            if c == groups - 2:
                halfway = do_partial(list(range(1, groups - 1)), token)
                ends.append(halfway)
            if c == groups:
                share = do_term(0, do_partial([groups - 1, groups], token, halfway))
                ends.append(share[0])
            if c == groups + 1:
                ends.append(do_chunk(0, token))
            if c == groups + 2:
                grads[0] = do_finish(0, share)
                halfway = do_partial([groups + 1, 0, groups + 2], token)
        grads[1] = do_finish(1, do_last(chunks - 1, halfway, halfway))
        outs = [
            jnp.concatenate([post[order.index((s, k))][0] for k in range(groups)], axis=1)
            for s in range(2)
        ]
        return (outs[0], outs[1], grads[0], grads[1])

    return body


def solution(mesh):
    rows = P(("dp", "seq"), None)
    both = P(("dp", "seq"), "chan")
    in_specs = (
        rows, rows, P(None, "chan"), P(), P(None, "chan"),
        P("chan"), P("chan"), P("chan"), both, both,
    )
    return jax.shard_map(
        local(mesh.shape["seq"], mesh.shape["chan"]),
        mesh=mesh,
        in_specs=in_specs,
        out_specs=(both,) * 4,
        check_vma=False,
    )
```

```python
import jax
import jax.numpy as jnp
from jax import lax
from jax.experimental import pallas as pl
from jax.experimental.pallas import tpu as pltpu
from jax.sharding import PartitionSpec as P

BF = jnp.bfloat16
F32 = jnp.float32
LANES = 128


def mm(a, b, ca=1, cb=0):
    return lax.dot_general(a, b, (((ca,), (cb,)), ((), ())), preferred_element_type=F32)


def halves(x):
    high = x.astype(BF)
    return high, (x - high.astype(F32)).astype(BF)


def mm_exact(a, b, ca=1, cb=0):
    first, rest = b.astype(BF), None
    rest = b - first.astype(F32)
    second = rest.astype(BF)
    third = (rest - second.astype(F32)).astype(BF)
    return mm(a, first, ca, cb) + mm(a, second, ca, cb) + mm(a, third, ca, cb)


def iotas(rows, columns):
    return (
        lax.broadcasted_iota(jnp.int32, (rows, columns), 0),
        lax.broadcasted_iota(jnp.int32, (rows, columns), 1),
    )


def spread(weights, base, width, head_width):
    heads = weights[0].shape[1]
    row, channel = iotas(2 * heads, width)
    start = (jnp.where(row >= heads, row - heads, row) - base) * head_width
    pick = ((channel >= start) & (channel < start + head_width)).astype(BF)
    stacked = jnp.concatenate(weights, axis=0) if len(weights) > 1 else weights[0]
    out = mm(jnp.concatenate(halves(stacked), axis=1), pick)
    result, at = [], 0
    for w in weights:
        result.append(out[at : at + w.shape[0]])
        at += w.shape[0]
    return result


def spread_rows(rows, base, width, head_width):
    heads = rows[0].shape[1]
    wide = spread([jnp.broadcast_to(r, (8, heads)) for r in rows], base, width, head_width)
    return [w[0:1] for w in wide]


def gather_heads(parts, base, head_width):
    width = parts[0].shape[1]
    channel, head = iotas(width, LANES)
    start = (head - base) * head_width
    pick = ((channel >= start) & (channel < start + head_width)).astype(BF)
    out = mm(jnp.concatenate([x.astype(BF) for x in parts], axis=0), pick)
    result, at = [], 0
    for x in parts:
        result.append(out[at : at + x.shape[0]])
        at += x.shape[0]
    return result


def reversal(size):
    i, j = iotas(size, size)
    return (i + j == size - 1).astype(BF)


def flip_block(size):
    return 256 if size % 256 == 0 else 128


def sds(shape, dtype=F32):
    return jax.ShapeDtypeStruct(shape, dtype)


class Block:
    def __init__(self, array, shape, index):
        self.array, self.shape, self.index = array, shape, index

    def view(self, ref):
        if self.shape == self.array.shape:
            return ref
        return ref.at[tuple(pl.ds(i * b, b) for i, b in zip(self.index, self.shape))]


class Copied:
    def __init__(self, item):
        self.item = item if isinstance(item, Block) else Block(item, item.shape, (0,) * item.ndim)


class Far:
    def __init__(self, array):
        self.array = array


def run(body, ins, outs, scratch=(), limit=16, stored=()):
    specs, arrays, copied = [], [], []
    for item in ins:
        if isinstance(item, Far):
            specs.append(pl.BlockSpec(memory_space=pl.ANY))
            arrays.append(item.array)
        elif isinstance(item, Copied):
            specs.append(pl.BlockSpec(memory_space=pltpu.HBM))
            arrays.append(item.item.array)
            copied.append(item.item)
        elif isinstance(item, Block):
            specs.append(pl.BlockSpec(memory_space=pltpu.VMEM))
            arrays.append(item.array)
        else:
            space = pltpu.SMEM if item.dtype == jnp.int32 else pltpu.VMEM
            specs.append(pl.BlockSpec(memory_space=space))
            arrays.append(item)
    out_specs = [
        pl.BlockSpec(memory_space=pltpu.HBM if n in stored else pltpu.VMEM)
        for n in range(len(outs))
    ]
    holds = [pltpu.VMEM(q.shape, q.array.dtype) for q in copied]
    holds += [pltpu.VMEM(outs[n].shape, outs[n].dtype) for n in stored]
    sems = [pltpu.SemaphoreType.DMA((max(len(holds), 1),))]

    def kernel(*refs):
        refs = list(refs)
        take = lambda n: [refs.pop(0) for _ in range(n)]
        sources, targets = take(len(ins)), take(len(outs))
        held, (sem,) = take(len(holds)), take(1)
        args, copies = [], []
        for ref, item in zip(sources, ins):
            if isinstance(item, Copied):
                n = len(copies)
                copies.append(pltpu.make_async_copy(item.item.view(ref), held[n], sem.at[n]))
                copies[-1].start()
                ref = held[n]
            elif isinstance(item, Block):
                ref = item.view(ref)
            args.append(ref)
        back = []
        for n, ref in enumerate(targets):
            if n in stored:
                k = len(copied) + stored.index(n)
                back.append(pltpu.make_async_copy(held[k], ref, sem.at[k]))
                ref = held[k]
            args.append(ref)
        waits = {"waits": [c.wait for c in copies]} if copies else {}
        body(*args, *refs, **waits)
        for copy in back:
            copy.start()
        for copy in back:
            copy.wait()

    return pl.pallas_call(
        kernel,
        in_specs=specs,
        out_specs=out_specs,
        out_shape=outs,
        scratch_shapes=holds + sems + list(scratch),
        compiler_params=pltpu.CompilerParams(vmem_limit_bytes=limit * 1024 * 1024),
        cost_estimate=pl.CostEstimate(flops=0, bytes_accessed=1024, transcendentals=0),
    )(*arrays)


def start_body(
    hidden, other, select, step, bias, rate, weight, cot,
    source, pack0, pack1, row, v_out, wide, waits,
):
    for wait in waits[0:2]:
        wait()
    length, width = hidden.shape
    heads = bias.shape[1]
    source[0:length, :] = hidden[...]
    block = flip_block(width)
    turn = reversal(block)
    for j in range(width // block):
        source[length : 2 * length, j * block : (j + 1) * block] = mm(
            other[:, width - (j + 1) * block : width - j * block], turn
        ).astype(BF)
    for wait in waits[2:6]:
        wait()
    keys = mm(source[...], select[...]).astype(BF).astype(F32)
    state = keys.shape[1] // 2
    raw = mm(source[...], step[...], 1, 1) + bias[...]
    dt = jnp.maximum(raw, 0.0) + jnp.log1p(jnp.exp(-jnp.abs(raw)))
    rise = jax.nn.sigmoid(raw)
    i, j = iotas(length, length)
    lower = (i >= j).astype(BF)
    for s, pack in enumerate((pack0, pack1)):
        rows = slice(s * length, (s + 1) * length)
        drop = dt[rows] * rate[...]
        total = mm_exact(lower, drop)
        pack[...] = jnp.zeros(pack.shape, F32)
        pack[:, 0 : 2 * state] = keys[rows]
        at = 2 * state
        for part in (dt[rows], total, total - drop, rise[rows]):
            pack[:, at : at + heads] = part
            at += heads
    row[...] = jnp.zeros(row.shape, F32)
    row[0:1, 0:heads] = jnp.exp(
        -pack1[length - 1 : length, 2 * state + heads : 2 * state + 2 * heads]
    )
    for wait in waits[6:]:
        wait()
    for at in columns_of(weight.shape[1]):
        piece = mm(source[...], weight[:, at]).astype(BF)
        for s in range(2):
            v_out[0, s, :, at] = piece[s * length : (s + 1) * length]
        wide[0:length, at] = piece[0:length].astype(F32)
    wide[length : 2 * length, :] = cot[...].astype(F32)
    for n in range(3):
        at = 2 * length + n * piece_rows(length, wide.shape[1])
        put_piece(wide, at, pack0[:, n * LANES : (n + 1) * LANES])


def columns_of(width):
    block = min(256, width)
    return [slice(k * block, (k + 1) * block) for k in range(width // block)]


def values_body(source, token, *rest):
    weights, v_out = rest[:-1], rest[-1]
    length = v_out.shape[2]
    for n, weight in enumerate(weights):
        for at in columns_of(weight.shape[1]):
            piece = mm(source[...], weight[:, at]).astype(BF)
            for s in range(2):
                v_out[n, s, :, at] = piece[s * length : (s + 1) * length]


class Pack:
    def __init__(self, write, read, stats, heads):
        self.write, self.read = write, read
        self.dt = stats[:, 0:heads]
        self.total = stats[:, heads : 2 * heads]
        self.before = stats[:, 2 * heads : 3 * heads]
        last = self.total.shape[0]
        self.whole = self.total[last - 1 : last, :]
        self.from_start = jnp.exp(-self.total)
        self.from_end = jnp.exp(self.before - self.whole)
        self.to_end = jnp.exp(self.total - self.whole)
        self.to_start = jnp.exp(-self.before)
        self.through = jnp.exp(-self.whole)


def own_pack(ref, heads):
    return Pack(*[ref[:, n * LANES : (n + 1) * LANES] for n in range(3)], heads)


def piece_rows(length, width):
    return length // (width // LANES)


def put_piece(ref, row, piece):
    count = piece_rows(piece.shape[0], ref.shape[1])
    for b in range(ref.shape[1] // LANES):
        ref[row : row + count, b * LANES : (b + 1) * LANES] = piece[b * count : (b + 1) * count]


def get_piece(ref, row, length):
    count = piece_rows(length, ref.shape[1])
    return jnp.concatenate(
        [
            ref[row : row + count, b * LANES : (b + 1) * LANES]
            for b in range(ref.shape[1] // LANES)
        ],
        axis=0,
    )


def pair_body(base, heads, head_width, piece_at):
    def body(place, v_own, g_own, x_far, far0, far1, far2, own_ref, token, up, down, near, keep):
        first = place[0] == 0
        length, width = g_own.shape
        own = own_pack(own_ref, heads)
        far = Pack(*[get_piece(f, at, length) for f, at in zip((far0, far1, far2), piece_at)], heads)
        own_row, far_row = own.through, far.through
        rows = spread_rows([own_row * far_row, far_row], base, width, head_width)
        keep[...] = jnp.zeros(keep.shape, F32)
        keep[0:1, :] = rows[0]
        keep[1:2, :] = rows[1]
        own_up, own_down = jnp.where(first, far_row, 1.0), jnp.where(first, 1.0, far_row)
        far_up, far_down = jnp.where(first, 1.0, own_row), jnp.where(first, own_row, 1.0)
        for kind in range(2):
            rows = slice(kind * LANES, (kind + 1) * LANES)
            if kind == 0:
                keys = (own.write, far.write)
                ups = (own.dt * own.to_end, far.dt * far.to_end)
                downs = (own.dt * own.to_start, far.dt * far.to_start)
            else:
                keys = (own.read, far.read)
                ups = (own.from_end, far.from_end)
                downs = (own.from_start, far.from_start)
            x_own = (v_own if kind == 0 else g_own)[...].reshape(length, width).astype(F32)
            x_other = x_far[kind * length : (kind + 1) * length, :]
            w = spread(
                [ups[0] * own_up, ups[1] * far_up, downs[0] * own_down, downs[1] * far_down,
                 jnp.where(first, downs[1], ups[1])],
                base, width, head_width,
            )
            key = jnp.concatenate(keys, axis=0).astype(BF)
            both = lambda a, b: jnp.concatenate([(a * x_own).astype(BF), (b * x_other).astype(BF)], axis=0)
            up[rows, :] = mm(key, both(w[0], w[1]), 0, 0)
            down[rows, :] = mm(key, both(w[2], w[3]), 0, 0)
            near[rows, :] = mm(keys[1].astype(BF), (w[4] * x_other).astype(BF), 0, 0)

    return body


def column_body(base, heads, head_width):
    def body(own_ref, source, weight, g_own, v_out, own_up, own_down, waits):
        length, width = g_own.shape
        own = own_pack(own_ref, heads)
        w_values = spread([own.dt * own.to_end, own.dt * own.to_start], base, width, head_width)
        w_grads = spread([own.from_end, own.from_start], base, width, head_width)
        write, read = own.write.astype(BF), own.read.astype(BF)
        waits[0]()
        for at in columns_of(width):
            piece = mm(source[...], weight[:, at]).astype(BF)
            for s in range(2):
                v_out[0, s, :, at] = piece[s * length : (s + 1) * length]
            v, g = piece[length:].astype(F32), g_own[:, at].astype(F32)
            for out, n in ((own_up, 0), (own_down, 1)):
                out[0:LANES, at] = mm(write, (w_values[n][:, at] * v).astype(BF), 0, 0)
                out[LANES : 2 * LANES, at] = mm(read, (w_grads[n][:, at] * g).astype(BF), 0, 0)

    return body


def column_totals(place, own_ref, far_row_ref, base, heads, head_width, owns, totals, keep):
    first = place[0] == 0
    width = keep.shape[1]
    own = own_pack(own_ref, heads)
    far_row = far_row_ref[0:1, 0:heads]
    rows = spread_rows([own.through * far_row, far_row, own.through], base, width, head_width)
    keep[...] = jnp.zeros(keep.shape, F32)
    for n, row in enumerate(rows):
        keep[n : n + 1, :] = row
    totals[0][...] = jnp.where(first, rows[1], 1.0) * owns[0][...]
    totals[1][...] = jnp.where(first, 1.0, rows[1]) * owns[1][...]


def first_step_body(pairs, base, heads, head_width, tokens):
    def body(place, own_ref, far_row_ref, own_up, own_down, *rest):
        send_a, send_b, token, up, down, keep = rest[tokens:]
        column_totals(
            place, own_ref, far_row_ref, base, heads, head_width, (own_up, own_down), (up, down), keep
        )
        token[...] = jnp.zeros(token.shape, F32)
        sends = (send_a, send_b)
        for d, total in enumerate((up, down)):
            spot = place[1] if d == 0 else pairs - 1 - place[1]
            for n in range(pairs):
                z = n if d == 0 else pairs - 1 - n
                send = sends[(z + d) % 2]

                @pl.when(spot == n)
                def _():
                    send[...] = total[...] if n == 0 else jnp.zeros(send.shape, F32)

    return body


def exchange_body(ups, downs):
    def body(place, own_up, own_down, keep, token, *rest):
        up_in, down_in = rest[0:ups], rest[ups : ups + downs]
        up_out, down_out, bufs, sems = rest[ups + downs :]
        up_spot, down_spot = place[1], len(up_in) - 1 - place[1]
        fetch_start(up_in, up_spot, bufs.at[0], sems.at[0])
        fetch_start(down_in, down_spot, bufs.at[1], sems.at[1])
        fetch_wait(up_in, up_spot, bufs.at[0], sems.at[0])
        fetch_wait(down_in, down_spot, bufs.at[1], sems.at[1])
        first = place[0] == 0
        row = keep[2:3, :]
        up_out[...] = jnp.where(first, row * bufs[0] + own_up[...], bufs[0])
        down_out[...] = jnp.where(first, bufs[1], row * bufs[1] + own_down[...])

    return body


def fetch_start(options, index, target, sem):
    for z, option in enumerate(options):
        if option is not None:

            @pl.when(index == z)
            def _():
                pltpu.make_async_copy(option, target, sem).start()


def fetch_wait(options, index, target, sem):
    for z, option in enumerate(options):
        if option is not None:

            @pl.when(index == z)
            def _():
                pltpu.make_async_copy(option, target, sem).wait()


def step_body(has, first_step, widen, pieces, tokens):
    pairs = len(has)

    def body(place, *rest):
        rest = list(rest)
        take = lambda n: [rest.pop(0) for _ in range(n)]
        sides = []
        for d in range(2):
            totals = [take(1)[0] if h else None for h in has]
            keeps = [take(1)[0] if h else None for h in has]
            sides.append((totals, keeps))
        got = None if first_step else take(2)
        chunk = take(2) if widen else None
        piece_refs = take(pieces)
        take(tokens)
        sends = take(2)
        token = take(1)[0]
        spots = (place[1], pairs - 1 - place[1])
        for d, (totals, keeps) in enumerate(sides):
            for n in range(pairs):
                z = n if d == 0 else pairs - 1 - n
                send = sends[(z + d) % 2]

                @pl.when(spots[d] == n)
                def _():
                    if not has[n]:
                        send[...] = jnp.zeros(send.shape, F32)
                    elif got is None or n == 0:
                        send[...] = totals[n][...]
                    else:
                        send[...] = totals[n][...] + keeps[n][0:1, :] * got[(z + 1 + d) % 2][...]

        token[...] = jnp.zeros(token.shape, F32)
        if widen:
            put_chunk(take(1)[0], *chunk, piece_refs)

    return body


def within_body(base, heads, head_width):
    def body(own_ref, v_ref, g_ref, rate, token, y_out, x_out, keys_out, steps_out, cols_s):
        own = own_pack(own_ref, heads)
        length, width = g_ref.shape
        write, read = own.write.astype(BF), own.read.astype(BF)
        scores = mm(read, write, 1, 1)
        i, j = iotas(length, length)
        low = i > j
        high = i < j
        doubled = jnp.where(i == j, 2.0, 1.0).astype(F32)
        scores2 = scores * doubled
        turned = own_ref[:, 2 * LANES : 3 * LANES].T
        lane = lax.broadcasted_iota(jnp.int32, (length, LANES), 1)
        d_scores = jnp.zeros((length, length), F32)
        out_low = jnp.zeros((length, LANES), F32)
        out_high = jnp.zeros((length, LANES), F32)
        cols_s[...] = jnp.zeros(cols_s.shape, F32)
        v_all = v_ref[...].reshape(length, width)
        per = LANES // head_width
        for n in range(width // LANES):
            at = slice(n * LANES, (n + 1) * LANES)
            v, g = v_all[:, at], g_ref[:, at]
            mine = [(lane >= m * head_width) & (lane < (m + 1) * head_width) for m in range(per)]
            v_heads = jnp.concatenate([jnp.where(x, v, jnp.zeros_like(v)) for x in mine], axis=0)
            g_heads = jnp.concatenate([jnp.where(x, g, jnp.zeros_like(g)) for x in mine], axis=0)
            products = mm(g_heads, v, 1, 1)
            plains, steppeds = [], []
            for m in range(per):
                h = base + n * per + m
                c_col = own.total[:, h : h + 1]
                e_col = own.before[:, h : h + 1]
                dt_row = turned[h : h + 1, :]
                c_row = turned[heads + h : heads + h + 1, :]
                e_row = turned[2 * heads + h : 2 * heads + h + 1, :]
                decay = jnp.exp(jnp.where(low, c_row - c_col, e_col - e_row))
                plain = decay * scores2
                plains.append(plain.astype(BF))
                steppeds.append((plain * dt_row).astype(BF))
                inner = decay * dt_row * products[m * length : (m + 1) * length]
                d_scores = d_scores + inner
                flow = inner * scores
                flow_low = jnp.where(low, flow, 0.0)
                flow_high = jnp.where(high, flow, 0.0)
                out_low = jnp.where(lane == h, jnp.sum(flow_low, 1, keepdims=True), out_low)
                out_high = jnp.where(lane == h, jnp.sum(flow_high, 1, keepdims=True), out_high)
                cols_s[0, h : h + 1, :] = jnp.sum(flow_low, 0, keepdims=True)
                cols_s[1, h : h + 1, :] = jnp.sum(flow_high, 0, keepdims=True)
            y_out[:, at] = mm(jnp.concatenate(steppeds, axis=1), v_heads)
            x_out[:, at] = mm(jnp.concatenate(plains, axis=0), g_heads, 0, 0)
        d_scores = (d_scores * doubled).astype(BF)
        keys_out[:, 0:LANES] = mm(d_scores, read, 0, 0)
        keys_out[:, LANES : 2 * LANES] = mm(d_scores, write)
        net_low = out_low - cols_s[0].T
        net_high = out_high - cols_s[1].T
        at_or_after = (j >= i).astype(BF)
        after = (j > i).astype(BF)
        steps_out[...] = -rate[...] * (mm_exact(at_or_after, net_low) - mm_exact(after, net_high))

    return body


def post_body(base, heads, head_width, ups, downs, columns=False):
    def body(
        place, own_ref, v_ref, g_ref, yw, xw, keys_w, steps_w, near, keep, skip, rate, token, *rest
    ):
        up_in, down_in = rest[0:ups], rest[ups : ups + downs]
        mixed, dv_out, keys_out, steps_out, bufs, sems = rest[ups + downs :]
        up_spot, down_spot = place[1], len(up_in) - 1 - place[1]
        fetch_start(up_in, up_spot, bufs.at[0], sems.at[0])
        fetch_start(down_in, down_spot, bufs.at[1], sems.at[1])
        first = place[0] == 0
        own = own_pack(own_ref, heads)
        length, width = g_ref.shape
        far_row = keep[1:2, :]
        own_row, gain = spread_rows([own.through, skip[...]], base, width, head_width)
        up_row = jnp.where(first, 1.0, far_row)
        down_row = jnp.where(first, far_row, 1.0)
        dt, from_start, from_end, to_end, to_start = spread(
            [own.dt, own.from_start, own.from_end, own.to_end, own.to_start],
            base, width, head_width,
        )
        write, read = own.write.astype(BF), own.read.astype(BF)
        v = v_ref[...].reshape(length, width).astype(F32)
        g = g_ref[...].astype(F32)
        fetch_wait(up_in, up_spot, bufs.at[0], sems.at[0])
        fetch_wait(down_in, down_spot, bufs.at[1], sems.at[1])
        if columns:
            up = up_row * bufs[0] + near[0][...]
            down = down_row * bufs[1] + near[1][...]
        else:
            up = up_row * bufs[0] + jnp.where(first, 0.0, near[...])
            down = down_row * bufs[1] + jnp.where(first, near[...], 0.0)
        p, ab = up[0:LANES], up[LANES : 2 * LANES]
        q, af = down[0:LANES], down[LANES : 2 * LANES]
        crossing = jnp.sum(p * af + q * ab, axis=0, keepdims=True)
        p, q, af, ab = p.astype(BF), q.astype(BF), af.astype(BF), ab.astype(BF)
        y_p = from_start * mm(read, p)
        y_q = from_end * mm(read, q)
        x_f = to_end * mm(write, af)
        x_b = to_start * mm(write, ab)
        mixed[...] = (yw[...] + y_p + y_q + gain * v).astype(BF)
        x = xw[...] + x_f + x_b
        dv_out[...] = (dt * x + gain * g).astype(BF)
        dtv = dt * v
        keys_out[:, 0:LANES] = (
            keys_w[:, 0:LANES]
            + mm((to_end * dtv).astype(BF), af, 1, 1)
            + mm((to_start * dtv).astype(BF), ab, 1, 1)
        )
        keys_out[:, LANES : 2 * LANES] = (
            keys_w[:, LANES : 2 * LANES]
            + mm((from_start * g).astype(BF), p, 1, 1)
            + mm((from_end * g).astype(BF), q, 1, 1)
        )
        lane = lax.broadcasted_iota(jnp.int32, (length, LANES), 1)
        steps = jnp.where(lane < heads, own_ref[:, 2 * LANES : 3 * LANES], 0.0)
        direct, a_p, a_q, b_f, b_b, through = gather_heads(
            [v * x, g * y_p, g * y_q, v * x_f, v * x_b, jnp.broadcast_to(crossing * own_row, (8, width))],
            base, head_width,
        )
        i, j = iotas(length, length)
        masks = jnp.concatenate([j >= i, j <= i, j < i, j > i], axis=1).astype(F32).astype(BF)
        high, low = halves(jnp.concatenate([a_p, a_q, b_f * steps, b_b * steps], axis=0))
        flow = mm(masks, high) + mm(masks, low) + through[0:1]
        steps_out[...] = steps_w[...] + direct - rate[...] * flow

    return body


class Either:
    def __init__(self, choice, a, b):
        self.choice, self.a, self.b = choice, a, b

    def __getitem__(self, index):
        return jnp.where(self.choice, self.a[index], self.b[index])


def either_within(post):
    def body(place, own_ref, v_ref, g_ref, *rest):
        merged = [Either(place[3] == 0, a, b) for a, b in zip(rest[0:4], rest[4:8])]
        post(place, own_ref, v_ref, g_ref, *merged, *rest[8:])

    return body


def split_body(within, post, columns):
    def body(place, own_ref, v_ref, g_ref, *rest):
        bufs, sems, yw, xw, keys_w, steps_w, cols_s = rest[-7:]
        before, rest = rest[0:4], rest[4:]
        nears = 2 if columns else 1
        near = rest[0:2] if columns else rest[0]
        keep, skip, rate, token, *rest = rest[nears:]

        @pl.when(place[3] == 1)
        def _():
            within(own_ref, v_ref, g_ref, rate, token, yw, xw, keys_w, steps_w, cols_s)

        merged = [Either(place[3] == 0, a, b) for a, b in zip(before, (yw, xw, keys_w, steps_w))]
        post(place, own_ref, v_ref, g_ref, *merged, near, keep, skip, rate, token, *rest[:-5])

    return body


def turn_body(works, strands, turn):
    def body(place, pack0, pack1, rate, *rest):
        count = len(works)
        blocks, token = rest[0 : 2 * count], rest[2 * count]
        outs, flows = rest[2 * count + 1 : -1], rest[-1]

        @pl.when(place[3] == turn)
        def _():
            for n, work in enumerate(works):
                work(
                    (pack0, pack1)[strands[n]], blocks[2 * n], blocks[2 * n + 1], rate, token,
                    *outs[4 * n : 4 * n + 4], flows,
                )

    return body


def chunk_body(within, post, columns):
    def body(place, own_ref, v_ref, g_ref, *rest):
        nears = 2 if columns else 1
        near = rest[0:2] if columns else rest[0]
        keep, skip, rate, token, *rest = rest[nears:]
        bufs, sems, yw, xw, keys_w, steps_w, cols_s = rest[-7:]
        within(own_ref, v_ref, g_ref, rate, token, yw, xw, keys_w, steps_w, cols_s)
        post(
            place, own_ref, v_ref, g_ref, yw, xw, keys_w, steps_w, near, keep, skip, rate, token,
            *rest[:-5],
        )

    return body


def partial_body(groups, more):
    def body(token, *rest):
        dvs, weights, rest = rest[0:groups], rest[groups : 2 * groups], rest[2 * groups :]
        out = rest[-1]
        for at in columns_of(out.shape[1]):
            total = rest[0][:, at] if more else 0.0
            for dv, weight in zip(dvs, weights):
                total = total + mm(dv[...], weight[at, :], 1, 1)
            out[:, at] = total

    return body


def term_body(groups, tails, heads, parts, swap):
    def body(place, own_ref, select, step, before, *rest):
        dvs, weights = rest[0:tails], rest[tails : 2 * tails]
        rest = rest[2 * tails :]
        keys, steps = rest[0:groups], rest[groups : 2 * groups]
        outs = rest[2 * groups :]
        d_keys, d_steps = keys[0][...], steps[0][...]
        for a, b in zip(keys[1:], steps[1:]):
            d_keys = d_keys + a[...]
            d_steps = d_steps + b[...]
        d_raw = d_steps[:, 0:heads] * own_ref[:, 2 * LANES + 3 * heads : 2 * LANES + 4 * heads]
        keys_high, keys_low = halves(d_keys)
        raw_high, raw_low = halves(d_raw)
        width = select.shape[0]
        block = width // parts
        tiles = []
        for b in range(parts):
            rows = slice(b * block, (b + 1) * block)
            total = before[:, rows]
            total = total + mm(keys_high, select[rows, :], 1, 1) + mm(keys_low, select[rows, :], 1, 1)
            total = total + mm(raw_high, step[:, rows]) + mm(raw_low, step[:, rows])
            for k in range(tails):
                total = total + mm(dvs[k][...], weights[k][rows, :], 1, 1)
            tiles.append(total)
        if swap:
            tiles = tiles[::-1]
        if parts == 2:
            first = place[2] == 0
            outs[0][...] = jnp.where(first, tiles[0], tiles[1])
            outs[1][...] = jnp.where(first, tiles[1], tiles[0])
        else:
            for b in range(parts):
                outs[0][:, b * block : (b + 1) * block] = tiles[b]

    return body


def tile_body(groups, tails, heads, swap, keep):
    def body(place, own_ref, select, step, before, *rest):
        dvs, weights = rest[0:tails], rest[tails : 2 * tails]
        rest = rest[2 * tails :]
        keys, steps, out = rest[0:groups], rest[groups : 2 * groups], rest[-1]
        d_keys, d_steps = keys[0][...], steps[0][...]
        for a, b in zip(keys[1:], steps[1:]):
            d_keys = d_keys + a[...]
            d_steps = d_steps + b[...]
        d_raw = d_steps[:, 0:heads] * own_ref[:, 2 * LANES + 3 * heads : 2 * LANES + 4 * heads]
        keys_high, keys_low = halves(d_keys)
        raw_high, raw_low = halves(d_raw)
        block = out.shape[1]
        mine = place[2] if keep != swap else 1 - place[2]
        rows = pl.ds(pl.multiple_of(mine * block, block), block)
        total = before[:, rows]
        total = total + mm(keys_high, select[rows, :], 1, 1) + mm(keys_low, select[rows, :], 1, 1)
        total = total + mm(raw_high, step[:, rows]) + mm(raw_low, step[:, rows])
        for dv, weight in zip(dvs, weights):
            total = total + mm(dv[...], weight[rows, :], 1, 1)
        out[...] = total

    return body


def last_body(work, term, work_ins):
    def body(place, *rest):
        rest = list(rest)
        take = lambda n: [rest.pop(0) for _ in range(n)]
        for_work = take(work_ins)
        select, step, before, weight = take(4)
        others = take(len(rest) - 7)
        half = len(others) // 2
        mixed, dv, keys, steps, out = take(5)
        bufs, sems = take(2)
        work(place, *for_work, mixed, dv, keys, steps, bufs, sems)
        term(
            place, for_work[0], select, step, before, dv, weight,
            *others[:half], keys, *others[half:], steps, out,
        )

    return body


def finish_body(flip):
    def body(a, b, out):
        total = (a[...] + b[...]).astype(BF)
        if not flip:
            out[...] = total
            return
        width = total.shape[1]
        block = flip_block(width)
        turn = reversal(block)
        for j in range(width // block):
            out[:, j * block : (j + 1) * block] = mm(
                total[:, width - (j + 1) * block : width - j * block], turn
            ).astype(BF)

    return body


def put_chunk(wide, v_ref, g_ref, pieces):
    length, width = g_ref.shape
    wide[0:length, :] = v_ref[...].reshape(length, width).astype(F32)
    wide[length : 2 * length, :] = g_ref[...].astype(F32)
    for n, piece in enumerate(pieces):
        put_piece(wide, 2 * length + n * piece_rows(length, width), piece[...])


def widen_body(v_ref, g_ref, token, *rest):
    put_chunk(rest[-1], v_ref, g_ref, rest[:-1])


def local(shards, parts):
    pairs = shards // 2

    def body(
        hidden, complement, inner_weight, select_weight, step_weight, step_bias, decay_rate,
        skip_gain, cotangent, complement_cotangent,
    ):
        length, width = hidden.shape
        inner = inner_weight.shape[1]
        heads = step_bias.shape[0]
        head_width = inner // heads
        groups = 4
        chunk = inner // groups
        group_heads = heads // groups
        seq = lax.axis_index("seq")
        place = jnp.stack(
            [seq % 2, seq // 2, lax.axis_index("chan"), lax.axis_index("dp")]
        ).astype(jnp.int32)
        bias = step_bias.reshape(1, heads)
        rate = decay_rate.reshape(1, heads)
        rate_row = jnp.pad(rate, ((0, 0), (0, LANES - heads)))
        gain = skip_gain.reshape(1, heads)
        step_rows = step_weight.T
        cots = (cotangent, complement_cotangent)
        swap_pairs = [(a, a ^ 1) for a in range(shards)]
        edges = []
        for start in range(2):
            meets = [(z, z + 1) for z in range(start, pairs - 1, 2)]
            paired = sum(meets, ())
            meets += [(b, a) for a, b in meets] + [(z, z) for z in range(pairs) if z not in paired]
            edges.append([(2 * a + y, 2 * b + y) for a, b in meets for y in range(2)])
        swap = lambda x: lax.ppermute(x, "seq", swap_pairs)
        pack_shape = (length, 3 * LANES)
        pair_shape = (2 * LANES, chunk)
        wide_shape = lambda pieces: sds((2 * length + pieces * piece_rows(length, chunk), chunk))
        token_shape = sds((8, LANES))
        work = lambda: [pltpu.VMEM((2,) + pair_shape, F32), pltpu.SemaphoreType.DMA((2,))]
        order = [(1, groups - 1)] + [(0, k) for k in range(groups)] + [(1, k) for k in range(groups - 1)]
        chunks = len(order)

        source, pack0, pack1, row, v_zero, wide = run(
            start_body,
            [*map(Copied, (hidden, complement, select_weight, step_rows, bias, rate)),
             Copied(Block(inner_weight, (width, chunk), (0, 0))),
             Copied(Block(cots[0], (length, chunk), (0, 0)))],
            [sds((2 * length, width), BF), sds(pack_shape), sds(pack_shape), token_shape,
             sds((1, 2, length, chunk), BF), wide_shape(3)],
            limit=57,
        )
        packs = (pack0, pack1)
        far_row = swap(row)

        def weight_of(k):
            return Block(inner_weight, (width, chunk), (0, k))

        def do_values(ks, token):
            return run(
                values_body,
                [source, Far(token), *map(weight_of, ks)],
                [sds((len(ks), 2, length, chunk), BF)],
            )[0]

        v_last, *own_states = run(
            column_body((groups - 1) * group_heads, heads, head_width),
            [pack1, source, Copied(weight_of(groups - 1)),
             Block(cots[1], (length, chunk), (0, groups - 1))],
            [sds((1, 2, length, chunk), BF), sds(pair_shape), sds(pair_shape)],
            limit=48,
        )
        v_more = None

        def value_block(c):
            s, k = order[c]
            array, n = {0: (v_zero, 0), groups - 1: (v_last, 0)}.get(k, (v_more, k - 1))
            return Block(array, (1, 1, length, chunk), (n, s, 0, 0))

        def cot_block(c):
            s, k = order[c]
            return Block(cots[s], (length, chunk), (0, k))

        def weight_block(c):
            return weight_of(order[c][1])

        far = {}
        totals, within, post = {}, {}, {}
        got = ([], [])
        grads = [None, None]
        riders = {2 + n: n for n in range(3)}
        columns = {}
        steps = chunks + pairs - 2

        def do_pair(c, token):
            s, k = order[c]
            rows = piece_rows(length, chunk)
            if s == 0:
                pieces, piece_at = [far[1]] * 3, [2 * length + n * rows for n in range(3)]
            else:
                pieces, piece_at = [far[r] for r in riders], [2 * length] * 3
            totals[c] = run(
                pair_body(k * group_heads, heads, head_width, piece_at),
                [place, value_block(c), cot_block(c), far[c], *pieces, packs[s], Far(token)],
                [sds(pair_shape), sds(pair_shape), sds(pair_shape), sds((8, chunk))],
            )
            return totals[c][3]

        within_shapes = [
            sds((length, chunk)), sds((length, chunk)), sds((length, 2 * LANES)), sds((length, LANES))
        ]
        post_shapes = [
            sds((length, chunk), BF), sds((length, chunk), BF), sds((length, 2 * LANES)), sds((length, LANES))
        ]
        flows = lambda: [pltpu.VMEM((2, LANES, length), F32)]

        def do_within(c, token):
            s, k = order[c]
            within[c] = run(
                within_body(k * group_heads, heads, head_width),
                [packs[s], value_block(c), cot_block(c), rate_row, Far(token)],
                within_shapes,
                scratch=flows(),
            )
            return within[c][3]

        def do_turn(cs, turn, token):
            blocks = [b for c in cs for b in (value_block(c), cot_block(c))]
            works = [within_body(order[c][1] * group_heads, heads, head_width) for c in cs]
            out = run(
                turn_body(works, [order[c][0] for c in cs], turn),
                [place, *packs, rate_row, *blocks, Far(token)],
                within_shapes * len(cs),
                scratch=flows(),
            )
            for n, c in enumerate(cs):
                within[c] = within.get(c, []) + list(out[4 * n : 4 * n + 4])
            return out[3]

        def post_parts(c, token):
            s, k = order[c]
            last = pairs - 1
            ups = [got[(z + 1) % 2][max(c + z - 1, c, 1 - z)] for z in range(pairs)]
            downs = [got[(last - z) % 2][max(c + z - 1, c, 1 - z)] for z in range(pairs)]
            body = post_body(k * group_heads, heads, head_width, len(ups), len(downs), c == 0)
            work = within_body(k * group_heads, heads, head_width)
            if len(within.get(c, ())) == 8:
                body = either_within(body)
            elif c in within:
                body = split_body(work, body, c == 0)
            else:
                body = chunk_body(work, body, c == 0)
            near = columns["far"] if c == 0 else [totals[c][2]]
            ins = [packs[s], value_block(c), cot_block(c), *within.get(c, []),
                   *near, totals[c][3], gain, rate_row, Far(token),
                   *map(Far, ups), *map(Far, downs)]
            return body, ins

        def do_chunk(c, token):
            body, ins = post_parts(c, token)
            more = [pltpu.VMEM(o.shape, o.dtype) for o in within_shapes] + flows()
            post[c] = run(body, [place, *ins], post_shapes, stored=(0,), scratch=work() + more)
            return post[c][3]

        def do_partial(cs, token, before=None):
            return run(
                partial_body(len(cs), before is not None),
                [Far(token), *[post[c][1] for c in cs], *[weight_block(c) for c in cs]]
                + ([] if before is None else [before]),
                [sds((length, width))],
            )[0]

        shares = [sds((length, width // parts))] * 2 if parts == 2 else [sds((length, width))]

        def send_share(term):
            if parts == 2:
                return term[0], lax.ppermute(term[1], "chan", [(0, 1), (1, 0)])
            share = lax.psum_scatter(term[0], "chan", scatter_dimension=1, tiled=True)
            return share, jnp.zeros_like(share)

        def do_term(s, before):
            mine = [c for c in range(chunks) if order[c][0] == s]
            return send_share(run(
                term_body(len(mine), 0, heads, parts, s == 1),
                [place, packs[s], select_weight, step_rows, before,
                 *[post[c][2] for c in mine], *[post[c][3] for c in mine]],
                shares,
            ))

        def do_last(c, before, token):
            s = order[c][0]
            mine = [n for n in range(chunks) if order[n][0] == s and n != c]
            body, ins = post_parts(c, token)
            sums = [select_weight, step_rows, before]
            others = [[post[n][k] for n in mine] for k in (2, 3)]
            if parts == 2:
                term = tile_body(len(mine) + 1, 1, heads, s == 1, False)
            else:
                term = term_body(len(mine) + 1, 1, heads, parts, s == 1)
            post[c] = run(
                last_body(body, term, len(ins)),
                [place, *ins, *sums, weight_block(c), *others[0], *others[1]],
                [*post_shapes, shares[0]],
                scratch=work(),
                stored=(0,),
            )
            if parts != 2:
                return send_share(post[c][4:])
            arriving = lax.ppermute(post[c][4], "chan", [(0, 1), (1, 0)])
            kept = run(
                tile_body(len(mine) + 1, 1, heads, s == 1, True),
                [place, packs[s], *sums, post[c][1], weight_block(c),
                 *others[0], post[c][2], *others[1], post[c][3]],
                [shares[0]],
            )[0]
            return kept, arriving

        def do_finish(s, share):
            return run(
                finish_body(s == 1), list(share), [sds((length, width // parts), BF)], stored=(0,)
            )[0]

        def do_step(k, widen, ends):
            has = [0 <= k - z < chunks and z < pairs - 1 for z in range(pairs)]
            ins = [place]
            for d in range(2):
                ins += [totals[k - z][d] for z in range(pairs) if has[z]]
                ins += [totals[k - z][3] for z in range(pairs) if has[z]]
            if k > 0:
                ins += [got[0][-1], got[1][-1] if k > 1 else got[0][-1]]
            outs = [sds(pair_shape), sds(pair_shape), token_shape]
            pieces = [] if widen is None else pieces_of(widen)
            if widen is not None:
                ins += [value_block(widen), cot_block(widen), *pieces]
                outs.append(wide_shape(len(pieces)))
            return run(
                step_body(has, k == 0, widen is not None, len(pieces), len(ends)),
                ins + [Far(e) for e in ends],
                outs,
            )

        def do_first_step(ends):
            s, k = order[0]
            out = run(
                first_step_body(pairs, k * group_heads, heads, head_width, len(ends)),
                [place, packs[s], far_row, *own_states, *map(Far, ends)],
                [sds(pair_shape), sds(pair_shape), token_shape, sds(pair_shape), sds(pair_shape),
                 sds((8, chunk))],
            )
            totals[0] = (out[3], out[4], None, out[5])
            columns["own"] = own_states
            return out

        def do_exchange(token):
            last = pairs - 1
            ups = [got[(z + 1) % 2][max(z - 1, 1 - z)] for z in range(pairs)]
            downs = [got[(last - z) % 2][max(z - 1, 1 - z)] for z in range(pairs)]
            sends = run(
                exchange_body(len(ups), len(downs)),
                [place, *columns["own"], totals[0][3], Far(token), *map(Far, ups), *map(Far, downs)],
                [sds(pair_shape), sds(pair_shape)],
                scratch=work(),
            )
            columns["far"] = [swap(x) for x in sends]

        def pieces_of(c):
            return [Block(packs[1], (length, LANES), (0, riders[c]))] if c in riders else []

        def do_widen(c, token):
            pieces = pieces_of(c)
            return run(
                widen_body, [value_block(c), cot_block(c), Far(token), *pieces], [wide_shape(len(pieces))]
            )[0]

        far[1] = swap(lax.optimization_barrier((wide, far_row))[0])
        ends = []
        halfway = None
        share = None
        for k in range(steps):
            queue = k + 2 if 0 < k < chunks - 2 else None
            made = do_first_step(ends) if k == 0 else do_step(k, queue, ends)
            token = made[2]
            got[0].append(lax.ppermute(made[0], "seq", edges[0]))
            got[1].append(lax.ppermute(made[1], "seq", edges[1]) if 0 < k < steps - 1 else None)
            ends = []
            if k == 0:
                v_more = do_values(list(range(1, groups - 1)), token)
                far[2] = swap(do_widen(2, token))
            if queue is not None:
                far[queue] = swap(made[3])
            if k + 1 < chunks:
                ends.append(do_pair(k + 1, token))
            if k == max(chunks - 2, pairs - 1):
                do_exchange(far[chunks - 1])
            if k == steps - 3:
                ends.append(columns["far"][0])
            for cs in {1: [(2, 3)], 2: [(4, 5)], 3: [(6, 0)], 4: [(7,)]}.get(k, ()):
                ends.append(do_turn(cs, 0, token))
            if k == steps - 1:
                do_turn((7,), 1, token)
            c = k - pairs + 1
            if c > 0:
                late = columns["far"][1] if k == steps - 2 else token
                ends.append(do_chunk(c, late))
            if c == groups - 2:
                halfway = do_partial(list(range(1, groups - 1)), token)
                ends.append(halfway)
            if c == groups:
                share = do_term(0, do_partial([groups - 1, groups], token, halfway))
                ends.append(share[0])
            if c == groups + 1:
                ends.append(do_chunk(0, token))
            if c == groups + 2:
                grads[0] = do_finish(0, share)
                halfway = do_partial([groups + 1, 0, groups + 2], token)
        grads[1] = do_finish(1, do_last(chunks - 1, halfway, halfway))
        outs = [
            jnp.concatenate([post[order.index((s, k))][0] for k in range(groups)], axis=1)
            for s in range(2)
        ]
        return (outs[0], outs[1], grads[0], grads[1])

    return body


def solution(mesh):
    rows = P(("dp", "seq"), None)
    both = P(("dp", "seq"), "chan")
    in_specs = (
        rows, rows, P(None, "chan"), P(), P(None, "chan"),
        P("chan"), P("chan"), P("chan"), both, both,
    )
    return jax.shard_map(
        local(mesh.shape["seq"], mesh.shape["chan"]),
        mesh=mesh,
        in_specs=in_specs,
        out_specs=(both,) * 4,
        check_vma=False,
    )
```

```python
import jax
import jax.numpy as jnp
from jax import lax
from jax.experimental import pallas as pl
from jax.experimental.pallas import tpu as pltpu
from jax.sharding import PartitionSpec as P

BF = jnp.bfloat16
F32 = jnp.float32
LANES = 128


def mm(a, b, ca=1, cb=0):
    return lax.dot_general(a, b, (((ca,), (cb,)), ((), ())), preferred_element_type=F32)


def halves(x):
    high = x.astype(BF)
    return high, (x - high.astype(F32)).astype(BF)


def mm_exact(a, b, ca=1, cb=0):
    first, rest = b.astype(BF), None
    rest = b - first.astype(F32)
    second = rest.astype(BF)
    third = (rest - second.astype(F32)).astype(BF)
    return mm(a, first, ca, cb) + mm(a, second, ca, cb) + mm(a, third, ca, cb)


def iotas(rows, columns):
    return (
        lax.broadcasted_iota(jnp.int32, (rows, columns), 0),
        lax.broadcasted_iota(jnp.int32, (rows, columns), 1),
    )


def spread(weights, base, width, head_width):
    heads = weights[0].shape[1]
    row, channel = iotas(2 * heads, width)
    start = (jnp.where(row >= heads, row - heads, row) - base) * head_width
    pick = ((channel >= start) & (channel < start + head_width)).astype(BF)
    stacked = jnp.concatenate(weights, axis=0) if len(weights) > 1 else weights[0]
    out = mm(jnp.concatenate(halves(stacked), axis=1), pick)
    result, at = [], 0
    for w in weights:
        result.append(out[at : at + w.shape[0]])
        at += w.shape[0]
    return result


def spread_rows(rows, base, width, head_width):
    heads = rows[0].shape[1]
    wide = spread([jnp.broadcast_to(r, (8, heads)) for r in rows], base, width, head_width)
    return [w[0:1] for w in wide]


def gather_heads(parts, base, head_width):
    width = parts[0].shape[1]
    channel, head = iotas(width, LANES)
    start = (head - base) * head_width
    pick = ((channel >= start) & (channel < start + head_width)).astype(BF)
    out = mm(jnp.concatenate([x.astype(BF) for x in parts], axis=0), pick)
    result, at = [], 0
    for x in parts:
        result.append(out[at : at + x.shape[0]])
        at += x.shape[0]
    return result


def reversal(size):
    i, j = iotas(size, size)
    return (i + j == size - 1).astype(BF)


def flip_block(size):
    return 256 if size % 256 == 0 else 128


def sds(shape, dtype=F32):
    return jax.ShapeDtypeStruct(shape, dtype)


class Block:
    def __init__(self, array, shape, index):
        self.array, self.shape, self.index = array, shape, index

    def view(self, ref):
        if self.shape == self.array.shape:
            return ref
        return ref.at[tuple(pl.ds(i * b, b) for i, b in zip(self.index, self.shape))]


class Copied:
    def __init__(self, item):
        self.item = item if isinstance(item, Block) else Block(item, item.shape, (0,) * item.ndim)


class Far:
    def __init__(self, array):
        self.array = array


def run(body, ins, outs, scratch=(), limit=16, stored=()):
    specs, arrays, copied = [], [], []
    for item in ins:
        if isinstance(item, Far):
            specs.append(pl.BlockSpec(memory_space=pl.ANY))
            arrays.append(item.array)
        elif isinstance(item, Copied):
            specs.append(pl.BlockSpec(memory_space=pltpu.HBM))
            arrays.append(item.item.array)
            copied.append(item.item)
        elif isinstance(item, Block):
            specs.append(pl.BlockSpec(memory_space=pltpu.VMEM))
            arrays.append(item.array)
        else:
            space = pltpu.SMEM if item.dtype == jnp.int32 else pltpu.VMEM
            specs.append(pl.BlockSpec(memory_space=space))
            arrays.append(item)
    out_specs = [
        pl.BlockSpec(memory_space=pltpu.HBM if n in stored else pltpu.VMEM)
        for n in range(len(outs))
    ]
    holds = [pltpu.VMEM(q.shape, q.array.dtype) for q in copied]
    holds += [pltpu.VMEM(outs[n].shape, outs[n].dtype) for n in stored]
    sems = [pltpu.SemaphoreType.DMA((max(len(holds), 1),))]

    def kernel(*refs):
        refs = list(refs)
        take = lambda n: [refs.pop(0) for _ in range(n)]
        sources, targets = take(len(ins)), take(len(outs))
        held, (sem,) = take(len(holds)), take(1)
        args, copies = [], []
        for ref, item in zip(sources, ins):
            if isinstance(item, Copied):
                n = len(copies)
                copies.append(pltpu.make_async_copy(item.item.view(ref), held[n], sem.at[n]))
                copies[-1].start()
                ref = held[n]
            elif isinstance(item, Block):
                ref = item.view(ref)
            args.append(ref)
        back = []
        for n, ref in enumerate(targets):
            if n in stored:
                k = len(copied) + stored.index(n)
                back.append(pltpu.make_async_copy(held[k], ref, sem.at[k]))
                ref = held[k]
            args.append(ref)
        waits = {"waits": [c.wait for c in copies]} if copies else {}
        body(*args, *refs, **waits)
        for copy in back:
            copy.start()
        for copy in back:
            copy.wait()

    return pl.pallas_call(
        kernel,
        in_specs=specs,
        out_specs=out_specs,
        out_shape=outs,
        scratch_shapes=holds + sems + list(scratch),
        compiler_params=pltpu.CompilerParams(vmem_limit_bytes=limit * 1024 * 1024),
        cost_estimate=pl.CostEstimate(flops=0, bytes_accessed=1024, transcendentals=0),
    )(*arrays)


def start_body(
    hidden, other, select, step, bias, rate, weight, cot,
    source, pack0, pack1, row, v_out, wide, waits,
):
    for wait in waits[0:2]:
        wait()
    length, width = hidden.shape
    heads = bias.shape[1]
    source[0:length, :] = hidden[...]
    block = flip_block(width)
    turn = reversal(block)
    for j in range(width // block):
        source[length : 2 * length, j * block : (j + 1) * block] = mm(
            other[:, width - (j + 1) * block : width - j * block], turn
        ).astype(BF)
    for wait in waits[2:6]:
        wait()
    keys = mm(source[...], select[...]).astype(BF).astype(F32)
    state = keys.shape[1] // 2
    raw = mm(source[...], step[...], 1, 1) + bias[...]
    dt = jnp.maximum(raw, 0.0) + jnp.log1p(jnp.exp(-jnp.abs(raw)))
    rise = jax.nn.sigmoid(raw)
    i, j = iotas(length, length)
    lower = (i >= j).astype(BF)
    for s, pack in enumerate((pack0, pack1)):
        rows = slice(s * length, (s + 1) * length)
        drop = dt[rows] * rate[...]
        total = mm_exact(lower, drop)
        pack[...] = jnp.zeros(pack.shape, F32)
        pack[:, 0 : 2 * state] = keys[rows]
        at = 2 * state
        for part in (dt[rows], total, total - drop, rise[rows]):
            pack[:, at : at + heads] = part
            at += heads
    row[...] = jnp.zeros(row.shape, F32)
    row[0:1, 0:heads] = jnp.exp(
        -pack1[length - 1 : length, 2 * state + heads : 2 * state + 2 * heads]
    )
    for wait in waits[6:]:
        wait()
    for at in columns_of(weight.shape[1]):
        piece = mm(source[...], weight[:, at]).astype(BF)
        for s in range(2):
            v_out[0, s, :, at] = piece[s * length : (s + 1) * length]
        wide[0:length, at] = piece[0:length].astype(F32)
    wide[length : 2 * length, :] = cot[...].astype(F32)
    for n in range(3):
        at = 2 * length + n * piece_rows(length, wide.shape[1])
        put_piece(wide, at, pack0[:, n * LANES : (n + 1) * LANES])


def columns_of(width):
    block = min(256, width)
    return [slice(k * block, (k + 1) * block) for k in range(width // block)]


def values_body(source, token, *rest):
    weights, v_out = rest[:-1], rest[-1]
    length = v_out.shape[2]
    for n, weight in enumerate(weights):
        for at in columns_of(weight.shape[1]):
            piece = mm(source[...], weight[:, at]).astype(BF)
            for s in range(2):
                v_out[n, s, :, at] = piece[s * length : (s + 1) * length]


class Pack:
    def __init__(self, write, read, stats, heads):
        self.write, self.read = write, read
        self.dt = stats[:, 0:heads]
        self.total = stats[:, heads : 2 * heads]
        self.before = stats[:, 2 * heads : 3 * heads]
        last = self.total.shape[0]
        self.whole = self.total[last - 1 : last, :]
        self.from_start = jnp.exp(-self.total)
        self.from_end = jnp.exp(self.before - self.whole)
        self.to_end = jnp.exp(self.total - self.whole)
        self.to_start = jnp.exp(-self.before)
        self.through = jnp.exp(-self.whole)


def own_pack(ref, heads):
    return Pack(*[ref[:, n * LANES : (n + 1) * LANES] for n in range(3)], heads)


def piece_rows(length, width):
    return length // (width // LANES)


def put_piece(ref, row, piece):
    count = piece_rows(piece.shape[0], ref.shape[1])
    for b in range(ref.shape[1] // LANES):
        ref[row : row + count, b * LANES : (b + 1) * LANES] = piece[b * count : (b + 1) * count]


def get_piece(ref, row, length):
    count = piece_rows(length, ref.shape[1])
    return jnp.concatenate(
        [
            ref[row : row + count, b * LANES : (b + 1) * LANES]
            for b in range(ref.shape[1] // LANES)
        ],
        axis=0,
    )


def pair_body(base, heads, head_width, piece_at):
    def body(place, v_own, g_own, x_far, far0, far1, far2, own_ref, token, up, down, near, keep):
        first = place[0] == 0
        length, width = g_own.shape
        own = own_pack(own_ref, heads)
        far = Pack(*[get_piece(f, at, length) for f, at in zip((far0, far1, far2), piece_at)], heads)
        own_row, far_row = own.through, far.through
        rows = spread_rows([own_row * far_row, far_row], base, width, head_width)
        keep[...] = jnp.zeros(keep.shape, F32)
        keep[0:1, :] = rows[0]
        keep[1:2, :] = rows[1]
        own_up, own_down = jnp.where(first, far_row, 1.0), jnp.where(first, 1.0, far_row)
        far_up, far_down = jnp.where(first, 1.0, own_row), jnp.where(first, own_row, 1.0)
        for kind in range(2):
            rows = slice(kind * LANES, (kind + 1) * LANES)
            if kind == 0:
                keys = (own.write, far.write)
                ups = (own.dt * own.to_end, far.dt * far.to_end)
                downs = (own.dt * own.to_start, far.dt * far.to_start)
            else:
                keys = (own.read, far.read)
                ups = (own.from_end, far.from_end)
                downs = (own.from_start, far.from_start)
            x_own = (v_own if kind == 0 else g_own)[...].reshape(length, width).astype(F32)
            x_other = x_far[kind * length : (kind + 1) * length, :]
            w = spread(
                [ups[0] * own_up, ups[1] * far_up, downs[0] * own_down, downs[1] * far_down,
                 jnp.where(first, downs[1], ups[1])],
                base, width, head_width,
            )
            key = jnp.concatenate(keys, axis=0).astype(BF)
            both = lambda a, b: jnp.concatenate([(a * x_own).astype(BF), (b * x_other).astype(BF)], axis=0)
            up[rows, :] = mm(key, both(w[0], w[1]), 0, 0)
            down[rows, :] = mm(key, both(w[2], w[3]), 0, 0)
            near[rows, :] = mm(keys[1].astype(BF), (w[4] * x_other).astype(BF), 0, 0)

    return body


def column_body(base, heads, head_width):
    def body(own_ref, source, weight, g_own, v_out, own_up, own_down, waits):
        length, width = g_own.shape
        own = own_pack(own_ref, heads)
        w_values = spread([own.dt * own.to_end, own.dt * own.to_start], base, width, head_width)
        w_grads = spread([own.from_end, own.from_start], base, width, head_width)
        write, read = own.write.astype(BF), own.read.astype(BF)
        waits[0]()
        for at in columns_of(width):
            piece = mm(source[...], weight[:, at]).astype(BF)
            for s in range(2):
                v_out[0, s, :, at] = piece[s * length : (s + 1) * length]
            v, g = piece[length:].astype(F32), g_own[:, at].astype(F32)
            for out, n in ((own_up, 0), (own_down, 1)):
                out[0:LANES, at] = mm(write, (w_values[n][:, at] * v).astype(BF), 0, 0)
                out[LANES : 2 * LANES, at] = mm(read, (w_grads[n][:, at] * g).astype(BF), 0, 0)

    return body


def column_totals(place, own_ref, far_row_ref, base, heads, head_width, owns, totals, keep):
    first = place[0] == 0
    width = keep.shape[1]
    own = own_pack(own_ref, heads)
    far_row = far_row_ref[0:1, 0:heads]
    rows = spread_rows([own.through * far_row, far_row, own.through], base, width, head_width)
    keep[...] = jnp.zeros(keep.shape, F32)
    for n, row in enumerate(rows):
        keep[n : n + 1, :] = row
    totals[0][...] = jnp.where(first, rows[1], 1.0) * owns[0][...]
    totals[1][...] = jnp.where(first, 1.0, rows[1]) * owns[1][...]


def first_step_body(pairs, base, heads, head_width, tokens):
    def body(place, own_ref, far_row_ref, own_up, own_down, *rest):
        send_a, send_b, token, up, down, keep = rest[tokens:]
        column_totals(
            place, own_ref, far_row_ref, base, heads, head_width, (own_up, own_down), (up, down), keep
        )
        token[...] = jnp.zeros(token.shape, F32)
        sends = (send_a, send_b)
        for d, total in enumerate((up, down)):
            spot = place[1] if d == 0 else pairs - 1 - place[1]
            for n in range(pairs):
                z = n if d == 0 else pairs - 1 - n
                send = sends[(z + d) % 2]

                @pl.when(spot == n)
                def _():
                    send[...] = total[...] if n == 0 else jnp.zeros(send.shape, F32)

    return body


def exchange_body(ups, downs):
    def body(place, own_up, own_down, keep, token, *rest):
        up_in, down_in = rest[0:ups], rest[ups : ups + downs]
        up_out, down_out, bufs, sems = rest[ups + downs :]
        up_spot, down_spot = place[1], len(up_in) - 1 - place[1]
        fetch_start(up_in, up_spot, bufs.at[0], sems.at[0])
        fetch_start(down_in, down_spot, bufs.at[1], sems.at[1])
        fetch_wait(up_in, up_spot, bufs.at[0], sems.at[0])
        fetch_wait(down_in, down_spot, bufs.at[1], sems.at[1])
        first = place[0] == 0
        row = keep[2:3, :]
        up_out[...] = jnp.where(first, row * bufs[0] + own_up[...], bufs[0])
        down_out[...] = jnp.where(first, bufs[1], row * bufs[1] + own_down[...])

    return body


def fetch_start(options, index, target, sem):
    for z, option in enumerate(options):
        if option is not None:

            @pl.when(index == z)
            def _():
                pltpu.make_async_copy(option, target, sem).start()


def fetch_wait(options, index, target, sem):
    for z, option in enumerate(options):
        if option is not None:

            @pl.when(index == z)
            def _():
                pltpu.make_async_copy(option, target, sem).wait()


def step_body(has, first_step, widen, pieces, tokens):
    pairs = len(has)

    def body(place, *rest):
        rest = list(rest)
        take = lambda n: [rest.pop(0) for _ in range(n)]
        sides = []
        for d in range(2):
            totals = [take(1)[0] if h else None for h in has]
            keeps = [take(1)[0] if h else None for h in has]
            sides.append((totals, keeps))
        got = None if first_step else take(2)
        chunk = take(2) if widen else None
        piece_refs = take(pieces)
        take(tokens)
        sends = take(2)
        token = take(1)[0]
        spots = (place[1], pairs - 1 - place[1])
        for d, (totals, keeps) in enumerate(sides):
            for n in range(pairs):
                z = n if d == 0 else pairs - 1 - n
                send = sends[(z + d) % 2]

                @pl.when(spots[d] == n)
                def _():
                    if not has[n]:
                        send[...] = jnp.zeros(send.shape, F32)
                    elif got is None or n == 0:
                        send[...] = totals[n][...]
                    else:
                        send[...] = totals[n][...] + keeps[n][0:1, :] * got[(z + 1 + d) % 2][...]

        token[...] = jnp.zeros(token.shape, F32)
        if widen:
            put_chunk(take(1)[0], *chunk, piece_refs)

    return body


def within_body(base, heads, head_width):
    def body(own_ref, v_ref, g_ref, rate, token, y_out, x_out, keys_out, steps_out, cols_s):
        own = own_pack(own_ref, heads)
        length, width = g_ref.shape
        write, read = own.write.astype(BF), own.read.astype(BF)
        scores = mm(read, write, 1, 1)
        i, j = iotas(length, length)
        low = i > j
        high = i < j
        doubled = jnp.where(i == j, 2.0, 1.0).astype(F32)
        scores2 = scores * doubled
        turned = own_ref[:, 2 * LANES : 3 * LANES].T
        lane = lax.broadcasted_iota(jnp.int32, (length, LANES), 1)
        d_scores = jnp.zeros((length, length), F32)
        out_low = jnp.zeros((length, LANES), F32)
        out_high = jnp.zeros((length, LANES), F32)
        cols_s[...] = jnp.zeros(cols_s.shape, F32)
        v_all = v_ref[...].reshape(length, width)
        per = LANES // head_width
        for n in range(width // LANES):
            at = slice(n * LANES, (n + 1) * LANES)
            v, g = v_all[:, at], g_ref[:, at]
            mine = [(lane >= m * head_width) & (lane < (m + 1) * head_width) for m in range(per)]
            v_heads = jnp.concatenate([jnp.where(x, v, jnp.zeros_like(v)) for x in mine], axis=0)
            g_heads = jnp.concatenate([jnp.where(x, g, jnp.zeros_like(g)) for x in mine], axis=0)
            products = mm(g_heads, v, 1, 1)
            plains, steppeds = [], []
            for m in range(per):
                h = base + n * per + m
                c_col = own.total[:, h : h + 1]
                e_col = own.before[:, h : h + 1]
                dt_row = turned[h : h + 1, :]
                c_row = turned[heads + h : heads + h + 1, :]
                e_row = turned[2 * heads + h : 2 * heads + h + 1, :]
                decay = jnp.exp(jnp.where(low, c_row - c_col, e_col - e_row))
                plain = decay * scores2
                plains.append(plain.astype(BF))
                steppeds.append((plain * dt_row).astype(BF))
                inner = decay * dt_row * products[m * length : (m + 1) * length]
                d_scores = d_scores + inner
                flow = inner * scores
                flow_low = jnp.where(low, flow, 0.0)
                flow_high = jnp.where(high, flow, 0.0)
                out_low = jnp.where(lane == h, jnp.sum(flow_low, 1, keepdims=True), out_low)
                out_high = jnp.where(lane == h, jnp.sum(flow_high, 1, keepdims=True), out_high)
                cols_s[0, h : h + 1, :] = jnp.sum(flow_low, 0, keepdims=True)
                cols_s[1, h : h + 1, :] = jnp.sum(flow_high, 0, keepdims=True)
            y_out[:, at] = mm(jnp.concatenate(steppeds, axis=1), v_heads)
            x_out[:, at] = mm(jnp.concatenate(plains, axis=0), g_heads, 0, 0)
        d_scores = (d_scores * doubled).astype(BF)
        keys_out[:, 0:LANES] = mm(d_scores, read, 0, 0)
        keys_out[:, LANES : 2 * LANES] = mm(d_scores, write)
        net_low = out_low - cols_s[0].T
        net_high = out_high - cols_s[1].T
        at_or_after = (j >= i).astype(BF)
        after = (j > i).astype(BF)
        steps_out[...] = -rate[...] * (mm_exact(at_or_after, net_low) - mm_exact(after, net_high))

    return body


def post_body(base, heads, head_width, ups, downs, columns=False):
    def body(
        place, own_ref, v_ref, g_ref, yw, xw, keys_w, steps_w, near, keep, skip, rate, token, *rest
    ):
        up_in, down_in = rest[0:ups], rest[ups : ups + downs]
        mixed, dv_out, keys_out, steps_out, bufs, sems = rest[ups + downs :]
        up_spot, down_spot = place[1], len(up_in) - 1 - place[1]
        fetch_start(up_in, up_spot, bufs.at[0], sems.at[0])
        fetch_start(down_in, down_spot, bufs.at[1], sems.at[1])
        first = place[0] == 0
        own = own_pack(own_ref, heads)
        length, width = g_ref.shape
        far_row = keep[1:2, :]
        own_row, gain = spread_rows([own.through, skip[...]], base, width, head_width)
        up_row = jnp.where(first, 1.0, far_row)
        down_row = jnp.where(first, far_row, 1.0)
        dt, from_start, from_end, to_end, to_start = spread(
            [own.dt, own.from_start, own.from_end, own.to_end, own.to_start],
            base, width, head_width,
        )
        write, read = own.write.astype(BF), own.read.astype(BF)
        v = v_ref[...].reshape(length, width).astype(F32)
        g = g_ref[...].astype(F32)
        fetch_wait(up_in, up_spot, bufs.at[0], sems.at[0])
        fetch_wait(down_in, down_spot, bufs.at[1], sems.at[1])
        if columns:
            up = up_row * bufs[0] + near[0][...]
            down = down_row * bufs[1] + near[1][...]
        else:
            up = up_row * bufs[0] + jnp.where(first, 0.0, near[...])
            down = down_row * bufs[1] + jnp.where(first, near[...], 0.0)
        p, ab = up[0:LANES], up[LANES : 2 * LANES]
        q, af = down[0:LANES], down[LANES : 2 * LANES]
        crossing = jnp.sum(p * af + q * ab, axis=0, keepdims=True)
        p, q, af, ab = p.astype(BF), q.astype(BF), af.astype(BF), ab.astype(BF)
        y_p = from_start * mm(read, p)
        y_q = from_end * mm(read, q)
        x_f = to_end * mm(write, af)
        x_b = to_start * mm(write, ab)
        mixed[...] = (yw[...] + y_p + y_q + gain * v).astype(BF)
        x = xw[...] + x_f + x_b
        dv_out[...] = (dt * x + gain * g).astype(BF)
        dtv = dt * v
        keys_out[:, 0:LANES] = (
            keys_w[:, 0:LANES]
            + mm((to_end * dtv).astype(BF), af, 1, 1)
            + mm((to_start * dtv).astype(BF), ab, 1, 1)
        )
        keys_out[:, LANES : 2 * LANES] = (
            keys_w[:, LANES : 2 * LANES]
            + mm((from_start * g).astype(BF), p, 1, 1)
            + mm((from_end * g).astype(BF), q, 1, 1)
        )
        lane = lax.broadcasted_iota(jnp.int32, (length, LANES), 1)
        steps = jnp.where(lane < heads, own_ref[:, 2 * LANES : 3 * LANES], 0.0)
        direct, a_p, a_q, b_f, b_b, through = gather_heads(
            [v * x, g * y_p, g * y_q, v * x_f, v * x_b, jnp.broadcast_to(crossing * own_row, (8, width))],
            base, head_width,
        )
        i, j = iotas(length, length)
        masks = jnp.concatenate([j >= i, j <= i, j < i, j > i], axis=1).astype(F32).astype(BF)
        high, low = halves(jnp.concatenate([a_p, a_q, b_f * steps, b_b * steps], axis=0))
        flow = mm(masks, high) + mm(masks, low) + through[0:1]
        steps_out[...] = steps_w[...] + direct - rate[...] * flow

    return body


class Either:
    def __init__(self, choice, a, b):
        self.choice, self.a, self.b = choice, a, b

    def __getitem__(self, index):
        return jnp.where(self.choice, self.a[index], self.b[index])


def either_within(post):
    def body(place, own_ref, v_ref, g_ref, *rest):
        merged = [Either(place[3] == 0, a, b) for a, b in zip(rest[0:4], rest[4:8])]
        post(place, own_ref, v_ref, g_ref, *merged, *rest[8:])

    return body


def split_body(within, post, columns):
    def body(place, own_ref, v_ref, g_ref, *rest):
        bufs, sems, yw, xw, keys_w, steps_w, cols_s = rest[-7:]
        before, rest = rest[0:4], rest[4:]
        nears = 2 if columns else 1
        near = rest[0:2] if columns else rest[0]
        keep, skip, rate, token, *rest = rest[nears:]

        @pl.when(place[3] == 1)
        def _():
            within(own_ref, v_ref, g_ref, rate, token, yw, xw, keys_w, steps_w, cols_s)

        merged = [Either(place[3] == 0, a, b) for a, b in zip(before, (yw, xw, keys_w, steps_w))]
        post(place, own_ref, v_ref, g_ref, *merged, near, keep, skip, rate, token, *rest[:-5])

    return body


def turn_body(works, strands, turn):
    def body(place, pack0, pack1, rate, *rest):
        count = len(works)
        blocks, token = rest[0 : 2 * count], rest[2 * count]
        outs, flows = rest[2 * count + 1 : -1], rest[-1]

        @pl.when(place[3] == turn)
        def _():
            for n, work in enumerate(works):
                work(
                    (pack0, pack1)[strands[n]], blocks[2 * n], blocks[2 * n + 1], rate, token,
                    *outs[4 * n : 4 * n + 4], flows,
                )

    return body


def chunk_body(within, post, columns):
    def body(place, own_ref, v_ref, g_ref, *rest):
        nears = 2 if columns else 1
        near = rest[0:2] if columns else rest[0]
        keep, skip, rate, token, *rest = rest[nears:]
        bufs, sems, yw, xw, keys_w, steps_w, cols_s = rest[-7:]
        within(own_ref, v_ref, g_ref, rate, token, yw, xw, keys_w, steps_w, cols_s)
        post(
            place, own_ref, v_ref, g_ref, yw, xw, keys_w, steps_w, near, keep, skip, rate, token,
            *rest[:-5],
        )

    return body


def partial_body(groups, more):
    def body(token, *rest):
        dvs, weights, rest = rest[0:groups], rest[groups : 2 * groups], rest[2 * groups :]
        out = rest[-1]
        for at in columns_of(out.shape[1]):
            total = rest[0][:, at] if more else 0.0
            for dv, weight in zip(dvs, weights):
                total = total + mm(dv[...], weight[at, :], 1, 1)
            out[:, at] = total

    return body


def term_body(groups, tails, heads, parts, swap):
    def body(place, own_ref, select, step, before, *rest):
        dvs, weights = rest[0:tails], rest[tails : 2 * tails]
        rest = rest[2 * tails :]
        keys, steps = rest[0:groups], rest[groups : 2 * groups]
        outs = rest[2 * groups :]
        d_keys, d_steps = keys[0][...], steps[0][...]
        for a, b in zip(keys[1:], steps[1:]):
            d_keys = d_keys + a[...]
            d_steps = d_steps + b[...]
        d_raw = d_steps[:, 0:heads] * own_ref[:, 2 * LANES + 3 * heads : 2 * LANES + 4 * heads]
        keys_high, keys_low = halves(d_keys)
        raw_high, raw_low = halves(d_raw)
        width = select.shape[0]
        block = width // parts
        tiles = []
        for b in range(parts):
            rows = slice(b * block, (b + 1) * block)
            total = before[:, rows]
            total = total + mm(keys_high, select[rows, :], 1, 1) + mm(keys_low, select[rows, :], 1, 1)
            total = total + mm(raw_high, step[:, rows]) + mm(raw_low, step[:, rows])
            for k in range(tails):
                total = total + mm(dvs[k][...], weights[k][rows, :], 1, 1)
            tiles.append(total)
        if swap:
            tiles = tiles[::-1]
        if parts == 2:
            first = place[2] == 0
            outs[0][...] = jnp.where(first, tiles[0], tiles[1])
            outs[1][...] = jnp.where(first, tiles[1], tiles[0])
        else:
            for b in range(parts):
                outs[0][:, b * block : (b + 1) * block] = tiles[b]

    return body


def tile_body(groups, tails, heads, swap, keep):
    def body(place, own_ref, select, step, before, *rest):
        dvs, weights = rest[0:tails], rest[tails : 2 * tails]
        rest = rest[2 * tails :]
        keys, steps, out = rest[0:groups], rest[groups : 2 * groups], rest[-1]
        d_keys, d_steps = keys[0][...], steps[0][...]
        for a, b in zip(keys[1:], steps[1:]):
            d_keys = d_keys + a[...]
            d_steps = d_steps + b[...]
        d_raw = d_steps[:, 0:heads] * own_ref[:, 2 * LANES + 3 * heads : 2 * LANES + 4 * heads]
        keys_high, keys_low = halves(d_keys)
        raw_high, raw_low = halves(d_raw)
        block = out.shape[1]
        mine = place[2] if keep != swap else 1 - place[2]
        rows = pl.ds(pl.multiple_of(mine * block, block), block)
        total = before[:, rows]
        total = total + mm(keys_high, select[rows, :], 1, 1) + mm(keys_low, select[rows, :], 1, 1)
        total = total + mm(raw_high, step[:, rows]) + mm(raw_low, step[:, rows])
        for dv, weight in zip(dvs, weights):
            total = total + mm(dv[...], weight[rows, :], 1, 1)
        out[...] = total

    return body


def last_body(work, term, work_ins):
    def body(place, *rest):
        rest = list(rest)
        take = lambda n: [rest.pop(0) for _ in range(n)]
        for_work = take(work_ins)
        select, step, before, weight = take(4)
        others = take(len(rest) - 7)
        half = len(others) // 2
        mixed, dv, keys, steps, out = take(5)
        bufs, sems = take(2)
        work(place, *for_work, mixed, dv, keys, steps, bufs, sems)
        term(
            place, for_work[0], select, step, before, dv, weight,
            *others[:half], keys, *others[half:], steps, out,
        )

    return body


def finish_body(flip):
    def body(a, b, out):
        total = (a[...] + b[...]).astype(BF)
        if not flip:
            out[...] = total
            return
        width = total.shape[1]
        block = flip_block(width)
        turn = reversal(block)
        for j in range(width // block):
            out[:, j * block : (j + 1) * block] = mm(
                total[:, width - (j + 1) * block : width - j * block], turn
            ).astype(BF)

    return body


def put_chunk(wide, v_ref, g_ref, pieces):
    length, width = g_ref.shape
    wide[0:length, :] = v_ref[...].reshape(length, width).astype(F32)
    wide[length : 2 * length, :] = g_ref[...].astype(F32)
    for n, piece in enumerate(pieces):
        put_piece(wide, 2 * length + n * piece_rows(length, width), piece[...])


def widen_body(v_ref, g_ref, token, *rest):
    put_chunk(rest[-1], v_ref, g_ref, rest[:-1])


def local(shards, parts):
    pairs = shards // 2

    def body(
        hidden, complement, inner_weight, select_weight, step_weight, step_bias, decay_rate,
        skip_gain, cotangent, complement_cotangent,
    ):
        length, width = hidden.shape
        inner = inner_weight.shape[1]
        heads = step_bias.shape[0]
        head_width = inner // heads
        groups = 4
        chunk = inner // groups
        group_heads = heads // groups
        seq = lax.axis_index("seq")
        place = jnp.stack(
            [seq % 2, seq // 2, lax.axis_index("chan"), lax.axis_index("dp")]
        ).astype(jnp.int32)
        bias = step_bias.reshape(1, heads)
        rate = decay_rate.reshape(1, heads)
        rate_row = jnp.pad(rate, ((0, 0), (0, LANES - heads)))
        gain = skip_gain.reshape(1, heads)
        step_rows = step_weight.T
        cots = (cotangent, complement_cotangent)
        swap_pairs = [(a, a ^ 1) for a in range(shards)]
        edges = []
        for start in range(2):
            meets = [(z, z + 1) for z in range(start, pairs - 1, 2)]
            paired = sum(meets, ())
            meets += [(b, a) for a, b in meets] + [(z, z) for z in range(pairs) if z not in paired]
            edges.append([(2 * a + y, 2 * b + y) for a, b in meets for y in range(2)])
        swap = lambda x: lax.ppermute(x, "seq", swap_pairs)
        pack_shape = (length, 3 * LANES)
        pair_shape = (2 * LANES, chunk)
        wide_shape = lambda pieces: sds((2 * length + pieces * piece_rows(length, chunk), chunk))
        token_shape = sds((8, LANES))
        work = lambda: [pltpu.VMEM((2,) + pair_shape, F32), pltpu.SemaphoreType.DMA((2,))]
        order = [(1, groups - 1)] + [(0, k) for k in range(groups)] + [(1, k) for k in range(groups - 1)]
        chunks = len(order)

        source, pack0, pack1, row, v_zero, wide = run(
            start_body,
            [*map(Copied, (hidden, complement, select_weight, step_rows, bias, rate)),
             Copied(Block(inner_weight, (width, chunk), (0, 0))),
             Copied(Block(cots[0], (length, chunk), (0, 0)))],
            [sds((2 * length, width), BF), sds(pack_shape), sds(pack_shape), token_shape,
             sds((1, 2, length, chunk), BF), wide_shape(3)],
            limit=57,
        )
        packs = (pack0, pack1)
        far_row = swap(row)

        def weight_of(k):
            return Block(inner_weight, (width, chunk), (0, k))

        def do_values(ks, token):
            return run(
                values_body,
                [source, Far(token), *map(weight_of, ks)],
                [sds((len(ks), 2, length, chunk), BF)],
            )[0]

        v_last, *own_states = run(
            column_body((groups - 1) * group_heads, heads, head_width),
            [pack1, source, Copied(weight_of(groups - 1)),
             Block(cots[1], (length, chunk), (0, groups - 1))],
            [sds((1, 2, length, chunk), BF), sds(pair_shape), sds(pair_shape)],
            limit=48,
        )
        v_more = None

        def value_block(c):
            s, k = order[c]
            array, n = {0: (v_zero, 0), groups - 1: (v_last, 0)}.get(k, (v_more, k - 1))
            return Block(array, (1, 1, length, chunk), (n, s, 0, 0))

        def cot_block(c):
            s, k = order[c]
            return Block(cots[s], (length, chunk), (0, k))

        def weight_block(c):
            return weight_of(order[c][1])

        far = {}
        totals, within, post = {}, {}, {}
        got = ([], [])
        grads = [None, None]
        riders = {2 + n: n for n in range(3)}
        columns = {}
        steps = chunks + pairs - 2

        def do_pair(c, token):
            s, k = order[c]
            rows = piece_rows(length, chunk)
            if s == 0:
                pieces, piece_at = [far[1]] * 3, [2 * length + n * rows for n in range(3)]
            else:
                pieces, piece_at = [far[r] for r in riders], [2 * length] * 3
            totals[c] = run(
                pair_body(k * group_heads, heads, head_width, piece_at),
                [place, value_block(c), cot_block(c), far[c], *pieces, packs[s], Far(token)],
                [sds(pair_shape), sds(pair_shape), sds(pair_shape), sds((8, chunk))],
            )
            return totals[c][3]

        within_shapes = [
            sds((length, chunk)), sds((length, chunk)), sds((length, 2 * LANES)), sds((length, LANES))
        ]
        post_shapes = [
            sds((length, chunk), BF), sds((length, chunk), BF), sds((length, 2 * LANES)), sds((length, LANES))
        ]
        flows = lambda: [pltpu.VMEM((2, LANES, length), F32)]

        def do_within(c, token):
            s, k = order[c]
            within[c] = run(
                within_body(k * group_heads, heads, head_width),
                [packs[s], value_block(c), cot_block(c), rate_row, Far(token)],
                within_shapes,
                scratch=flows(),
            )
            return within[c][3]

        def do_turn(cs, turn, token):
            blocks = [b for c in cs for b in (value_block(c), cot_block(c))]
            works = [within_body(order[c][1] * group_heads, heads, head_width) for c in cs]
            out = run(
                turn_body(works, [order[c][0] for c in cs], turn),
                [place, *packs, rate_row, *blocks, Far(token)],
                within_shapes * len(cs),
                scratch=flows(),
            )
            for n, c in enumerate(cs):
                within[c] = within.get(c, []) + list(out[4 * n : 4 * n + 4])
            return out[3]

        def post_parts(c, token):
            s, k = order[c]
            last = pairs - 1
            ups = [got[(z + 1) % 2][max(c + z - 1, c, 1 - z)] for z in range(pairs)]
            downs = [got[(last - z) % 2][max(c + z - 1, c, 1 - z)] for z in range(pairs)]
            body = post_body(k * group_heads, heads, head_width, len(ups), len(downs), c == 0)
            work = within_body(k * group_heads, heads, head_width)
            if len(within.get(c, ())) == 8:
                body = either_within(body)
            elif c in within:
                body = split_body(work, body, c == 0)
            else:
                body = chunk_body(work, body, c == 0)
            near = columns["far"] if c == 0 else [totals[c][2]]
            ins = [packs[s], value_block(c), cot_block(c), *within.get(c, []),
                   *near, totals[c][3], gain, rate_row, Far(token),
                   *map(Far, ups), *map(Far, downs)]
            return body, ins

        def do_chunk(c, token):
            body, ins = post_parts(c, token)
            more = [pltpu.VMEM(o.shape, o.dtype) for o in within_shapes] + flows()
            post[c] = run(body, [place, *ins], post_shapes, stored=(0,), scratch=work() + more)
            return post[c][3]

        def do_partial(cs, token, before=None):
            return run(
                partial_body(len(cs), before is not None),
                [Far(token), *[post[c][1] for c in cs], *[weight_block(c) for c in cs]]
                + ([] if before is None else [before]),
                [sds((length, width))],
            )[0]

        shares = [sds((length, width // parts))] * 2 if parts == 2 else [sds((length, width))]

        def send_share(term):
            if parts == 2:
                return term[0], lax.ppermute(term[1], "chan", [(0, 1), (1, 0)])
            share = lax.psum_scatter(term[0], "chan", scatter_dimension=1, tiled=True)
            return share, jnp.zeros_like(share)

        def do_term(s, before):
            mine = [c for c in range(chunks) if order[c][0] == s]
            return send_share(run(
                term_body(len(mine), 0, heads, parts, s == 1),
                [place, packs[s], select_weight, step_rows, before,
                 *[post[c][2] for c in mine], *[post[c][3] for c in mine]],
                shares,
            ))

        def do_last(c, before, token):
            s = order[c][0]
            mine = [n for n in range(chunks) if order[n][0] == s and n != c]
            body, ins = post_parts(c, token)
            sums = [select_weight, step_rows, before]
            others = [[post[n][k] for n in mine] for k in (2, 3)]
            if parts == 2:
                term = tile_body(len(mine) + 1, 1, heads, s == 1, False)
            else:
                term = term_body(len(mine) + 1, 1, heads, parts, s == 1)
            post[c] = run(
                last_body(body, term, len(ins)),
                [place, *ins, *sums, weight_block(c), *others[0], *others[1]],
                [*post_shapes, shares[0]],
                scratch=work(),
                stored=(0,),
            )
            if parts != 2:
                return send_share(post[c][4:])
            arriving = lax.ppermute(post[c][4], "chan", [(0, 1), (1, 0)])
            kept = run(
                tile_body(len(mine) + 1, 1, heads, s == 1, True),
                [place, packs[s], *sums, post[c][1], weight_block(c),
                 *others[0], post[c][2], *others[1], post[c][3]],
                [shares[0]],
            )[0]
            return kept, arriving

        def do_finish(s, share):
            return run(
                finish_body(s == 1), list(share), [sds((length, width // parts), BF)], stored=(0,)
            )[0]

        def do_step(k, widen, ends):
            has = [0 <= k - z < chunks and z < pairs - 1 for z in range(pairs)]
            ins = [place]
            for d in range(2):
                ins += [totals[k - z][d] for z in range(pairs) if has[z]]
                ins += [totals[k - z][3] for z in range(pairs) if has[z]]
            if k > 0:
                ins += [got[0][-1], got[1][-1] if k > 1 else got[0][-1]]
            outs = [sds(pair_shape), sds(pair_shape), token_shape]
            pieces = [] if widen is None else pieces_of(widen)
            if widen is not None:
                ins += [value_block(widen), cot_block(widen), *pieces]
                outs.append(wide_shape(len(pieces)))
            return run(
                step_body(has, k == 0, widen is not None, len(pieces), len(ends)),
                ins + [Far(e) for e in ends],
                outs,
            )

        def do_first_step(ends):
            s, k = order[0]
            out = run(
                first_step_body(pairs, k * group_heads, heads, head_width, len(ends)),
                [place, packs[s], far_row, *own_states, *map(Far, ends)],
                [sds(pair_shape), sds(pair_shape), token_shape, sds(pair_shape), sds(pair_shape),
                 sds((8, chunk))],
            )
            totals[0] = (out[3], out[4], None, out[5])
            columns["own"] = own_states
            return out

        def do_exchange(token):
            last = pairs - 1
            ups = [got[(z + 1) % 2][max(z - 1, 1 - z)] for z in range(pairs)]
            downs = [got[(last - z) % 2][max(z - 1, 1 - z)] for z in range(pairs)]
            sends = run(
                exchange_body(len(ups), len(downs)),
                [place, *columns["own"], totals[0][3], Far(token), *map(Far, ups), *map(Far, downs)],
                [sds(pair_shape), sds(pair_shape)],
                scratch=work(),
            )
            columns["far"] = [swap(x) for x in sends]

        def pieces_of(c):
            return [Block(packs[1], (length, LANES), (0, riders[c]))] if c in riders else []

        def do_widen(c, token):
            pieces = pieces_of(c)
            return run(
                widen_body, [value_block(c), cot_block(c), Far(token), *pieces], [wide_shape(len(pieces))]
            )[0]

        far[1] = swap(lax.optimization_barrier((wide, far_row))[0])
        ends = [do_turn((1, groups), 0, far_row)]
        halfway = None
        share = None
        for k in range(steps):
            queue = k + 2 if 0 < k < chunks - 2 else None
            made = do_first_step(ends) if k == 0 else do_step(k, queue, ends)
            token = made[2]
            got[0].append(lax.ppermute(made[0], "seq", edges[0]))
            got[1].append(lax.ppermute(made[1], "seq", edges[1]) if 0 < k < steps - 1 else None)
            ends = []
            if k == 0:
                v_more = do_values(list(range(1, groups - 1)), token)
                far[2] = swap(do_widen(2, token))
            if queue is not None:
                far[queue] = swap(made[3])
            if k + 1 < chunks:
                ends.append(do_pair(k + 1, token))
            if k == max(chunks - 2, pairs - 1):
                do_exchange(far[chunks - 1])
            if k == steps - 3:
                ends.append(columns["far"][0])
            for cs in {1: [(2, 3)], 2: [(5,)], 3: [(6, 0)], 4: [(7,)]}.get(k, ()):
                ends.append(do_turn(cs, 0, token))
            if k == steps - 1:
                do_turn((7,), 1, token)
            c = k - pairs + 1
            if c > 0:
                late = columns["far"][1] if k == steps - 2 else token
                ends.append(do_chunk(c, late))
            if c == groups - 2:
                halfway = do_partial(list(range(1, groups - 1)), token)
                ends.append(halfway)
            if c == groups:
                share = do_term(0, do_partial([groups - 1, groups], token, halfway))
                ends.append(share[0])
            if c == groups + 1:
                ends.append(do_chunk(0, token))
            if c == groups + 2:
                grads[0] = do_finish(0, share)
                halfway = do_partial([groups + 1, 0, groups + 2], token)
        grads[1] = do_finish(1, do_last(chunks - 1, halfway, halfway))
        outs = [
            jnp.concatenate([post[order.index((s, k))][0] for k in range(groups)], axis=1)
            for s in range(2)
        ]
        return (outs[0], outs[1], grads[0], grads[1])

    return body


def solution(mesh):
    rows = P(("dp", "seq"), None)
    both = P(("dp", "seq"), "chan")
    in_specs = (
        rows, rows, P(None, "chan"), P(), P(None, "chan"),
        P("chan"), P("chan"), P("chan"), both, both,
    )
    return jax.shard_map(
        local(mesh.shape["seq"], mesh.shape["chan"]),
        mesh=mesh,
        in_specs=in_specs,
        out_specs=(both,) * 4,
        check_vma=False,
    )
```

```python
import jax
import jax.numpy as jnp
from jax import lax
from jax.experimental import pallas as pl
from jax.experimental.pallas import tpu as pltpu
from jax.sharding import PartitionSpec as P

BF = jnp.bfloat16
F32 = jnp.float32
LANES = 128


def mm(a, b, ca=1, cb=0):
    return lax.dot_general(a, b, (((ca,), (cb,)), ((), ())), preferred_element_type=F32)


def halves(x):
    high = x.astype(BF)
    return high, (x - high.astype(F32)).astype(BF)


def mm_exact(a, b, ca=1, cb=0):
    first, rest = b.astype(BF), None
    rest = b - first.astype(F32)
    second = rest.astype(BF)
    third = (rest - second.astype(F32)).astype(BF)
    return mm(a, first, ca, cb) + mm(a, second, ca, cb) + mm(a, third, ca, cb)


def iotas(rows, columns):
    return (
        lax.broadcasted_iota(jnp.int32, (rows, columns), 0),
        lax.broadcasted_iota(jnp.int32, (rows, columns), 1),
    )


def spread(weights, base, width, head_width):
    heads = weights[0].shape[1]
    row, channel = iotas(2 * heads, width)
    start = (jnp.where(row >= heads, row - heads, row) - base) * head_width
    pick = ((channel >= start) & (channel < start + head_width)).astype(BF)
    stacked = jnp.concatenate(weights, axis=0) if len(weights) > 1 else weights[0]
    out = mm(jnp.concatenate(halves(stacked), axis=1), pick)
    result, at = [], 0
    for w in weights:
        result.append(out[at : at + w.shape[0]])
        at += w.shape[0]
    return result


def spread_rows(rows, base, width, head_width):
    heads = rows[0].shape[1]
    wide = spread([jnp.broadcast_to(r, (8, heads)) for r in rows], base, width, head_width)
    return [w[0:1] for w in wide]


def gather_heads(parts, base, head_width):
    width = parts[0].shape[1]
    channel, head = iotas(width, LANES)
    start = (head - base) * head_width
    pick = ((channel >= start) & (channel < start + head_width)).astype(BF)
    out = mm(jnp.concatenate([x.astype(BF) for x in parts], axis=0), pick)
    result, at = [], 0
    for x in parts:
        result.append(out[at : at + x.shape[0]])
        at += x.shape[0]
    return result


def reversal(size):
    i, j = iotas(size, size)
    return (i + j == size - 1).astype(BF)


def flip_block(size):
    return 256 if size % 256 == 0 else 128


def sds(shape, dtype=F32):
    return jax.ShapeDtypeStruct(shape, dtype)


class Block:
    def __init__(self, array, shape, index):
        self.array, self.shape, self.index = array, shape, index

    def view(self, ref):
        if self.shape == self.array.shape:
            return ref
        return ref.at[tuple(pl.ds(i * b, b) for i, b in zip(self.index, self.shape))]


class Copied:
    def __init__(self, item):
        self.item = item if isinstance(item, Block) else Block(item, item.shape, (0,) * item.ndim)


class Far:
    def __init__(self, array):
        self.array = array


def run(body, ins, outs, scratch=(), limit=16, stored=()):
    specs, arrays, copied = [], [], []
    for item in ins:
        if isinstance(item, Far):
            specs.append(pl.BlockSpec(memory_space=pl.ANY))
            arrays.append(item.array)
        elif isinstance(item, Copied):
            specs.append(pl.BlockSpec(memory_space=pltpu.HBM))
            arrays.append(item.item.array)
            copied.append(item.item)
        elif isinstance(item, Block):
            specs.append(pl.BlockSpec(memory_space=pltpu.VMEM))
            arrays.append(item.array)
        else:
            space = pltpu.SMEM if item.dtype == jnp.int32 else pltpu.VMEM
            specs.append(pl.BlockSpec(memory_space=space))
            arrays.append(item)
    out_specs = [
        pl.BlockSpec(memory_space=pltpu.HBM if n in stored else pltpu.VMEM)
        for n in range(len(outs))
    ]
    holds = [pltpu.VMEM(q.shape, q.array.dtype) for q in copied]
    holds += [pltpu.VMEM(outs[n].shape, outs[n].dtype) for n in stored]
    sems = [pltpu.SemaphoreType.DMA((max(len(holds), 1),))]

    def kernel(*refs):
        refs = list(refs)
        take = lambda n: [refs.pop(0) for _ in range(n)]
        sources, targets = take(len(ins)), take(len(outs))
        held, (sem,) = take(len(holds)), take(1)
        args, copies = [], []
        for ref, item in zip(sources, ins):
            if isinstance(item, Copied):
                n = len(copies)
                copies.append(pltpu.make_async_copy(item.item.view(ref), held[n], sem.at[n]))
                copies[-1].start()
                ref = held[n]
            elif isinstance(item, Block):
                ref = item.view(ref)
            args.append(ref)
        back = []
        for n, ref in enumerate(targets):
            if n in stored:
                k = len(copied) + stored.index(n)
                back.append(pltpu.make_async_copy(held[k], ref, sem.at[k]))
                ref = held[k]
            args.append(ref)
        waits = {"waits": [c.wait for c in copies]} if copies else {}
        body(*args, *refs, **waits)
        for copy in back:
            copy.start()
        for copy in back:
            copy.wait()

    return pl.pallas_call(
        kernel,
        in_specs=specs,
        out_specs=out_specs,
        out_shape=outs,
        scratch_shapes=holds + sems + list(scratch),
        compiler_params=pltpu.CompilerParams(vmem_limit_bytes=limit * 1024 * 1024),
        cost_estimate=pl.CostEstimate(flops=0, bytes_accessed=1024, transcendentals=0),
    )(*arrays)


def start_body(
    hidden, other, select, step, bias, rate, weight, cot,
    source, pack0, pack1, row, v_out, wide, waits,
):
    for wait in waits[0:2]:
        wait()
    length, width = hidden.shape
    heads = bias.shape[1]
    source[0:length, :] = hidden[...]
    block = flip_block(width)
    turn = reversal(block)
    for j in range(width // block):
        source[length : 2 * length, j * block : (j + 1) * block] = mm(
            other[:, width - (j + 1) * block : width - j * block], turn
        ).astype(BF)
    for wait in waits[2:6]:
        wait()
    keys = mm(source[...], select[...]).astype(BF).astype(F32)
    state = keys.shape[1] // 2
    raw = mm(source[...], step[...], 1, 1) + bias[...]
    dt = jnp.maximum(raw, 0.0) + jnp.log1p(jnp.exp(-jnp.abs(raw)))
    rise = jax.nn.sigmoid(raw)
    i, j = iotas(length, length)
    lower = (i >= j).astype(BF)
    for s, pack in enumerate((pack0, pack1)):
        rows = slice(s * length, (s + 1) * length)
        drop = dt[rows] * rate[...]
        total = mm_exact(lower, drop)
        pack[...] = jnp.zeros(pack.shape, F32)
        pack[:, 0 : 2 * state] = keys[rows]
        at = 2 * state
        for part in (dt[rows], total, total - drop, rise[rows]):
            pack[:, at : at + heads] = part
            at += heads
    row[...] = jnp.zeros(row.shape, F32)
    row[0:1, 0:heads] = jnp.exp(
        -pack1[length - 1 : length, 2 * state + heads : 2 * state + 2 * heads]
    )
    for wait in waits[6:]:
        wait()
    for at in columns_of(weight.shape[1]):
        piece = mm(source[...], weight[:, at]).astype(BF)
        for s in range(2):
            v_out[0, s, :, at] = piece[s * length : (s + 1) * length]
        wide[0:length, at] = piece[0:length].astype(F32)
    wide[length : 2 * length, :] = cot[...].astype(F32)
    for n in range(3):
        at = 2 * length + n * piece_rows(length, wide.shape[1])
        put_piece(wide, at, pack0[:, n * LANES : (n + 1) * LANES])


def columns_of(width):
    block = min(256, width)
    return [slice(k * block, (k + 1) * block) for k in range(width // block)]


def values_body(source, token, *rest):
    weights, v_out = rest[:-1], rest[-1]
    length = v_out.shape[2]
    for n, weight in enumerate(weights):
        for at in columns_of(weight.shape[1]):
            piece = mm(source[...], weight[:, at]).astype(BF)
            for s in range(2):
                v_out[n, s, :, at] = piece[s * length : (s + 1) * length]


class Pack:
    def __init__(self, write, read, stats, heads):
        self.write, self.read = write, read
        self.dt = stats[:, 0:heads]
        self.total = stats[:, heads : 2 * heads]
        self.before = stats[:, 2 * heads : 3 * heads]
        last = self.total.shape[0]
        self.whole = self.total[last - 1 : last, :]
        self.from_start = jnp.exp(-self.total)
        self.from_end = jnp.exp(self.before - self.whole)
        self.to_end = jnp.exp(self.total - self.whole)
        self.to_start = jnp.exp(-self.before)
        self.through = jnp.exp(-self.whole)


def own_pack(ref, heads):
    return Pack(*[ref[:, n * LANES : (n + 1) * LANES] for n in range(3)], heads)


def piece_rows(length, width):
    return length // (width // LANES)


def put_piece(ref, row, piece):
    count = piece_rows(piece.shape[0], ref.shape[1])
    for b in range(ref.shape[1] // LANES):
        ref[row : row + count, b * LANES : (b + 1) * LANES] = piece[b * count : (b + 1) * count]


def get_piece(ref, row, length):
    count = piece_rows(length, ref.shape[1])
    return jnp.concatenate(
        [
            ref[row : row + count, b * LANES : (b + 1) * LANES]
            for b in range(ref.shape[1] // LANES)
        ],
        axis=0,
    )


def pair_body(base, heads, head_width, piece_at):
    def body(place, v_own, g_own, x_far, far0, far1, far2, own_ref, token, up, down, near, keep):
        first = place[0] == 0
        length, width = g_own.shape
        own = own_pack(own_ref, heads)
        far = Pack(*[get_piece(f, at, length) for f, at in zip((far0, far1, far2), piece_at)], heads)
        own_row, far_row = own.through, far.through
        rows = spread_rows([own_row * far_row, far_row], base, width, head_width)
        keep[...] = jnp.zeros(keep.shape, F32)
        keep[0:1, :] = rows[0]
        keep[1:2, :] = rows[1]
        own_up, own_down = jnp.where(first, far_row, 1.0), jnp.where(first, 1.0, far_row)
        far_up, far_down = jnp.where(first, 1.0, own_row), jnp.where(first, own_row, 1.0)
        for kind in range(2):
            rows = slice(kind * LANES, (kind + 1) * LANES)
            if kind == 0:
                keys = (own.write, far.write)
                ups = (own.dt * own.to_end, far.dt * far.to_end)
                downs = (own.dt * own.to_start, far.dt * far.to_start)
            else:
                keys = (own.read, far.read)
                ups = (own.from_end, far.from_end)
                downs = (own.from_start, far.from_start)
            x_own = (v_own if kind == 0 else g_own)[...].reshape(length, width).astype(F32)
            x_other = x_far[kind * length : (kind + 1) * length, :]
            w = spread(
                [ups[0] * own_up, ups[1] * far_up, downs[0] * own_down, downs[1] * far_down,
                 jnp.where(first, downs[1], ups[1])],
                base, width, head_width,
            )
            key = jnp.concatenate(keys, axis=0).astype(BF)
            both = lambda a, b: jnp.concatenate([(a * x_own).astype(BF), (b * x_other).astype(BF)], axis=0)
            up[rows, :] = mm(key, both(w[0], w[1]), 0, 0)
            down[rows, :] = mm(key, both(w[2], w[3]), 0, 0)
            near[rows, :] = mm(keys[1].astype(BF), (w[4] * x_other).astype(BF), 0, 0)

    return body


def column_body(base, heads, head_width):
    def body(own_ref, source, weight, g_own, v_out, own_up, own_down, waits):
        length, width = g_own.shape
        own = own_pack(own_ref, heads)
        w_values = spread([own.dt * own.to_end, own.dt * own.to_start], base, width, head_width)
        w_grads = spread([own.from_end, own.from_start], base, width, head_width)
        write, read = own.write.astype(BF), own.read.astype(BF)
        waits[0]()
        for at in columns_of(width):
            piece = mm(source[...], weight[:, at]).astype(BF)
            for s in range(2):
                v_out[0, s, :, at] = piece[s * length : (s + 1) * length]
            v, g = piece[length:].astype(F32), g_own[:, at].astype(F32)
            for out, n in ((own_up, 0), (own_down, 1)):
                out[0:LANES, at] = mm(write, (w_values[n][:, at] * v).astype(BF), 0, 0)
                out[LANES : 2 * LANES, at] = mm(read, (w_grads[n][:, at] * g).astype(BF), 0, 0)

    return body


def column_totals(place, own_ref, far_row_ref, base, heads, head_width, owns, totals, keep):
    first = place[0] == 0
    width = keep.shape[1]
    own = own_pack(own_ref, heads)
    far_row = far_row_ref[0:1, 0:heads]
    rows = spread_rows([own.through * far_row, far_row, own.through], base, width, head_width)
    keep[...] = jnp.zeros(keep.shape, F32)
    for n, row in enumerate(rows):
        keep[n : n + 1, :] = row
    totals[0][...] = jnp.where(first, rows[1], 1.0) * owns[0][...]
    totals[1][...] = jnp.where(first, 1.0, rows[1]) * owns[1][...]


def first_step_body(pairs, base, heads, head_width, tokens):
    def body(place, own_ref, far_row_ref, own_up, own_down, *rest):
        send_a, send_b, token, up, down, keep = rest[tokens:]
        column_totals(
            place, own_ref, far_row_ref, base, heads, head_width, (own_up, own_down), (up, down), keep
        )
        token[...] = jnp.zeros(token.shape, F32)
        sends = (send_a, send_b)
        for d, total in enumerate((up, down)):
            spot = place[1] if d == 0 else pairs - 1 - place[1]
            for n in range(pairs):
                z = n if d == 0 else pairs - 1 - n
                send = sends[(z + d) % 2]

                @pl.when(spot == n)
                def _():
                    send[...] = total[...] if n == 0 else jnp.zeros(send.shape, F32)

    return body


def exchange_body(ups, downs):
    def body(place, own_up, own_down, keep, token, *rest):
        up_in, down_in = rest[0:ups], rest[ups : ups + downs]
        up_out, down_out, bufs, sems = rest[ups + downs :]
        up_spot, down_spot = place[1], len(up_in) - 1 - place[1]
        fetch_start(up_in, up_spot, bufs.at[0], sems.at[0])
        fetch_start(down_in, down_spot, bufs.at[1], sems.at[1])
        fetch_wait(up_in, up_spot, bufs.at[0], sems.at[0])
        fetch_wait(down_in, down_spot, bufs.at[1], sems.at[1])
        first = place[0] == 0
        row = keep[2:3, :]
        up_out[...] = jnp.where(first, row * bufs[0] + own_up[...], bufs[0])
        down_out[...] = jnp.where(first, bufs[1], row * bufs[1] + own_down[...])

    return body


def fetch_start(options, index, target, sem):
    for z, option in enumerate(options):
        if option is not None:

            @pl.when(index == z)
            def _():
                pltpu.make_async_copy(option, target, sem).start()


def fetch_wait(options, index, target, sem):
    for z, option in enumerate(options):
        if option is not None:

            @pl.when(index == z)
            def _():
                pltpu.make_async_copy(option, target, sem).wait()


def step_body(has, first_step, widen, pieces, tokens):
    pairs = len(has)

    def body(place, *rest):
        rest = list(rest)
        take = lambda n: [rest.pop(0) for _ in range(n)]
        sides = []
        for d in range(2):
            totals = [take(1)[0] if h else None for h in has]
            keeps = [take(1)[0] if h else None for h in has]
            sides.append((totals, keeps))
        got = None if first_step else take(2)
        chunk = take(2) if widen else None
        piece_refs = take(pieces)
        take(tokens)
        sends = take(2)
        token = take(1)[0]
        spots = (place[1], pairs - 1 - place[1])
        for d, (totals, keeps) in enumerate(sides):
            for n in range(pairs):
                z = n if d == 0 else pairs - 1 - n
                send = sends[(z + d) % 2]

                @pl.when(spots[d] == n)
                def _():
                    if not has[n]:
                        send[...] = jnp.zeros(send.shape, F32)
                    elif got is None or n == 0:
                        send[...] = totals[n][...]
                    else:
                        send[...] = totals[n][...] + keeps[n][0:1, :] * got[(z + 1 + d) % 2][...]

        token[...] = jnp.zeros(token.shape, F32)
        if widen:
            put_chunk(take(1)[0], *chunk, piece_refs)

    return body


def within_body(base, heads, head_width):
    def body(own_ref, v_ref, g_ref, rate, token, y_out, x_out, keys_out, steps_out, cols_s):
        own = own_pack(own_ref, heads)
        length, width = g_ref.shape
        write, read = own.write.astype(BF), own.read.astype(BF)
        scores = mm(read, write, 1, 1)
        i, j = iotas(length, length)
        low = i > j
        high = i < j
        doubled = jnp.where(i == j, 2.0, 1.0).astype(F32)
        scores2 = scores * doubled
        turned = own_ref[:, 2 * LANES : 3 * LANES].T
        lane = lax.broadcasted_iota(jnp.int32, (length, LANES), 1)
        d_scores = jnp.zeros((length, length), F32)
        out_low = jnp.zeros((length, LANES), F32)
        out_high = jnp.zeros((length, LANES), F32)
        cols_s[...] = jnp.zeros(cols_s.shape, F32)
        v_all = v_ref[...].reshape(length, width)
        per = LANES // head_width
        for n in range(width // LANES):
            at = slice(n * LANES, (n + 1) * LANES)
            v, g = v_all[:, at], g_ref[:, at]
            mine = [(lane >= m * head_width) & (lane < (m + 1) * head_width) for m in range(per)]
            v_heads = jnp.concatenate([jnp.where(x, v, jnp.zeros_like(v)) for x in mine], axis=0)
            g_heads = jnp.concatenate([jnp.where(x, g, jnp.zeros_like(g)) for x in mine], axis=0)
            products = mm(g_heads, v, 1, 1)
            plains, steppeds = [], []
            for m in range(per):
                h = base + n * per + m
                c_col = own.total[:, h : h + 1]
                e_col = own.before[:, h : h + 1]
                dt_row = turned[h : h + 1, :]
                c_row = turned[heads + h : heads + h + 1, :]
                e_row = turned[2 * heads + h : 2 * heads + h + 1, :]
                decay = jnp.exp(jnp.where(low, c_row - c_col, e_col - e_row))
                plain = decay * scores2
                plains.append(plain.astype(BF))
                steppeds.append((plain * dt_row).astype(BF))
                inner = decay * dt_row * products[m * length : (m + 1) * length]
                d_scores = d_scores + inner
                flow = inner * scores
                flow_low = jnp.where(low, flow, 0.0)
                flow_high = jnp.where(high, flow, 0.0)
                out_low = jnp.where(lane == h, jnp.sum(flow_low, 1, keepdims=True), out_low)
                out_high = jnp.where(lane == h, jnp.sum(flow_high, 1, keepdims=True), out_high)
                cols_s[0, h : h + 1, :] = jnp.sum(flow_low, 0, keepdims=True)
                cols_s[1, h : h + 1, :] = jnp.sum(flow_high, 0, keepdims=True)
            y_out[:, at] = mm(jnp.concatenate(steppeds, axis=1), v_heads)
            x_out[:, at] = mm(jnp.concatenate(plains, axis=0), g_heads, 0, 0)
        d_scores = (d_scores * doubled).astype(BF)
        keys_out[:, 0:LANES] = mm(d_scores, read, 0, 0)
        keys_out[:, LANES : 2 * LANES] = mm(d_scores, write)
        net_low = out_low - cols_s[0].T
        net_high = out_high - cols_s[1].T
        at_or_after = (j >= i).astype(BF)
        after = (j > i).astype(BF)
        steps_out[...] = -rate[...] * (mm_exact(at_or_after, net_low) - mm_exact(after, net_high))

    return body


def post_body(base, heads, head_width, ups, downs, columns=False):
    def body(
        place, own_ref, v_ref, g_ref, yw, xw, keys_w, steps_w, near, keep, skip, rate, token, *rest
    ):
        up_in, down_in = rest[0:ups], rest[ups : ups + downs]
        mixed, dv_out, keys_out, steps_out, bufs, sems = rest[ups + downs :]
        up_spot, down_spot = place[1], len(up_in) - 1 - place[1]
        fetch_start(up_in, up_spot, bufs.at[0], sems.at[0])
        fetch_start(down_in, down_spot, bufs.at[1], sems.at[1])
        first = place[0] == 0
        own = own_pack(own_ref, heads)
        length, width = g_ref.shape
        far_row = keep[1:2, :]
        own_row, gain = spread_rows([own.through, skip[...]], base, width, head_width)
        up_row = jnp.where(first, 1.0, far_row)
        down_row = jnp.where(first, far_row, 1.0)
        dt, from_start, from_end, to_end, to_start = spread(
            [own.dt, own.from_start, own.from_end, own.to_end, own.to_start],
            base, width, head_width,
        )
        write, read = own.write.astype(BF), own.read.astype(BF)
        v = v_ref[...].reshape(length, width).astype(F32)
        g = g_ref[...].astype(F32)
        fetch_wait(up_in, up_spot, bufs.at[0], sems.at[0])
        fetch_wait(down_in, down_spot, bufs.at[1], sems.at[1])
        if columns:
            up = up_row * bufs[0] + near[0][...]
            down = down_row * bufs[1] + near[1][...]
        else:
            up = up_row * bufs[0] + jnp.where(first, 0.0, near[...])
            down = down_row * bufs[1] + jnp.where(first, near[...], 0.0)
        p, ab = up[0:LANES], up[LANES : 2 * LANES]
        q, af = down[0:LANES], down[LANES : 2 * LANES]
        crossing = jnp.sum(p * af + q * ab, axis=0, keepdims=True)
        p, q, af, ab = p.astype(BF), q.astype(BF), af.astype(BF), ab.astype(BF)
        y_p = from_start * mm(read, p)
        y_q = from_end * mm(read, q)
        x_f = to_end * mm(write, af)
        x_b = to_start * mm(write, ab)
        mixed[...] = (yw[...] + y_p + y_q + gain * v).astype(BF)
        x = xw[...] + x_f + x_b
        dv_out[...] = (dt * x + gain * g).astype(BF)
        dtv = dt * v
        keys_out[:, 0:LANES] = (
            keys_w[:, 0:LANES]
            + mm((to_end * dtv).astype(BF), af, 1, 1)
            + mm((to_start * dtv).astype(BF), ab, 1, 1)
        )
        keys_out[:, LANES : 2 * LANES] = (
            keys_w[:, LANES : 2 * LANES]
            + mm((from_start * g).astype(BF), p, 1, 1)
            + mm((from_end * g).astype(BF), q, 1, 1)
        )
        lane = lax.broadcasted_iota(jnp.int32, (length, LANES), 1)
        steps = jnp.where(lane < heads, own_ref[:, 2 * LANES : 3 * LANES], 0.0)
        direct, a_p, a_q, b_f, b_b, through = gather_heads(
            [v * x, g * y_p, g * y_q, v * x_f, v * x_b, jnp.broadcast_to(crossing * own_row, (8, width))],
            base, head_width,
        )
        i, j = iotas(length, length)
        masks = jnp.concatenate([j >= i, j <= i, j < i, j > i], axis=1).astype(F32).astype(BF)
        high, low = halves(jnp.concatenate([a_p, a_q, b_f * steps, b_b * steps], axis=0))
        flow = mm(masks, high) + mm(masks, low) + through[0:1]
        steps_out[...] = steps_w[...] + direct - rate[...] * flow

    return body


class Either:
    def __init__(self, choice, a, b):
        self.choice, self.a, self.b = choice, a, b

    def __getitem__(self, index):
        return jnp.where(self.choice, self.a[index], self.b[index])


def either_within(post):
    def body(place, own_ref, v_ref, g_ref, *rest):
        merged = [Either(place[3] == 0, a, b) for a, b in zip(rest[0:4], rest[4:8])]
        post(place, own_ref, v_ref, g_ref, *merged, *rest[8:])

    return body


def split_body(within, post, columns):
    def body(place, own_ref, v_ref, g_ref, *rest):
        bufs, sems, yw, xw, keys_w, steps_w, cols_s = rest[-7:]
        before, rest = rest[0:4], rest[4:]
        nears = 2 if columns else 1
        near = rest[0:2] if columns else rest[0]
        keep, skip, rate, token, *rest = rest[nears:]

        @pl.when(place[3] == 1)
        def _():
            within(own_ref, v_ref, g_ref, rate, token, yw, xw, keys_w, steps_w, cols_s)

        merged = [Either(place[3] == 0, a, b) for a, b in zip(before, (yw, xw, keys_w, steps_w))]
        post(place, own_ref, v_ref, g_ref, *merged, near, keep, skip, rate, token, *rest[:-5])

    return body


def turn_body(works, strands, turn):
    def body(place, pack0, pack1, rate, *rest):
        count = len(works)
        blocks, token = rest[0 : 2 * count], rest[2 * count]
        outs, flows = rest[2 * count + 1 : -1], rest[-1]

        @pl.when(place[3] == turn)
        def _():
            for n, work in enumerate(works):
                work(
                    (pack0, pack1)[strands[n]], blocks[2 * n], blocks[2 * n + 1], rate, token,
                    *outs[4 * n : 4 * n + 4], flows,
                )

    return body


def chunk_body(within, post, columns):
    def body(place, own_ref, v_ref, g_ref, *rest):
        nears = 2 if columns else 1
        near = rest[0:2] if columns else rest[0]
        keep, skip, rate, token, *rest = rest[nears:]
        bufs, sems, yw, xw, keys_w, steps_w, cols_s = rest[-7:]
        within(own_ref, v_ref, g_ref, rate, token, yw, xw, keys_w, steps_w, cols_s)
        post(
            place, own_ref, v_ref, g_ref, yw, xw, keys_w, steps_w, near, keep, skip, rate, token,
            *rest[:-5],
        )

    return body


def partial_body(groups, more):
    def body(token, *rest):
        dvs, weights, rest = rest[0:groups], rest[groups : 2 * groups], rest[2 * groups :]
        out = rest[-1]
        for at in columns_of(out.shape[1]):
            total = rest[0][:, at] if more else 0.0
            for dv, weight in zip(dvs, weights):
                total = total + mm(dv[...], weight[at, :], 1, 1)
            out[:, at] = total

    return body


def term_body(groups, tails, heads, parts, swap):
    def body(place, own_ref, select, step, before, *rest):
        dvs, weights = rest[0:tails], rest[tails : 2 * tails]
        rest = rest[2 * tails :]
        keys, steps = rest[0:groups], rest[groups : 2 * groups]
        outs = rest[2 * groups :]
        d_keys, d_steps = keys[0][...], steps[0][...]
        for a, b in zip(keys[1:], steps[1:]):
            d_keys = d_keys + a[...]
            d_steps = d_steps + b[...]
        d_raw = d_steps[:, 0:heads] * own_ref[:, 2 * LANES + 3 * heads : 2 * LANES + 4 * heads]
        keys_high, keys_low = halves(d_keys)
        raw_high, raw_low = halves(d_raw)
        width = select.shape[0]
        block = width // parts
        tiles = []
        for b in range(parts):
            rows = slice(b * block, (b + 1) * block)
            total = before[:, rows]
            total = total + mm(keys_high, select[rows, :], 1, 1) + mm(keys_low, select[rows, :], 1, 1)
            total = total + mm(raw_high, step[:, rows]) + mm(raw_low, step[:, rows])
            for k in range(tails):
                total = total + mm(dvs[k][...], weights[k][rows, :], 1, 1)
            tiles.append(total)
        if swap:
            tiles = tiles[::-1]
        if parts == 2:
            first = place[2] == 0
            outs[0][...] = jnp.where(first, tiles[0], tiles[1])
            outs[1][...] = jnp.where(first, tiles[1], tiles[0])
        else:
            for b in range(parts):
                outs[0][:, b * block : (b + 1) * block] = tiles[b]

    return body


def tile_body(groups, tails, heads, swap, keep):
    def body(place, own_ref, select, step, before, *rest):
        dvs, weights = rest[0:tails], rest[tails : 2 * tails]
        rest = rest[2 * tails :]
        keys, steps, out = rest[0:groups], rest[groups : 2 * groups], rest[-1]
        d_keys, d_steps = keys[0][...], steps[0][...]
        for a, b in zip(keys[1:], steps[1:]):
            d_keys = d_keys + a[...]
            d_steps = d_steps + b[...]
        d_raw = d_steps[:, 0:heads] * own_ref[:, 2 * LANES + 3 * heads : 2 * LANES + 4 * heads]
        keys_high, keys_low = halves(d_keys)
        raw_high, raw_low = halves(d_raw)
        block = out.shape[1]
        mine = place[2] if keep != swap else 1 - place[2]
        rows = pl.ds(pl.multiple_of(mine * block, block), block)
        total = before[:, rows]
        total = total + mm(keys_high, select[rows, :], 1, 1) + mm(keys_low, select[rows, :], 1, 1)
        total = total + mm(raw_high, step[:, rows]) + mm(raw_low, step[:, rows])
        for dv, weight in zip(dvs, weights):
            total = total + mm(dv[...], weight[rows, :], 1, 1)
        out[...] = total

    return body


def last_body(work, term, work_ins):
    def body(place, *rest):
        rest = list(rest)
        take = lambda n: [rest.pop(0) for _ in range(n)]
        for_work = take(work_ins)
        select, step, before, weight = take(4)
        others = take(len(rest) - 7)
        half = len(others) // 2
        mixed, dv, keys, steps, out = take(5)
        bufs, sems = take(2)
        work(place, *for_work, mixed, dv, keys, steps, bufs, sems)
        term(
            place, for_work[0], select, step, before, dv, weight,
            *others[:half], keys, *others[half:], steps, out,
        )

    return body


def finish_body(flip):
    def body(a, b, out):
        total = (a[...] + b[...]).astype(BF)
        if not flip:
            out[...] = total
            return
        width = total.shape[1]
        block = flip_block(width)
        turn = reversal(block)
        for j in range(width // block):
            out[:, j * block : (j + 1) * block] = mm(
                total[:, width - (j + 1) * block : width - j * block], turn
            ).astype(BF)

    return body


def put_chunk(wide, v_ref, g_ref, pieces):
    length, width = g_ref.shape
    wide[0:length, :] = v_ref[...].reshape(length, width).astype(F32)
    wide[length : 2 * length, :] = g_ref[...].astype(F32)
    for n, piece in enumerate(pieces):
        put_piece(wide, 2 * length + n * piece_rows(length, width), piece[...])


def widen_body(v_ref, g_ref, token, *rest):
    put_chunk(rest[-1], v_ref, g_ref, rest[:-1])


def local(shards, parts):
    pairs = shards // 2

    def body(
        hidden, complement, inner_weight, select_weight, step_weight, step_bias, decay_rate,
        skip_gain, cotangent, complement_cotangent,
    ):
        length, width = hidden.shape
        inner = inner_weight.shape[1]
        heads = step_bias.shape[0]
        head_width = inner // heads
        groups = 4
        chunk = inner // groups
        group_heads = heads // groups
        seq = lax.axis_index("seq")
        place = jnp.stack(
            [seq % 2, seq // 2, lax.axis_index("chan"), lax.axis_index("dp")]
        ).astype(jnp.int32)
        bias = step_bias.reshape(1, heads)
        rate = decay_rate.reshape(1, heads)
        rate_row = jnp.pad(rate, ((0, 0), (0, LANES - heads)))
        gain = skip_gain.reshape(1, heads)
        step_rows = step_weight.T
        cots = (cotangent, complement_cotangent)
        swap_pairs = [(a, a ^ 1) for a in range(shards)]
        edges = []
        for start in range(2):
            meets = [(z, z + 1) for z in range(start, pairs - 1, 2)]
            paired = sum(meets, ())
            meets += [(b, a) for a, b in meets] + [(z, z) for z in range(pairs) if z not in paired]
            edges.append([(2 * a + y, 2 * b + y) for a, b in meets for y in range(2)])
        swap = lambda x: lax.ppermute(x, "seq", swap_pairs)
        pack_shape = (length, 3 * LANES)
        pair_shape = (2 * LANES, chunk)
        wide_shape = lambda pieces: sds((2 * length + pieces * piece_rows(length, chunk), chunk))
        token_shape = sds((8, LANES))
        work = lambda: [pltpu.VMEM((2,) + pair_shape, F32), pltpu.SemaphoreType.DMA((2,))]
        order = [(1, groups - 1)] + [(0, k) for k in range(groups)] + [(1, k) for k in range(groups - 1)]
        chunks = len(order)

        source, pack0, pack1, row, v_zero, wide = run(
            start_body,
            [*map(Copied, (hidden, complement, select_weight, step_rows, bias, rate)),
             Copied(Block(inner_weight, (width, chunk), (0, 0))),
             Copied(Block(cots[0], (length, chunk), (0, 0)))],
            [sds((2 * length, width), BF), sds(pack_shape), sds(pack_shape), token_shape,
             sds((1, 2, length, chunk), BF), wide_shape(3)],
            limit=57,
        )
        packs = (pack0, pack1)
        far_row = swap(row)

        def weight_of(k):
            return Block(inner_weight, (width, chunk), (0, k))

        def do_values(ks, token):
            return run(
                values_body,
                [source, Far(token), *map(weight_of, ks)],
                [sds((len(ks), 2, length, chunk), BF)],
            )[0]

        v_last, *own_states = run(
            column_body((groups - 1) * group_heads, heads, head_width),
            [pack1, source, Copied(weight_of(groups - 1)),
             Block(cots[1], (length, chunk), (0, groups - 1))],
            [sds((1, 2, length, chunk), BF), sds(pair_shape), sds(pair_shape)],
            limit=48,
        )
        v_more = None

        def value_block(c):
            s, k = order[c]
            array, n = {0: (v_zero, 0), groups - 1: (v_last, 0)}.get(k, (v_more, k - 1))
            return Block(array, (1, 1, length, chunk), (n, s, 0, 0))

        def cot_block(c):
            s, k = order[c]
            return Block(cots[s], (length, chunk), (0, k))

        def weight_block(c):
            return weight_of(order[c][1])

        far = {}
        totals, within, post = {}, {}, {}
        got = ([], [])
        grads = [None, None]
        riders = {2 + n: n for n in range(3)}
        columns = {}
        steps = chunks + pairs - 2

        def do_pair(c, token):
            s, k = order[c]
            rows = piece_rows(length, chunk)
            if s == 0:
                pieces, piece_at = [far[1]] * 3, [2 * length + n * rows for n in range(3)]
            else:
                pieces, piece_at = [far[r] for r in riders], [2 * length] * 3
            totals[c] = run(
                pair_body(k * group_heads, heads, head_width, piece_at),
                [place, value_block(c), cot_block(c), far[c], *pieces, packs[s], Far(token)],
                [sds(pair_shape), sds(pair_shape), sds(pair_shape), sds((8, chunk))],
            )
            return totals[c][3]

        within_shapes = [
            sds((length, chunk)), sds((length, chunk)), sds((length, 2 * LANES)), sds((length, LANES))
        ]
        post_shapes = [
            sds((length, chunk), BF), sds((length, chunk), BF), sds((length, 2 * LANES)), sds((length, LANES))
        ]
        flows = lambda: [pltpu.VMEM((2, LANES, length), F32)]

        def do_within(c, token):
            s, k = order[c]
            within[c] = run(
                within_body(k * group_heads, heads, head_width),
                [packs[s], value_block(c), cot_block(c), rate_row, Far(token)],
                within_shapes,
                scratch=flows(),
            )
            return within[c][3]

        def do_turn(cs, turn, token):
            blocks = [b for c in cs for b in (value_block(c), cot_block(c))]
            works = [within_body(order[c][1] * group_heads, heads, head_width) for c in cs]
            out = run(
                turn_body(works, [order[c][0] for c in cs], turn),
                [place, *packs, rate_row, *blocks, Far(token)],
                within_shapes * len(cs),
                scratch=flows(),
            )
            for n, c in enumerate(cs):
                within[c] = within.get(c, []) + list(out[4 * n : 4 * n + 4])
            return out[3]

        def post_parts(c, token):
            s, k = order[c]
            last = pairs - 1
            ups = [got[(z + 1) % 2][max(c + z - 1, c, 1 - z)] for z in range(pairs)]
            downs = [got[(last - z) % 2][max(c + z - 1, c, 1 - z)] for z in range(pairs)]
            body = post_body(k * group_heads, heads, head_width, len(ups), len(downs), c == 0)
            work = within_body(k * group_heads, heads, head_width)
            if len(within.get(c, ())) == 8:
                body = either_within(body)
            elif c in within:
                body = split_body(work, body, c == 0)
            else:
                body = chunk_body(work, body, c == 0)
            near = columns["far"] if c == 0 else [totals[c][2]]
            ins = [packs[s], value_block(c), cot_block(c), *within.get(c, []),
                   *near, totals[c][3], gain, rate_row, Far(token),
                   *map(Far, ups), *map(Far, downs)]
            return body, ins

        def do_chunk(c, token):
            body, ins = post_parts(c, token)
            more = [pltpu.VMEM(o.shape, o.dtype) for o in within_shapes] + flows()
            post[c] = run(body, [place, *ins], post_shapes, stored=(0,), scratch=work() + more)
            return post[c][3]

        def do_partial(cs, token, before=None):
            return run(
                partial_body(len(cs), before is not None),
                [Far(token), *[post[c][1] for c in cs], *[weight_block(c) for c in cs]]
                + ([] if before is None else [before]),
                [sds((length, width))],
            )[0]

        shares = [sds((length, width // parts))] * 2 if parts == 2 else [sds((length, width))]

        def send_share(term):
            if parts == 2:
                return term[0], lax.ppermute(term[1], "chan", [(0, 1), (1, 0)])
            share = lax.psum_scatter(term[0], "chan", scatter_dimension=1, tiled=True)
            return share, jnp.zeros_like(share)

        def do_term(s, before):
            mine = [c for c in range(chunks) if order[c][0] == s]
            return send_share(run(
                term_body(len(mine), 0, heads, parts, s == 1),
                [place, packs[s], select_weight, step_rows, before,
                 *[post[c][2] for c in mine], *[post[c][3] for c in mine]],
                shares,
            ))

        def do_last(c, before, token):
            s = order[c][0]
            mine = [n for n in range(chunks) if order[n][0] == s and n != c]
            body, ins = post_parts(c, token)
            sums = [select_weight, step_rows, before]
            others = [[post[n][k] for n in mine] for k in (2, 3)]
            if parts == 2:
                term = tile_body(len(mine) + 1, 1, heads, s == 1, False)
            else:
                term = term_body(len(mine) + 1, 1, heads, parts, s == 1)
            post[c] = run(
                last_body(body, term, len(ins)),
                [place, *ins, *sums, weight_block(c), *others[0], *others[1]],
                [*post_shapes, shares[0]],
                scratch=work(),
                stored=(0,),
            )
            if parts != 2:
                return send_share(post[c][4:])
            arriving = lax.ppermute(post[c][4], "chan", [(0, 1), (1, 0)])
            kept = run(
                tile_body(len(mine) + 1, 1, heads, s == 1, True),
                [place, packs[s], *sums, post[c][1], weight_block(c),
                 *others[0], post[c][2], *others[1], post[c][3]],
                [shares[0]],
            )[0]
            return kept, arriving

        def do_finish(s, share):
            return run(
                finish_body(s == 1), list(share), [sds((length, width // parts), BF)], stored=(0,)
            )[0]

        def do_step(k, widen, ends):
            has = [0 <= k - z < chunks and z < pairs - 1 for z in range(pairs)]
            ins = [place]
            for d in range(2):
                ins += [totals[k - z][d] for z in range(pairs) if has[z]]
                ins += [totals[k - z][3] for z in range(pairs) if has[z]]
            if k > 0:
                ins += [got[0][-1], got[1][-1] if k > 1 else got[0][-1]]
            outs = [sds(pair_shape), sds(pair_shape), token_shape]
            pieces = [] if widen is None else pieces_of(widen)
            if widen is not None:
                ins += [value_block(widen), cot_block(widen), *pieces]
                outs.append(wide_shape(len(pieces)))
            return run(
                step_body(has, k == 0, widen is not None, len(pieces), len(ends)),
                ins + [Far(e) for e in ends],
                outs,
            )

        def do_first_step(ends):
            s, k = order[0]
            out = run(
                first_step_body(pairs, k * group_heads, heads, head_width, len(ends)),
                [place, packs[s], far_row, *own_states, *map(Far, ends)],
                [sds(pair_shape), sds(pair_shape), token_shape, sds(pair_shape), sds(pair_shape),
                 sds((8, chunk))],
            )
            totals[0] = (out[3], out[4], None, out[5])
            columns["own"] = own_states
            return out

        def do_exchange(token):
            last = pairs - 1
            ups = [got[(z + 1) % 2][max(z - 1, 1 - z)] for z in range(pairs)]
            downs = [got[(last - z) % 2][max(z - 1, 1 - z)] for z in range(pairs)]
            sends = run(
                exchange_body(len(ups), len(downs)),
                [place, *columns["own"], totals[0][3], Far(token), *map(Far, ups), *map(Far, downs)],
                [sds(pair_shape), sds(pair_shape)],
                scratch=work(),
            )
            columns["far"] = [swap(x) for x in sends]

        def pieces_of(c):
            return [Block(packs[1], (length, LANES), (0, riders[c]))] if c in riders else []

        def do_widen(c, token):
            pieces = pieces_of(c)
            return run(
                widen_body, [value_block(c), cot_block(c), Far(token), *pieces], [wide_shape(len(pieces))]
            )[0]

        far[1] = swap(lax.optimization_barrier((wide, far_row))[0])
        ends = []
        halfway = None
        share = None
        for k in range(steps):
            queue = k + 2 if 0 < k < chunks - 2 else None
            made = do_first_step(ends) if k == 0 else do_step(k, queue, ends)
            token = made[2]
            got[0].append(lax.ppermute(made[0], "seq", edges[0]))
            got[1].append(lax.ppermute(made[1], "seq", edges[1]) if 0 < k < steps - 1 else None)
            ends = []
            if k == 0:
                v_more = do_values(list(range(1, groups - 1)), token)
                far[2] = swap(do_widen(2, token))
            if queue is not None:
                far[queue] = swap(made[3])
            if k + 1 < chunks:
                ends.append(do_pair(k + 1, token))
            if k == max(chunks - 2, pairs - 1):
                do_exchange(far[chunks - 1])
            if k == steps - 3:
                ends.append(columns["far"][0])
            for cs in {0: [(1, 7)], 1: [(2, 3)], 2: [(4, 5)], 3: [(6, 0)]}.get(k, ()):
                ends.append(do_turn(cs, 0, token))
            if k == steps - 1:
                do_turn((7,), 1, token)
            c = k - pairs + 1
            if c > 0:
                late = columns["far"][1] if k == steps - 2 else token
                ends.append(do_chunk(c, late))
            if c == groups - 2:
                halfway = do_partial(list(range(1, groups - 1)), token)
                ends.append(halfway)
            if c == groups:
                share = do_term(0, do_partial([groups - 1, groups], token, halfway))
                ends.append(share[0])
            if c == groups + 1:
                ends.append(do_chunk(0, token))
            if c == groups + 2:
                grads[0] = do_finish(0, share)
                halfway = do_partial([groups + 1, 0, groups + 2], token)
        grads[1] = do_finish(1, do_last(chunks - 1, halfway, halfway))
        outs = [
            jnp.concatenate([post[order.index((s, k))][0] for k in range(groups)], axis=1)
            for s in range(2)
        ]
        return (outs[0], outs[1], grads[0], grads[1])

    return body


def solution(mesh):
    rows = P(("dp", "seq"), None)
    both = P(("dp", "seq"), "chan")
    in_specs = (
        rows, rows, P(None, "chan"), P(), P(None, "chan"),
        P("chan"), P("chan"), P("chan"), both, both,
    )
    return jax.shard_map(
        local(mesh.shape["seq"], mesh.shape["chan"]),
        mesh=mesh,
        in_specs=in_specs,
        out_specs=(both,) * 4,
        check_vma=False,
    )
```

```python
import jax
import jax.numpy as jnp
from jax import lax
from jax.experimental import pallas as pl
from jax.experimental.pallas import tpu as pltpu
from jax.sharding import PartitionSpec as P

BF = jnp.bfloat16
F32 = jnp.float32
LANES = 128


def mm(a, b, ca=1, cb=0):
    return lax.dot_general(a, b, (((ca,), (cb,)), ((), ())), preferred_element_type=F32)


def halves(x):
    high = x.astype(BF)
    return high, (x - high.astype(F32)).astype(BF)


def mm_exact(a, b, ca=1, cb=0):
    first, rest = b.astype(BF), None
    rest = b - first.astype(F32)
    second = rest.astype(BF)
    third = (rest - second.astype(F32)).astype(BF)
    return mm(a, first, ca, cb) + mm(a, second, ca, cb) + mm(a, third, ca, cb)


def iotas(rows, columns):
    return (
        lax.broadcasted_iota(jnp.int32, (rows, columns), 0),
        lax.broadcasted_iota(jnp.int32, (rows, columns), 1),
    )


def spread(weights, base, width, head_width):
    heads = weights[0].shape[1]
    row, channel = iotas(2 * heads, width)
    start = (jnp.where(row >= heads, row - heads, row) - base) * head_width
    pick = ((channel >= start) & (channel < start + head_width)).astype(BF)
    stacked = jnp.concatenate(weights, axis=0) if len(weights) > 1 else weights[0]
    out = mm(jnp.concatenate(halves(stacked), axis=1), pick)
    result, at = [], 0
    for w in weights:
        result.append(out[at : at + w.shape[0]])
        at += w.shape[0]
    return result


def spread_rows(rows, base, width, head_width):
    heads = rows[0].shape[1]
    wide = spread([jnp.broadcast_to(r, (8, heads)) for r in rows], base, width, head_width)
    return [w[0:1] for w in wide]


def gather_heads(parts, base, head_width):
    width = parts[0].shape[1]
    channel, head = iotas(width, LANES)
    start = (head - base) * head_width
    pick = ((channel >= start) & (channel < start + head_width)).astype(BF)
    out = mm(jnp.concatenate([x.astype(BF) for x in parts], axis=0), pick)
    result, at = [], 0
    for x in parts:
        result.append(out[at : at + x.shape[0]])
        at += x.shape[0]
    return result


def reversal(size):
    i, j = iotas(size, size)
    return (i + j == size - 1).astype(BF)


def flip_block(size):
    return 256 if size % 256 == 0 else 128


def sds(shape, dtype=F32):
    return jax.ShapeDtypeStruct(shape, dtype)


class Block:
    def __init__(self, array, shape, index):
        self.array, self.shape, self.index = array, shape, index

    def view(self, ref):
        if self.shape == self.array.shape:
            return ref
        return ref.at[tuple(pl.ds(i * b, b) for i, b in zip(self.index, self.shape))]


class Copied:
    def __init__(self, item):
        self.item = item if isinstance(item, Block) else Block(item, item.shape, (0,) * item.ndim)


class Far:
    def __init__(self, array):
        self.array = array


def run(body, ins, outs, scratch=(), limit=16, stored=()):
    specs, arrays, copied = [], [], []
    for item in ins:
        if isinstance(item, Far):
            specs.append(pl.BlockSpec(memory_space=pl.ANY))
            arrays.append(item.array)
        elif isinstance(item, Copied):
            specs.append(pl.BlockSpec(memory_space=pltpu.HBM))
            arrays.append(item.item.array)
            copied.append(item.item)
        elif isinstance(item, Block):
            specs.append(pl.BlockSpec(memory_space=pltpu.VMEM))
            arrays.append(item.array)
        else:
            space = pltpu.SMEM if item.dtype == jnp.int32 else pltpu.VMEM
            specs.append(pl.BlockSpec(memory_space=space))
            arrays.append(item)
    out_specs = [
        pl.BlockSpec(memory_space=pltpu.HBM if n in stored else pltpu.VMEM)
        for n in range(len(outs))
    ]
    holds = [pltpu.VMEM(q.shape, q.array.dtype) for q in copied]
    holds += [pltpu.VMEM(outs[n].shape, outs[n].dtype) for n in stored]
    sems = [pltpu.SemaphoreType.DMA((max(len(holds), 1),))]

    def kernel(*refs):
        refs = list(refs)
        take = lambda n: [refs.pop(0) for _ in range(n)]
        sources, targets = take(len(ins)), take(len(outs))
        held, (sem,) = take(len(holds)), take(1)
        args, copies = [], []
        for ref, item in zip(sources, ins):
            if isinstance(item, Copied):
                n = len(copies)
                copies.append(pltpu.make_async_copy(item.item.view(ref), held[n], sem.at[n]))
                copies[-1].start()
                ref = held[n]
            elif isinstance(item, Block):
                ref = item.view(ref)
            args.append(ref)
        back = []
        for n, ref in enumerate(targets):
            if n in stored:
                k = len(copied) + stored.index(n)
                back.append(pltpu.make_async_copy(held[k], ref, sem.at[k]))
                ref = held[k]
            args.append(ref)
        waits = {"waits": [c.wait for c in copies]} if copies else {}
        body(*args, *refs, **waits)
        for copy in back:
            copy.start()
        for copy in back:
            copy.wait()

    return pl.pallas_call(
        kernel,
        in_specs=specs,
        out_specs=out_specs,
        out_shape=outs,
        scratch_shapes=holds + sems + list(scratch),
        compiler_params=pltpu.CompilerParams(vmem_limit_bytes=limit * 1024 * 1024),
        cost_estimate=pl.CostEstimate(flops=0, bytes_accessed=1024, transcendentals=0),
    )(*arrays)


def start_body(
    hidden, other, select, step, bias, rate, weight, cot,
    source, pack0, pack1, row, v_out, wide, waits,
):
    for wait in waits[0:2]:
        wait()
    length, width = hidden.shape
    heads = bias.shape[1]
    source[0:length, :] = hidden[...]
    block = flip_block(width)
    turn = reversal(block)
    for j in range(width // block):
        source[length : 2 * length, j * block : (j + 1) * block] = mm(
            other[:, width - (j + 1) * block : width - j * block], turn
        ).astype(BF)
    for wait in waits[2:6]:
        wait()
    keys = mm(source[...], select[...]).astype(BF).astype(F32)
    state = keys.shape[1] // 2
    raw = mm(source[...], step[...], 1, 1) + bias[...]
    dt = jnp.maximum(raw, 0.0) + jnp.log1p(jnp.exp(-jnp.abs(raw)))
    rise = jax.nn.sigmoid(raw)
    i, j = iotas(length, length)
    lower = (i >= j).astype(BF)
    for s, pack in enumerate((pack0, pack1)):
        rows = slice(s * length, (s + 1) * length)
        drop = dt[rows] * rate[...]
        total = mm_exact(lower, drop)
        pack[...] = jnp.zeros(pack.shape, F32)
        pack[:, 0 : 2 * state] = keys[rows]
        at = 2 * state
        for part in (dt[rows], total, total - drop, rise[rows]):
            pack[:, at : at + heads] = part
            at += heads
    row[...] = jnp.zeros(row.shape, F32)
    row[0:1, 0:heads] = jnp.exp(
        -pack1[length - 1 : length, 2 * state + heads : 2 * state + 2 * heads]
    )
    for wait in waits[6:]:
        wait()
    for at in columns_of(weight.shape[1]):
        piece = mm(source[...], weight[:, at]).astype(BF)
        for s in range(2):
            v_out[0, s, :, at] = piece[s * length : (s + 1) * length]
        wide[0:length, at] = piece[0:length].astype(F32)
    wide[length : 2 * length, :] = cot[...].astype(F32)
    for n in range(3):
        at = 2 * length + n * piece_rows(length, wide.shape[1])
        put_piece(wide, at, pack0[:, n * LANES : (n + 1) * LANES])


def columns_of(width):
    block = min(256, width)
    return [slice(k * block, (k + 1) * block) for k in range(width // block)]


def values_body(source, token, *rest):
    weights, v_out = rest[:-1], rest[-1]
    length = v_out.shape[2]
    for n, weight in enumerate(weights):
        for at in columns_of(weight.shape[1]):
            piece = mm(source[...], weight[:, at]).astype(BF)
            for s in range(2):
                v_out[n, s, :, at] = piece[s * length : (s + 1) * length]


class Pack:
    def __init__(self, write, read, stats, heads):
        self.write, self.read = write, read
        self.dt = stats[:, 0:heads]
        self.total = stats[:, heads : 2 * heads]
        self.before = stats[:, 2 * heads : 3 * heads]
        last = self.total.shape[0]
        self.whole = self.total[last - 1 : last, :]
        self.from_start = jnp.exp(-self.total)
        self.from_end = jnp.exp(self.before - self.whole)
        self.to_end = jnp.exp(self.total - self.whole)
        self.to_start = jnp.exp(-self.before)
        self.through = jnp.exp(-self.whole)


def own_pack(ref, heads):
    return Pack(*[ref[:, n * LANES : (n + 1) * LANES] for n in range(3)], heads)


def piece_rows(length, width):
    return length // (width // LANES)


def put_piece(ref, row, piece):
    count = piece_rows(piece.shape[0], ref.shape[1])
    for b in range(ref.shape[1] // LANES):
        ref[row : row + count, b * LANES : (b + 1) * LANES] = piece[b * count : (b + 1) * count]


def get_piece(ref, row, length):
    count = piece_rows(length, ref.shape[1])
    return jnp.concatenate(
        [
            ref[row : row + count, b * LANES : (b + 1) * LANES]
            for b in range(ref.shape[1] // LANES)
        ],
        axis=0,
    )


def pair_body(base, heads, head_width, piece_at):
    def body(place, v_own, g_own, x_far, far0, far1, far2, own_ref, token, up, down, near, keep):
        first = place[0] == 0
        length, width = g_own.shape
        own = own_pack(own_ref, heads)
        far = Pack(*[get_piece(f, at, length) for f, at in zip((far0, far1, far2), piece_at)], heads)
        own_row, far_row = own.through, far.through
        rows = spread_rows([own_row * far_row, far_row], base, width, head_width)
        keep[...] = jnp.zeros(keep.shape, F32)
        keep[0:1, :] = rows[0]
        keep[1:2, :] = rows[1]
        own_up, own_down = jnp.where(first, far_row, 1.0), jnp.where(first, 1.0, far_row)
        far_up, far_down = jnp.where(first, 1.0, own_row), jnp.where(first, own_row, 1.0)
        for kind in range(2):
            rows = slice(kind * LANES, (kind + 1) * LANES)
            if kind == 0:
                keys = (own.write, far.write)
                ups = (own.dt * own.to_end, far.dt * far.to_end)
                downs = (own.dt * own.to_start, far.dt * far.to_start)
            else:
                keys = (own.read, far.read)
                ups = (own.from_end, far.from_end)
                downs = (own.from_start, far.from_start)
            x_own = (v_own if kind == 0 else g_own)[...].reshape(length, width).astype(F32)
            x_other = x_far[kind * length : (kind + 1) * length, :]
            w = spread(
                [ups[0] * own_up, ups[1] * far_up, downs[0] * own_down, downs[1] * far_down,
                 jnp.where(first, downs[1], ups[1])],
                base, width, head_width,
            )
            key = jnp.concatenate(keys, axis=0).astype(BF)
            both = lambda a, b: jnp.concatenate([(a * x_own).astype(BF), (b * x_other).astype(BF)], axis=0)
            up[rows, :] = mm(key, both(w[0], w[1]), 0, 0)
            down[rows, :] = mm(key, both(w[2], w[3]), 0, 0)
            near[rows, :] = mm(keys[1].astype(BF), (w[4] * x_other).astype(BF), 0, 0)

    return body


def column_body(base, heads, head_width):
    def body(own_ref, source, weight, g_own, v_out, own_up, own_down, waits):
        length, width = g_own.shape
        own = own_pack(own_ref, heads)
        w_values = spread([own.dt * own.to_end, own.dt * own.to_start], base, width, head_width)
        w_grads = spread([own.from_end, own.from_start], base, width, head_width)
        write, read = own.write.astype(BF), own.read.astype(BF)
        waits[0]()
        for at in columns_of(width):
            piece = mm(source[...], weight[:, at]).astype(BF)
            for s in range(2):
                v_out[0, s, :, at] = piece[s * length : (s + 1) * length]
            v, g = piece[length:].astype(F32), g_own[:, at].astype(F32)
            for out, n in ((own_up, 0), (own_down, 1)):
                out[0:LANES, at] = mm(write, (w_values[n][:, at] * v).astype(BF), 0, 0)
                out[LANES : 2 * LANES, at] = mm(read, (w_grads[n][:, at] * g).astype(BF), 0, 0)

    return body


def column_totals(place, own_ref, far_row_ref, base, heads, head_width, owns, totals, keep):
    first = place[0] == 0
    width = keep.shape[1]
    own = own_pack(own_ref, heads)
    far_row = far_row_ref[0:1, 0:heads]
    rows = spread_rows([own.through * far_row, far_row, own.through], base, width, head_width)
    keep[...] = jnp.zeros(keep.shape, F32)
    for n, row in enumerate(rows):
        keep[n : n + 1, :] = row
    totals[0][...] = jnp.where(first, rows[1], 1.0) * owns[0][...]
    totals[1][...] = jnp.where(first, 1.0, rows[1]) * owns[1][...]


def first_step_body(pairs, base, heads, head_width, tokens):
    def body(place, own_ref, far_row_ref, own_up, own_down, *rest):
        send_a, send_b, token, up, down, keep = rest[tokens:]
        column_totals(
            place, own_ref, far_row_ref, base, heads, head_width, (own_up, own_down), (up, down), keep
        )
        token[...] = jnp.zeros(token.shape, F32)
        sends = (send_a, send_b)
        for d, total in enumerate((up, down)):
            spot = place[1] if d == 0 else pairs - 1 - place[1]
            for n in range(pairs):
                z = n if d == 0 else pairs - 1 - n
                send = sends[(z + d) % 2]

                @pl.when(spot == n)
                def _():
                    send[...] = total[...] if n == 0 else jnp.zeros(send.shape, F32)

    return body


def exchange_body(ups, downs):
    def body(place, own_up, own_down, keep, token, *rest):
        up_in, down_in = rest[0:ups], rest[ups : ups + downs]
        up_out, down_out, bufs, sems = rest[ups + downs :]
        up_spot, down_spot = place[1], len(up_in) - 1 - place[1]
        fetch_start(up_in, up_spot, bufs.at[0], sems.at[0])
        fetch_start(down_in, down_spot, bufs.at[1], sems.at[1])
        fetch_wait(up_in, up_spot, bufs.at[0], sems.at[0])
        fetch_wait(down_in, down_spot, bufs.at[1], sems.at[1])
        first = place[0] == 0
        row = keep[2:3, :]
        up_out[...] = jnp.where(first, row * bufs[0] + own_up[...], bufs[0])
        down_out[...] = jnp.where(first, bufs[1], row * bufs[1] + own_down[...])

    return body


def fetch_start(options, index, target, sem):
    for z, option in enumerate(options):
        if option is not None:

            @pl.when(index == z)
            def _():
                pltpu.make_async_copy(option, target, sem).start()


def fetch_wait(options, index, target, sem):
    for z, option in enumerate(options):
        if option is not None:

            @pl.when(index == z)
            def _():
                pltpu.make_async_copy(option, target, sem).wait()


def step_body(has, first_step, widen, pieces, tokens):
    pairs = len(has)

    def body(place, *rest):
        rest = list(rest)
        take = lambda n: [rest.pop(0) for _ in range(n)]
        sides = []
        for d in range(2):
            totals = [take(1)[0] if h else None for h in has]
            keeps = [take(1)[0] if h else None for h in has]
            sides.append((totals, keeps))
        got = None if first_step else take(2)
        chunk = take(2) if widen else None
        piece_refs = take(pieces)
        take(tokens)
        sends = take(2)
        token = take(1)[0]
        spots = (place[1], pairs - 1 - place[1])
        for d, (totals, keeps) in enumerate(sides):
            for n in range(pairs):
                z = n if d == 0 else pairs - 1 - n
                send = sends[(z + d) % 2]

                @pl.when(spots[d] == n)
                def _():
                    if not has[n]:
                        send[...] = jnp.zeros(send.shape, F32)
                    elif got is None or n == 0:
                        send[...] = totals[n][...]
                    else:
                        send[...] = totals[n][...] + keeps[n][0:1, :] * got[(z + 1 + d) % 2][...]

        token[...] = jnp.zeros(token.shape, F32)
        if widen:
            put_chunk(take(1)[0], *chunk, piece_refs)

    return body


def within_body(base, heads, head_width):
    def body(own_ref, v_ref, g_ref, rate, token, y_out, x_out, keys_out, steps_out, cols_s):
        own = own_pack(own_ref, heads)
        length, width = g_ref.shape
        write, read = own.write.astype(BF), own.read.astype(BF)
        scores = mm(read, write, 1, 1)
        i, j = iotas(length, length)
        low = i > j
        high = i < j
        doubled = jnp.where(i == j, 2.0, 1.0).astype(F32)
        scores2 = scores * doubled
        turned = own_ref[:, 2 * LANES : 3 * LANES].T
        lane = lax.broadcasted_iota(jnp.int32, (length, LANES), 1)
        d_scores = jnp.zeros((length, length), F32)
        out_low = jnp.zeros((length, LANES), F32)
        out_high = jnp.zeros((length, LANES), F32)
        cols_s[...] = jnp.zeros(cols_s.shape, F32)
        v_all = v_ref[...].reshape(length, width)
        per = LANES // head_width
        for n in range(width // LANES):
            at = slice(n * LANES, (n + 1) * LANES)
            v, g = v_all[:, at], g_ref[:, at]
            mine = [(lane >= m * head_width) & (lane < (m + 1) * head_width) for m in range(per)]
            v_heads = jnp.concatenate([jnp.where(x, v, jnp.zeros_like(v)) for x in mine], axis=0)
            g_heads = jnp.concatenate([jnp.where(x, g, jnp.zeros_like(g)) for x in mine], axis=0)
            products = mm(g_heads, v, 1, 1)
            plains, steppeds = [], []
            for m in range(per):
                h = base + n * per + m
                c_col = own.total[:, h : h + 1]
                e_col = own.before[:, h : h + 1]
                dt_row = turned[h : h + 1, :]
                c_row = turned[heads + h : heads + h + 1, :]
                e_row = turned[2 * heads + h : 2 * heads + h + 1, :]
                decay = jnp.exp(jnp.where(low, c_row - c_col, e_col - e_row))
                plain = decay * scores2
                plains.append(plain.astype(BF))
                steppeds.append((plain * dt_row).astype(BF))
                inner = decay * dt_row * products[m * length : (m + 1) * length]
                d_scores = d_scores + inner
                flow = inner * scores
                flow_low = jnp.where(low, flow, 0.0)
                flow_high = jnp.where(high, flow, 0.0)
                out_low = jnp.where(lane == h, jnp.sum(flow_low, 1, keepdims=True), out_low)
                out_high = jnp.where(lane == h, jnp.sum(flow_high, 1, keepdims=True), out_high)
                cols_s[0, h : h + 1, :] = jnp.sum(flow_low, 0, keepdims=True)
                cols_s[1, h : h + 1, :] = jnp.sum(flow_high, 0, keepdims=True)
            y_out[:, at] = mm(jnp.concatenate(steppeds, axis=1), v_heads)
            x_out[:, at] = mm(jnp.concatenate(plains, axis=0), g_heads, 0, 0)
        d_scores = (d_scores * doubled).astype(BF)
        keys_out[:, 0:LANES] = mm(d_scores, read, 0, 0)
        keys_out[:, LANES : 2 * LANES] = mm(d_scores, write)
        net_low = out_low - cols_s[0].T
        net_high = out_high - cols_s[1].T
        at_or_after = (j >= i).astype(BF)
        after = (j > i).astype(BF)
        steps_out[...] = -rate[...] * (mm_exact(at_or_after, net_low) - mm_exact(after, net_high))

    return body


def post_body(base, heads, head_width, ups, downs, columns=False):
    def body(
        place, own_ref, v_ref, g_ref, yw, xw, keys_w, steps_w, near, keep, skip, rate, token, *rest
    ):
        up_in, down_in = rest[0:ups], rest[ups : ups + downs]
        mixed, dv_out, keys_out, steps_out, bufs, sems = rest[ups + downs :]
        up_spot, down_spot = place[1], len(up_in) - 1 - place[1]
        fetch_start(up_in, up_spot, bufs.at[0], sems.at[0])
        fetch_start(down_in, down_spot, bufs.at[1], sems.at[1])
        first = place[0] == 0
        own = own_pack(own_ref, heads)
        length, width = g_ref.shape
        far_row = keep[1:2, :]
        own_row, gain = spread_rows([own.through, skip[...]], base, width, head_width)
        up_row = jnp.where(first, 1.0, far_row)
        down_row = jnp.where(first, far_row, 1.0)
        dt, from_start, from_end, to_end, to_start = spread(
            [own.dt, own.from_start, own.from_end, own.to_end, own.to_start],
            base, width, head_width,
        )
        write, read = own.write.astype(BF), own.read.astype(BF)
        v = v_ref[...].reshape(length, width).astype(F32)
        g = g_ref[...].astype(F32)
        fetch_wait(up_in, up_spot, bufs.at[0], sems.at[0])
        fetch_wait(down_in, down_spot, bufs.at[1], sems.at[1])
        if columns:
            up = up_row * bufs[0] + near[0][...]
            down = down_row * bufs[1] + near[1][...]
        else:
            up = up_row * bufs[0] + jnp.where(first, 0.0, near[...])
            down = down_row * bufs[1] + jnp.where(first, near[...], 0.0)
        p, ab = up[0:LANES], up[LANES : 2 * LANES]
        q, af = down[0:LANES], down[LANES : 2 * LANES]
        crossing = jnp.sum(p * af + q * ab, axis=0, keepdims=True)
        p, q, af, ab = p.astype(BF), q.astype(BF), af.astype(BF), ab.astype(BF)
        y_p = from_start * mm(read, p)
        y_q = from_end * mm(read, q)
        x_f = to_end * mm(write, af)
        x_b = to_start * mm(write, ab)
        mixed[...] = (yw[...] + y_p + y_q + gain * v).astype(BF)
        x = xw[...] + x_f + x_b
        dv_out[...] = (dt * x + gain * g).astype(BF)
        dtv = dt * v
        keys_out[:, 0:LANES] = (
            keys_w[:, 0:LANES]
            + mm((to_end * dtv).astype(BF), af, 1, 1)
            + mm((to_start * dtv).astype(BF), ab, 1, 1)
        )
        keys_out[:, LANES : 2 * LANES] = (
            keys_w[:, LANES : 2 * LANES]
            + mm((from_start * g).astype(BF), p, 1, 1)
            + mm((from_end * g).astype(BF), q, 1, 1)
        )
        lane = lax.broadcasted_iota(jnp.int32, (length, LANES), 1)
        steps = jnp.where(lane < heads, own_ref[:, 2 * LANES : 3 * LANES], 0.0)
        direct, a_p, a_q, b_f, b_b, through = gather_heads(
            [v * x, g * y_p, g * y_q, v * x_f, v * x_b, jnp.broadcast_to(crossing * own_row, (8, width))],
            base, head_width,
        )
        i, j = iotas(length, length)
        masks = jnp.concatenate([j >= i, j <= i, j < i, j > i], axis=1).astype(F32).astype(BF)
        high, low = halves(jnp.concatenate([a_p, a_q, b_f * steps, b_b * steps], axis=0))
        flow = mm(masks, high) + mm(masks, low) + through[0:1]
        steps_out[...] = steps_w[...] + direct - rate[...] * flow

    return body


class Either:
    def __init__(self, choice, a, b):
        self.choice, self.a, self.b = choice, a, b

    def __getitem__(self, index):
        return jnp.where(self.choice, self.a[index], self.b[index])


def either_within(post):
    def body(place, own_ref, v_ref, g_ref, *rest):
        merged = [Either(place[3] == 0, a, b) for a, b in zip(rest[0:4], rest[4:8])]
        post(place, own_ref, v_ref, g_ref, *merged, *rest[8:])

    return body


def split_body(within, post, columns):
    def body(place, own_ref, v_ref, g_ref, *rest):
        bufs, sems, yw, xw, keys_w, steps_w, cols_s = rest[-7:]
        before, rest = rest[0:4], rest[4:]
        nears = 2 if columns else 1
        near = rest[0:2] if columns else rest[0]
        keep, skip, rate, token, *rest = rest[nears:]

        @pl.when(place[3] == 1)
        def _():
            within(own_ref, v_ref, g_ref, rate, token, yw, xw, keys_w, steps_w, cols_s)

        merged = [Either(place[3] == 0, a, b) for a, b in zip(before, (yw, xw, keys_w, steps_w))]
        post(place, own_ref, v_ref, g_ref, *merged, near, keep, skip, rate, token, *rest[:-5])

    return body


def turn_body(works, strands, turn):
    def body(place, pack0, pack1, rate, *rest):
        count = len(works)
        blocks, token = rest[0 : 2 * count], rest[2 * count]
        outs, flows = rest[2 * count + 1 : -1], rest[-1]

        @pl.when(place[3] == turn)
        def _():
            for n, work in enumerate(works):
                work(
                    (pack0, pack1)[strands[n]], blocks[2 * n], blocks[2 * n + 1], rate, token,
                    *outs[4 * n : 4 * n + 4], flows,
                )

    return body


def chunk_body(within, post, columns):
    def body(place, own_ref, v_ref, g_ref, *rest):
        nears = 2 if columns else 1
        near = rest[0:2] if columns else rest[0]
        keep, skip, rate, token, *rest = rest[nears:]
        bufs, sems, yw, xw, keys_w, steps_w, cols_s = rest[-7:]
        within(own_ref, v_ref, g_ref, rate, token, yw, xw, keys_w, steps_w, cols_s)
        post(
            place, own_ref, v_ref, g_ref, yw, xw, keys_w, steps_w, near, keep, skip, rate, token,
            *rest[:-5],
        )

    return body


def partial_body(groups, more):
    def body(token, *rest):
        dvs, weights, rest = rest[0:groups], rest[groups : 2 * groups], rest[2 * groups :]
        out = rest[-1]
        for at in columns_of(out.shape[1]):
            total = rest[0][:, at] if more else 0.0
            for dv, weight in zip(dvs, weights):
                total = total + mm(dv[...], weight[at, :], 1, 1)
            out[:, at] = total

    return body


def term_body(groups, tails, heads, parts, swap):
    def body(place, own_ref, select, step, before, *rest):
        dvs, weights = rest[0:tails], rest[tails : 2 * tails]
        rest = rest[2 * tails :]
        keys, steps = rest[0:groups], rest[groups : 2 * groups]
        outs = rest[2 * groups :]
        d_keys, d_steps = keys[0][...], steps[0][...]
        for a, b in zip(keys[1:], steps[1:]):
            d_keys = d_keys + a[...]
            d_steps = d_steps + b[...]
        d_raw = d_steps[:, 0:heads] * own_ref[:, 2 * LANES + 3 * heads : 2 * LANES + 4 * heads]
        keys_high, keys_low = halves(d_keys)
        raw_high, raw_low = halves(d_raw)
        width = select.shape[0]
        block = width // parts
        tiles = []
        for b in range(parts):
            rows = slice(b * block, (b + 1) * block)
            total = before[:, rows]
            total = total + mm(keys_high, select[rows, :], 1, 1) + mm(keys_low, select[rows, :], 1, 1)
            total = total + mm(raw_high, step[:, rows]) + mm(raw_low, step[:, rows])
            for k in range(tails):
                total = total + mm(dvs[k][...], weights[k][rows, :], 1, 1)
            tiles.append(total)
        if swap:
            tiles = tiles[::-1]
        if parts == 2:
            first = place[2] == 0
            outs[0][...] = jnp.where(first, tiles[0], tiles[1])
            outs[1][...] = jnp.where(first, tiles[1], tiles[0])
        else:
            for b in range(parts):
                outs[0][:, b * block : (b + 1) * block] = tiles[b]

    return body


def tile_body(groups, tails, heads, swap, keep):
    def body(place, own_ref, select, step, before, *rest):
        dvs, weights = rest[0:tails], rest[tails : 2 * tails]
        rest = rest[2 * tails :]
        keys, steps, out = rest[0:groups], rest[groups : 2 * groups], rest[-1]
        d_keys, d_steps = keys[0][...], steps[0][...]
        for a, b in zip(keys[1:], steps[1:]):
            d_keys = d_keys + a[...]
            d_steps = d_steps + b[...]
        d_raw = d_steps[:, 0:heads] * own_ref[:, 2 * LANES + 3 * heads : 2 * LANES + 4 * heads]
        keys_high, keys_low = halves(d_keys)
        raw_high, raw_low = halves(d_raw)
        block = out.shape[1]
        mine = place[2] if keep != swap else 1 - place[2]
        rows = pl.ds(pl.multiple_of(mine * block, block), block)
        total = before[:, rows]
        total = total + mm(keys_high, select[rows, :], 1, 1) + mm(keys_low, select[rows, :], 1, 1)
        total = total + mm(raw_high, step[:, rows]) + mm(raw_low, step[:, rows])
        for dv, weight in zip(dvs, weights):
            total = total + mm(dv[...], weight[rows, :], 1, 1)
        out[...] = total

    return body


def last_body(work, term, work_ins):
    def body(place, *rest):
        rest = list(rest)
        take = lambda n: [rest.pop(0) for _ in range(n)]
        for_work = take(work_ins)
        select, step, before, weight = take(4)
        others = take(len(rest) - 7)
        half = len(others) // 2
        mixed, dv, keys, steps, out = take(5)
        bufs, sems = take(2)
        work(place, *for_work, mixed, dv, keys, steps, bufs, sems)
        term(
            place, for_work[0], select, step, before, dv, weight,
            *others[:half], keys, *others[half:], steps, out,
        )

    return body


def finish_body(flip):
    def body(a, b, out):
        total = (a[...] + b[...]).astype(BF)
        if not flip:
            out[...] = total
            return
        width = total.shape[1]
        block = flip_block(width)
        turn = reversal(block)
        for j in range(width // block):
            out[:, j * block : (j + 1) * block] = mm(
                total[:, width - (j + 1) * block : width - j * block], turn
            ).astype(BF)

    return body


def put_chunk(wide, v_ref, g_ref, pieces):
    length, width = g_ref.shape
    wide[0:length, :] = v_ref[...].reshape(length, width).astype(F32)
    wide[length : 2 * length, :] = g_ref[...].astype(F32)
    for n, piece in enumerate(pieces):
        put_piece(wide, 2 * length + n * piece_rows(length, width), piece[...])


def widen_body(v_ref, g_ref, token, *rest):
    put_chunk(rest[-1], v_ref, g_ref, rest[:-1])


def local(shards, parts):
    pairs = shards // 2

    def body(
        hidden, complement, inner_weight, select_weight, step_weight, step_bias, decay_rate,
        skip_gain, cotangent, complement_cotangent,
    ):
        length, width = hidden.shape
        inner = inner_weight.shape[1]
        heads = step_bias.shape[0]
        head_width = inner // heads
        groups = 4
        chunk = inner // groups
        group_heads = heads // groups
        seq = lax.axis_index("seq")
        place = jnp.stack(
            [seq % 2, seq // 2, lax.axis_index("chan"), lax.axis_index("dp")]
        ).astype(jnp.int32)
        bias = step_bias.reshape(1, heads)
        rate = decay_rate.reshape(1, heads)
        rate_row = jnp.pad(rate, ((0, 0), (0, LANES - heads)))
        gain = skip_gain.reshape(1, heads)
        step_rows = step_weight.T
        cots = (cotangent, complement_cotangent)
        swap_pairs = [(a, a ^ 1) for a in range(shards)]
        edges = []
        for start in range(2):
            meets = [(z, z + 1) for z in range(start, pairs - 1, 2)]
            paired = sum(meets, ())
            meets += [(b, a) for a, b in meets] + [(z, z) for z in range(pairs) if z not in paired]
            edges.append([(2 * a + y, 2 * b + y) for a, b in meets for y in range(2)])
        swap = lambda x: lax.ppermute(x, "seq", swap_pairs)
        pack_shape = (length, 3 * LANES)
        pair_shape = (2 * LANES, chunk)
        wide_shape = lambda pieces: sds((2 * length + pieces * piece_rows(length, chunk), chunk))
        token_shape = sds((8, LANES))
        work = lambda: [pltpu.VMEM((2,) + pair_shape, F32), pltpu.SemaphoreType.DMA((2,))]
        order = [(1, groups - 1)] + [(0, k) for k in range(groups)] + [(1, k) for k in range(groups - 1)]
        chunks = len(order)

        source, pack0, pack1, row, v_zero, wide = run(
            start_body,
            [*map(Copied, (hidden, complement, select_weight, step_rows, bias, rate)),
             Copied(Block(inner_weight, (width, chunk), (0, 0))),
             Copied(Block(cots[0], (length, chunk), (0, 0)))],
            [sds((2 * length, width), BF), sds(pack_shape), sds(pack_shape), token_shape,
             sds((1, 2, length, chunk), BF), wide_shape(3)],
            limit=57,
        )
        packs = (pack0, pack1)
        far_row = swap(row)

        def weight_of(k):
            return Block(inner_weight, (width, chunk), (0, k))

        def do_values(ks, token):
            return run(
                values_body,
                [source, Far(token), *map(weight_of, ks)],
                [sds((len(ks), 2, length, chunk), BF)],
            )[0]

        v_last, *own_states = run(
            column_body((groups - 1) * group_heads, heads, head_width),
            [pack1, source, Copied(weight_of(groups - 1)),
             Block(cots[1], (length, chunk), (0, groups - 1))],
            [sds((1, 2, length, chunk), BF), sds(pair_shape), sds(pair_shape)],
            limit=48,
        )
        v_more = None

        def value_block(c):
            s, k = order[c]
            array, n = {0: (v_zero, 0), groups - 1: (v_last, 0)}.get(k, (v_more, k - 1))
            return Block(array, (1, 1, length, chunk), (n, s, 0, 0))

        def cot_block(c):
            s, k = order[c]
            return Block(cots[s], (length, chunk), (0, k))

        def weight_block(c):
            return weight_of(order[c][1])

        far = {}
        totals, within, post = {}, {}, {}
        got = ([], [])
        grads = [None, None]
        riders = {2 + n: n for n in range(3)}
        columns = {}
        steps = chunks + pairs - 2

        def do_pair(c, token):
            s, k = order[c]
            rows = piece_rows(length, chunk)
            if s == 0:
                pieces, piece_at = [far[1]] * 3, [2 * length + n * rows for n in range(3)]
            else:
                pieces, piece_at = [far[r] for r in riders], [2 * length] * 3
            totals[c] = run(
                pair_body(k * group_heads, heads, head_width, piece_at),
                [place, value_block(c), cot_block(c), far[c], *pieces, packs[s], Far(token)],
                [sds(pair_shape), sds(pair_shape), sds(pair_shape), sds((8, chunk))],
            )
            return totals[c][3]

        within_shapes = [
            sds((length, chunk)), sds((length, chunk)), sds((length, 2 * LANES)), sds((length, LANES))
        ]
        post_shapes = [
            sds((length, chunk), BF), sds((length, chunk), BF), sds((length, 2 * LANES)), sds((length, LANES))
        ]
        flows = lambda: [pltpu.VMEM((2, LANES, length), F32)]

        def do_within(c, token):
            s, k = order[c]
            within[c] = run(
                within_body(k * group_heads, heads, head_width),
                [packs[s], value_block(c), cot_block(c), rate_row, Far(token)],
                within_shapes,
                scratch=flows(),
            )
            return within[c][3]

        def do_turn(cs, turn, token):
            blocks = [b for c in cs for b in (value_block(c), cot_block(c))]
            works = [within_body(order[c][1] * group_heads, heads, head_width) for c in cs]
            out = run(
                turn_body(works, [order[c][0] for c in cs], turn),
                [place, *packs, rate_row, *blocks, Far(token)],
                within_shapes * len(cs),
                scratch=flows(),
            )
            for n, c in enumerate(cs):
                within[c] = within.get(c, []) + list(out[4 * n : 4 * n + 4])
            return out[3]

        def post_parts(c, token):
            s, k = order[c]
            last = pairs - 1
            ups = [got[(z + 1) % 2][max(c + z - 1, c, 1 - z)] for z in range(pairs)]
            downs = [got[(last - z) % 2][max(c + z - 1, c, 1 - z)] for z in range(pairs)]
            body = post_body(k * group_heads, heads, head_width, len(ups), len(downs), c == 0)
            work = within_body(k * group_heads, heads, head_width)
            if len(within.get(c, ())) == 8:
                body = either_within(body)
            elif c in within:
                body = split_body(work, body, c == 0)
            else:
                body = chunk_body(work, body, c == 0)
            near = columns["far"] if c == 0 else [totals[c][2]]
            ins = [packs[s], value_block(c), cot_block(c), *within.get(c, []),
                   *near, totals[c][3], gain, rate_row, Far(token),
                   *map(Far, ups), *map(Far, downs)]
            return body, ins

        def do_chunk(c, token):
            body, ins = post_parts(c, token)
            more = [pltpu.VMEM(o.shape, o.dtype) for o in within_shapes] + flows()
            post[c] = run(body, [place, *ins], post_shapes, stored=(0,), scratch=work() + more)
            return post[c][3]

        def do_partial(cs, token, before=None):
            return run(
                partial_body(len(cs), before is not None),
                [Far(token), *[post[c][1] for c in cs], *[weight_block(c) for c in cs]]
                + ([] if before is None else [before]),
                [sds((length, width))],
            )[0]

        shares = [sds((length, width // parts))] * 2 if parts == 2 else [sds((length, width))]

        def send_share(term):
            if parts == 2:
                return term[0], lax.ppermute(term[1], "chan", [(0, 1), (1, 0)])
            share = lax.psum_scatter(term[0], "chan", scatter_dimension=1, tiled=True)
            return share, jnp.zeros_like(share)

        def do_term(s, before):
            mine = [c for c in range(chunks) if order[c][0] == s]
            return send_share(run(
                term_body(len(mine), 0, heads, parts, s == 1),
                [place, packs[s], select_weight, step_rows, before,
                 *[post[c][2] for c in mine], *[post[c][3] for c in mine]],
                shares,
            ))

        def do_last(c, before, token):
            s = order[c][0]
            mine = [n for n in range(chunks) if order[n][0] == s and n != c]
            body, ins = post_parts(c, token)
            sums = [select_weight, step_rows, before]
            others = [[post[n][k] for n in mine] for k in (2, 3)]
            if parts == 2:
                term = tile_body(len(mine) + 1, 1, heads, s == 1, False)
            else:
                term = term_body(len(mine) + 1, 1, heads, parts, s == 1)
            post[c] = run(
                last_body(body, term, len(ins)),
                [place, *ins, *sums, weight_block(c), *others[0], *others[1]],
                [*post_shapes, shares[0]],
                scratch=work(),
            )
            if parts != 2:
                return send_share(post[c][4:])
            arriving = lax.ppermute(post[c][4], "chan", [(0, 1), (1, 0)])
            kept = run(
                tile_body(len(mine) + 1, 1, heads, s == 1, True),
                [place, packs[s], *sums, post[c][1], weight_block(c),
                 *others[0], post[c][2], *others[1], post[c][3]],
                [shares[0]],
            )[0]
            return kept, arriving

        def do_finish(s, share):
            return run(
                finish_body(s == 1), list(share), [sds((length, width // parts), BF)], stored=(0,)
            )[0]

        def do_step(k, widen, ends):
            has = [0 <= k - z < chunks and z < pairs - 1 for z in range(pairs)]
            ins = [place]
            for d in range(2):
                ins += [totals[k - z][d] for z in range(pairs) if has[z]]
                ins += [totals[k - z][3] for z in range(pairs) if has[z]]
            if k > 0:
                ins += [got[0][-1], got[1][-1] if k > 1 else got[0][-1]]
            outs = [sds(pair_shape), sds(pair_shape), token_shape]
            pieces = [] if widen is None else pieces_of(widen)
            if widen is not None:
                ins += [value_block(widen), cot_block(widen), *pieces]
                outs.append(wide_shape(len(pieces)))
            return run(
                step_body(has, k == 0, widen is not None, len(pieces), len(ends)),
                ins + [Far(e) for e in ends],
                outs,
            )

        def do_first_step(ends):
            s, k = order[0]
            out = run(
                first_step_body(pairs, k * group_heads, heads, head_width, len(ends)),
                [place, packs[s], far_row, *own_states, *map(Far, ends)],
                [sds(pair_shape), sds(pair_shape), token_shape, sds(pair_shape), sds(pair_shape),
                 sds((8, chunk))],
            )
            totals[0] = (out[3], out[4], None, out[5])
            columns["own"] = own_states
            return out

        def do_exchange(token):
            last = pairs - 1
            ups = [got[(z + 1) % 2][max(z - 1, 1 - z)] for z in range(pairs)]
            downs = [got[(last - z) % 2][max(z - 1, 1 - z)] for z in range(pairs)]
            sends = run(
                exchange_body(len(ups), len(downs)),
                [place, *columns["own"], totals[0][3], Far(token), *map(Far, ups), *map(Far, downs)],
                [sds(pair_shape), sds(pair_shape)],
                scratch=work(),
            )
            columns["far"] = [swap(x) for x in sends]

        def pieces_of(c):
            return [Block(packs[1], (length, LANES), (0, riders[c]))] if c in riders else []

        def do_widen(c, token):
            pieces = pieces_of(c)
            return run(
                widen_body, [value_block(c), cot_block(c), Far(token), *pieces], [wide_shape(len(pieces))]
            )[0]

        far[1] = swap(lax.optimization_barrier((wide, far_row))[0])
        ends = []
        halfway = None
        share = None
        for k in range(steps):
            queue = k + 2 if 0 < k < chunks - 2 else None
            made = do_first_step(ends) if k == 0 else do_step(k, queue, ends)
            token = made[2]
            got[0].append(lax.ppermute(made[0], "seq", edges[0]))
            got[1].append(lax.ppermute(made[1], "seq", edges[1]) if 0 < k < steps - 1 else None)
            ends = []
            if k == 0:
                v_more = do_values(list(range(1, groups - 1)), token)
                far[2] = swap(do_widen(2, token))
            if queue is not None:
                far[queue] = swap(made[3])
            if k + 1 < chunks:
                ends.append(do_pair(k + 1, token))
            if k == max(chunks - 2, pairs - 1):
                do_exchange(far[chunks - 1])
            if k == steps - 3:
                ends.append(columns["far"][0])
            for cs in {1: [(2, 3)], 2: [(4, 5)], 3: [(6, 0)], 4: [(7,)]}.get(k, ()):
                ends.append(do_turn(cs, 0, token))
            if k == steps - 1:
                do_turn((7,), 1, token)
            c = k - pairs + 1
            if c > 0:
                late = columns["far"][1] if k == steps - 2 else token
                ends.append(do_chunk(c, late))
            if c == groups - 2:
                halfway = do_partial(list(range(1, groups - 1)), token)
                ends.append(halfway)
            if c == groups:
                share = do_term(0, do_partial([groups - 1, groups], token, halfway))
                ends.append(share[0])
            if c == groups + 1:
                ends.append(do_chunk(0, token))
            if c == groups + 2:
                grads[0] = do_finish(0, share)
                halfway = do_partial([groups + 1, 0, groups + 2], token)
        grads[1] = do_finish(1, do_last(chunks - 1, halfway, halfway))
        outs = [
            jnp.concatenate([post[order.index((s, k))][0] for k in range(groups)], axis=1)
            for s in range(2)
        ]
        return (outs[0], outs[1], grads[0], grads[1])

    return body


def solution(mesh):
    rows = P(("dp", "seq"), None)
    both = P(("dp", "seq"), "chan")
    in_specs = (
        rows, rows, P(None, "chan"), P(), P(None, "chan"),
        P("chan"), P("chan"), P("chan"), both, both,
    )
    return jax.shard_map(
        local(mesh.shape["seq"], mesh.shape["chan"]),
        mesh=mesh,
        in_specs=in_specs,
        out_specs=(both,) * 4,
        check_vma=False,
    )
```
